128 devices in a mesh: section: 2 (over core), kv: 16 (over z, y), tp: 4 (over x).
Axes of the slice: x: 4, y: 4, z: 4, core: 2. Of those that a mesh axis runs over, the one named last changes fastest.
Arguments:
- segments_in: bfloat16 [3, 128, 8192], P(None, None, 'kv'), may hold values from -12 to 12
- gain: float32 [2, 8192], P('section', 'kv'), may hold values from 0.1 to 1.9
- query_weight: bfloat16 [2, 8192, 8192], P('section', 'kv', 'tp'), may hold values from -0.0625 to 0.0625
- kv_weight: bfloat16 [2, 8192, 2, 1024], P('section', 'kv', None, 'tp'), may hold values from -0.0625 to 0.0625
- out_weight: bfloat16 [2, 8192, 8192], P('section', 'tp', 'kv'), may hold values from -1 to 1
- kv_cache: bfloat16 [2, 24576, 2, 1024], P('section', 'kv', None, 'tp'), may hold values from -110 to 110
- block_logical: int32 [192], P('kv'), may hold values from 0 to 191, each once
- segment_block: int32 [3], replicated, may hold values from 48 to 192, as said below
Outputs:
- hidden_states: bfloat16 [2, 3, 128, 8192], P('section', None, None, 'kv')
The draws below stay inside these ranges and needn't reach their ends.
Inputs may be any that keep to these rules, and one draw needn't show every extreme that they name: Stored block b is held by kv index b // 12 and covers the positions from block_logical[b] * 128 on; each block number appears once. Segment s starts at position segment_block[s] * 128; the last segment starts at block 192.
All inputs are finite; a program needn't handle non-finite values.
Results may differ from the reference program's by a relative error of at most 0.03.
Values may be sent and summed in bfloat16 or wider, within the bound.
No kernel may reach another device: no remote copies, remote signals or barrier semaphores. Data moves between devices by JAX's collectives and lax.ppermute only.
A program may use at most 128 MiB of HBM per device.

```python
import math
import jax
import jax.numpy as jnp
from jax import lax

D = 8192
HEADS = 64
KV_HEADS = 8
HEAD_DIM = 128
SEG_LEN = 128
BLOCK = 128
NSEG = 3
LAYERS = 2
NBLK = 192
PRIOR = 24576


def draw_kv_cache(key, part):
    key = jax.random.fold_in(key, 11)
    shape = (LAYERS, PRIOR, 2, KV_HEADS * HEAD_DIM)
    values = jax.random.normal(key, shape, jnp.float32)
    return jnp.clip(values, -6.0, 6.0).astype(jnp.bfloat16)


def draw_segments_in(key, part):
    key = jax.random.fold_in(key, 37)
    shape = (NSEG, SEG_LEN, D)
    ramp = jnp.arange(D, dtype=jnp.float32) / max(D - 1, 1) - 0.5
    base = jnp.clip(jax.random.normal(key, shape, jnp.float32), -6.0, 6.0)
    column_scale = jnp.exp(ramp * math.log(3.0))
    return (base * column_scale[None, None, :]).astype(jnp.bfloat16)


def draw_segment_block(key, part):
    key = jax.random.fold_in(key, 23)
    starts = jax.random.randint(key, (NSEG,), NBLK // 4, NBLK + 1)
    return starts.at[NSEG - 1].set(NBLK).astype(jnp.int32)


def shard_levels(key, shape, cuts, low, top_value):
    factor_of = 1.0
    for axis_at, shards_of in cuts:
        steps = jax.random.uniform(jax.random.fold_in(jax.random.fold_in(key, 6), axis_at), (shards_of,), jnp.float32, low / len(cuts), top_value / len(cuts))
        factor_of = factor_of * jnp.repeat(jnp.exp(steps), shape[axis_at] // shards_of).reshape((-1,) + (1,) * (len(shape) - 1 - axis_at))
    return factor_of


def normal_values(own_key, dims, width, limit, shards=(), kind=jnp.bfloat16):
    result = jax.random.normal(own_key, dims, jnp.float32) * width
    if len(shards) > 0:
        result = shard_levels(own_key, dims, shards, -0.22, 0.18) * result
    return jnp.clip(result, min=-limit, max=limit).astype(kind)


def setup_inputs(seed: int = 0) -> dict:
    splits = jax.random.split(jax.random.key(seed), 9)
    return {
        "segments_in": draw_segments_in(jax.random.fold_in(splits[8], 71), 0),
        "gain": jnp.clip(1.0 + 0.18 * jax.random.normal(splits[1], (LAYERS, D), jnp.float32), 0.1, 1.9),
        "query_weight": normal_values(splits[2], (LAYERS, D, HEADS * HEAD_DIM), D ** -0.5, 0.0625, ((0, 2), (1, 16), (2, 4))),
        "kv_weight": normal_values(splits[3], (LAYERS, D, 2, KV_HEADS * HEAD_DIM), D ** -0.5, 0.0625, ((0, 2), (1, 16), (3, 4))),
        "out_weight": normal_values(splits[4], (LAYERS, HEADS * HEAD_DIM, D), (max(HEADS * HEAD_DIM // 256, 1)) ** -0.5, 1.0, ((0, 2), (1, 4), (2, 16))),
        "kv_cache": draw_kv_cache(jax.random.fold_in(splits[8], 71), 0),
        "block_logical": jax.random.permutation(splits[6], NBLK).astype(jnp.int32),
        "segment_block": draw_segment_block(jax.random.fold_in(splits[8], 71), 0),
    }


EPSILON = 1e-05
NEGATIVE = -1e+30

def attend_layer(hidden_in, gain_row, query_proj, kv_proj, out_proj, cache_layer, cache_open, causal_open):
    as_float = hidden_in.astype(jnp.float32)
    normed = (as_float * lax.rsqrt(lax.optimization_barrier(jnp.mean(as_float * as_float, axis=1, keepdims=True)) + EPSILON) * gain_row[None, :]).astype(jnp.bfloat16)
    queries = jnp.dot(normed, query_proj, preferred_element_type=jnp.float32).astype(jnp.bfloat16)
    fresh = jnp.dot(normed, kv_proj.reshape(D, 2 * KV_HEADS * HEAD_DIM), preferred_element_type=jnp.float32).astype(jnp.bfloat16)
    fresh = fresh.reshape(SEG_LEN, 2, KV_HEADS, HEAD_DIM)
    group_size = HEADS // KV_HEADS
    query_heads = queries.reshape(SEG_LEN, KV_HEADS, group_size, HEAD_DIM).transpose(1, 0, 2, 3)
    cache_keys = cache_layer[:, 0].reshape(PRIOR, KV_HEADS, HEAD_DIM).transpose(1, 0, 2)
    cache_values = cache_layer[:, 1].reshape(PRIOR, KV_HEADS, HEAD_DIM).transpose(1, 0, 2)
    fresh_keys = fresh[:, 0].transpose(1, 0, 2)
    fresh_values = fresh[:, 1].transpose(1, 0, 2)
    allowed = jnp.concatenate([jnp.broadcast_to(cache_open[None, :], (SEG_LEN, PRIOR)), causal_open], axis=1)
    inv_scale = 1.0 / math.sqrt(HEAD_DIM)

    def one_head(items):
        head_queries, head_ckeys, head_cvalues, head_nkeys, head_nvalues = items
        all_keys = jnp.concatenate([head_ckeys, head_nkeys], axis=0).astype(jnp.float32)
        all_values = jnp.concatenate([head_cvalues, head_nvalues], axis=0).astype(jnp.float32)
        scores = jnp.einsum('cgd,nd->gcn', head_queries.astype(jnp.float32), all_keys, precision=lax.Precision.HIGHEST) * inv_scale
        scores = jnp.where(allowed[None], scores, NEGATIVE)
        peak = lax.optimization_barrier(jnp.max(scores, axis=2, keepdims=True))
        weights = jnp.where(allowed[None], jnp.exp(scores - peak), 0.0)
        mass = lax.optimization_barrier(jnp.sum(weights, axis=2))
        rounded = lax.optimization_barrier(weights.astype(jnp.bfloat16)).astype(jnp.float32)
        weighted = jnp.einsum('gcn,nd->cgd', rounded, all_values, precision=lax.Precision.HIGHEST)
        return weighted / jnp.transpose(mass)[:, :, None]
    attended = lax.map(one_head, (query_heads, cache_keys, cache_values, fresh_keys, fresh_values))
    attended = attended.transpose(1, 0, 2, 3).reshape(SEG_LEN, HEADS * HEAD_DIM).astype(jnp.bfloat16)
    return (as_float + jnp.dot(attended, out_proj, preferred_element_type=jnp.float32)).astype(jnp.bfloat16)

def reference(segments_in, gain, query_weight, kv_weight, out_weight, kv_cache, block_logical, segment_block):
    causal_open = jnp.arange(SEG_LEN)[:, None] >= jnp.arange(SEG_LEN)[None, :]
    current = segments_in
    layer_outputs = []
    for layer_index in range(LAYERS):
        produced = []
        for seg_index in range(NSEG):
            open_blocks = block_logical < segment_block[seg_index]
            cache_open = jnp.broadcast_to(open_blocks[:, None], (NBLK, BLOCK)).reshape(PRIOR)
            produced.append(attend_layer(current[seg_index], gain[layer_index], query_weight[layer_index], kv_weight[layer_index], out_weight[layer_index], kv_cache[layer_index], cache_open, causal_open))
        current = jnp.stack(produced)
        layer_outputs.append(current)
    return jnp.stack(layer_outputs)
```

```python
import functools
import math

import jax
import jax.numpy as jnp
from jax import lax
from jax.experimental import pallas as pl
from jax.experimental.pallas import tpu as pltpu
from jax.sharding import PartitionSpec as P

D = 8192
HEAD_DIM = 128
BLOCK = 128
NSEG = 3
SEG_LEN = 128
TOKENS = NSEG * SEG_LEN
GROUP = 8
LAYERS = 2
EPSILON = 1e-05
CLOSED = -1e30
FLOOR = -134217728.0
RANGE = 32000.0
HEADS_STEP = 2
SCALE = math.log2(math.e) / math.sqrt(HEAD_DIM)
F32 = jnp.float32
BF16 = jnp.bfloat16
VMEM_BYTES = 48 * 1024 * 1024


def call(kernel, out_shape, in_specs, out_specs, **rest):
    return pl.pallas_call(
        kernel,
        out_shape=out_shape,
        in_specs=in_specs,
        out_specs=out_specs,
        compiler_params=pltpu.CompilerParams(vmem_limit_bytes=VMEM_BYTES),
        **rest,
    )


IN_VMEM = pl.BlockSpec(memory_space=pltpu.VMEM)
IN_SMEM = pl.BlockSpec(memory_space=pltpu.SMEM)


def encode(block):
    top = jnp.maximum(jnp.max(jnp.abs(block), axis=0, keepdims=True), 1e-30)
    level = jnp.ceil(jnp.log2(top) * 64.0)
    return jnp.round(block * (jnp.exp2(level * (-1.0 / 64.0)) * RANGE)), level


def stack_rows(rows):
    width = rows[0].shape[1]
    place = lax.broadcasted_iota(jnp.int32, (16, width), 0)
    filled = jnp.zeros((16, width), F32)
    for number, row in enumerate(rows):
        filled = jnp.where(place == number, row, filled)
    return filled


def short(value):
    return value.astype(jnp.int32).astype(jnp.int16)


def wide(value):
    return value.astype(jnp.int32).astype(F32)


def square_rows(x):
    squares = jnp.sum(x * x, axis=1, keepdims=True)
    squares = jnp.broadcast_to(squares, (x.shape[0], 128))
    missing = -x.shape[0] % 128
    if missing:
        squares = jnp.concatenate([squares, jnp.zeros((missing, 128), F32)], axis=0)
    return squares.T[0:8]


def norm_columns(parts_ref):
    total = parts_ref[0]
    for peer in range(1, parts_ref.shape[0]):
        total = total + parts_ref[peer]
    factor = lax.rsqrt(total[0:1] / D + EPSILON)
    return jnp.broadcast_to(factor, (128, factor.shape[1])).T


def squares_kernel(count, x_ref, out_ref):
    rows = square_rows(x_ref[...].astype(F32))
    for peer in range(count):
        out_ref[peer] = rows


def first_project_kernel(count, x_ref, squares_ref, gain_ref, query_ref, kv_ref, out_ref):
    factor = norm_columns(squares_ref)[:, 0:1]
    normed = (x_ref[...].astype(F32) * factor * gain_ref[...]).astype(BF16)
    project(count, normed, query_ref, kv_ref, out_ref)


def project_kernel(count, core_ref, own_ref, other_ref, gain_ref, query_ref, kv_ref, out_ref, x_ref):
    share = TOKENS // 2
    width = gain_ref.shape[1]
    x_ref[pl.ds(core_ref[0] * share, share), :] = own_ref[...]
    x_ref[pl.ds((1 - core_ref[0]) * share, share), :] = other_ref[...]
    thirds = x_ref[:, width : width + 128].astype(F32)
    factor = thirds[:, 0:1] + thirds[:, 1:2] + thirds[:, 2:3]
    normed = (x_ref[:, 0:width].astype(F32) * factor * gain_ref[...]).astype(BF16)
    project(count, normed, query_ref, kv_ref, out_ref)


def project(count, scaled, query_ref, kv_ref, out_ref):
    half = HEAD_DIM // 2
    columns = query_ref.shape[1]
    rows = SEG_LEN // count
    fresh = jnp.dot(scaled, kv_ref[...], preferred_element_type=F32)
    for start in range(0, columns, 256):
        part = jnp.dot(scaled, query_ref[:, start : start + 256], preferred_element_type=F32)
        turned = part.T
        for piece in range(256 // half):
            peer = start // half + piece
            query, query_level = encode(turned[piece * half : (piece + 1) * half])
            out_ref[peer, 0:half, :] = short(query)
            kinds = []
            for kind in range(2):
                lanes = slice(kind * HEAD_DIM, (kind + 1) * HEAD_DIM)
                block = jnp.concatenate(
                    [
                        fresh[seg * SEG_LEN + peer * rows : seg * SEG_LEN + (peer + 1) * rows, lanes]
                        for seg in range(NSEG)
                    ],
                    axis=1,
                )
                kinds.append(encode(block))
            out_ref[peer, half : half + 2 * rows, :] = short(
                jnp.concatenate([kinds[0][0], kinds[1][0]], axis=0)
            )
            out_ref[peer, half + 2 * rows : half + 2 * rows + 16, :] = short(
                stack_rows([query_level, kinds[0][1], kinds[1][1]])
            )


def finish_projection_kernel(count, parts_ref, query_out, fresh_out):
    half = HEAD_DIM // 2
    rows = SEG_LEN // count
    query = jnp.zeros((half, TOKENS), F32)
    fresh = [jnp.zeros((rows, TOKENS), F32) for _ in range(2)]
    for peer in range(count):
        notes = wide(parts_ref[peer, half + 2 * rows : half + 2 * rows + 16, :])
        factors = jnp.exp2(notes * (1.0 / 64.0)) * (1.0 / RANGE)
        query = query + wide(parts_ref[peer, 0:half, :]) * factors[0:1]
        both = wide(parts_ref[peer, half : half + 2 * rows, :])
        fresh[0] = fresh[0] + both[0:rows] * factors[1:2]
        fresh[1] = fresh[1] + both[rows : 2 * rows] * factors[2:3]
    query = query.astype(BF16)
    for peer in range(count):
        query_out[peer] = query
    filler = jnp.zeros((SEG_LEN - NSEG * rows, HEAD_DIM), F32)
    for kind in range(2):
        pieces = [
            fresh[kind][:, seg * SEG_LEN : (seg + 1) * SEG_LEN] for seg in range(NSEG)
        ]
        fresh_out[kind] = jnp.concatenate(pieces + [filler], axis=0).astype(BF16)


def attend_kernel(
    rows, index_ref, logical_ref, start_ref, query_ref, keys_ref, values_ref, fresh_ref,
    out_ref, all_keys, turned_values, scores, weights,
):
    blocks = keys_ref.shape[0] // BLOCK
    stored = blocks * BLOCK
    half = HEAD_DIM // 2

    @pl.when(pl.program_id(0) == 0)
    def _():
        all_keys[0:stored, :] = keys_ref[...]
        all_keys[stored : stored + SEG_LEN, :] = fresh_ref[0]
        for block in range(blocks):
            at = slice(block * BLOCK, (block + 1) * BLOCK)
            turned_values[:, at] = values_ref[at, :].T
        turned_values[:, stored : stored + SEG_LEN] = fresh_ref[1].T

    key_row = lax.broadcasted_iota(jnp.int32, (SEG_LEN, SEG_LEN), 0)
    token = lax.broadcasted_iota(jnp.int32, (SEG_LEN, SEG_LEN), 1)
    heads = query_ref.shape[0]
    for head in range(heads):
        scores[head] = jnp.dot(all_keys[...], query_ref[head], preferred_element_type=F32)
    for head in range(heads):
        peaks = []
        masses = []
        for seg in range(NSEG):
            lanes = slice(seg * SEG_LEN, (seg + 1) * SEG_LEN)
            local = key_row - seg * rows
            fresh_open = (local >= 0) & (local < rows) & (local + index_ref[0] * rows <= token)
            fresh_scores = jnp.where(
                fresh_open, scores[head, stored : stored + SEG_LEN, lanes] * SCALE, CLOSED
            )
            peak = jnp.max(fresh_scores, axis=0, keepdims=True)
            offsets = []
            for block in range(blocks):
                offset = jnp.where(logical_ref[block] < start_ref[seg], 0.0, CLOSED)
                offsets.append(offset)
                at = slice(block * BLOCK, (block + 1) * BLOCK)
                top = jnp.max(scores[head, at, lanes], axis=0, keepdims=True)
                peak = jnp.maximum(peak, top * SCALE + offset)
            peak = jnp.ceil(jnp.maximum(peak, FLOOR))
            weight = jnp.exp2(fresh_scores - peak)
            mass = weight
            weights[head, stored : stored + SEG_LEN, lanes] = weight.astype(BF16)
            for block in range(blocks):
                at = slice(block * BLOCK, (block + 1) * BLOCK)
                weight = jnp.exp2(scores[head, at, lanes] * SCALE + (offsets[block] - peak))
                mass = mass + weight
                weights[head, at, lanes] = weight.astype(BF16)
            peaks.append(peak)
            masses.append(jnp.sum(mass, axis=0, keepdims=True))
        sums = jnp.dot(turned_values[...], weights[head], preferred_element_type=F32)
        peak = jnp.concatenate(peaks, axis=1)
        mass = jnp.concatenate(masses, axis=1) * 16.0
        peak_high = jnp.floor(peak * (1.0 / 8192.0))
        mass_high = jnp.floor(mass)
        notes = [
            peak_high,
            peak - peak_high * 8192.0,
            mass_high,
            jnp.round((mass - mass_high) * RANGE),
        ]
        for piece in range(2):
            value, level = encode(sums[piece * half : (piece + 1) * half])
            out_ref[2 * head + piece, 0:half, :] = short(value)
            out_ref[2 * head + piece, half : half + 16, :] = short(stack_rows([level] + notes))


def combine_kernel(count, parts_ref, out_ref):
    half = HEAD_DIM // 2
    notes = [wide(parts_ref[peer, half : half + 16, :]) for peer in range(count)]
    peaks = [note[1:2] * 8192.0 + note[2:3] for note in notes]
    top = peaks[0]
    for peer in range(1, count):
        top = jnp.maximum(top, peaks[peer])
    mass = jnp.zeros((1, TOKENS), F32)
    sums = jnp.zeros((half, TOKENS), F32)
    for peer in range(count):
        note = notes[peer]
        factor = jnp.exp2(peaks[peer] - top)
        mass = mass + factor * ((note[3:4] + note[4:5] * (1.0 / RANGE)) * (1.0 / 16.0))
        factor = factor * (jnp.exp2(note[0:1] * (1.0 / 64.0)) * (1.0 / RANGE))
        sums = sums + factor * wide(parts_ref[peer, 0:half, :])
    attended = (sums / mass).astype(BF16)
    for peer in range(count):
        out_ref[peer] = attended


def output_kernel(core_ref, attended_ref, weight_ref, keep_ref, send_ref, scratch):
    share = TOKENS // 2
    scratch[...] = lax.dot_general(
        attended_ref[...], weight_ref[...], (((0,), (0,)), ((), ())), preferred_element_type=F32
    )
    keep_ref[...] = scratch[pl.ds(core_ref[0] * share, share), :]
    send_ref[...] = scratch[pl.ds((1 - core_ref[0]) * share, share), :]


def add_kernel(keep_ref, received_ref, out_ref):
    out_ref[...] = keep_ref[...] + received_ref[...]


def add_residual(parts_ref, x_ref):
    total = parts_ref[0]
    for peer in range(1, parts_ref.shape[0]):
        total = total + parts_ref[peer]
    return (x_ref[...].astype(F32) + total).astype(BF16)


def residual_kernel(count, parts_ref, x_ref, out_ref, squares_ref):
    produced = add_residual(parts_ref, x_ref)
    out_ref[...] = produced
    rows = square_rows(produced.astype(F32))
    for peer in range(count):
        squares_ref[peer] = rows


def last_residual_kernel(parts_ref, x_ref, out_ref):
    produced = add_residual(parts_ref, x_ref)
    for peer in range(out_ref.shape[0]):
        out_ref[peer] = produced


def spread_kernel(squares_ref, x_ref, out_ref):
    tokens, width = x_ref.shape
    factor = norm_columns(squares_ref)[0:tokens]
    first = factor.astype(BF16).astype(F32)
    second = (factor - first).astype(BF16).astype(F32)
    lane = lax.broadcasted_iota(jnp.int32, factor.shape, 1)
    thirds = jnp.where(lane == 0, first, jnp.where(lane == 1, second, factor - first - second))
    for peer in range(out_ref.shape[0]):
        out_ref[peer, :, 0:width] = x_ref[...]
        out_ref[peer, :, width : width + 128] = thirds.astype(BF16)


def choose_kernel(core_ref, own0_ref, other0_ref, own1_ref, other1_ref, out_ref):
    share = TOKENS // 2
    width = out_ref.shape[1]
    first = core_ref[0] == 0
    at = pl.ds(core_ref[0] * share, share)
    out_ref[at, :] = jnp.where(first, own0_ref[:, 0:width], own1_ref[...])
    at = pl.ds((1 - core_ref[0]) * share, share)
    out_ref[at, :] = jnp.where(first, other0_ref[:, 0:width], other1_ref[...])


def exchange(value, axes):
    return lax.all_to_all(value, axes, 0, 0, tiled=True)


def swap(value):
    return lax.ppermute(value, "section", [(0, 1), (1, 0)])


def layer(
    which, x, mine, gain, query_proj, kv_proj, out_proj, keys, values, logical, starts, index, core
):
    count = lax.axis_size("kv")
    peers = lax.axis_size("tp")
    rows = SEG_LEN // count
    half = HEAD_DIM // 2
    width = query_proj.shape[0]
    share = TOKENS // 2
    part = share // peers
    with jax.named_scope("project"):
        shape = jax.ShapeDtypeStruct((count, half + 2 * rows + 16, TOKENS), jnp.int16)
        if which == 0:
            squares = call(
                functools.partial(squares_kernel, count),
                jax.ShapeDtypeStruct((count, 8, TOKENS), F32),
                [IN_VMEM],
                IN_VMEM,
            )(x)
            squares = exchange(squares, "kv")
            sent = call(
                functools.partial(first_project_kernel, count), shape, [IN_VMEM] * 5, IN_VMEM
            )(x, squares, gain, query_proj, kv_proj)
        else:
            sent = call(
                functools.partial(project_kernel, count),
                shape,
                [IN_SMEM] + [IN_VMEM] * 5,
                IN_VMEM,
                scratch_shapes=[pltpu.VMEM((TOKENS, width + 128), BF16)],
            )(core, x[0], x[1], gain, query_proj, kv_proj)
        parts = exchange(sent, "kv")
    with jax.named_scope("queries"):
        query, fresh = call(
            functools.partial(finish_projection_kernel, count),
            (
                jax.ShapeDtypeStruct((count, half, TOKENS), BF16),
                jax.ShapeDtypeStruct((2, SEG_LEN, HEAD_DIM), BF16),
            ),
            [IN_VMEM],
            (IN_VMEM, IN_VMEM),
        )(parts)
        query = exchange(query, "kv").reshape(GROUP, HEAD_DIM, TOKENS)
    with jax.named_scope("attend"):
        stored = keys.shape[0]
        sent = call(
            functools.partial(attend_kernel, rows),
            jax.ShapeDtypeStruct((count, half + 16, TOKENS), jnp.int16),
            [
                IN_SMEM,
                IN_SMEM,
                IN_SMEM,
                pl.BlockSpec((HEADS_STEP, HEAD_DIM, TOKENS), lambda h: (h, 0, 0)),
                pl.BlockSpec((stored, HEAD_DIM), lambda h: (0, 0)),
                pl.BlockSpec((stored, HEAD_DIM), lambda h: (0, 0)),
                pl.BlockSpec((2, SEG_LEN, HEAD_DIM), lambda h: (0, 0, 0)),
            ],
            pl.BlockSpec((2 * HEADS_STEP, half + 16, TOKENS), lambda h: (h, 0, 0)),
            grid=(GROUP // HEADS_STEP,),
            scratch_shapes=[
                pltpu.VMEM((stored + SEG_LEN, HEAD_DIM), BF16),
                pltpu.VMEM((HEAD_DIM, stored + SEG_LEN), BF16),
                pltpu.VMEM((HEADS_STEP, stored + SEG_LEN, TOKENS), F32),
                pltpu.VMEM((HEADS_STEP, stored + SEG_LEN, TOKENS), BF16),
            ],
        )(index, logical, starts, query, keys, values, fresh)
        parts = exchange(sent, "kv")
    with jax.named_scope("combine"):
        attended = call(
            functools.partial(combine_kernel, count),
            jax.ShapeDtypeStruct((count, half, TOKENS), BF16),
            [IN_VMEM],
            IN_VMEM,
        )(parts)
        attended = exchange(attended, "kv").reshape(GROUP * HEAD_DIM, TOKENS)
    with jax.named_scope("output"):
        keep, send = call(
            output_kernel,
            (jax.ShapeDtypeStruct((share, width), F32),) * 2,
            [IN_SMEM] + [IN_VMEM] * 2,
            (IN_VMEM, IN_VMEM),
            scratch_shapes=[pltpu.VMEM((TOKENS, width), F32)],
        )(core, attended, out_proj)
        half_sum = call(
            add_kernel,
            jax.ShapeDtypeStruct((share, width), F32),
            [IN_VMEM] * 2,
            IN_VMEM,
        )(keep, swap(send))
        parts = exchange(half_sum.reshape(peers, part, width), "tp")
    with jax.named_scope("residual"):
        if which == LAYERS - 1:
            produced = call(
                last_residual_kernel,
                jax.ShapeDtypeStruct((peers, part, width), BF16),
                [IN_VMEM] * 2,
                IN_VMEM,
            )(parts, mine)
            mine = None
        else:
            mine, squares = call(
                functools.partial(residual_kernel, count),
                (
                    jax.ShapeDtypeStruct((part, width), BF16),
                    jax.ShapeDtypeStruct((count, 8, 128), F32),
                ),
                [IN_VMEM] * 2,
                (IN_VMEM, IN_VMEM),
            )(parts, mine)
            produced = call(
                spread_kernel,
                jax.ShapeDtypeStruct((peers, part, width + 128), BF16),
                [IN_VMEM] * 2,
                IN_VMEM,
            )(exchange(squares, "kv"), mine)
        own = exchange(produced, "tp").reshape(share, -1)
        return (own, swap(own)), mine


def per_device(
    segments_in, gain, query_weight, kv_weight, out_weight, kv_cache, block_logical, segment_block
):
    width = segments_in.shape[2]
    core = lax.axis_index("section")
    core_at = core.astype(jnp.int32)[None]
    index = lax.axis_index("kv").astype(jnp.int32)[None]
    per_core = GROUP * HEAD_DIM
    share = TOKENS // 2

    def pick(which):
        at = which * per_core
        kv_at = which * HEAD_DIM
        return (
            lax.dynamic_slice_in_dim(query_weight[0], at, per_core, 1),
            lax.dynamic_slice_in_dim(kv_weight[0], kv_at, HEAD_DIM, 2).reshape(width, -1),
            lax.dynamic_slice_in_dim(kv_cache[0, :, 0], kv_at, HEAD_DIM, 1),
            lax.dynamic_slice_in_dim(kv_cache[0, :, 1], kv_at, HEAD_DIM, 1),
            lax.dynamic_slice_in_dim(out_weight[0], at, per_core, 0),
            gain,
        )

    kept = pick(core)
    received = tuple(swap(v) for v in pick(1 - core))
    x = segments_in.reshape(TOKENS, width)
    part = share // lax.axis_size("tp")
    mine = lax.dynamic_slice_in_dim(x, core * share + lax.axis_index("tp") * part, part, 0)
    outputs = []
    for which in range(LAYERS):
        query_proj, kv_proj, keys, values, out_proj, gain_row = (
            jnp.where(core == which, here, other) for here, other in zip(kept, received)
        )
        x, mine = layer(
            which, x, mine, gain_row, query_proj, kv_proj, out_proj, keys, values,
            block_logical, segment_block, index, core_at,
        )
        outputs.extend(x)
    result = call(
        choose_kernel,
        jax.ShapeDtypeStruct((TOKENS, width), BF16),
        [IN_SMEM] + [IN_VMEM] * 4,
        IN_VMEM,
    )(core_at, *outputs)
    return result.reshape(1, NSEG, SEG_LEN, width)


def solution(mesh):
    placed = (
        P(None, None, "kv"),
        P("section", "kv"),
        P("section", "kv", "tp"),
        P("section", "kv", None, "tp"),
        P("section", "tp", "kv"),
        P("section", "kv", None, "tp"),
        P("kv"),
        P(),
    )
    return jax.shard_map(
        per_device,
        mesh=mesh,
        in_specs=placed,
        out_specs=P("section", None, None, "kv"),
        check_vma=False,
    )
```

```python
import functools
import math

import jax
import jax.numpy as jnp
from jax import lax
from jax.experimental import pallas as pl
from jax.experimental.pallas import tpu as pltpu
from jax.sharding import PartitionSpec as P

D = 8192
HEAD_DIM = 128
BLOCK = 128
NSEG = 3
SEG_LEN = 128
TOKENS = NSEG * SEG_LEN
GROUP = 8
LAYERS = 2
EPSILON = 1e-05
CLOSED = -1e30
FRESH = 128
RANGE = 32000.0
HEADS_STEP = 2
SCALE = math.log2(math.e) / math.sqrt(HEAD_DIM)
F32 = jnp.float32
BF16 = jnp.bfloat16
VMEM_BYTES = 48 * 1024 * 1024


def call(kernel, out_shape, in_specs, out_specs, **rest):
    return pl.pallas_call(
        kernel,
        out_shape=out_shape,
        in_specs=in_specs,
        out_specs=out_specs,
        compiler_params=pltpu.CompilerParams(vmem_limit_bytes=VMEM_BYTES),
        **rest,
    )


IN_VMEM = pl.BlockSpec(memory_space=pltpu.VMEM)
IN_SMEM = pl.BlockSpec(memory_space=pltpu.SMEM)


def encode(block):
    top = jnp.maximum(jnp.max(jnp.abs(block), axis=0, keepdims=True), 1e-30)
    level = jnp.ceil(jnp.log2(top) * 64.0)
    return jnp.round(block * (jnp.exp2(level * (-1.0 / 64.0)) * RANGE)), level


def stack_rows(rows):
    width = rows[0].shape[1]
    place = lax.broadcasted_iota(jnp.int32, (16, width), 0)
    filled = jnp.zeros((16, width), F32)
    for number, row in enumerate(rows):
        filled = jnp.where(place == number, row, filled)
    return filled


def short(value):
    return value.astype(jnp.int32).astype(jnp.int16)


def wide(value):
    return value.astype(jnp.int32).astype(F32)


def square_rows(x):
    squares = jnp.sum(x * x, axis=1, keepdims=True)
    squares = jnp.broadcast_to(squares, (x.shape[0], 128))
    missing = -x.shape[0] % 128
    if missing:
        squares = jnp.concatenate([squares, jnp.zeros((missing, 128), F32)], axis=0)
    return squares.T[0:8]


def norm_columns(parts_ref):
    total = parts_ref[0]
    for peer in range(1, parts_ref.shape[0]):
        total = total + parts_ref[peer]
    factor = lax.rsqrt(total[0:1] / D + EPSILON)
    return jnp.broadcast_to(factor, (128, factor.shape[1])).T


def squares_kernel(count, x_ref, out_ref):
    rows = square_rows(x_ref[...].astype(F32))
    for peer in range(count):
        out_ref[peer] = rows


def first_project_kernel(count, x_ref, squares_ref, gain_ref, query_ref, kv_ref, out_ref):
    factor = norm_columns(squares_ref)[:, 0:1]
    normed = (x_ref[...].astype(F32) * factor * gain_ref[...]).astype(BF16)
    project(count, normed, query_ref, kv_ref, out_ref)


def project_kernel(count, core_ref, own_ref, other_ref, gain_ref, query_ref, kv_ref, out_ref, x_ref):
    share = TOKENS // 2
    width = gain_ref.shape[1]
    x_ref[pl.ds(core_ref[0] * share, share), :] = own_ref[...]
    x_ref[pl.ds((1 - core_ref[0]) * share, share), :] = other_ref[...]
    thirds = x_ref[:, width : width + 128].astype(F32)
    factor = thirds[:, 0:1] + thirds[:, 1:2] + thirds[:, 2:3]
    normed = (x_ref[:, 0:width].astype(F32) * factor * gain_ref[...]).astype(BF16)
    project(count, normed, query_ref, kv_ref, out_ref)


def project(count, scaled, query_ref, kv_ref, out_ref):
    half = HEAD_DIM // 2
    columns = query_ref.shape[1]
    rows = SEG_LEN // count
    fresh = jnp.dot(scaled, kv_ref[...], preferred_element_type=F32)
    for start in range(0, columns, 256):
        part = jnp.dot(scaled, query_ref[:, start : start + 256], preferred_element_type=F32)
        turned = part.T
        for piece in range(256 // half):
            peer = start // half + piece
            query, query_level = encode(turned[piece * half : (piece + 1) * half])
            out_ref[peer, 0:half, :] = short(query)
            kinds = []
            for kind in range(2):
                lanes = slice(kind * HEAD_DIM, (kind + 1) * HEAD_DIM)
                block = jnp.concatenate(
                    [
                        fresh[seg * SEG_LEN + peer * rows : seg * SEG_LEN + (peer + 1) * rows, lanes]
                        for seg in range(NSEG)
                    ],
                    axis=1,
                )
                kinds.append(encode(block))
            out_ref[peer, half : half + 2 * rows, :] = short(
                jnp.concatenate([kinds[0][0], kinds[1][0]], axis=0)
            )
            out_ref[peer, half + 2 * rows : half + 2 * rows + 16, :] = short(
                stack_rows([query_level, kinds[0][1], kinds[1][1]])
            )


def finish_projection_kernel(count, parts_ref, query_out, fresh_out):
    half = HEAD_DIM // 2
    rows = SEG_LEN // count
    query = jnp.zeros((half, TOKENS), F32)
    fresh = [jnp.zeros((rows, TOKENS), F32) for _ in range(2)]
    for peer in range(count):
        notes = wide(parts_ref[peer, half + 2 * rows : half + 2 * rows + 16, :])
        factors = jnp.exp2(notes * (1.0 / 64.0)) * (1.0 / RANGE)
        query = query + wide(parts_ref[peer, 0:half, :]) * factors[0:1]
        both = wide(parts_ref[peer, half : half + 2 * rows, :])
        fresh[0] = fresh[0] + both[0:rows] * factors[1:2]
        fresh[1] = fresh[1] + both[rows : 2 * rows] * factors[2:3]
    query = query.astype(BF16)
    for peer in range(count):
        query_out[peer] = query
    filler = jnp.zeros((FRESH - NSEG * rows, HEAD_DIM), F32)
    for kind in range(2):
        pieces = [
            fresh[kind][:, seg * SEG_LEN : (seg + 1) * SEG_LEN] for seg in range(NSEG)
        ]
        fresh_out[kind] = jnp.concatenate(pieces + [filler], axis=0).astype(BF16)


def fresh_mask(rows, index_ref, seg):
    key_row = lax.broadcasted_iota(jnp.int32, (FRESH, SEG_LEN), 0)
    token = lax.broadcasted_iota(jnp.int32, (FRESH, SEG_LEN), 1)
    local = key_row - seg * rows
    return (local >= 0) & (local < rows) & (local + index_ref[0] * rows <= token)


def peak_kernel(
    rows, index_ref, logical_ref, start_ref, query_ref, keys_ref, fresh_ref, out_ref, peaks
):
    blocks = keys_ref.shape[0] // BLOCK
    heads = query_ref.shape[0]
    step = pl.program_id(0)
    for head in range(heads):
        query = query_ref[head]
        scores = jnp.dot(fresh_ref[0], query, preferred_element_type=F32)
        tops = []
        for seg in range(NSEG):
            lanes = slice(seg * SEG_LEN, (seg + 1) * SEG_LEN)
            masked = jnp.where(fresh_mask(rows, index_ref, seg), scores[:, lanes], CLOSED)
            tops.append(jnp.max(masked.reshape(FRESH // 8, 8, SEG_LEN), axis=0))
        for block in range(blocks):
            at = slice(block * BLOCK, (block + 1) * BLOCK)
            scores = jnp.dot(keys_ref[at, :], query, preferred_element_type=F32)
            top = jnp.max(scores.reshape(BLOCK // 8, 8, TOKENS), axis=0)
            for seg in range(NSEG):
                lanes = slice(seg * SEG_LEN, (seg + 1) * SEG_LEN)
                is_open = logical_ref[block] < start_ref[seg]
                tops[seg] = jnp.maximum(tops[seg], jnp.where(is_open, top[:, lanes], CLOSED))
        peaks[step * heads + head] = jnp.concatenate(
            [jnp.max(top, axis=0, keepdims=True) for top in tops], axis=1
        )

    @pl.when(step == pl.num_programs(0) - 1)
    def _():
        found = jnp.concatenate([peaks[head] for head in range(GROUP)], axis=0)
        for peer in range(out_ref.shape[0]):
            out_ref[peer] = found


def attend_kernel(
    rows, index_ref, logical_ref, start_ref, query_ref, keys_ref, values_ref, fresh_ref, peaks_ref,
    out_ref, turned_values, peaks, weights,
):
    blocks = keys_ref.shape[0] // BLOCK
    stored = blocks * BLOCK
    half = HEAD_DIM // 2
    heads = query_ref.shape[0]
    step = pl.program_id(0)

    @pl.when(step == 0)
    def _():
        for block in range(blocks):
            at = slice(block * BLOCK, (block + 1) * BLOCK)
            turned_values[:, at] = values_ref[at, :].T
        turned_values[:, stored : stored + FRESH] = fresh_ref[1].T
        top = peaks_ref[0]
        for peer in range(1, peaks_ref.shape[0]):
            top = jnp.maximum(top, peaks_ref[peer])
        for head in range(GROUP):
            peaks[head] = top[head : head + 1]

    for head in range(heads):
        query = query_ref[head]
        peak = peaks[step * heads + head]
        scores = jnp.dot(fresh_ref[0], query, preferred_element_type=F32)
        masses = []
        for seg in range(NSEG):
            lanes = slice(seg * SEG_LEN, (seg + 1) * SEG_LEN)
            weight = jnp.exp2((scores[:, lanes] - peak[:, lanes]) * SCALE)
            weight = jnp.where(fresh_mask(rows, index_ref, seg), weight, 0.0)
            weights[head, stored : stored + FRESH, lanes] = weight.astype(BF16)
            masses.append(jnp.sum(weight.reshape(FRESH // 8, 8, SEG_LEN), axis=0))
        for block in range(blocks):
            at = slice(block * BLOCK, (block + 1) * BLOCK)
            scores = jnp.dot(keys_ref[at, :], query, preferred_element_type=F32)
            for seg in range(NSEG):
                lanes = slice(seg * SEG_LEN, (seg + 1) * SEG_LEN)
                is_open = logical_ref[block] < start_ref[seg]
                offset = jnp.where(is_open, peak[:, lanes], -CLOSED)
                weight = jnp.exp2((scores[:, lanes] - offset) * SCALE)
                weights[head, at, lanes] = weight.astype(BF16)
                masses[seg] = masses[seg] + jnp.sum(
                    weight.reshape(BLOCK // 8, 8, SEG_LEN), axis=0
                )
        sums = jnp.dot(turned_values[...], weights[head], preferred_element_type=F32)
        mass = jnp.concatenate(
            [jnp.sum(part, axis=0, keepdims=True) for part in masses], axis=1
        ) * 16.0
        mass_high = jnp.floor(mass)
        notes = [mass_high, jnp.round((mass - mass_high) * RANGE)]
        for piece in range(2):
            value, level = encode(sums[piece * half : (piece + 1) * half])
            out_ref[2 * head + piece, 0:half, :] = short(value)
            out_ref[2 * head + piece, half : half + 16, :] = short(stack_rows([level] + notes))


def combine_kernel(count, parts_ref, out_ref):
    half = HEAD_DIM // 2
    mass = jnp.zeros((1, TOKENS), F32)
    sums = jnp.zeros((half, TOKENS), F32)
    for peer in range(count):
        note = wide(parts_ref[peer, half : half + 16, :])
        mass = mass + (note[1:2] + note[2:3] * (1.0 / RANGE))
        factor = jnp.exp2(note[0:1] * (1.0 / 64.0)) * (16.0 / RANGE)
        sums = sums + factor * wide(parts_ref[peer, 0:half, :])
    attended = (sums / mass).astype(BF16)
    for peer in range(count):
        out_ref[peer] = attended


def output_kernel(core_ref, attended_ref, weight_ref, keep_ref, send_ref, scratch):
    share = TOKENS // 2
    scratch[...] = lax.dot_general(
        attended_ref[...], weight_ref[...], (((0,), (0,)), ((), ())), preferred_element_type=F32
    )
    keep_ref[...] = scratch[pl.ds(core_ref[0] * share, share), :]
    send_ref[...] = scratch[pl.ds((1 - core_ref[0]) * share, share), :]


def add_kernel(keep_ref, received_ref, out_ref):
    out_ref[...] = keep_ref[...] + received_ref[...]


def add_residual(parts_ref, x_ref):
    total = parts_ref[0]
    for peer in range(1, parts_ref.shape[0]):
        total = total + parts_ref[peer]
    return (x_ref[...].astype(F32) + total).astype(BF16)


def residual_kernel(count, parts_ref, x_ref, out_ref, squares_ref):
    produced = add_residual(parts_ref, x_ref)
    out_ref[...] = produced
    rows = square_rows(produced.astype(F32))
    for peer in range(count):
        squares_ref[peer] = rows


def last_residual_kernel(parts_ref, x_ref, out_ref):
    produced = add_residual(parts_ref, x_ref)
    for peer in range(out_ref.shape[0]):
        out_ref[peer] = produced


def spread_kernel(squares_ref, x_ref, out_ref):
    tokens, width = x_ref.shape
    factor = norm_columns(squares_ref)[0:tokens]
    first = factor.astype(BF16).astype(F32)
    second = (factor - first).astype(BF16).astype(F32)
    lane = lax.broadcasted_iota(jnp.int32, factor.shape, 1)
    thirds = jnp.where(lane == 0, first, jnp.where(lane == 1, second, factor - first - second))
    for peer in range(out_ref.shape[0]):
        out_ref[peer, :, 0:width] = x_ref[...]
        out_ref[peer, :, width : width + 128] = thirds.astype(BF16)


def choose_kernel(core_ref, own0_ref, other0_ref, own1_ref, other1_ref, out_ref):
    share = TOKENS // 2
    width = out_ref.shape[1]
    first = core_ref[0] == 0
    at = pl.ds(core_ref[0] * share, share)
    out_ref[at, :] = jnp.where(first, own0_ref[:, 0:width], own1_ref[...])
    at = pl.ds((1 - core_ref[0]) * share, share)
    out_ref[at, :] = jnp.where(first, other0_ref[:, 0:width], other1_ref[...])


def exchange(value, axes):
    return lax.all_to_all(value, axes, 0, 0, tiled=True)


def swap(value):
    return lax.ppermute(value, "section", [(0, 1), (1, 0)])


def layer(
    which, x, mine, gain, query_proj, kv_proj, out_proj, keys, values, logical, starts, index, core
):
    count = lax.axis_size("kv")
    peers = lax.axis_size("tp")
    rows = SEG_LEN // count
    half = HEAD_DIM // 2
    width = query_proj.shape[0]
    share = TOKENS // 2
    part = share // peers
    with jax.named_scope("project"):
        shape = jax.ShapeDtypeStruct((count, half + 2 * rows + 16, TOKENS), jnp.int16)
        if which == 0:
            squares = call(
                functools.partial(squares_kernel, count),
                jax.ShapeDtypeStruct((count, 8, TOKENS), F32),
                [IN_VMEM],
                IN_VMEM,
            )(x)
            squares = exchange(squares, "kv")
            sent = call(
                functools.partial(first_project_kernel, count), shape, [IN_VMEM] * 5, IN_VMEM
            )(x, squares, gain, query_proj, kv_proj)
        else:
            sent = call(
                functools.partial(project_kernel, count),
                shape,
                [IN_SMEM] + [IN_VMEM] * 5,
                IN_VMEM,
                scratch_shapes=[pltpu.VMEM((TOKENS, width + 128), BF16)],
            )(core, x[0], x[1], gain, query_proj, kv_proj)
        parts = exchange(sent, "kv")
    with jax.named_scope("queries"):
        query, fresh = call(
            functools.partial(finish_projection_kernel, count),
            (
                jax.ShapeDtypeStruct((count, half, TOKENS), BF16),
                jax.ShapeDtypeStruct((2, FRESH, HEAD_DIM), BF16),
            ),
            [IN_VMEM],
            (IN_VMEM, IN_VMEM),
        )(parts)
        query = exchange(query, "kv").reshape(GROUP, HEAD_DIM, TOKENS)
    stored = keys.shape[0]
    by_head = [
        IN_SMEM,
        IN_SMEM,
        IN_SMEM,
        pl.BlockSpec((HEADS_STEP, HEAD_DIM, TOKENS), lambda h: (h, 0, 0)),
        pl.BlockSpec((stored, HEAD_DIM), lambda h: (0, 0)),
    ]
    whole_values = pl.BlockSpec((stored, HEAD_DIM), lambda h: (0, 0))
    whole_fresh = pl.BlockSpec((2, FRESH, HEAD_DIM), lambda h: (0, 0, 0))
    whole_peaks = pl.BlockSpec((count, GROUP, TOKENS), lambda h: (0, 0, 0))
    with jax.named_scope("peaks"):
        peaks = call(
            functools.partial(peak_kernel, rows),
            jax.ShapeDtypeStruct((count, GROUP, TOKENS), F32),
            by_head + [whole_fresh],
            whole_peaks,
            grid=(GROUP // HEADS_STEP,),
            scratch_shapes=[pltpu.VMEM((GROUP, 1, TOKENS), F32)],
        )(index, logical, starts, query, keys, fresh)
        peaks = exchange(peaks, "kv")
    with jax.named_scope("attend"):
        sent = call(
            functools.partial(attend_kernel, rows),
            jax.ShapeDtypeStruct((count, half + 16, TOKENS), jnp.int16),
            by_head + [whole_values, whole_fresh, whole_peaks],
            pl.BlockSpec((2 * HEADS_STEP, half + 16, TOKENS), lambda h: (h, 0, 0)),
            grid=(GROUP // HEADS_STEP,),
            scratch_shapes=[
                pltpu.VMEM((HEAD_DIM, stored + FRESH), BF16),
                pltpu.VMEM((GROUP, 1, TOKENS), F32),
                pltpu.VMEM((HEADS_STEP, stored + FRESH, TOKENS), BF16),
            ],
        )(index, logical, starts, query, keys, values, fresh, peaks)
        parts = exchange(sent, "kv")
    with jax.named_scope("combine"):
        attended = call(
            functools.partial(combine_kernel, count),
            jax.ShapeDtypeStruct((count, half, TOKENS), BF16),
            [IN_VMEM],
            IN_VMEM,
        )(parts)
        attended = exchange(attended, "kv").reshape(GROUP * HEAD_DIM, TOKENS)
    with jax.named_scope("output"):
        keep, send = call(
            output_kernel,
            (jax.ShapeDtypeStruct((share, width), F32),) * 2,
            [IN_SMEM] + [IN_VMEM] * 2,
            (IN_VMEM, IN_VMEM),
            scratch_shapes=[pltpu.VMEM((TOKENS, width), F32)],
        )(core, attended, out_proj)
        half_sum = call(
            add_kernel,
            jax.ShapeDtypeStruct((share, width), F32),
            [IN_VMEM] * 2,
            IN_VMEM,
        )(keep, swap(send))
        parts = exchange(half_sum.reshape(peers, part, width), "tp")
    with jax.named_scope("residual"):
        if which == LAYERS - 1:
            produced = call(
                last_residual_kernel,
                jax.ShapeDtypeStruct((peers, part, width), BF16),
                [IN_VMEM] * 2,
                IN_VMEM,
            )(parts, mine)
            mine = None
        else:
            mine, squares = call(
                functools.partial(residual_kernel, count),
                (
                    jax.ShapeDtypeStruct((part, width), BF16),
                    jax.ShapeDtypeStruct((count, 8, 128), F32),
                ),
                [IN_VMEM] * 2,
                (IN_VMEM, IN_VMEM),
            )(parts, mine)
            produced = call(
                spread_kernel,
                jax.ShapeDtypeStruct((peers, part, width + 128), BF16),
                [IN_VMEM] * 2,
                IN_VMEM,
            )(exchange(squares, "kv"), mine)
        own = exchange(produced, "tp").reshape(share, -1)
        return (own, swap(own)), mine


def per_device(
    segments_in, gain, query_weight, kv_weight, out_weight, kv_cache, block_logical, segment_block
):
    width = segments_in.shape[2]
    core = lax.axis_index("section")
    core_at = core.astype(jnp.int32)[None]
    index = lax.axis_index("kv").astype(jnp.int32)[None]
    per_core = GROUP * HEAD_DIM
    share = TOKENS // 2

    def pick(which):
        at = which * per_core
        kv_at = which * HEAD_DIM
        return (
            lax.dynamic_slice_in_dim(query_weight[0], at, per_core, 1),
            lax.dynamic_slice_in_dim(kv_weight[0], kv_at, HEAD_DIM, 2).reshape(width, -1),
            lax.dynamic_slice_in_dim(kv_cache[0, :, 0], kv_at, HEAD_DIM, 1),
            lax.dynamic_slice_in_dim(kv_cache[0, :, 1], kv_at, HEAD_DIM, 1),
            lax.dynamic_slice_in_dim(out_weight[0], at, per_core, 0),
            gain,
        )

    kept = pick(core)
    received = tuple(swap(v) for v in pick(1 - core))
    x = segments_in.reshape(TOKENS, width)
    part = share // lax.axis_size("tp")
    mine = lax.dynamic_slice_in_dim(x, core * share + lax.axis_index("tp") * part, part, 0)
    outputs = []
    for which in range(LAYERS):
        query_proj, kv_proj, keys, values, out_proj, gain_row = (
            jnp.where(core == which, here, other) for here, other in zip(kept, received)
        )
        x, mine = layer(
            which, x, mine, gain_row, query_proj, kv_proj, out_proj, keys, values,
            block_logical, segment_block, index, core_at,
        )
        outputs.extend(x)
    result = call(
        choose_kernel,
        jax.ShapeDtypeStruct((TOKENS, width), BF16),
        [IN_SMEM] + [IN_VMEM] * 4,
        IN_VMEM,
    )(core_at, *outputs)
    return result.reshape(1, NSEG, SEG_LEN, width)


def solution(mesh):
    placed = (
        P(None, None, "kv"),
        P("section", "kv"),
        P("section", "kv", "tp"),
        P("section", "kv", None, "tp"),
        P("section", "tp", "kv"),
        P("section", "kv", None, "tp"),
        P("kv"),
        P(),
    )
    return jax.shard_map(
        per_device,
        mesh=mesh,
        in_specs=placed,
        out_specs=P("section", None, None, "kv"),
        check_vma=False,
    )
```

```python
import functools
import math

import jax
import jax.numpy as jnp
from jax import lax
from jax.experimental import pallas as pl
from jax.experimental.pallas import tpu as pltpu
from jax.sharding import PartitionSpec as P

D = 8192
HEAD_DIM = 128
BLOCK = 128
NSEG = 3
SEG_LEN = 128
TOKENS = NSEG * SEG_LEN
GROUP = 8
LAYERS = 2
EPSILON = 1e-05
CLOSED = -1e30
FRESH = 128
RANGE = 520000.0
MIDDLE = 524288
LEVELS = 2048
MASS_UNIT = 262144.0
HEADS_STEP = 2
SCALE = math.log2(math.e) / math.sqrt(HEAD_DIM)
F32 = jnp.float32
BF16 = jnp.bfloat16
VMEM_BYTES = 48 * 1024 * 1024


def call(kernel, out_shape, in_specs, out_specs, **rest):
    return pl.pallas_call(
        kernel,
        out_shape=out_shape,
        in_specs=in_specs,
        out_specs=out_specs,
        compiler_params=pltpu.CompilerParams(vmem_limit_bytes=VMEM_BYTES),
        **rest,
    )


IN_VMEM = pl.BlockSpec(memory_space=pltpu.VMEM)
IN_SMEM = pl.BlockSpec(memory_space=pltpu.SMEM)


def encode(block):
    top = jnp.maximum(jnp.max(jnp.abs(block), axis=0, keepdims=True), 1e-30)
    level = jnp.ceil(jnp.log2(top) * 16.0)
    value = jnp.round(block * (jnp.exp2(level * (-1.0 / 16.0)) * RANGE))
    return value.astype(jnp.int32) + MIDDLE, level.astype(jnp.int32)


def level_factor(level):
    return jnp.exp2(level.astype(F32) * (1.0 / 16.0)) * (1.0 / RANGE)


def pack(value):
    part = [value[8 * at : 8 * at + 8] for at in range(8)]
    lows = [
        part[5] & 0xFFF,
        (part[5] >> 12) | ((part[6] & 0xF) << 8),
        (part[6] >> 4) & 0xFFF,
        (part[6] >> 16) | ((part[7] & 0xFF) << 4),
        part[7] >> 8,
    ]
    return [(part[at] << 12) | lows[at] for at in range(5)]


def top_bits(word):
    return lax.shift_right_logical(word, jnp.int32(12))


def unpack(words):
    lows = [word & 0xFFF for word in words]
    part = [top_bits(word) for word in words]
    part.append(lows[0] | ((lows[1] & 0xFF) << 12))
    part.append((lows[1] >> 8) | (lows[2] << 4) | ((lows[3] & 0xF) << 16))
    part.append((lows[3] >> 4) | (lows[4] << 8))
    return (jnp.concatenate(part, axis=0) - MIDDLE).astype(F32)


def first_rows(rows, count=8):
    place = lax.broadcasted_iota(jnp.int32, (count, rows[0].shape[1]), 0)
    filled = jnp.zeros_like(place)
    for number, row in enumerate(rows):
        filled = jnp.where(place == number, row, filled)
    return filled


def square_rows(x):
    squares = jnp.sum(x * x, axis=1, keepdims=True)
    squares = jnp.broadcast_to(squares, (x.shape[0], 128))
    missing = -x.shape[0] % 128
    if missing:
        squares = jnp.concatenate([squares, jnp.zeros((missing, 128), F32)], axis=0)
    return squares.T[0:8]


def norm_columns(parts_ref):
    total = parts_ref[0]
    for peer in range(1, parts_ref.shape[0]):
        total = total + parts_ref[peer]
    factor = lax.rsqrt(total[0:1] / D + EPSILON)
    return jnp.broadcast_to(factor, (128, factor.shape[1])).T


def squares_kernel(count, x_ref, out_ref):
    rows = square_rows(x_ref[...].astype(F32))
    for peer in range(count):
        out_ref[peer] = rows


def first_project_kernel(count, x_ref, squares_ref, gain_ref, query_ref, kv_ref, out_ref):
    factor = norm_columns(squares_ref)[:, 0:1]
    normed = (x_ref[...].astype(F32) * factor * gain_ref[...]).astype(BF16)
    project(count, normed, query_ref, kv_ref, out_ref)


def project_kernel(count, core_ref, own_ref, other_ref, gain_ref, query_ref, kv_ref, out_ref, x_ref):
    share = TOKENS // 2
    width = gain_ref.shape[1]
    x_ref[pl.ds(core_ref[0] * share, share), :] = own_ref[...]
    x_ref[pl.ds((1 - core_ref[0]) * share, share), :] = other_ref[...]
    thirds = x_ref[:, width : width + 128].astype(F32)
    factor = thirds[:, 0:1] + thirds[:, 1:2] + thirds[:, 2:3]
    normed = (x_ref[:, 0:width].astype(F32) * factor * gain_ref[...]).astype(BF16)
    project(count, normed, query_ref, kv_ref, out_ref)


def project(count, scaled, query_ref, kv_ref, out_ref):
    half = HEAD_DIM // 2
    columns = query_ref.shape[1]
    rows = SEG_LEN // count
    fresh = jnp.dot(scaled, kv_ref[...], preferred_element_type=F32)
    for start in range(0, columns, 256):
        part = jnp.dot(scaled, query_ref[:, start : start + 256], preferred_element_type=F32)
        turned = part.T
        for piece in range(256 // half):
            peer = start // half + piece
            query, query_level = encode(turned[piece * half : (piece + 1) * half])
            words = pack(query)
            kinds = []
            for kind in range(2):
                lanes = slice(kind * HEAD_DIM, (kind + 1) * HEAD_DIM)
                block = jnp.concatenate(
                    [
                        fresh[seg * SEG_LEN + peer * rows : seg * SEG_LEN + (peer + 1) * rows, lanes]
                        for seg in range(NSEG)
                    ],
                    axis=1,
                )
                kinds.append(encode(block))
            levels = first_rows([query_level, kinds[0][1], kinds[1][1]]) + LEVELS
            words.append((kinds[0][0] << 12) | levels)
            words.append(kinds[1][0] << 12)
            for at, word in enumerate(words):
                out_ref[peer, 8 * at : 8 * at + 8, :] = word


def finish_projection_kernel(count, parts_ref, query_out, fresh_out):
    half = HEAD_DIM // 2
    rows = SEG_LEN // count
    query = jnp.zeros((half, TOKENS), F32)
    fresh = [jnp.zeros((rows, TOKENS), F32) for _ in range(2)]
    for peer in range(count):
        words = [parts_ref[peer, 8 * at : 8 * at + 8, :] for at in range(7)]
        factors = level_factor((words[5] & 0xFFF) - LEVELS)
        query = query + unpack(words[0:5]) * factors[0:1]
        for kind in range(2):
            value = (top_bits(words[5 + kind]) - MIDDLE).astype(F32)
            fresh[kind] = fresh[kind] + value * factors[1 + kind : 2 + kind]
    query = query.astype(BF16)
    for peer in range(count):
        query_out[peer] = query
    filler = jnp.zeros((FRESH - NSEG * rows, HEAD_DIM), F32)
    for kind in range(2):
        pieces = [
            fresh[kind][:, seg * SEG_LEN : (seg + 1) * SEG_LEN] for seg in range(NSEG)
        ]
        fresh_out[kind] = jnp.concatenate(pieces + [filler], axis=0).astype(BF16)


def fresh_mask(rows, index_ref, seg):
    key_row = lax.broadcasted_iota(jnp.int32, (FRESH, SEG_LEN), 0)
    token = lax.broadcasted_iota(jnp.int32, (FRESH, SEG_LEN), 1)
    local = key_row - seg * rows
    return (local >= 0) & (local < rows) & (local + index_ref[0] * rows <= token)


def peak_kernel(
    rows, index_ref, logical_ref, start_ref, query_ref, keys_ref, fresh_ref, out_ref, peaks
):
    blocks = keys_ref.shape[0] // BLOCK
    heads = query_ref.shape[0]
    step = pl.program_id(0)
    for head in range(heads):
        query = query_ref[head]
        scores = jnp.dot(fresh_ref[0], query, preferred_element_type=F32)
        tops = []
        for seg in range(NSEG):
            lanes = slice(seg * SEG_LEN, (seg + 1) * SEG_LEN)
            masked = jnp.where(fresh_mask(rows, index_ref, seg), scores[:, lanes], CLOSED)
            tops.append(jnp.max(masked.reshape(FRESH // 8, 8, SEG_LEN), axis=0))
        for block in range(blocks):
            at = slice(block * BLOCK, (block + 1) * BLOCK)
            scores = jnp.dot(keys_ref[at, :], query, preferred_element_type=F32)
            top = jnp.max(scores.reshape(BLOCK // 8, 8, TOKENS), axis=0)
            for seg in range(NSEG):
                lanes = slice(seg * SEG_LEN, (seg + 1) * SEG_LEN)
                is_open = logical_ref[block] < start_ref[seg]
                tops[seg] = jnp.maximum(tops[seg], jnp.where(is_open, top[:, lanes], CLOSED))
        peaks[step * heads + head] = jnp.concatenate(
            [jnp.max(top, axis=0, keepdims=True) for top in tops], axis=1
        )

    @pl.when(step == pl.num_programs(0) - 1)
    def _():
        found = jnp.concatenate([peaks[head] for head in range(GROUP)], axis=0)
        for peer in range(out_ref.shape[0]):
            out_ref[peer] = found


def attend_kernel(
    rows, index_ref, logical_ref, start_ref, query_ref, keys_ref, values_ref, fresh_ref, peaks_ref,
    out_ref, turned_values, peaks, weights,
):
    blocks = keys_ref.shape[0] // BLOCK
    stored = blocks * BLOCK
    half = HEAD_DIM // 2
    heads = query_ref.shape[0]
    step = pl.program_id(0)

    @pl.when(step == 0)
    def _():
        for block in range(blocks):
            at = slice(block * BLOCK, (block + 1) * BLOCK)
            turned_values[:, at] = values_ref[at, :].T
        turned_values[:, stored : stored + FRESH] = fresh_ref[1].T
        top = peaks_ref[0]
        for peer in range(1, peaks_ref.shape[0]):
            top = jnp.maximum(top, peaks_ref[peer])
        for head in range(GROUP):
            peaks[head] = top[head : head + 1]

    for head in range(heads):
        query = query_ref[head]
        peak = peaks[step * heads + head]
        scores = jnp.dot(fresh_ref[0], query, preferred_element_type=F32)
        masses = []
        for seg in range(NSEG):
            lanes = slice(seg * SEG_LEN, (seg + 1) * SEG_LEN)
            weight = jnp.exp2((scores[:, lanes] - peak[:, lanes]) * SCALE)
            weight = jnp.where(fresh_mask(rows, index_ref, seg), weight, 0.0)
            weights[head, stored : stored + FRESH, lanes] = weight.astype(BF16)
            masses.append(jnp.sum(weight.reshape(FRESH // 8, 8, SEG_LEN), axis=0))
        for block in range(blocks):
            at = slice(block * BLOCK, (block + 1) * BLOCK)
            scores = jnp.dot(keys_ref[at, :], query, preferred_element_type=F32)
            for seg in range(NSEG):
                lanes = slice(seg * SEG_LEN, (seg + 1) * SEG_LEN)
                is_open = logical_ref[block] < start_ref[seg]
                offset = jnp.where(is_open, peak[:, lanes], -CLOSED)
                weight = jnp.exp2((scores[:, lanes] - offset) * SCALE)
                weights[head, at, lanes] = weight.astype(BF16)
                masses[seg] = masses[seg] + jnp.sum(
                    weight.reshape(BLOCK // 8, 8, SEG_LEN), axis=0
                )
        sums = jnp.dot(turned_values[...], weights[head], preferred_element_type=F32)
        mass = jnp.concatenate(
            [jnp.sum(part, axis=0, keepdims=True) for part in masses], axis=1
        )
        mass = jnp.round(mass * MASS_UNIT).astype(jnp.int32)
        for piece in range(2):
            value, level = encode(sums[piece * half : (piece + 1) * half])
            for at, word in enumerate(pack(value) + [first_rows([level, mass])]):
                out_ref[2 * head + piece, 8 * at : 8 * at + 8, :] = word


def combine_kernel(count, parts_ref, out_ref):
    half = HEAD_DIM // 2
    mass = jnp.zeros((1, TOKENS), F32)
    sums = jnp.zeros((half, TOKENS), F32)
    for peer in range(count):
        words = [parts_ref[peer, 8 * at : 8 * at + 8, :] for at in range(6)]
        mass = mass + words[5][1:2].astype(F32) * (1.0 / MASS_UNIT)
        sums = sums + unpack(words[0:5]) * level_factor(words[5][0:1])
    attended = (sums / mass).astype(BF16)
    for peer in range(count):
        out_ref[peer] = attended


def output_kernel(core_ref, attended_ref, weight_ref, keep_ref, send_ref, scratch):
    share = TOKENS // 2
    scratch[...] = lax.dot_general(
        attended_ref[...], weight_ref[...], (((0,), (0,)), ((), ())), preferred_element_type=F32
    )
    keep_ref[...] = scratch[pl.ds(core_ref[0] * share, share), :]
    send_ref[...] = scratch[pl.ds((1 - core_ref[0]) * share, share), :]


def add_kernel(keep_ref, received_ref, out_ref):
    out_ref[...] = keep_ref[...] + received_ref[...]


def add_residual(parts_ref, x_ref):
    total = parts_ref[0]
    for peer in range(1, parts_ref.shape[0]):
        total = total + parts_ref[peer]
    return (x_ref[...].astype(F32) + total).astype(BF16)


def residual_kernel(count, parts_ref, x_ref, out_ref, squares_ref):
    produced = add_residual(parts_ref, x_ref)
    out_ref[...] = produced
    rows = square_rows(produced.astype(F32))
    for peer in range(count):
        squares_ref[peer] = rows


def last_residual_kernel(parts_ref, x_ref, out_ref):
    produced = add_residual(parts_ref, x_ref)
    for peer in range(out_ref.shape[0]):
        out_ref[peer] = produced


def spread_kernel(squares_ref, x_ref, out_ref):
    tokens, width = x_ref.shape
    factor = norm_columns(squares_ref)[0:tokens]
    first = factor.astype(BF16).astype(F32)
    second = (factor - first).astype(BF16).astype(F32)
    lane = lax.broadcasted_iota(jnp.int32, factor.shape, 1)
    thirds = jnp.where(lane == 0, first, jnp.where(lane == 1, second, factor - first - second))
    for peer in range(out_ref.shape[0]):
        out_ref[peer, :, 0:width] = x_ref[...]
        out_ref[peer, :, width : width + 128] = thirds.astype(BF16)


def choose_kernel(core_ref, own0_ref, other0_ref, own1_ref, other1_ref, out_ref):
    share = TOKENS // 2
    width = out_ref.shape[1]
    first = core_ref[0] == 0
    at = pl.ds(core_ref[0] * share, share)
    out_ref[at, :] = jnp.where(first, own0_ref[:, 0:width], own1_ref[...])
    at = pl.ds((1 - core_ref[0]) * share, share)
    out_ref[at, :] = jnp.where(first, other0_ref[:, 0:width], other1_ref[...])


def exchange(value, axes):
    return lax.all_to_all(value, axes, 0, 0, tiled=True)


def swap(value):
    return lax.ppermute(value, "section", [(0, 1), (1, 0)])


def layer(
    which, x, mine, gain, query_proj, kv_proj, out_proj, keys, values, logical, starts, index, core
):
    count = lax.axis_size("kv")
    peers = lax.axis_size("tp")
    rows = SEG_LEN // count
    half = HEAD_DIM // 2
    width = query_proj.shape[0]
    share = TOKENS // 2
    part = share // peers
    with jax.named_scope("project"):
        shape = jax.ShapeDtypeStruct((count, 7 * 8, TOKENS), jnp.int32)
        if which == 0:
            squares = call(
                functools.partial(squares_kernel, count),
                jax.ShapeDtypeStruct((count, 8, TOKENS), F32),
                [IN_VMEM],
                IN_VMEM,
            )(x)
            squares = exchange(squares, "kv")
            sent = call(
                functools.partial(first_project_kernel, count), shape, [IN_VMEM] * 5, IN_VMEM
            )(x, squares, gain, query_proj, kv_proj)
        else:
            sent = call(
                functools.partial(project_kernel, count),
                shape,
                [IN_SMEM] + [IN_VMEM] * 5,
                IN_VMEM,
                scratch_shapes=[pltpu.VMEM((TOKENS, width + 128), BF16)],
            )(core, x[0], x[1], gain, query_proj, kv_proj)
        parts = exchange(sent, "kv")
    with jax.named_scope("queries"):
        query, fresh = call(
            functools.partial(finish_projection_kernel, count),
            (
                jax.ShapeDtypeStruct((count, half, TOKENS), BF16),
                jax.ShapeDtypeStruct((2, FRESH, HEAD_DIM), BF16),
            ),
            [IN_VMEM],
            (IN_VMEM, IN_VMEM),
        )(parts)
        query = exchange(query, "kv").reshape(GROUP, HEAD_DIM, TOKENS)
    stored = keys.shape[0]
    by_head = [
        IN_SMEM,
        IN_SMEM,
        IN_SMEM,
        pl.BlockSpec((HEADS_STEP, HEAD_DIM, TOKENS), lambda h: (h, 0, 0)),
        pl.BlockSpec((stored, HEAD_DIM), lambda h: (0, 0)),
    ]
    whole_values = pl.BlockSpec((stored, HEAD_DIM), lambda h: (0, 0))
    whole_fresh = pl.BlockSpec((2, FRESH, HEAD_DIM), lambda h: (0, 0, 0))
    whole_peaks = pl.BlockSpec((count, GROUP, TOKENS), lambda h: (0, 0, 0))
    with jax.named_scope("peaks"):
        peaks = call(
            functools.partial(peak_kernel, rows),
            jax.ShapeDtypeStruct((count, GROUP, TOKENS), F32),
            by_head + [whole_fresh],
            whole_peaks,
            grid=(GROUP // HEADS_STEP,),
            scratch_shapes=[pltpu.VMEM((GROUP, 1, TOKENS), F32)],
        )(index, logical, starts, query, keys, fresh)
        peaks = exchange(peaks, "kv")
    with jax.named_scope("attend"):
        sent = call(
            functools.partial(attend_kernel, rows),
            jax.ShapeDtypeStruct((count, 6 * 8, TOKENS), jnp.int32),
            by_head + [whole_values, whole_fresh, whole_peaks],
            pl.BlockSpec((2 * HEADS_STEP, 6 * 8, TOKENS), lambda h: (h, 0, 0)),
            grid=(GROUP // HEADS_STEP,),
            scratch_shapes=[
                pltpu.VMEM((HEAD_DIM, stored + FRESH), BF16),
                pltpu.VMEM((GROUP, 1, TOKENS), F32),
                pltpu.VMEM((HEADS_STEP, stored + FRESH, TOKENS), BF16),
            ],
        )(index, logical, starts, query, keys, values, fresh, peaks)
        parts = exchange(sent, "kv")
    with jax.named_scope("combine"):
        attended = call(
            functools.partial(combine_kernel, count),
            jax.ShapeDtypeStruct((count, half, TOKENS), BF16),
            [IN_VMEM],
            IN_VMEM,
        )(parts)
        attended = exchange(attended, "kv").reshape(GROUP * HEAD_DIM, TOKENS)
    with jax.named_scope("output"):
        keep, send = call(
            output_kernel,
            (jax.ShapeDtypeStruct((share, width), F32),) * 2,
            [IN_SMEM] + [IN_VMEM] * 2,
            (IN_VMEM, IN_VMEM),
            scratch_shapes=[pltpu.VMEM((TOKENS, width), F32)],
        )(core, attended, out_proj)
        half_sum = call(
            add_kernel,
            jax.ShapeDtypeStruct((share, width), F32),
            [IN_VMEM] * 2,
            IN_VMEM,
        )(keep, swap(send))
        parts = exchange(half_sum.reshape(peers, part, width), "tp")
    with jax.named_scope("residual"):
        if which == LAYERS - 1:
            produced = call(
                last_residual_kernel,
                jax.ShapeDtypeStruct((peers, part, width), BF16),
                [IN_VMEM] * 2,
                IN_VMEM,
            )(parts, mine)
            mine = None
        else:
            mine, squares = call(
                functools.partial(residual_kernel, count),
                (
                    jax.ShapeDtypeStruct((part, width), BF16),
                    jax.ShapeDtypeStruct((count, 8, 128), F32),
                ),
                [IN_VMEM] * 2,
                (IN_VMEM, IN_VMEM),
            )(parts, mine)
            produced = call(
                spread_kernel,
                jax.ShapeDtypeStruct((peers, part, width + 128), BF16),
                [IN_VMEM] * 2,
                IN_VMEM,
            )(exchange(squares, "kv"), mine)
        own = exchange(produced, "tp").reshape(share, -1)
        return (own, swap(own)), mine


def per_device(
    segments_in, gain, query_weight, kv_weight, out_weight, kv_cache, block_logical, segment_block
):
    width = segments_in.shape[2]
    core = lax.axis_index("section")
    core_at = core.astype(jnp.int32)[None]
    index = lax.axis_index("kv").astype(jnp.int32)[None]
    per_core = GROUP * HEAD_DIM
    share = TOKENS // 2

    def pick(which):
        at = which * per_core
        kv_at = which * HEAD_DIM
        return (
            lax.dynamic_slice_in_dim(query_weight[0], at, per_core, 1),
            lax.dynamic_slice_in_dim(kv_weight[0], kv_at, HEAD_DIM, 2).reshape(width, -1),
            lax.dynamic_slice_in_dim(kv_cache[0, :, 0], kv_at, HEAD_DIM, 1),
            lax.dynamic_slice_in_dim(kv_cache[0, :, 1], kv_at, HEAD_DIM, 1),
            lax.dynamic_slice_in_dim(out_weight[0], at, per_core, 0),
            gain,
        )

    kept = pick(core)
    received = tuple(swap(v) for v in pick(1 - core))
    x = segments_in.reshape(TOKENS, width)
    part = share // lax.axis_size("tp")
    mine = lax.dynamic_slice_in_dim(x, core * share + lax.axis_index("tp") * part, part, 0)
    outputs = []
    for which in range(LAYERS):
        query_proj, kv_proj, keys, values, out_proj, gain_row = (
            jnp.where(core == which, here, other) for here, other in zip(kept, received)
        )
        x, mine = layer(
            which, x, mine, gain_row, query_proj, kv_proj, out_proj, keys, values,
            block_logical, segment_block, index, core_at,
        )
        outputs.extend(x)
    result = call(
        choose_kernel,
        jax.ShapeDtypeStruct((TOKENS, width), BF16),
        [IN_SMEM] + [IN_VMEM] * 4,
        IN_VMEM,
    )(core_at, *outputs)
    return result.reshape(1, NSEG, SEG_LEN, width)


def solution(mesh):
    placed = (
        P(None, None, "kv"),
        P("section", "kv"),
        P("section", "kv", "tp"),
        P("section", "kv", None, "tp"),
        P("section", "tp", "kv"),
        P("section", "kv", None, "tp"),
        P("kv"),
        P(),
    )
    return jax.shard_map(
        per_device,
        mesh=mesh,
        in_specs=placed,
        out_specs=P("section", None, None, "kv"),
        check_vma=False,
    )
```

```python
import functools
import math

import jax
import jax.numpy as jnp
from jax import lax
from jax.experimental import pallas as pl
from jax.experimental.pallas import tpu as pltpu
from jax.sharding import PartitionSpec as P

D = 8192
HEAD_DIM = 128
BLOCK = 128
NSEG = 3
SEG_LEN = 128
TOKENS = NSEG * SEG_LEN
GROUP = 8
LAYERS = 2
EPSILON = 1e-05
CLOSED = -1e30
FRESH = 128
RANGE = 520000.0
MIDDLE = 524288
LEVELS = 2048
MASS_UNIT = 262144.0
HEADS_STEP = 2
SCALE = math.log2(math.e) / math.sqrt(HEAD_DIM)
F32 = jnp.float32
BF16 = jnp.bfloat16
VMEM_BYTES = 48 * 1024 * 1024


def call(kernel, out_shape, in_specs, out_specs, **rest):
    return pl.pallas_call(
        kernel,
        out_shape=out_shape,
        in_specs=in_specs,
        out_specs=out_specs,
        compiler_params=pltpu.CompilerParams(vmem_limit_bytes=VMEM_BYTES),
        **rest,
    )


IN_VMEM = pl.BlockSpec(memory_space=pltpu.VMEM)
IN_SMEM = pl.BlockSpec(memory_space=pltpu.SMEM)


def encode(block):
    top = jnp.maximum(jnp.max(jnp.abs(block), axis=0, keepdims=True), 1e-30)
    level = jnp.ceil(jnp.log2(top) * 16.0)
    value = jnp.round(block * (jnp.exp2(level * (-1.0 / 16.0)) * RANGE))
    return value.astype(jnp.int32) + MIDDLE, level.astype(jnp.int32)


def level_factor(level):
    return jnp.exp2(level.astype(F32) * (1.0 / 16.0)) * (1.0 / RANGE)


def pack(value):
    part = [value[8 * at : 8 * at + 8] for at in range(8)]
    lows = [
        part[5] & 0xFFF,
        (part[5] >> 12) | ((part[6] & 0xF) << 8),
        (part[6] >> 4) & 0xFFF,
        (part[6] >> 16) | ((part[7] & 0xFF) << 4),
        part[7] >> 8,
    ]
    return [(part[at] << 12) | lows[at] for at in range(5)]


def top_bits(word):
    return lax.shift_right_logical(word, jnp.int32(12))


def unpack(words):
    lows = [word & 0xFFF for word in words]
    part = [top_bits(word) for word in words]
    part.append(lows[0] | ((lows[1] & 0xFF) << 12))
    part.append((lows[1] >> 8) | (lows[2] << 4) | ((lows[3] & 0xF) << 16))
    part.append((lows[3] >> 4) | (lows[4] << 8))
    return (jnp.concatenate(part, axis=0) - MIDDLE).astype(F32)


def first_rows(rows, count=8):
    place = lax.broadcasted_iota(jnp.int32, (count, rows[0].shape[1]), 0)
    filled = jnp.zeros_like(place)
    for number, row in enumerate(rows):
        filled = jnp.where(place == number, row, filled)
    return filled


def square_rows(x):
    squares = jnp.sum(x * x, axis=1, keepdims=True)
    squares = jnp.broadcast_to(squares, (x.shape[0], 128))
    missing = -x.shape[0] % 128
    if missing:
        squares = jnp.concatenate([squares, jnp.zeros((missing, 128), F32)], axis=0)
    return squares.T[0:8]


def norm_columns(parts_ref):
    total = parts_ref[0]
    for peer in range(1, parts_ref.shape[0]):
        total = total + parts_ref[peer]
    factor = lax.rsqrt(total[0:1] / D + EPSILON)
    return jnp.broadcast_to(factor, (128, factor.shape[1])).T


def squares_kernel(count, x_ref, out_ref):
    rows = square_rows(x_ref[...].astype(F32))
    for peer in range(count):
        out_ref[peer] = rows


def first_project_kernel(count, x_ref, squares_ref, gain_ref, query_ref, kv_ref, out_ref):
    factor = norm_columns(squares_ref)[:, 0:1]
    normed = (x_ref[...].astype(F32) * factor * gain_ref[...]).astype(BF16)
    project(count, normed, query_ref, kv_ref, out_ref)


def project_kernel(count, core_ref, own_ref, other_ref, gain_ref, query_ref, kv_ref, out_ref, x_ref):
    share = TOKENS // 2
    width = gain_ref.shape[1]
    x_ref[pl.ds(core_ref[0] * share, share), :] = own_ref[...]
    x_ref[pl.ds((1 - core_ref[0]) * share, share), :] = other_ref[...]
    thirds = x_ref[:, width : width + 128].astype(F32)
    factor = thirds[:, 0:1] + thirds[:, 1:2] + thirds[:, 2:3]
    normed = (x_ref[:, 0:width].astype(F32) * factor * gain_ref[...]).astype(BF16)
    project(count, normed, query_ref, kv_ref, out_ref, True)


def swap_lanes(tile):
    return pltpu.roll(tile, SEG_LEN // 2, 1)


def left(shape):
    return lax.broadcasted_iota(jnp.int32, shape, 1) < SEG_LEN // 2


def fold(head, side):
    half = HEAD_DIM // 2
    tile = 2 * side * SEG_LEN
    low, high = head[0:half], head[half:]
    middle = slice(SEG_LEN, 2 * SEG_LEN)
    own = left((half, SEG_LEN))
    if side == 0:
        last = jnp.where(own, low[:, middle], swap_lanes(high[:, middle]))
    else:
        last = jnp.where(own, swap_lanes(low[:, middle]), high[:, middle])
    return jnp.concatenate([low[:, tile : tile + SEG_LEN], high[:, tile : tile + SEG_LEN], last], axis=1)


def project(count, scaled, query_ref, kv_ref, out_ref, folded=False):
    half = HEAD_DIM // 2
    columns = query_ref.shape[1]
    rows = SEG_LEN // count
    fresh = jnp.dot(scaled, kv_ref[...], preferred_element_type=F32)
    for start in range(0, columns, 256):
        part = jnp.dot(scaled, query_ref[:, start : start + 256], preferred_element_type=F32)
        turned = part.T
        for piece in range(256 // half):
            peer = start // half + piece
            if folded:
                head = turned[piece // 2 * HEAD_DIM : (piece // 2 + 1) * HEAD_DIM]
                block = fold(head, piece % 2)
            else:
                block = turned[piece * half : (piece + 1) * half]
            query, query_level = encode(block)
            words = pack(query)
            kinds = []
            for kind in range(2):
                lanes = slice(kind * HEAD_DIM, (kind + 1) * HEAD_DIM)
                block = jnp.concatenate(
                    [
                        fresh[seg * SEG_LEN + peer * rows : seg * SEG_LEN + (peer + 1) * rows, lanes]
                        for seg in range(NSEG)
                    ],
                    axis=1,
                )
                kinds.append(encode(block))
            levels = first_rows([query_level, kinds[0][1], kinds[1][1]]) + LEVELS
            words.append((kinds[0][0] << 12) | levels)
            words.append(kinds[1][0] << 12)
            for at, word in enumerate(words):
                out_ref[peer, 8 * at : 8 * at + 8, :] = word


def add_projection(count, parts_ref):
    half = HEAD_DIM // 2
    rows = SEG_LEN // count
    query = jnp.zeros((half, TOKENS), F32)
    fresh = [jnp.zeros((rows, TOKENS), F32) for _ in range(2)]
    for peer in range(count):
        words = [parts_ref[peer, 8 * at : 8 * at + 8, :] for at in range(7)]
        factors = level_factor((words[5] & 0xFFF) - LEVELS)
        query = query + unpack(words[0:5]) * factors[0:1]
        for kind in range(2):
            value = (top_bits(words[5 + kind]) - MIDDLE).astype(F32)
            fresh[kind] = fresh[kind] + value * factors[1 + kind : 2 + kind]
    return query, fresh


def finish_projection_kernel(count, parts_ref, query_out, fresh_out):
    rows = SEG_LEN // count
    query, fresh = add_projection(count, parts_ref)
    query = query.astype(BF16)
    for peer in range(count):
        query_out[peer] = query
    filler = jnp.zeros((FRESH - NSEG * rows, HEAD_DIM), F32)
    for kind in range(2):
        pieces = [
            fresh[kind][:, seg * SEG_LEN : (seg + 1) * SEG_LEN] for seg in range(NSEG)
        ]
        fresh_out[kind] = jnp.concatenate(pieces + [filler], axis=0).astype(BF16)


def finish_folded_kernel(count, parts_ref, query_out, fresh_out):
    half = HEAD_DIM // 2
    rows = SEG_LEN // count
    query, fresh = add_projection(count, parts_ref)
    own = left((half, SEG_LEN))
    last = query[:, 2 * SEG_LEN :]
    zero = jnp.zeros_like(last)
    low = jnp.concatenate([query[:, 0:SEG_LEN], jnp.where(own, last, zero)], axis=1)
    high = jnp.concatenate(
        [query[:, SEG_LEN : 2 * SEG_LEN], jnp.where(own, swap_lanes(last), zero)], axis=1
    )
    query_out[...] = jnp.concatenate([low, high], axis=0).astype(BF16)
    filler = jnp.zeros((rows, HEAD_DIM), F32)
    for kind in range(2):
        pieces = [
            fresh[kind][:, seg * SEG_LEN : (seg + 1) * SEG_LEN] for seg in range(NSEG)
        ]
        block = jnp.concatenate(pieces + [filler], axis=0).astype(BF16)
        for peer in range(count):
            fresh_out[peer, kind] = block


def segment_of(side, tile):
    return 2 * side if tile == 0 else 1


def far_peak_kernel(side_ref, logical_ref, start_ref, query_ref, keys_ref, out_ref, top_ref):
    step = pl.program_id(0)
    blocks = keys_ref.shape[1] // BLOCK

    @pl.when(step == 0)
    def _():
        top_ref[...] = jnp.full(top_ref.shape, CLOSED, F32)

    tops = [top_ref[:, tile * SEG_LEN : (tile + 1) * SEG_LEN] for tile in range(2)]
    for block in range(blocks):
        at = slice(block * BLOCK, (block + 1) * BLOCK)
        scores = jnp.dot(keys_ref[0, at, :], query_ref[...], preferred_element_type=F32)
        top = jnp.max(scores.reshape(BLOCK // 8, 8, 2 * SEG_LEN), axis=0)
        for tile in range(2):
            lanes = slice(tile * SEG_LEN, (tile + 1) * SEG_LEN)
            begin = start_ref[segment_of(side_ref[0], tile)]
            is_open = logical_ref[step * blocks + block] < begin
            tops[tile] = jnp.maximum(tops[tile], jnp.where(is_open, top[:, lanes], CLOSED))
    for tile in range(2):
        top_ref[:, tile * SEG_LEN : (tile + 1) * SEG_LEN] = tops[tile]

    @pl.when(step == pl.num_programs(0) - 1)
    def _():
        out_ref[...] = top_ref[...]


def whole_attend_kernel(
    rows, side_ref, logical_ref, start_ref, query_ref, keys_ref, values_ref, fresh_ref, top_ref,
    out_ref, peak_ref, mass_ref, sums_ref, weights, fresh_weights,
):
    step = pl.program_id(0)
    count = pl.num_programs(0)
    blocks = keys_ref.shape[1] // BLOCK
    half = HEAD_DIM // 2
    per_peer = fresh_ref.shape[2]
    new = fresh_ref.shape[0] * per_peer

    @pl.when(step == 0)
    def _():
        keys = fresh_ref[:, 0].reshape(new, HEAD_DIM)
        scores = jnp.dot(keys, query_ref[...], preferred_element_type=F32)
        row = lax.broadcasted_iota(jnp.int32, (new, SEG_LEN), 0)
        lane = lax.broadcasted_iota(jnp.int32, (new, SEG_LEN), 1)
        inner = row & (per_peer - 1)
        position = (row // per_peer) * rows + (inner & (rows - 1))
        for tile in range(2):
            lanes = slice(tile * SEG_LEN, (tile + 1) * SEG_LEN)
            token = lane if tile == 0 else lane + side_ref[0] * (SEG_LEN // 2)
            is_open = (inner // rows == segment_of(side_ref[0], tile)) & (position <= token)
            masked = jnp.where(is_open, scores[:, lanes], CLOSED)
            peak = jnp.maximum(
                jnp.max(masked, axis=0, keepdims=True),
                jnp.max(top_ref[:, lanes], axis=0, keepdims=True),
            )
            peak_ref[:, lanes] = peak
            weight = jnp.where(is_open, jnp.exp2((masked - peak) * SCALE), 0.0)
            mass_ref[:, lanes] = jnp.sum(weight.reshape(new // 8, 8, SEG_LEN), axis=0)
            fresh_weights[:, lanes] = weight.astype(BF16)
        values = fresh_ref[:, 1].reshape(new, HEAD_DIM).T
        sums_ref[...] = jnp.dot(values, fresh_weights[...], preferred_element_type=F32)

    masses = [mass_ref[:, tile * SEG_LEN : (tile + 1) * SEG_LEN] for tile in range(2)]
    peaks = [peak_ref[:, tile * SEG_LEN : (tile + 1) * SEG_LEN] for tile in range(2)]
    for block in range(blocks):
        at = slice(block * BLOCK, (block + 1) * BLOCK)
        scores = jnp.dot(keys_ref[0, at, :], query_ref[...], preferred_element_type=F32)
        for tile in range(2):
            lanes = slice(tile * SEG_LEN, (tile + 1) * SEG_LEN)
            begin = start_ref[segment_of(side_ref[0], tile)]
            is_open = logical_ref[step * blocks + block] < begin
            offset = jnp.where(is_open, peaks[tile], -CLOSED)
            weight = jnp.exp2((scores[:, lanes] - offset) * SCALE)
            weights[at, lanes] = weight.astype(BF16)
            masses[tile] = masses[tile] + jnp.sum(weight.reshape(BLOCK // 8, 8, SEG_LEN), axis=0)
    for tile in range(2):
        mass_ref[:, tile * SEG_LEN : (tile + 1) * SEG_LEN] = masses[tile]
    sums_ref[...] += jnp.dot(values_ref[0], weights[...], preferred_element_type=F32)

    @pl.when(step == count - 1)
    def _():
        attended = sums_ref[...] / jnp.sum(mass_ref[...], axis=0, keepdims=True)
        low, high = attended[0:half], attended[half:]
        own = left((half, SEG_LEN))
        last = jnp.where(own, low[:, SEG_LEN:], swap_lanes(high[:, SEG_LEN:]))
        block = jnp.concatenate([low[:, 0:SEG_LEN], high[:, 0:SEG_LEN], last], axis=1).astype(BF16)
        for peer in range(out_ref.shape[0]):
            out_ref[peer] = block


def fresh_mask(rows, index_ref, seg):
    key_row = lax.broadcasted_iota(jnp.int32, (FRESH, SEG_LEN), 0)
    token = lax.broadcasted_iota(jnp.int32, (FRESH, SEG_LEN), 1)
    local = key_row - seg * rows
    return (local >= 0) & (local < rows) & (local + index_ref[0] * rows <= token)


def peak_kernel(
    rows, index_ref, logical_ref, start_ref, query_ref, keys_ref, fresh_ref, out_ref, peaks
):
    blocks = keys_ref.shape[0] // BLOCK
    heads = query_ref.shape[0]
    step = pl.program_id(0)
    for head in range(heads):
        query = query_ref[head]
        scores = jnp.dot(fresh_ref[0], query, preferred_element_type=F32)
        tops = []
        for seg in range(NSEG):
            lanes = slice(seg * SEG_LEN, (seg + 1) * SEG_LEN)
            masked = jnp.where(fresh_mask(rows, index_ref, seg), scores[:, lanes], CLOSED)
            tops.append(jnp.max(masked.reshape(FRESH // 8, 8, SEG_LEN), axis=0))
        for block in range(blocks):
            at = slice(block * BLOCK, (block + 1) * BLOCK)
            scores = jnp.dot(keys_ref[at, :], query, preferred_element_type=F32)
            top = jnp.max(scores.reshape(BLOCK // 8, 8, TOKENS), axis=0)
            for seg in range(NSEG):
                lanes = slice(seg * SEG_LEN, (seg + 1) * SEG_LEN)
                is_open = logical_ref[block] < start_ref[seg]
                tops[seg] = jnp.maximum(tops[seg], jnp.where(is_open, top[:, lanes], CLOSED))
        peaks[step * heads + head] = jnp.concatenate(
            [jnp.max(top, axis=0, keepdims=True) for top in tops], axis=1
        )

    @pl.when(step == pl.num_programs(0) - 1)
    def _():
        found = jnp.concatenate([peaks[head] for head in range(GROUP)], axis=0)
        for peer in range(out_ref.shape[0]):
            out_ref[peer] = found


def attend_kernel(
    rows, index_ref, logical_ref, start_ref, query_ref, keys_ref, values_ref, fresh_ref, peaks_ref,
    out_ref, turned_values, peaks, weights,
):
    blocks = keys_ref.shape[0] // BLOCK
    stored = blocks * BLOCK
    half = HEAD_DIM // 2
    heads = query_ref.shape[0]
    step = pl.program_id(0)

    @pl.when(step == 0)
    def _():
        for block in range(blocks):
            at = slice(block * BLOCK, (block + 1) * BLOCK)
            turned_values[:, at] = values_ref[at, :].T
        turned_values[:, stored : stored + FRESH] = fresh_ref[1].T
        top = peaks_ref[0]
        for peer in range(1, peaks_ref.shape[0]):
            top = jnp.maximum(top, peaks_ref[peer])
        for head in range(GROUP):
            peaks[head] = top[head : head + 1]

    for head in range(heads):
        query = query_ref[head]
        peak = peaks[step * heads + head]
        scores = jnp.dot(fresh_ref[0], query, preferred_element_type=F32)
        masses = []
        for seg in range(NSEG):
            lanes = slice(seg * SEG_LEN, (seg + 1) * SEG_LEN)
            weight = jnp.exp2((scores[:, lanes] - peak[:, lanes]) * SCALE)
            weight = jnp.where(fresh_mask(rows, index_ref, seg), weight, 0.0)
            weights[head, stored : stored + FRESH, lanes] = weight.astype(BF16)
            masses.append(jnp.sum(weight.reshape(FRESH // 8, 8, SEG_LEN), axis=0))
        for block in range(blocks):
            at = slice(block * BLOCK, (block + 1) * BLOCK)
            scores = jnp.dot(keys_ref[at, :], query, preferred_element_type=F32)
            for seg in range(NSEG):
                lanes = slice(seg * SEG_LEN, (seg + 1) * SEG_LEN)
                is_open = logical_ref[block] < start_ref[seg]
                offset = jnp.where(is_open, peak[:, lanes], -CLOSED)
                weight = jnp.exp2((scores[:, lanes] - offset) * SCALE)
                weights[head, at, lanes] = weight.astype(BF16)
                masses[seg] = masses[seg] + jnp.sum(
                    weight.reshape(BLOCK // 8, 8, SEG_LEN), axis=0
                )
        sums = jnp.dot(turned_values[...], weights[head], preferred_element_type=F32)
        mass = jnp.concatenate(
            [jnp.sum(part, axis=0, keepdims=True) for part in masses], axis=1
        )
        mass = jnp.round(mass * MASS_UNIT).astype(jnp.int32)
        for piece in range(2):
            value, level = encode(sums[piece * half : (piece + 1) * half])
            for at, word in enumerate(pack(value) + [first_rows([level, mass])]):
                out_ref[2 * head + piece, 8 * at : 8 * at + 8, :] = word


def combine_kernel(count, parts_ref, out_ref):
    half = HEAD_DIM // 2
    mass = jnp.zeros((1, TOKENS), F32)
    sums = jnp.zeros((half, TOKENS), F32)
    for peer in range(count):
        words = [parts_ref[peer, 8 * at : 8 * at + 8, :] for at in range(6)]
        mass = mass + words[5][1:2].astype(F32) * (1.0 / MASS_UNIT)
        sums = sums + unpack(words[0:5]) * level_factor(words[5][0:1])
    attended = (sums / mass).astype(BF16)
    for peer in range(count):
        out_ref[peer] = attended


def output_kernel(core_ref, attended_ref, weight_ref, keep_ref, send_ref, scratch):
    project_output(core_ref, attended_ref, weight_ref, keep_ref, send_ref, scratch)


def project_output(core_ref, attended_ref, weight_ref, keep_ref, send_ref, scratch):
    share = TOKENS // 2
    scratch[...] = lax.dot_general(
        attended_ref[...], weight_ref[...], (((0,), (0,)), ((), ())), preferred_element_type=F32
    )
    keep_ref[...] = scratch[pl.ds(core_ref[0] * share, share), :]
    send_ref[...] = scratch[pl.ds((1 - core_ref[0]) * share, share), :]


def folded_output_kernel(core_ref, parts_ref, weight_ref, keep_ref, send_ref, scratch, attended):
    half = HEAD_DIM // 2
    own = left((half, SEG_LEN))
    for head in range(parts_ref.shape[0] // 2):
        at = head * HEAD_DIM
        for side in range(2):
            lanes = slice(2 * side * SEG_LEN, (2 * side + 1) * SEG_LEN)
            part = parts_ref[2 * head + side]
            attended[at : at + half, lanes] = part[:, 0:SEG_LEN]
            attended[at + half : at + HEAD_DIM, lanes] = part[:, SEG_LEN : 2 * SEG_LEN]
        first, second = (
            parts_ref[2 * head + side][:, 2 * SEG_LEN :].astype(F32) for side in range(2)
        )
        lanes = slice(SEG_LEN, 2 * SEG_LEN)
        attended[at : at + half, lanes] = jnp.where(own, first, swap_lanes(second)).astype(BF16)
        attended[at + half : at + HEAD_DIM, lanes] = jnp.where(
            own, swap_lanes(first), second
        ).astype(BF16)
    project_output(core_ref, attended, weight_ref, keep_ref, send_ref, scratch)


def add_kernel(keep_ref, received_ref, out_ref):
    out_ref[...] = keep_ref[...] + received_ref[...]


def add_residual(parts_ref, x_ref):
    total = parts_ref[0]
    for peer in range(1, parts_ref.shape[0]):
        total = total + parts_ref[peer]
    return (x_ref[...].astype(F32) + total).astype(BF16)


def residual_kernel(count, parts_ref, x_ref, out_ref, squares_ref):
    produced = add_residual(parts_ref, x_ref)
    out_ref[...] = produced
    rows = square_rows(produced.astype(F32))
    for peer in range(count):
        squares_ref[peer] = rows


def last_residual_kernel(parts_ref, x_ref, out_ref):
    produced = add_residual(parts_ref, x_ref)
    for peer in range(out_ref.shape[0]):
        out_ref[peer] = produced


def spread_kernel(squares_ref, x_ref, out_ref):
    tokens, width = x_ref.shape
    factor = norm_columns(squares_ref)[0:tokens]
    first = factor.astype(BF16).astype(F32)
    second = (factor - first).astype(BF16).astype(F32)
    lane = lax.broadcasted_iota(jnp.int32, factor.shape, 1)
    thirds = jnp.where(lane == 0, first, jnp.where(lane == 1, second, factor - first - second))
    for peer in range(out_ref.shape[0]):
        out_ref[peer, :, 0:width] = x_ref[...]
        out_ref[peer, :, width : width + 128] = thirds.astype(BF16)


def choose_kernel(core_ref, own0_ref, other0_ref, own1_ref, other1_ref, out_ref):
    share = TOKENS // 2
    width = out_ref.shape[1]
    first = core_ref[0] == 0
    at = pl.ds(core_ref[0] * share, share)
    out_ref[at, :] = jnp.where(first, own0_ref[:, 0:width], own1_ref[...])
    at = pl.ds((1 - core_ref[0]) * share, share)
    out_ref[at, :] = jnp.where(first, other0_ref[:, 0:width], other1_ref[...])


def exchange(value, axes):
    return lax.all_to_all(value, axes, 0, 0, tiled=True)


def swap(value):
    return lax.ppermute(value, "section", [(0, 1), (1, 0)])


def split_attention(parts, keys, values, logical, starts, index):
    count = lax.axis_size("kv")
    rows = SEG_LEN // count
    half = HEAD_DIM // 2
    with jax.named_scope("queries"):
        query, fresh = call(
            functools.partial(finish_projection_kernel, count),
            (
                jax.ShapeDtypeStruct((count, half, TOKENS), BF16),
                jax.ShapeDtypeStruct((2, FRESH, HEAD_DIM), BF16),
            ),
            [IN_VMEM],
            (IN_VMEM, IN_VMEM),
        )(parts)
        query = exchange(query, "kv").reshape(GROUP, HEAD_DIM, TOKENS)
    stored = keys.shape[0]
    by_head = [
        IN_SMEM,
        IN_SMEM,
        IN_SMEM,
        pl.BlockSpec((HEADS_STEP, HEAD_DIM, TOKENS), lambda h: (h, 0, 0)),
        pl.BlockSpec((stored, HEAD_DIM), lambda h: (0, 0)),
    ]
    whole_values = pl.BlockSpec((stored, HEAD_DIM), lambda h: (0, 0))
    whole_fresh = pl.BlockSpec((2, FRESH, HEAD_DIM), lambda h: (0, 0, 0))
    whole_peaks = pl.BlockSpec((count, GROUP, TOKENS), lambda h: (0, 0, 0))
    with jax.named_scope("peaks"):
        peaks = call(
            functools.partial(peak_kernel, rows),
            jax.ShapeDtypeStruct((count, GROUP, TOKENS), F32),
            by_head + [whole_fresh],
            whole_peaks,
            grid=(GROUP // HEADS_STEP,),
            scratch_shapes=[pltpu.VMEM((GROUP, 1, TOKENS), F32)],
        )(index, logical, starts, query, keys, fresh)
        peaks = exchange(peaks, "kv")
    with jax.named_scope("attend"):
        sent = call(
            functools.partial(attend_kernel, rows),
            jax.ShapeDtypeStruct((count, 6 * 8, TOKENS), jnp.int32),
            by_head + [whole_values, whole_fresh, whole_peaks],
            pl.BlockSpec((2 * HEADS_STEP, 6 * 8, TOKENS), lambda h: (h, 0, 0)),
            grid=(GROUP // HEADS_STEP,),
            scratch_shapes=[
                pltpu.VMEM((HEAD_DIM, stored + FRESH), BF16),
                pltpu.VMEM((GROUP, 1, TOKENS), F32),
                pltpu.VMEM((HEADS_STEP, stored + FRESH, TOKENS), BF16),
            ],
        )(index, logical, starts, query, keys, values, fresh, peaks)
        parts = exchange(sent, "kv")
    with jax.named_scope("combine"):
        attended = call(
            functools.partial(combine_kernel, count),
            jax.ShapeDtypeStruct((count, half, TOKENS), BF16),
            [IN_VMEM],
            IN_VMEM,
        )(parts)
        return exchange(attended, "kv").reshape(GROUP * HEAD_DIM, TOKENS)


def whole_attention(parts, keys, values, logical, starts, side):
    count = lax.axis_size("kv")
    rows = SEG_LEN // count
    half = HEAD_DIM // 2
    stored = keys.shape[1]
    with jax.named_scope("queries"):
        query, fresh = call(
            functools.partial(finish_folded_kernel, count),
            (
                jax.ShapeDtypeStruct((HEAD_DIM, 2 * SEG_LEN), BF16),
                jax.ShapeDtypeStruct((count, 2, 4 * rows, HEAD_DIM), BF16),
            ),
            [IN_VMEM],
            (IN_VMEM, IN_VMEM),
        )(parts)
        fresh = exchange(fresh, "kv")
    whole_query = pl.BlockSpec((HEAD_DIM, 2 * SEG_LEN), lambda k: (0, 0))
    whole_top = pl.BlockSpec((8, 2 * SEG_LEN), lambda k: (0, 0))
    by_holder = [
        IN_SMEM,
        IN_SMEM,
        IN_SMEM,
        whole_query,
        pl.BlockSpec((1, stored, HEAD_DIM), lambda k: (k, 0, 0)),
    ]
    with jax.named_scope("peaks"):
        top = call(
            far_peak_kernel,
            jax.ShapeDtypeStruct((8, 2 * SEG_LEN), F32),
            by_holder,
            whole_top,
            grid=(count,),
            scratch_shapes=[pltpu.VMEM((8, 2 * SEG_LEN), F32)],
        )(side, logical, starts, query, keys)
    with jax.named_scope("attend"):
        attended = call(
            functools.partial(whole_attend_kernel, rows),
            jax.ShapeDtypeStruct((count, half, TOKENS), BF16),
            by_holder
            + [
                pl.BlockSpec((1, HEAD_DIM, stored), lambda k: (k, 0, 0)),
                pl.BlockSpec((count, 2, 4 * rows, HEAD_DIM), lambda k: (0, 0, 0, 0)),
                whole_top,
            ],
            pl.BlockSpec((count, half, TOKENS), lambda k: (0, 0, 0)),
            grid=(count,),
            scratch_shapes=[
                pltpu.VMEM((1, 2 * SEG_LEN), F32),
                pltpu.VMEM((8, 2 * SEG_LEN), F32),
                pltpu.VMEM((HEAD_DIM, 2 * SEG_LEN), F32),
                pltpu.VMEM((stored, 2 * SEG_LEN), BF16),
                pltpu.VMEM((count * 4 * rows, 2 * SEG_LEN), BF16),
            ],
        )(side, logical, starts, query, keys, values, fresh, top)
        return exchange(attended, "kv")


def layer(
    which, x, mine, gain, query_proj, kv_proj, out_proj, keys, values, logical, starts, index, core
):
    count = lax.axis_size("kv")
    peers = lax.axis_size("tp")
    rows = SEG_LEN // count
    half = HEAD_DIM // 2
    width = query_proj.shape[0]
    share = TOKENS // 2
    part = share // peers
    with jax.named_scope("project"):
        shape = jax.ShapeDtypeStruct((count, 7 * 8, TOKENS), jnp.int32)
        if which == 0:
            squares = call(
                functools.partial(squares_kernel, count),
                jax.ShapeDtypeStruct((count, 8, TOKENS), F32),
                [IN_VMEM],
                IN_VMEM,
            )(x)
            squares = exchange(squares, "kv")
            sent = call(
                functools.partial(first_project_kernel, count), shape, [IN_VMEM] * 5, IN_VMEM
            )(x, squares, gain, query_proj, kv_proj)
        else:
            sent = call(
                functools.partial(project_kernel, count),
                shape,
                [IN_SMEM] + [IN_VMEM] * 5,
                IN_VMEM,
                scratch_shapes=[pltpu.VMEM((TOKENS, width + 128), BF16)],
            )(core, x[0], x[1], gain, query_proj, kv_proj)
        parts = exchange(sent, "kv")
    if which == 0:
        attended = split_attention(parts, keys, values, logical, starts, index)
        kernel, scratch = output_kernel, []
    else:
        attended = whole_attention(parts, keys, values, logical, starts, index)
        kernel, scratch = folded_output_kernel, [pltpu.VMEM((GROUP * HEAD_DIM, TOKENS), BF16)]
    with jax.named_scope("output"):
        keep, send = call(
            kernel,
            (jax.ShapeDtypeStruct((share, width), F32),) * 2,
            [IN_SMEM] + [IN_VMEM] * 2,
            (IN_VMEM, IN_VMEM),
            scratch_shapes=[pltpu.VMEM((TOKENS, width), F32)] + scratch,
        )(core, attended, out_proj)
        half_sum = call(
            add_kernel,
            jax.ShapeDtypeStruct((share, width), F32),
            [IN_VMEM] * 2,
            IN_VMEM,
        )(keep, swap(send))
        parts = exchange(half_sum.reshape(peers, part, width), "tp")
    with jax.named_scope("residual"):
        if which == LAYERS - 1:
            produced = call(
                last_residual_kernel,
                jax.ShapeDtypeStruct((peers, part, width), BF16),
                [IN_VMEM] * 2,
                IN_VMEM,
            )(parts, mine)
            mine = None
        else:
            mine, squares = call(
                functools.partial(residual_kernel, count),
                (
                    jax.ShapeDtypeStruct((part, width), BF16),
                    jax.ShapeDtypeStruct((count, 8, 128), F32),
                ),
                [IN_VMEM] * 2,
                (IN_VMEM, IN_VMEM),
            )(parts, mine)
            produced = call(
                spread_kernel,
                jax.ShapeDtypeStruct((peers, part, width + 128), BF16),
                [IN_VMEM] * 2,
                IN_VMEM,
            )(exchange(squares, "kv"), mine)
        own = exchange(produced, "tp").reshape(share, -1)
        return (own, swap(own)), mine


def per_device(
    segments_in, gain, query_weight, kv_weight, out_weight, kv_cache, block_logical, segment_block
):
    width = segments_in.shape[2]
    core = lax.axis_index("section")
    core_at = core.astype(jnp.int32)[None]
    index = lax.axis_index("kv").astype(jnp.int32)[None]
    per_core = GROUP * HEAD_DIM
    share = TOKENS // 2

    def pick(which):
        at = which * per_core
        kv_at = which * HEAD_DIM
        return (
            lax.dynamic_slice_in_dim(query_weight[0], at, per_core, 1),
            lax.dynamic_slice_in_dim(kv_weight[0], kv_at, HEAD_DIM, 2).reshape(width, -1),
            lax.dynamic_slice_in_dim(kv_cache[0, :, 0], kv_at, HEAD_DIM, 1),
            lax.dynamic_slice_in_dim(kv_cache[0, :, 1], kv_at, HEAD_DIM, 1),
            lax.dynamic_slice_in_dim(out_weight[0], at, per_core, 0),
            gain,
        )

    kept = pick(core)
    received = tuple(swap(v) for v in pick(1 - core))
    x = segments_in.reshape(TOKENS, width)
    part = share // lax.axis_size("tp")
    mine = lax.dynamic_slice_in_dim(x, core * share + lax.axis_index("tp") * part, part, 0)
    params = [
        [jnp.where(core == which, here, other) for here, other in zip(kept, received)]
        for which in range(LAYERS)
    ]
    all_keys = lax.all_gather(params[1][2], "kv")
    all_values = lax.all_gather(params[1][3].T, "kv")
    all_logical = lax.all_gather(block_logical, "kv", tiled=True)
    outputs = []
    for which in range(LAYERS):
        query_proj, kv_proj, keys, values, out_proj, gain_row = params[which]
        if which == 0:
            cache = (keys, values, block_logical, segment_block, index)
        else:
            cache = (all_keys, all_values, all_logical, segment_block, lax.rem(index, 2))
        x, mine = layer(which, x, mine, gain_row, query_proj, kv_proj, out_proj, *cache, core_at)
        outputs.extend(x)
    result = call(
        choose_kernel,
        jax.ShapeDtypeStruct((TOKENS, width), BF16),
        [IN_SMEM] + [IN_VMEM] * 4,
        IN_VMEM,
    )(core_at, *outputs)
    return result.reshape(1, NSEG, SEG_LEN, width)


def solution(mesh):
    placed = (
        P(None, None, "kv"),
        P("section", "kv"),
        P("section", "kv", "tp"),
        P("section", "kv", None, "tp"),
        P("section", "tp", "kv"),
        P("section", "kv", None, "tp"),
        P("kv"),
        P(),
    )
    return jax.shard_map(
        per_device,
        mesh=mesh,
        in_specs=placed,
        out_specs=P("section", None, None, "kv"),
        check_vma=False,
    )
```

```python
import functools
import math

import jax
import jax.numpy as jnp
from jax import lax
from jax.experimental import pallas as pl
from jax.experimental.pallas import tpu as pltpu
from jax.sharding import PartitionSpec as P

D = 8192
HEAD_DIM = 128
BLOCK = 128
NSEG = 3
SEG_LEN = 128
TOKENS = NSEG * SEG_LEN
GROUP = 8
LAYERS = 2
EPSILON = 1e-05
CLOSED = -1e30
FRESH = 128
RANGE = 520000.0
MIDDLE = 524288
LEVELS = 2048
MASS_UNIT = 262144.0
HEADS_STEP = 2
ABREAST = 4
SCALE = math.log2(math.e) / math.sqrt(HEAD_DIM)
F32 = jnp.float32
BF16 = jnp.bfloat16
VMEM_BYTES = 48 * 1024 * 1024


def call(kernel, out_shape, in_specs, out_specs, **rest):
    return pl.pallas_call(
        kernel,
        out_shape=out_shape,
        in_specs=in_specs,
        out_specs=out_specs,
        compiler_params=pltpu.CompilerParams(vmem_limit_bytes=VMEM_BYTES),
        **rest,
    )


IN_VMEM = pl.BlockSpec(memory_space=pltpu.VMEM)
IN_SMEM = pl.BlockSpec(memory_space=pltpu.SMEM)


def encode(block):
    top = jnp.maximum(jnp.max(jnp.abs(block), axis=0, keepdims=True), 1e-30)
    level = jnp.ceil(jnp.log2(top) * 16.0)
    value = jnp.round(block * (jnp.exp2(level * (-1.0 / 16.0)) * RANGE))
    return value.astype(jnp.int32) + MIDDLE, level.astype(jnp.int32)


def level_factor(level):
    return jnp.exp2(level.astype(F32) * (1.0 / 16.0)) * (1.0 / RANGE)


def pack(value):
    part = [value[8 * at : 8 * at + 8] for at in range(8)]
    lows = [
        part[5] & 0xFFF,
        (part[5] >> 12) | ((part[6] & 0xF) << 8),
        (part[6] >> 4) & 0xFFF,
        (part[6] >> 16) | ((part[7] & 0xFF) << 4),
        part[7] >> 8,
    ]
    return [(part[at] << 12) | lows[at] for at in range(5)]


def top_bits(word):
    return lax.shift_right_logical(word, jnp.int32(12))


def unpack(words):
    lows = [word & 0xFFF for word in words]
    part = [top_bits(word) for word in words]
    part.append(lows[0] | ((lows[1] & 0xFF) << 12))
    part.append((lows[1] >> 8) | (lows[2] << 4) | ((lows[3] & 0xF) << 16))
    part.append((lows[3] >> 4) | (lows[4] << 8))
    return (jnp.concatenate(part, axis=0) - MIDDLE).astype(F32)


def first_rows(rows, count=8):
    place = lax.broadcasted_iota(jnp.int32, (count, rows[0].shape[1]), 0)
    filled = jnp.zeros_like(place)
    for number, row in enumerate(rows):
        filled = jnp.where(place == number, row, filled)
    return filled


def square_rows(x):
    squares = jnp.sum(x * x, axis=1, keepdims=True)
    squares = jnp.broadcast_to(squares, (x.shape[0], 128))
    missing = -x.shape[0] % 128
    if missing:
        squares = jnp.concatenate([squares, jnp.zeros((missing, 128), F32)], axis=0)
    return squares.T[0:8]


def norm_columns(parts_ref):
    total = parts_ref[0]
    for peer in range(1, parts_ref.shape[0]):
        total = total + parts_ref[peer]
    factor = lax.rsqrt(total[0:1] / D + EPSILON)
    return jnp.broadcast_to(factor, (128, factor.shape[1])).T


def squares_kernel(count, x_ref, logical_ref, out_ref):
    rows = square_rows(x_ref[...].astype(F32))
    row = lax.broadcasted_iota(jnp.int32, rows.shape, 0)
    rows = jnp.where(row == 0, rows, logical_ref[...])
    for peer in range(count):
        out_ref[peer] = rows


def turn_kernel(values_ref, out_ref):
    for block in range(values_ref.shape[0] // BLOCK):
        at = slice(block * BLOCK, (block + 1) * BLOCK)
        out_ref[:, at] = values_ref[at, :].T


def first_project_kernel(count, x_ref, squares_ref, gain_ref, query_ref, kv_ref, out_ref):
    factor = norm_columns(squares_ref)[:, 0:1]
    normed = (x_ref[...].astype(F32) * factor * gain_ref[...]).astype(BF16)
    project(count, normed, query_ref, kv_ref, out_ref)


def project_kernel(count, core_ref, own_ref, other_ref, gain_ref, query_ref, kv_ref, out_ref, x_ref):
    share = TOKENS // 2
    width = gain_ref.shape[1]
    x_ref[pl.ds(core_ref[0] * share, share), :] = own_ref[...]
    x_ref[pl.ds((1 - core_ref[0]) * share, share), :] = other_ref[...]
    thirds = x_ref[:, width : width + 128].astype(F32)
    factor = thirds[:, 0:1] + thirds[:, 1:2] + thirds[:, 2:3]
    normed = (x_ref[:, 0:width].astype(F32) * factor * gain_ref[...]).astype(BF16)
    project(count, normed, query_ref, kv_ref, out_ref, True)


def swap_lanes(tile):
    return pltpu.roll(tile, SEG_LEN // 2, 1)


def left(shape):
    return lax.broadcasted_iota(jnp.int32, shape, 1) < SEG_LEN // 2


def fold(head, side):
    half = HEAD_DIM // 2
    tile = 2 * side * SEG_LEN
    low, high = head[0:half], head[half:]
    middle = slice(SEG_LEN, 2 * SEG_LEN)
    own = left((half, SEG_LEN))
    if side == 0:
        last = jnp.where(own, low[:, middle], swap_lanes(high[:, middle]))
    else:
        last = jnp.where(own, swap_lanes(low[:, middle]), high[:, middle])
    return jnp.concatenate([low[:, tile : tile + SEG_LEN], high[:, tile : tile + SEG_LEN], last], axis=1)


def project(count, scaled, query_ref, kv_ref, out_ref, folded=False):
    half = HEAD_DIM // 2
    columns = query_ref.shape[1]
    rows = SEG_LEN // count
    fresh = jnp.dot(scaled, kv_ref[...], preferred_element_type=F32)
    for start in range(0, columns, 256):
        part = jnp.dot(scaled, query_ref[:, start : start + 256], preferred_element_type=F32)
        turned = part.T
        for piece in range(256 // half):
            peer = start // half + piece
            if folded:
                head = turned[piece // 2 * HEAD_DIM : (piece // 2 + 1) * HEAD_DIM]
                block = fold(head, piece % 2)
            else:
                block = turned[piece * half : (piece + 1) * half]
            query, query_level = encode(block)
            words = pack(query)
            kinds = []
            for kind in range(2):
                lanes = slice(kind * HEAD_DIM, (kind + 1) * HEAD_DIM)
                block = jnp.concatenate(
                    [
                        fresh[seg * SEG_LEN + peer * rows : seg * SEG_LEN + (peer + 1) * rows, lanes]
                        for seg in range(NSEG)
                    ],
                    axis=1,
                )
                kinds.append(encode(block))
            levels = first_rows([query_level, kinds[0][1], kinds[1][1]]) + LEVELS
            words.append((kinds[0][0] << 12) | levels)
            words.append(kinds[1][0] << 12)
            for at, word in enumerate(words):
                out_ref[peer, 8 * at : 8 * at + 8, :] = word


def add_projection(count, parts_ref):
    half = HEAD_DIM // 2
    rows = SEG_LEN // count
    query = jnp.zeros((half, TOKENS), F32)
    fresh = [jnp.zeros((rows, TOKENS), F32) for _ in range(2)]
    for peer in range(count):
        words = [parts_ref[peer, 8 * at : 8 * at + 8, :] for at in range(7)]
        factors = level_factor((words[5] & 0xFFF) - LEVELS)
        query = query + unpack(words[0:5]) * factors[0:1]
        for kind in range(2):
            value = (top_bits(words[5 + kind]) - MIDDLE).astype(F32)
            fresh[kind] = fresh[kind] + value * factors[1 + kind : 2 + kind]
    return query, fresh


def finish_projection_kernel(count, parts_ref, query_out, fresh_out):
    rows = SEG_LEN // count
    query, fresh = add_projection(count, parts_ref)
    query = query.astype(BF16)
    for peer in range(count):
        query_out[peer] = query
    filler = jnp.zeros((FRESH - NSEG * rows, HEAD_DIM), F32)
    for kind in range(2):
        pieces = [
            fresh[kind][:, seg * SEG_LEN : (seg + 1) * SEG_LEN] for seg in range(NSEG)
        ]
        fresh_out[kind] = jnp.concatenate(pieces + [filler], axis=0).astype(BF16)


def finish_folded_kernel(count, parts_ref, query_out, fresh_out):
    half = HEAD_DIM // 2
    rows = SEG_LEN // count
    query, fresh = add_projection(count, parts_ref)
    own = left((half, SEG_LEN))
    last = query[:, 2 * SEG_LEN :]
    zero = jnp.zeros_like(last)
    low = jnp.concatenate([query[:, 0:SEG_LEN], jnp.where(own, last, zero)], axis=1)
    high = jnp.concatenate(
        [query[:, SEG_LEN : 2 * SEG_LEN], jnp.where(own, swap_lanes(last), zero)], axis=1
    )
    query_out[...] = jnp.concatenate([low, high], axis=0).astype(BF16)
    filler = jnp.zeros((rows, HEAD_DIM), F32)
    for kind in range(2):
        pieces = [
            fresh[kind][:, seg * SEG_LEN : (seg + 1) * SEG_LEN] for seg in range(NSEG)
        ]
        block = jnp.concatenate(pieces + [filler], axis=0).astype(BF16)
        for peer in range(count):
            fresh_out[peer, kind] = block


def segment_of(side, tile):
    return 2 * side if tile == 0 else 1


def far_peak_kernel(side_ref, logical_ref, start_ref, query_ref, *refs):
    keys_refs, (out_ref, top_ref) = refs[0:ABREAST], refs[ABREAST:]
    step = pl.program_id(0)
    blocks = keys_refs[0].shape[1] // BLOCK

    @pl.when(step == 0)
    def _():
        top_ref[...] = jnp.full(top_ref.shape, CLOSED, F32)

    tops = [top_ref[:, tile * SEG_LEN : (tile + 1) * SEG_LEN] for tile in range(2)]
    for number in range(ABREAST * blocks):
        block = number % blocks
        at = slice(block * BLOCK, (block + 1) * BLOCK)
        keys = keys_refs[number // blocks][0, at, :]
        scores = jnp.dot(keys, query_ref[...], preferred_element_type=F32)
        top = jnp.max(scores.reshape(BLOCK // 8, 8, 2 * SEG_LEN), axis=0)
        for tile in range(2):
            lanes = slice(tile * SEG_LEN, (tile + 1) * SEG_LEN)
            begin = start_ref[segment_of(side_ref[0], tile)]
            is_open = logical_ref[step * ABREAST * blocks + number] < begin
            tops[tile] = jnp.maximum(tops[tile], jnp.where(is_open, top[:, lanes], CLOSED))
    for tile in range(2):
        top_ref[:, tile * SEG_LEN : (tile + 1) * SEG_LEN] = tops[tile]

    @pl.when(step == pl.num_programs(0) - 1)
    def _():
        out_ref[...] = top_ref[...]


def whole_attend_kernel(
    rows, side_ref, logical_ref, start_ref, query_ref, *refs
):
    keys_refs, values_refs = refs[0:ABREAST], refs[ABREAST : 2 * ABREAST]
    fresh_ref, top_ref, out_ref, peak_ref, mass_ref, sums_ref, weights, fresh_weights = refs[
        2 * ABREAST :
    ]
    step = pl.program_id(0)
    stored = keys_refs[0].shape[1]
    blocks = stored // BLOCK
    half = HEAD_DIM // 2
    per_peer = fresh_ref.shape[2]
    new = fresh_ref.shape[0] * per_peer

    @pl.when(step == 0)
    def _():
        keys = fresh_ref[:, 0].reshape(new, HEAD_DIM)
        scores = jnp.dot(keys, query_ref[...], preferred_element_type=F32)
        row = lax.broadcasted_iota(jnp.int32, (new, SEG_LEN), 0)
        lane = lax.broadcasted_iota(jnp.int32, (new, SEG_LEN), 1)
        inner = row & (per_peer - 1)
        position = (row // per_peer) * rows + (inner & (rows - 1))
        for tile in range(2):
            lanes = slice(tile * SEG_LEN, (tile + 1) * SEG_LEN)
            token = lane if tile == 0 else lane + side_ref[0] * (SEG_LEN // 2)
            is_open = (inner // rows == segment_of(side_ref[0], tile)) & (position <= token)
            masked = jnp.where(is_open, scores[:, lanes], CLOSED)
            peak = jnp.maximum(
                jnp.max(masked, axis=0, keepdims=True),
                jnp.max(top_ref[:, lanes], axis=0, keepdims=True),
            )
            peak_ref[:, lanes] = peak
            weight = jnp.where(is_open, jnp.exp2((masked - peak) * SCALE), 0.0)
            mass_ref[:, lanes] = jnp.sum(weight.reshape(new // 8, 8, SEG_LEN), axis=0)
            fresh_weights[:, lanes] = weight.astype(BF16)
        values = fresh_ref[:, 1].reshape(new, HEAD_DIM).T
        sums_ref[...] = jnp.dot(values, fresh_weights[...], preferred_element_type=F32)

    masses = [mass_ref[:, tile * SEG_LEN : (tile + 1) * SEG_LEN] for tile in range(2)]
    peaks = [peak_ref[:, tile * SEG_LEN : (tile + 1) * SEG_LEN] for tile in range(2)]
    for number in range(ABREAST * blocks):
        block = number % blocks
        at = slice(block * BLOCK, (block + 1) * BLOCK)
        keys = keys_refs[number // blocks][0, at, :]
        scores = jnp.dot(keys, query_ref[...], preferred_element_type=F32)
        for tile in range(2):
            lanes = slice(tile * SEG_LEN, (tile + 1) * SEG_LEN)
            begin = start_ref[segment_of(side_ref[0], tile)]
            is_open = logical_ref[step * ABREAST * blocks + number] < begin
            offset = jnp.where(is_open, peaks[tile], -CLOSED)
            weight = jnp.exp2((scores[:, lanes] - offset) * SCALE)
            weights[number * BLOCK : (number + 1) * BLOCK, lanes] = weight.astype(BF16)
            masses[tile] = masses[tile] + jnp.sum(weight.reshape(BLOCK // 8, 8, SEG_LEN), axis=0)
    for tile in range(2):
        mass_ref[:, tile * SEG_LEN : (tile + 1) * SEG_LEN] = masses[tile]
    sums = sums_ref[...]
    for holder in range(ABREAST):
        sums = sums + jnp.dot(
            values_refs[holder][0],
            weights[holder * stored : (holder + 1) * stored, :],
            preferred_element_type=F32,
        )
    sums_ref[...] = sums

    @pl.when(step == pl.num_programs(0) - 1)
    def _():
        attended = sums_ref[...] / jnp.sum(mass_ref[...], axis=0, keepdims=True)
        low, high = attended[0:half], attended[half:]
        own = left((half, SEG_LEN))
        last = jnp.where(own, low[:, SEG_LEN:], swap_lanes(high[:, SEG_LEN:]))
        block = jnp.concatenate([low[:, 0:SEG_LEN], high[:, 0:SEG_LEN], last], axis=1).astype(BF16)
        for peer in range(out_ref.shape[0]):
            out_ref[peer] = block


def fresh_mask(rows, index_ref, seg):
    key_row = lax.broadcasted_iota(jnp.int32, (FRESH, SEG_LEN), 0)
    token = lax.broadcasted_iota(jnp.int32, (FRESH, SEG_LEN), 1)
    local = key_row - seg * rows
    return (local >= 0) & (local < rows) & (local + index_ref[0] * rows <= token)


def peak_kernel(
    rows, index_ref, logical_ref, start_ref, query_ref, keys_ref, fresh_ref, out_ref, peaks
):
    blocks = keys_ref.shape[0] // BLOCK
    heads = query_ref.shape[0]
    step = pl.program_id(0)
    for head in range(heads):
        query = query_ref[head]
        scores = jnp.dot(fresh_ref[0], query, preferred_element_type=F32)
        tops = []
        for seg in range(NSEG):
            lanes = slice(seg * SEG_LEN, (seg + 1) * SEG_LEN)
            masked = jnp.where(fresh_mask(rows, index_ref, seg), scores[:, lanes], CLOSED)
            tops.append(jnp.max(masked.reshape(FRESH // 8, 8, SEG_LEN), axis=0))
        for block in range(blocks):
            at = slice(block * BLOCK, (block + 1) * BLOCK)
            scores = jnp.dot(keys_ref[at, :], query, preferred_element_type=F32)
            top = jnp.max(scores.reshape(BLOCK // 8, 8, TOKENS), axis=0)
            for seg in range(NSEG):
                lanes = slice(seg * SEG_LEN, (seg + 1) * SEG_LEN)
                is_open = logical_ref[block] < start_ref[seg]
                tops[seg] = jnp.maximum(tops[seg], jnp.where(is_open, top[:, lanes], CLOSED))
        peaks[step * heads + head] = jnp.concatenate(
            [jnp.max(top, axis=0, keepdims=True) for top in tops], axis=1
        )

    @pl.when(step == pl.num_programs(0) - 1)
    def _():
        found = jnp.concatenate([peaks[head] for head in range(GROUP)], axis=0)
        for peer in range(out_ref.shape[0]):
            out_ref[peer] = found


def attend_kernel(
    rows, index_ref, logical_ref, start_ref, query_ref, keys_ref, values_ref, fresh_ref, peaks_ref,
    out_ref, turned_values, peaks, weights,
):
    blocks = keys_ref.shape[0] // BLOCK
    stored = blocks * BLOCK
    half = HEAD_DIM // 2
    heads = query_ref.shape[0]
    step = pl.program_id(0)

    @pl.when(step == 0)
    def _():
        for block in range(blocks):
            at = slice(block * BLOCK, (block + 1) * BLOCK)
            turned_values[:, at] = values_ref[at, :].T
        turned_values[:, stored : stored + FRESH] = fresh_ref[1].T
        top = peaks_ref[0]
        for peer in range(1, peaks_ref.shape[0]):
            top = jnp.maximum(top, peaks_ref[peer])
        for head in range(GROUP):
            peaks[head] = top[head : head + 1]

    for head in range(heads):
        query = query_ref[head]
        peak = peaks[step * heads + head]
        scores = jnp.dot(fresh_ref[0], query, preferred_element_type=F32)
        masses = []
        for seg in range(NSEG):
            lanes = slice(seg * SEG_LEN, (seg + 1) * SEG_LEN)
            weight = jnp.exp2((scores[:, lanes] - peak[:, lanes]) * SCALE)
            weight = jnp.where(fresh_mask(rows, index_ref, seg), weight, 0.0)
            weights[head, stored : stored + FRESH, lanes] = weight.astype(BF16)
            masses.append(jnp.sum(weight.reshape(FRESH // 8, 8, SEG_LEN), axis=0))
        for block in range(blocks):
            at = slice(block * BLOCK, (block + 1) * BLOCK)
            scores = jnp.dot(keys_ref[at, :], query, preferred_element_type=F32)
            for seg in range(NSEG):
                lanes = slice(seg * SEG_LEN, (seg + 1) * SEG_LEN)
                is_open = logical_ref[block] < start_ref[seg]
                offset = jnp.where(is_open, peak[:, lanes], -CLOSED)
                weight = jnp.exp2((scores[:, lanes] - offset) * SCALE)
                weights[head, at, lanes] = weight.astype(BF16)
                masses[seg] = masses[seg] + jnp.sum(
                    weight.reshape(BLOCK // 8, 8, SEG_LEN), axis=0
                )
        sums = jnp.dot(turned_values[...], weights[head], preferred_element_type=F32)
        mass = jnp.concatenate(
            [jnp.sum(part, axis=0, keepdims=True) for part in masses], axis=1
        )
        mass = jnp.round(mass * MASS_UNIT).astype(jnp.int32)
        for piece in range(2):
            value, level = encode(sums[piece * half : (piece + 1) * half])
            for at, word in enumerate(pack(value) + [first_rows([level, mass])]):
                out_ref[2 * head + piece, 8 * at : 8 * at + 8, :] = word


def combine_kernel(count, parts_ref, out_ref):
    half = HEAD_DIM // 2
    mass = jnp.zeros((1, TOKENS), F32)
    sums = jnp.zeros((half, TOKENS), F32)
    for peer in range(count):
        words = [parts_ref[peer, 8 * at : 8 * at + 8, :] for at in range(6)]
        mass = mass + words[5][1:2].astype(F32) * (1.0 / MASS_UNIT)
        sums = sums + unpack(words[0:5]) * level_factor(words[5][0:1])
    attended = (sums / mass).astype(BF16)
    for peer in range(count):
        out_ref[peer] = attended


def output_kernel(core_ref, attended_ref, weight_ref, keep_ref, send_ref, scratch):
    project_output(core_ref, attended_ref, weight_ref, keep_ref, send_ref, scratch)


def project_output(core_ref, attended_ref, weight_ref, keep_ref, send_ref, scratch):
    share = TOKENS // 2
    scratch[...] = lax.dot_general(
        attended_ref[...], weight_ref[...], (((0,), (0,)), ((), ())), preferred_element_type=F32
    )
    keep_ref[...] = scratch[pl.ds(core_ref[0] * share, share), :]
    send_ref[...] = scratch[pl.ds((1 - core_ref[0]) * share, share), :]


def folded_output_kernel(core_ref, parts_ref, weight_ref, keep_ref, send_ref, scratch, attended):
    half = HEAD_DIM // 2
    own = left((half, SEG_LEN))
    for head in range(parts_ref.shape[0] // 2):
        at = head * HEAD_DIM
        for side in range(2):
            lanes = slice(2 * side * SEG_LEN, (2 * side + 1) * SEG_LEN)
            part = parts_ref[2 * head + side]
            attended[at : at + half, lanes] = part[:, 0:SEG_LEN]
            attended[at + half : at + HEAD_DIM, lanes] = part[:, SEG_LEN : 2 * SEG_LEN]
        first, second = (
            parts_ref[2 * head + side][:, 2 * SEG_LEN :].astype(F32) for side in range(2)
        )
        lanes = slice(SEG_LEN, 2 * SEG_LEN)
        attended[at : at + half, lanes] = jnp.where(own, first, swap_lanes(second)).astype(BF16)
        attended[at + half : at + HEAD_DIM, lanes] = jnp.where(
            own, swap_lanes(first), second
        ).astype(BF16)
    project_output(core_ref, attended, weight_ref, keep_ref, send_ref, scratch)


def add_kernel(keep_ref, received_ref, out_ref):
    out_ref[...] = keep_ref[...] + received_ref[...]


def add_residual(parts_ref, x_ref):
    total = parts_ref[0]
    for peer in range(1, parts_ref.shape[0]):
        total = total + parts_ref[peer]
    return (x_ref[...].astype(F32) + total).astype(BF16)


def residual_kernel(count, parts_ref, x_ref, out_ref, squares_ref):
    produced = add_residual(parts_ref, x_ref)
    out_ref[...] = produced
    rows = square_rows(produced.astype(F32))
    for peer in range(count):
        squares_ref[peer] = rows


def last_residual_kernel(parts_ref, x_ref, out_ref):
    produced = add_residual(parts_ref, x_ref)
    for peer in range(out_ref.shape[0]):
        out_ref[peer] = produced


def spread_kernel(squares_ref, x_ref, out_ref):
    tokens, width = x_ref.shape
    factor = norm_columns(squares_ref)[0:tokens]
    first = factor.astype(BF16).astype(F32)
    second = (factor - first).astype(BF16).astype(F32)
    lane = lax.broadcasted_iota(jnp.int32, factor.shape, 1)
    thirds = jnp.where(lane == 0, first, jnp.where(lane == 1, second, factor - first - second))
    for peer in range(out_ref.shape[0]):
        out_ref[peer, :, 0:width] = x_ref[...]
        out_ref[peer, :, width : width + 128] = thirds.astype(BF16)


def choose_kernel(core_ref, own0_ref, other0_ref, own1_ref, other1_ref, out_ref):
    share = TOKENS // 2
    width = out_ref.shape[1]
    first = core_ref[0] == 0
    at = pl.ds(core_ref[0] * share, share)
    out_ref[at, :] = jnp.where(first, own0_ref[:, 0:width], own1_ref[...])
    at = pl.ds((1 - core_ref[0]) * share, share)
    out_ref[at, :] = jnp.where(first, other0_ref[:, 0:width], other1_ref[...])


def exchange(value, axes):
    return lax.all_to_all(value, axes, 0, 0, tiled=True)


def swap(value):
    return lax.ppermute(value, "section", [(0, 1), (1, 0)])


def split_attention(parts, keys, values, logical, starts, index):
    count = lax.axis_size("kv")
    rows = SEG_LEN // count
    half = HEAD_DIM // 2
    with jax.named_scope("queries"):
        query, fresh = call(
            functools.partial(finish_projection_kernel, count),
            (
                jax.ShapeDtypeStruct((count, half, TOKENS), BF16),
                jax.ShapeDtypeStruct((2, FRESH, HEAD_DIM), BF16),
            ),
            [IN_VMEM],
            (IN_VMEM, IN_VMEM),
        )(parts)
        query = exchange(query, "kv").reshape(GROUP, HEAD_DIM, TOKENS)
    stored = keys.shape[0]
    by_head = [
        IN_SMEM,
        IN_SMEM,
        IN_SMEM,
        pl.BlockSpec((HEADS_STEP, HEAD_DIM, TOKENS), lambda h: (h, 0, 0)),
        pl.BlockSpec((stored, HEAD_DIM), lambda h: (0, 0)),
    ]
    whole_values = pl.BlockSpec((stored, HEAD_DIM), lambda h: (0, 0))
    whole_fresh = pl.BlockSpec((2, FRESH, HEAD_DIM), lambda h: (0, 0, 0))
    whole_peaks = pl.BlockSpec((count, GROUP, TOKENS), lambda h: (0, 0, 0))
    with jax.named_scope("peaks"):
        peaks = call(
            functools.partial(peak_kernel, rows),
            jax.ShapeDtypeStruct((count, GROUP, TOKENS), F32),
            by_head + [whole_fresh],
            whole_peaks,
            grid=(GROUP // HEADS_STEP,),
            scratch_shapes=[pltpu.VMEM((GROUP, 1, TOKENS), F32)],
        )(index, logical, starts, query, keys, fresh)
        peaks = exchange(peaks, "kv")
    with jax.named_scope("attend"):
        sent = call(
            functools.partial(attend_kernel, rows),
            jax.ShapeDtypeStruct((count, 6 * 8, TOKENS), jnp.int32),
            by_head + [whole_values, whole_fresh, whole_peaks],
            pl.BlockSpec((2 * HEADS_STEP, 6 * 8, TOKENS), lambda h: (h, 0, 0)),
            grid=(GROUP // HEADS_STEP,),
            scratch_shapes=[
                pltpu.VMEM((HEAD_DIM, stored + FRESH), BF16),
                pltpu.VMEM((GROUP, 1, TOKENS), F32),
                pltpu.VMEM((HEADS_STEP, stored + FRESH, TOKENS), BF16),
            ],
        )(index, logical, starts, query, keys, values, fresh, peaks)
        parts = exchange(sent, "kv")
    with jax.named_scope("combine"):
        attended = call(
            functools.partial(combine_kernel, count),
            jax.ShapeDtypeStruct((count, half, TOKENS), BF16),
            [IN_VMEM],
            IN_VMEM,
        )(parts)
        return exchange(attended, "kv").reshape(GROUP * HEAD_DIM, TOKENS)


def whole_attention(parts, keys, values, logical, starts, side):
    count = lax.axis_size("kv")
    rows = SEG_LEN // count
    half = HEAD_DIM // 2
    stored = keys.shape[1]
    with jax.named_scope("queries"):
        query, fresh = call(
            functools.partial(finish_folded_kernel, count),
            (
                jax.ShapeDtypeStruct((HEAD_DIM, 2 * SEG_LEN), BF16),
                jax.ShapeDtypeStruct((count, 2, 4 * rows, HEAD_DIM), BF16),
            ),
            [IN_VMEM],
            (IN_VMEM, IN_VMEM),
        )(parts)
        fresh = exchange(fresh, "kv")
    whole_query = pl.BlockSpec((HEAD_DIM, 2 * SEG_LEN), lambda k: (0, 0))
    whole_top = pl.BlockSpec((8, 2 * SEG_LEN), lambda k: (0, 0))
    by_holder = [
        IN_SMEM,
        IN_SMEM,
        IN_SMEM,
        whole_query,
    ]
    by_holder += [
        pl.BlockSpec((1, stored, HEAD_DIM), lambda k, n=number: (ABREAST * k + n, 0, 0))
        for number in range(ABREAST)
    ]
    with jax.named_scope("peaks"):
        top = call(
            far_peak_kernel,
            jax.ShapeDtypeStruct((8, 2 * SEG_LEN), F32),
            by_holder,
            whole_top,
            grid=(count // ABREAST,),
            scratch_shapes=[pltpu.VMEM((8, 2 * SEG_LEN), F32)],
        )(side, logical, starts, query, *[keys] * ABREAST)
    with jax.named_scope("attend"):
        attended = call(
            functools.partial(whole_attend_kernel, rows),
            jax.ShapeDtypeStruct((count, half, TOKENS), BF16),
            by_holder
            + [
                pl.BlockSpec((1, HEAD_DIM, stored), lambda k, n=number: (ABREAST * k + n, 0, 0))
                for number in range(ABREAST)
            ]
            + [
                pl.BlockSpec((count, 2, 4 * rows, HEAD_DIM), lambda k: (0, 0, 0, 0)),
                whole_top,
            ],
            pl.BlockSpec((count, half, TOKENS), lambda k: (0, 0, 0)),
            grid=(count // ABREAST,),
            scratch_shapes=[
                pltpu.VMEM((1, 2 * SEG_LEN), F32),
                pltpu.VMEM((8, 2 * SEG_LEN), F32),
                pltpu.VMEM((HEAD_DIM, 2 * SEG_LEN), F32),
                pltpu.VMEM((ABREAST * stored, 2 * SEG_LEN), BF16),
                pltpu.VMEM((count * 4 * rows, 2 * SEG_LEN), BF16),
            ],
        )(side, logical, starts, query, *[keys] * ABREAST, *[values] * ABREAST, fresh, top)
        return exchange(attended, "kv")


def layer(
    which, x, mine, gain, query_proj, kv_proj, out_proj, keys, values, logical, starts, index, core,
    later=None,
):
    count = lax.axis_size("kv")
    peers = lax.axis_size("tp")
    rows = SEG_LEN // count
    half = HEAD_DIM // 2
    width = query_proj.shape[0]
    share = TOKENS // 2
    part = share // peers
    with jax.named_scope("project"):
        shape = jax.ShapeDtypeStruct((count, 7 * 8, TOKENS), jnp.int32)
        if which == 0:
            squares = call(
                functools.partial(squares_kernel, count),
                jax.ShapeDtypeStruct((count, 8, TOKENS), F32),
                [IN_VMEM] * 2,
                IN_VMEM,
            )(x, jnp.pad(logical.astype(F32), (0, TOKENS - logical.shape[0]))[None])
            squares = exchange(squares, "kv")
            all_logical = squares[:, 1, 0 : logical.shape[0]].astype(jnp.int32).reshape(-1)
            sent = call(
                functools.partial(first_project_kernel, count), shape, [IN_VMEM] * 5, IN_VMEM
            )(x, squares, gain, query_proj, kv_proj)
        else:
            sent = call(
                functools.partial(project_kernel, count),
                shape,
                [IN_SMEM] + [IN_VMEM] * 5,
                IN_VMEM,
                scratch_shapes=[pltpu.VMEM((TOKENS, width + 128), BF16)],
            )(core, x[0], x[1], gain, query_proj, kv_proj)
        parts = exchange(sent, "kv")
    if which == 0:
        parts, later = lax.optimization_barrier((parts, later))
        later = tuple(lax.all_gather(v, "kv") for v in later) + (all_logical,)
        attended = split_attention(parts, keys, values, logical, starts, index)
        kernel, scratch = output_kernel, []
    else:
        attended = whole_attention(parts, keys, values, logical, starts, index)
        kernel, scratch = folded_output_kernel, [pltpu.VMEM((GROUP * HEAD_DIM, TOKENS), BF16)]
    with jax.named_scope("output"):
        keep, send = call(
            kernel,
            (jax.ShapeDtypeStruct((share, width), F32),) * 2,
            [IN_SMEM] + [IN_VMEM] * 2,
            (IN_VMEM, IN_VMEM),
            scratch_shapes=[pltpu.VMEM((TOKENS, width), F32)] + scratch,
        )(core, attended, out_proj)
        half_sum = call(
            add_kernel,
            jax.ShapeDtypeStruct((share, width), F32),
            [IN_VMEM] * 2,
            IN_VMEM,
        )(keep, swap(send))
        parts = exchange(half_sum.reshape(peers, part, width), "tp")
    with jax.named_scope("residual"):
        if which == LAYERS - 1:
            produced = call(
                last_residual_kernel,
                jax.ShapeDtypeStruct((peers, part, width), BF16),
                [IN_VMEM] * 2,
                IN_VMEM,
            )(parts, mine)
            mine = None
        else:
            mine, squares = call(
                functools.partial(residual_kernel, count),
                (
                    jax.ShapeDtypeStruct((part, width), BF16),
                    jax.ShapeDtypeStruct((count, 8, 128), F32),
                ),
                [IN_VMEM] * 2,
                (IN_VMEM, IN_VMEM),
            )(parts, mine)
            produced = call(
                spread_kernel,
                jax.ShapeDtypeStruct((peers, part, width + 128), BF16),
                [IN_VMEM] * 2,
                IN_VMEM,
            )(exchange(squares, "kv"), mine)
        own = exchange(produced, "tp").reshape(share, -1)
        return (own, swap(own)), mine, later


def per_device(
    segments_in, gain, query_weight, kv_weight, out_weight, kv_cache, block_logical, segment_block
):
    width = segments_in.shape[2]
    core = lax.axis_index("section")
    core_at = core.astype(jnp.int32)[None]
    index = lax.axis_index("kv").astype(jnp.int32)[None]
    per_core = GROUP * HEAD_DIM
    share = TOKENS // 2

    def pick(which):
        at = which * per_core
        kv_at = which * HEAD_DIM
        return (
            lax.dynamic_slice_in_dim(query_weight[0], at, per_core, 1),
            lax.dynamic_slice_in_dim(kv_weight[0], kv_at, HEAD_DIM, 2).reshape(width, -1),
            lax.dynamic_slice_in_dim(kv_cache[0, :, 0], kv_at, HEAD_DIM, 1),
            lax.dynamic_slice_in_dim(kv_cache[0, :, 1], kv_at, HEAD_DIM, 1),
            lax.dynamic_slice_in_dim(out_weight[0], at, per_core, 0),
            gain,
        )

    kept = pick(core)
    received = tuple(swap(v) for v in pick(1 - core))
    x = segments_in.reshape(TOKENS, width)
    part = share // lax.axis_size("tp")
    mine = lax.dynamic_slice_in_dim(x, core * share + lax.axis_index("tp") * part, part, 0)
    params = [
        [jnp.where(core == which, here, other) for here, other in zip(kept, received)]
        for which in range(LAYERS)
    ]
    turned = call(
        turn_kernel,
        jax.ShapeDtypeStruct(params[1][3].shape[::-1], BF16),
        [IN_VMEM],
        IN_VMEM,
    )(params[1][3])
    query_proj, kv_proj, keys, values, out_proj, gain_row = params[0]
    first, mine, (all_keys, all_values, all_logical) = layer(
        0, x, mine, gain_row, query_proj, kv_proj, out_proj, keys, values,
        block_logical, segment_block, index, core_at, (params[1][2], turned),
    )
    query_proj, kv_proj, _, _, out_proj, gain_row = params[1]
    second, _, _ = layer(
        1, first, mine, gain_row, query_proj, kv_proj, out_proj, all_keys, all_values,
        all_logical, segment_block, lax.rem(index, 2), core_at,
    )
    outputs = first + second
    result = call(
        choose_kernel,
        jax.ShapeDtypeStruct((TOKENS, width), BF16),
        [IN_SMEM] + [IN_VMEM] * 4,
        IN_VMEM,
    )(core_at, *outputs)
    return result.reshape(1, NSEG, SEG_LEN, width)


def solution(mesh):
    placed = (
        P(None, None, "kv"),
        P("section", "kv"),
        P("section", "kv", "tp"),
        P("section", "kv", None, "tp"),
        P("section", "tp", "kv"),
        P("section", "kv", None, "tp"),
        P("kv"),
        P(),
    )
    return jax.shard_map(
        per_device,
        mesh=mesh,
        in_specs=placed,
        out_specs=P("section", None, None, "kv"),
        check_vma=False,
    )
```

```python
import functools
import math

import jax
import jax.numpy as jnp
from jax import lax
from jax.experimental import pallas as pl
from jax.experimental.pallas import tpu as pltpu
from jax.sharding import PartitionSpec as P

D = 8192
HEAD_DIM = 128
BLOCK = 128
NSEG = 3
SEG_LEN = 128
TOKENS = NSEG * SEG_LEN
GROUP = 8
LAYERS = 2
EPSILON = 1e-05
CLOSED = -1e30
FRESH = 128
RANGE = 520000.0
MIDDLE = 524288
LEVELS = 2048
MASS_UNIT = 262144.0
HEADS_STEP = 2
ABREAST = 4
SCALE = math.log2(math.e) / math.sqrt(HEAD_DIM)
F32 = jnp.float32
BF16 = jnp.bfloat16
VMEM_BYTES = 48 * 1024 * 1024


def call(kernel, out_shape, in_specs, out_specs, **rest):
    return pl.pallas_call(
        kernel,
        out_shape=out_shape,
        in_specs=in_specs,
        out_specs=out_specs,
        compiler_params=pltpu.CompilerParams(vmem_limit_bytes=VMEM_BYTES),
        **rest,
    )


IN_VMEM = pl.BlockSpec(memory_space=pltpu.VMEM)
IN_SMEM = pl.BlockSpec(memory_space=pltpu.SMEM)


def encode(block):
    top = jnp.maximum(jnp.max(jnp.abs(block), axis=0, keepdims=True), 1e-30)
    level = jnp.ceil(jnp.log2(top) * 16.0)
    value = jnp.round(block * (jnp.exp2(level * (-1.0 / 16.0)) * RANGE))
    return value.astype(jnp.int32) + MIDDLE, level.astype(jnp.int32)


def level_factor(level):
    return jnp.exp2(level.astype(F32) * (1.0 / 16.0)) * (1.0 / RANGE)


def pack(value):
    part = [value[8 * at : 8 * at + 8] for at in range(8)]
    lows = [
        part[5] & 0xFFF,
        (part[5] >> 12) | ((part[6] & 0xF) << 8),
        (part[6] >> 4) & 0xFFF,
        (part[6] >> 16) | ((part[7] & 0xFF) << 4),
        part[7] >> 8,
    ]
    return [(part[at] << 12) | lows[at] for at in range(5)]


def top_bits(word):
    return lax.shift_right_logical(word, jnp.int32(12))


def unpack(words):
    lows = [word & 0xFFF for word in words]
    part = [top_bits(word) for word in words]
    part.append(lows[0] | ((lows[1] & 0xFF) << 12))
    part.append((lows[1] >> 8) | (lows[2] << 4) | ((lows[3] & 0xF) << 16))
    part.append((lows[3] >> 4) | (lows[4] << 8))
    return (jnp.concatenate(part, axis=0) - MIDDLE).astype(F32)


def first_rows(rows, count=8):
    place = lax.broadcasted_iota(jnp.int32, (count, rows[0].shape[1]), 0)
    filled = jnp.zeros_like(place)
    for number, row in enumerate(rows):
        filled = jnp.where(place == number, row, filled)
    return filled


def square_rows(x):
    squares = jnp.sum(x * x, axis=1, keepdims=True)
    squares = jnp.broadcast_to(squares, (x.shape[0], 128))
    missing = -x.shape[0] % 128
    if missing:
        squares = jnp.concatenate([squares, jnp.zeros((missing, 128), F32)], axis=0)
    return squares.T[0:8]


def norm_columns(parts_ref):
    total = parts_ref[0]
    for peer in range(1, parts_ref.shape[0]):
        total = total + parts_ref[peer]
    factor = lax.rsqrt(total[0:1] / D + EPSILON)
    return jnp.broadcast_to(factor, (128, factor.shape[1])).T


def squares_kernel(count, x_ref, logical_ref, out_ref):
    rows = square_rows(x_ref[...].astype(F32))
    row = lax.broadcasted_iota(jnp.int32, rows.shape, 0)
    rows = jnp.where(row == 0, rows, logical_ref[...])
    for peer in range(count):
        out_ref[peer] = rows


def cache_kernel(keys_ref, values_ref, out_ref):
    out_ref[0] = keys_ref[...]
    for block in range(values_ref.shape[0] // BLOCK):
        at = slice(block * BLOCK, (block + 1) * BLOCK)
        out_ref[1, at, :] = values_ref[at, :].T


def first_project_kernel(count, x_ref, squares_ref, gain_ref, query_ref, kv_ref, out_ref):
    factor = norm_columns(squares_ref)[:, 0:1]
    normed = (x_ref[...].astype(F32) * factor * gain_ref[...]).astype(BF16)
    project(count, normed, query_ref, kv_ref, out_ref)


def project_kernel(count, core_ref, own_ref, other_ref, gain_ref, query_ref, kv_ref, out_ref, x_ref):
    share = TOKENS // 2
    width = gain_ref.shape[1]
    x_ref[pl.ds(core_ref[0] * share, share), :] = own_ref[...]
    x_ref[pl.ds((1 - core_ref[0]) * share, share), :] = other_ref[...]
    thirds = x_ref[:, width : width + 128].astype(F32)
    factor = thirds[:, 0:1] + thirds[:, 1:2] + thirds[:, 2:3]
    normed = (x_ref[:, 0:width].astype(F32) * factor * gain_ref[...]).astype(BF16)
    project(count, normed, query_ref, kv_ref, out_ref, True)


def swap_lanes(tile):
    return pltpu.roll(tile, SEG_LEN // 2, 1)


def left(shape):
    return lax.broadcasted_iota(jnp.int32, shape, 1) < SEG_LEN // 2


def fold(head, side):
    half = HEAD_DIM // 2
    tile = 2 * side * SEG_LEN
    low, high = head[0:half], head[half:]
    middle = slice(SEG_LEN, 2 * SEG_LEN)
    own = left((half, SEG_LEN))
    if side == 0:
        last = jnp.where(own, low[:, middle], swap_lanes(high[:, middle]))
    else:
        last = jnp.where(own, swap_lanes(low[:, middle]), high[:, middle])
    return jnp.concatenate([low[:, tile : tile + SEG_LEN], high[:, tile : tile + SEG_LEN], last], axis=1)


def project(count, scaled, query_ref, kv_ref, out_ref, folded=False):
    half = HEAD_DIM // 2
    columns = query_ref.shape[1]
    rows = SEG_LEN // count
    fresh = jnp.dot(scaled, kv_ref[...], preferred_element_type=F32)
    for start in range(0, columns, 256):
        part = jnp.dot(scaled, query_ref[:, start : start + 256], preferred_element_type=F32)
        turned = part.T
        for piece in range(256 // half):
            peer = start // half + piece
            if folded:
                head = turned[piece // 2 * HEAD_DIM : (piece // 2 + 1) * HEAD_DIM]
                block = fold(head, piece % 2)
            else:
                block = turned[piece * half : (piece + 1) * half]
            query, query_level = encode(block)
            words = pack(query)
            kinds = []
            for kind in range(2):
                lanes = slice(kind * HEAD_DIM, (kind + 1) * HEAD_DIM)
                block = jnp.concatenate(
                    [
                        fresh[seg * SEG_LEN + peer * rows : seg * SEG_LEN + (peer + 1) * rows, lanes]
                        for seg in range(NSEG)
                    ],
                    axis=1,
                )
                kinds.append(encode(block))
            levels = first_rows([query_level, kinds[0][1], kinds[1][1]]) + LEVELS
            words.append((kinds[0][0] << 12) | levels)
            words.append(kinds[1][0] << 12)
            for at, word in enumerate(words):
                out_ref[peer, 8 * at : 8 * at + 8, :] = word


def add_projection(count, parts_ref):
    half = HEAD_DIM // 2
    rows = SEG_LEN // count
    query = jnp.zeros((half, TOKENS), F32)
    fresh = [jnp.zeros((rows, TOKENS), F32) for _ in range(2)]
    for peer in range(count):
        words = [parts_ref[peer, 8 * at : 8 * at + 8, :] for at in range(7)]
        factors = level_factor((words[5] & 0xFFF) - LEVELS)
        query = query + unpack(words[0:5]) * factors[0:1]
        for kind in range(2):
            value = (top_bits(words[5 + kind]) - MIDDLE).astype(F32)
            fresh[kind] = fresh[kind] + value * factors[1 + kind : 2 + kind]
    return query, fresh


def finish_projection_kernel(count, parts_ref, query_out, fresh_out):
    rows = SEG_LEN // count
    query, fresh = add_projection(count, parts_ref)
    query = query.astype(BF16)
    for peer in range(count):
        query_out[peer] = query
    filler = jnp.zeros((FRESH - NSEG * rows, HEAD_DIM), F32)
    for kind in range(2):
        pieces = [
            fresh[kind][:, seg * SEG_LEN : (seg + 1) * SEG_LEN] for seg in range(NSEG)
        ]
        fresh_out[kind] = jnp.concatenate(pieces + [filler], axis=0).astype(BF16)


def finish_folded_kernel(count, parts_ref, query_out, fresh_out):
    half = HEAD_DIM // 2
    rows = SEG_LEN // count
    query, fresh = add_projection(count, parts_ref)
    own = left((half, SEG_LEN))
    last = query[:, 2 * SEG_LEN :]
    zero = jnp.zeros_like(last)
    low = jnp.concatenate([query[:, 0:SEG_LEN], jnp.where(own, last, zero)], axis=1)
    high = jnp.concatenate(
        [query[:, SEG_LEN : 2 * SEG_LEN], jnp.where(own, swap_lanes(last), zero)], axis=1
    )
    query_out[...] = jnp.concatenate([low, high], axis=0).astype(BF16)
    filler = jnp.zeros((rows, HEAD_DIM), F32)
    for kind in range(2):
        pieces = [
            fresh[kind][:, seg * SEG_LEN : (seg + 1) * SEG_LEN] for seg in range(NSEG)
        ]
        block = jnp.concatenate(pieces + [filler], axis=0).astype(BF16)
        for peer in range(count):
            fresh_out[peer, kind] = block


def segment_of(side, tile):
    return 2 * side if tile == 0 else 1


def far_peak_kernel(side_ref, logical_ref, start_ref, query_ref, *refs):
    keys_refs, (out_ref, top_ref) = refs[0:ABREAST], refs[ABREAST:]
    step = pl.program_id(0)
    blocks = keys_refs[0].shape[2] // BLOCK

    @pl.when(step == 0)
    def _():
        top_ref[...] = jnp.full(top_ref.shape, CLOSED, F32)

    tops = [top_ref[:, tile * SEG_LEN : (tile + 1) * SEG_LEN] for tile in range(2)]
    for number in range(ABREAST * blocks):
        block = number % blocks
        at = slice(block * BLOCK, (block + 1) * BLOCK)
        keys = keys_refs[number // blocks][0, 0, at, :]
        scores = jnp.dot(keys, query_ref[...], preferred_element_type=F32)
        top = jnp.max(scores.reshape(BLOCK // 8, 8, 2 * SEG_LEN), axis=0)
        for tile in range(2):
            lanes = slice(tile * SEG_LEN, (tile + 1) * SEG_LEN)
            begin = start_ref[segment_of(side_ref[0], tile)]
            is_open = logical_ref[step * ABREAST * blocks + number] < begin
            tops[tile] = jnp.maximum(tops[tile], jnp.where(is_open, top[:, lanes], CLOSED))
    for tile in range(2):
        top_ref[:, tile * SEG_LEN : (tile + 1) * SEG_LEN] = tops[tile]

    @pl.when(step == pl.num_programs(0) - 1)
    def _():
        out_ref[...] = top_ref[...]


def whole_attend_kernel(
    rows, side_ref, logical_ref, start_ref, query_ref, *refs
):
    keys_refs, values_refs = refs[0:ABREAST], refs[ABREAST : 2 * ABREAST]
    fresh_ref, top_ref, out_ref, peak_ref, mass_ref, sums_ref, weights, fresh_weights = refs[
        2 * ABREAST :
    ]
    step = pl.program_id(0)
    stored = keys_refs[0].shape[2]
    blocks = stored // BLOCK
    half = HEAD_DIM // 2
    per_peer = fresh_ref.shape[2]
    new = fresh_ref.shape[0] * per_peer

    @pl.when(step == 0)
    def _():
        keys = fresh_ref[:, 0].reshape(new, HEAD_DIM)
        scores = jnp.dot(keys, query_ref[...], preferred_element_type=F32)
        row = lax.broadcasted_iota(jnp.int32, (new, SEG_LEN), 0)
        lane = lax.broadcasted_iota(jnp.int32, (new, SEG_LEN), 1)
        inner = row & (per_peer - 1)
        position = (row // per_peer) * rows + (inner & (rows - 1))
        for tile in range(2):
            lanes = slice(tile * SEG_LEN, (tile + 1) * SEG_LEN)
            token = lane if tile == 0 else lane + side_ref[0] * (SEG_LEN // 2)
            is_open = (inner // rows == segment_of(side_ref[0], tile)) & (position <= token)
            masked = jnp.where(is_open, scores[:, lanes], CLOSED)
            peak = jnp.maximum(
                jnp.max(masked, axis=0, keepdims=True),
                jnp.max(top_ref[:, lanes], axis=0, keepdims=True),
            )
            peak_ref[:, lanes] = peak
            weight = jnp.where(is_open, jnp.exp2((masked - peak) * SCALE), 0.0)
            mass_ref[:, lanes] = jnp.sum(weight.reshape(new // 8, 8, SEG_LEN), axis=0)
            fresh_weights[:, lanes] = weight.astype(BF16)
        values = fresh_ref[:, 1].reshape(new, HEAD_DIM).T
        sums_ref[...] = jnp.dot(values, fresh_weights[...], preferred_element_type=F32)

    masses = [mass_ref[:, tile * SEG_LEN : (tile + 1) * SEG_LEN] for tile in range(2)]
    peaks = [peak_ref[:, tile * SEG_LEN : (tile + 1) * SEG_LEN] for tile in range(2)]
    for number in range(ABREAST * blocks):
        block = number % blocks
        at = slice(block * BLOCK, (block + 1) * BLOCK)
        keys = keys_refs[number // blocks][0, 0, at, :]
        scores = jnp.dot(keys, query_ref[...], preferred_element_type=F32)
        for tile in range(2):
            lanes = slice(tile * SEG_LEN, (tile + 1) * SEG_LEN)
            begin = start_ref[segment_of(side_ref[0], tile)]
            is_open = logical_ref[step * ABREAST * blocks + number] < begin
            offset = jnp.where(is_open, peaks[tile], -CLOSED)
            weight = jnp.exp2((scores[:, lanes] - offset) * SCALE)
            weights[number * BLOCK : (number + 1) * BLOCK, lanes] = weight.astype(BF16)
            masses[tile] = masses[tile] + jnp.sum(weight.reshape(BLOCK // 8, 8, SEG_LEN), axis=0)
    for tile in range(2):
        mass_ref[:, tile * SEG_LEN : (tile + 1) * SEG_LEN] = masses[tile]
    sums = sums_ref[...]
    for holder in range(ABREAST):
        values = [
            values_refs[holder][0, 0, block * BLOCK : (block + 1) * BLOCK, :]
            for block in range(blocks)
        ]
        sums = sums + jnp.dot(
            jnp.concatenate(values, axis=1),
            weights[holder * stored : (holder + 1) * stored, :],
            preferred_element_type=F32,
        )
    sums_ref[...] = sums

    @pl.when(step == pl.num_programs(0) - 1)
    def _():
        attended = sums_ref[...] / jnp.sum(mass_ref[...], axis=0, keepdims=True)
        low, high = attended[0:half], attended[half:]
        own = left((half, SEG_LEN))
        last = jnp.where(own, low[:, SEG_LEN:], swap_lanes(high[:, SEG_LEN:]))
        block = jnp.concatenate([low[:, 0:SEG_LEN], high[:, 0:SEG_LEN], last], axis=1).astype(BF16)
        for peer in range(out_ref.shape[0]):
            out_ref[peer] = block


def fresh_mask(rows, index_ref, seg):
    key_row = lax.broadcasted_iota(jnp.int32, (FRESH, SEG_LEN), 0)
    token = lax.broadcasted_iota(jnp.int32, (FRESH, SEG_LEN), 1)
    local = key_row - seg * rows
    return (local >= 0) & (local < rows) & (local + index_ref[0] * rows <= token)


def peak_kernel(
    rows, index_ref, logical_ref, start_ref, query_ref, keys_ref, fresh_ref, out_ref, peaks
):
    blocks = keys_ref.shape[0] // BLOCK
    heads = query_ref.shape[0]
    step = pl.program_id(0)
    for head in range(heads):
        query = query_ref[head]
        scores = jnp.dot(fresh_ref[0], query, preferred_element_type=F32)
        tops = []
        for seg in range(NSEG):
            lanes = slice(seg * SEG_LEN, (seg + 1) * SEG_LEN)
            masked = jnp.where(fresh_mask(rows, index_ref, seg), scores[:, lanes], CLOSED)
            tops.append(jnp.max(masked.reshape(FRESH // 8, 8, SEG_LEN), axis=0))
        for block in range(blocks):
            at = slice(block * BLOCK, (block + 1) * BLOCK)
            scores = jnp.dot(keys_ref[at, :], query, preferred_element_type=F32)
            top = jnp.max(scores.reshape(BLOCK // 8, 8, TOKENS), axis=0)
            for seg in range(NSEG):
                lanes = slice(seg * SEG_LEN, (seg + 1) * SEG_LEN)
                is_open = logical_ref[block] < start_ref[seg]
                tops[seg] = jnp.maximum(tops[seg], jnp.where(is_open, top[:, lanes], CLOSED))
        peaks[step * heads + head] = jnp.concatenate(
            [jnp.max(top, axis=0, keepdims=True) for top in tops], axis=1
        )

    @pl.when(step == pl.num_programs(0) - 1)
    def _():
        found = jnp.concatenate([peaks[head] for head in range(GROUP)], axis=0)
        for peer in range(out_ref.shape[0]):
            out_ref[peer] = found


def attend_kernel(
    rows, index_ref, logical_ref, start_ref, query_ref, keys_ref, values_ref, fresh_ref, peaks_ref,
    out_ref, turned_values, peaks, weights,
):
    blocks = keys_ref.shape[0] // BLOCK
    stored = blocks * BLOCK
    half = HEAD_DIM // 2
    heads = query_ref.shape[0]
    step = pl.program_id(0)

    @pl.when(step == 0)
    def _():
        for block in range(blocks):
            at = slice(block * BLOCK, (block + 1) * BLOCK)
            turned_values[:, at] = values_ref[at, :].T
        turned_values[:, stored : stored + FRESH] = fresh_ref[1].T
        top = peaks_ref[0]
        for peer in range(1, peaks_ref.shape[0]):
            top = jnp.maximum(top, peaks_ref[peer])
        for head in range(GROUP):
            peaks[head] = top[head : head + 1]

    for head in range(heads):
        query = query_ref[head]
        peak = peaks[step * heads + head]
        scores = jnp.dot(fresh_ref[0], query, preferred_element_type=F32)
        masses = []
        for seg in range(NSEG):
            lanes = slice(seg * SEG_LEN, (seg + 1) * SEG_LEN)
            weight = jnp.exp2((scores[:, lanes] - peak[:, lanes]) * SCALE)
            weight = jnp.where(fresh_mask(rows, index_ref, seg), weight, 0.0)
            weights[head, stored : stored + FRESH, lanes] = weight.astype(BF16)
            masses.append(jnp.sum(weight.reshape(FRESH // 8, 8, SEG_LEN), axis=0))
        for block in range(blocks):
            at = slice(block * BLOCK, (block + 1) * BLOCK)
            scores = jnp.dot(keys_ref[at, :], query, preferred_element_type=F32)
            for seg in range(NSEG):
                lanes = slice(seg * SEG_LEN, (seg + 1) * SEG_LEN)
                is_open = logical_ref[block] < start_ref[seg]
                offset = jnp.where(is_open, peak[:, lanes], -CLOSED)
                weight = jnp.exp2((scores[:, lanes] - offset) * SCALE)
                weights[head, at, lanes] = weight.astype(BF16)
                masses[seg] = masses[seg] + jnp.sum(
                    weight.reshape(BLOCK // 8, 8, SEG_LEN), axis=0
                )
        sums = jnp.dot(turned_values[...], weights[head], preferred_element_type=F32)
        mass = jnp.concatenate(
            [jnp.sum(part, axis=0, keepdims=True) for part in masses], axis=1
        )
        mass = jnp.round(mass * MASS_UNIT).astype(jnp.int32)
        for piece in range(2):
            value, level = encode(sums[piece * half : (piece + 1) * half])
            for at, word in enumerate(pack(value) + [first_rows([level, mass])]):
                out_ref[2 * head + piece, 8 * at : 8 * at + 8, :] = word


def combine_kernel(count, parts_ref, out_ref):
    half = HEAD_DIM // 2
    mass = jnp.zeros((1, TOKENS), F32)
    sums = jnp.zeros((half, TOKENS), F32)
    for peer in range(count):
        words = [parts_ref[peer, 8 * at : 8 * at + 8, :] for at in range(6)]
        mass = mass + words[5][1:2].astype(F32) * (1.0 / MASS_UNIT)
        sums = sums + unpack(words[0:5]) * level_factor(words[5][0:1])
    attended = (sums / mass).astype(BF16)
    for peer in range(count):
        out_ref[peer] = attended


def output_kernel(core_ref, attended_ref, weight_ref, keep_ref, send_ref, scratch):
    project_output(core_ref, attended_ref, weight_ref, keep_ref, send_ref, scratch)


def project_output(core_ref, attended_ref, weight_ref, keep_ref, send_ref, scratch):
    share = TOKENS // 2
    scratch[...] = lax.dot_general(
        attended_ref[...], weight_ref[...], (((0,), (0,)), ((), ())), preferred_element_type=F32
    )
    keep_ref[...] = scratch[pl.ds(core_ref[0] * share, share), :]
    send_ref[...] = scratch[pl.ds((1 - core_ref[0]) * share, share), :]


def folded_output_kernel(core_ref, parts_ref, weight_ref, keep_ref, send_ref, scratch, attended):
    half = HEAD_DIM // 2
    own = left((half, SEG_LEN))
    for head in range(parts_ref.shape[0] // 2):
        at = head * HEAD_DIM
        for side in range(2):
            lanes = slice(2 * side * SEG_LEN, (2 * side + 1) * SEG_LEN)
            part = parts_ref[2 * head + side]
            attended[at : at + half, lanes] = part[:, 0:SEG_LEN]
            attended[at + half : at + HEAD_DIM, lanes] = part[:, SEG_LEN : 2 * SEG_LEN]
        first, second = (
            parts_ref[2 * head + side][:, 2 * SEG_LEN :].astype(F32) for side in range(2)
        )
        lanes = slice(SEG_LEN, 2 * SEG_LEN)
        attended[at : at + half, lanes] = jnp.where(own, first, swap_lanes(second)).astype(BF16)
        attended[at + half : at + HEAD_DIM, lanes] = jnp.where(
            own, swap_lanes(first), second
        ).astype(BF16)
    project_output(core_ref, attended, weight_ref, keep_ref, send_ref, scratch)


def add_kernel(keep_ref, received_ref, out_ref):
    out_ref[...] = keep_ref[...] + received_ref[...]


def add_residual(parts_ref, x_ref):
    total = parts_ref[0]
    for peer in range(1, parts_ref.shape[0]):
        total = total + parts_ref[peer]
    return (x_ref[...].astype(F32) + total).astype(BF16)


def residual_kernel(count, parts_ref, x_ref, out_ref, squares_ref):
    produced = add_residual(parts_ref, x_ref)
    out_ref[...] = produced
    rows = square_rows(produced.astype(F32))
    for peer in range(count):
        squares_ref[peer] = rows


def last_residual_kernel(parts_ref, x_ref, out_ref):
    produced = add_residual(parts_ref, x_ref)
    for peer in range(out_ref.shape[0]):
        out_ref[peer] = produced


def spread_kernel(squares_ref, x_ref, out_ref):
    tokens, width = x_ref.shape
    factor = norm_columns(squares_ref)[0:tokens]
    first = factor.astype(BF16).astype(F32)
    second = (factor - first).astype(BF16).astype(F32)
    lane = lax.broadcasted_iota(jnp.int32, factor.shape, 1)
    thirds = jnp.where(lane == 0, first, jnp.where(lane == 1, second, factor - first - second))
    for peer in range(out_ref.shape[0]):
        out_ref[peer, :, 0:width] = x_ref[...]
        out_ref[peer, :, width : width + 128] = thirds.astype(BF16)


def choose_kernel(core_ref, own0_ref, other0_ref, own1_ref, other1_ref, out_ref):
    share = TOKENS // 2
    width = out_ref.shape[1]
    first = core_ref[0] == 0
    at = pl.ds(core_ref[0] * share, share)
    out_ref[at, :] = jnp.where(first, own0_ref[:, 0:width], own1_ref[...])
    at = pl.ds((1 - core_ref[0]) * share, share)
    out_ref[at, :] = jnp.where(first, other0_ref[:, 0:width], other1_ref[...])


def exchange(value, axes):
    return lax.all_to_all(value, axes, 0, 0, tiled=True)


def swap(value):
    return lax.ppermute(value, "section", [(0, 1), (1, 0)])


RING = 4


def ring_pairs(first, step):
    pairs = []
    for core in range(2):
        along_y = (core == 0) == first
        for kv in range(RING * RING):
            z, y = divmod(kv, RING)
            if along_y:
                y = (y + step) % RING
            else:
                z = (z + step) % RING
            pairs.append((core * RING * RING + kv, core * RING * RING + z * RING + y))
    return pairs


def ring_sides(block, first):
    return tuple(
        lax.ppermute(block, ("section", "kv"), ring_pairs(first, step)) for step in (1, -1)
    )


def ring_opposite(before, after, first):
    half = before.shape[0] // 2
    parts = [
        lax.ppermute(part, ("section", "kv"), ring_pairs(first, step))
        for part, step in ((before[:half], 1), (after[half:], -1))
    ]
    return jnp.concatenate(parts, axis=0)


def gathered_blocks(all_logical, core, index):
    offsets = jnp.array([0, -1, 1, 2], jnp.int32)
    near = offsets[:, None] + jnp.zeros((1, RING), jnp.int32)
    far = offsets[None, :] + jnp.zeros((RING, 1), jnp.int32)
    y = index % RING + jnp.where(core == 0, near, far)
    z = index // RING + jnp.where(core == 0, far, near)
    holder = (z % RING) * RING + y % RING
    return all_logical[holder.reshape(-1)].reshape(-1)


def split_attention(parts, keys, values, logical, starts, index, cache):
    parts, cache = lax.optimization_barrier((parts, cache))
    sides = ring_sides(cache, True)
    count = lax.axis_size("kv")
    rows = SEG_LEN // count
    half = HEAD_DIM // 2
    with jax.named_scope("queries"):
        query, fresh = call(
            functools.partial(finish_projection_kernel, count),
            (
                jax.ShapeDtypeStruct((count, half, TOKENS), BF16),
                jax.ShapeDtypeStruct((2, FRESH, HEAD_DIM), BF16),
            ),
            [IN_VMEM],
            (IN_VMEM, IN_VMEM),
        )(parts)
        query = exchange(query, "kv").reshape(GROUP, HEAD_DIM, TOKENS)
        query, sides = lax.optimization_barrier((query, sides))
        opposite = ring_opposite(*sides, True)
    stored = keys.shape[0]
    by_head = [
        IN_SMEM,
        IN_SMEM,
        IN_SMEM,
        pl.BlockSpec((HEADS_STEP, HEAD_DIM, TOKENS), lambda h: (h, 0, 0)),
        pl.BlockSpec((stored, HEAD_DIM), lambda h: (0, 0)),
    ]
    whole_values = pl.BlockSpec((stored, HEAD_DIM), lambda h: (0, 0))
    whole_fresh = pl.BlockSpec((2, FRESH, HEAD_DIM), lambda h: (0, 0, 0))
    whole_peaks = pl.BlockSpec((count, GROUP, TOKENS), lambda h: (0, 0, 0))
    with jax.named_scope("peaks"):
        peaks = call(
            functools.partial(peak_kernel, rows),
            jax.ShapeDtypeStruct((count, GROUP, TOKENS), F32),
            by_head + [whole_fresh],
            whole_peaks,
            grid=(GROUP // HEADS_STEP,),
            scratch_shapes=[pltpu.VMEM((GROUP, 1, TOKENS), F32)],
        )(index, logical, starts, query, keys, fresh)
        peaks = exchange(peaks, "kv")
        peaks, opposite = lax.optimization_barrier((peaks, opposite))
        near = jnp.stack((cache,) + sides + (opposite,))
        far_sides = ring_sides(near, False)
    with jax.named_scope("attend"):
        sent = call(
            functools.partial(attend_kernel, rows),
            jax.ShapeDtypeStruct((count, 6 * 8, TOKENS), jnp.int32),
            by_head + [whole_values, whole_fresh, whole_peaks],
            pl.BlockSpec((2 * HEADS_STEP, 6 * 8, TOKENS), lambda h: (h, 0, 0)),
            grid=(GROUP // HEADS_STEP,),
            scratch_shapes=[
                pltpu.VMEM((HEAD_DIM, stored + FRESH), BF16),
                pltpu.VMEM((GROUP, 1, TOKENS), F32),
                pltpu.VMEM((HEADS_STEP, stored + FRESH, TOKENS), BF16),
            ],
        )(index, logical, starts, query, keys, values, fresh, peaks)
        parts = exchange(sent, "kv")
    with jax.named_scope("combine"):
        attended = call(
            functools.partial(combine_kernel, count),
            jax.ShapeDtypeStruct((count, half, TOKENS), BF16),
            [IN_VMEM],
            IN_VMEM,
        )(parts)
        attended = exchange(attended, "kv").reshape(GROUP * HEAD_DIM, TOKENS)
        attended, far_sides = lax.optimization_barrier((attended, far_sides))
        return attended, (near,) + far_sides + (ring_opposite(*far_sides, False),)


def whole_attention(parts, caches, logical, starts, side):
    count = lax.axis_size("kv")
    rows = SEG_LEN // count
    half = HEAD_DIM // 2
    stored = caches[0].shape[2]
    with jax.named_scope("queries"):
        query, fresh = call(
            functools.partial(finish_folded_kernel, count),
            (
                jax.ShapeDtypeStruct((HEAD_DIM, 2 * SEG_LEN), BF16),
                jax.ShapeDtypeStruct((count, 2, 4 * rows, HEAD_DIM), BF16),
            ),
            [IN_VMEM],
            (IN_VMEM, IN_VMEM),
        )(parts)
        fresh = exchange(fresh, "kv")
    whole_query = pl.BlockSpec((HEAD_DIM, 2 * SEG_LEN), lambda k: (0, 0))
    whole_top = pl.BlockSpec((8, 2 * SEG_LEN), lambda k: (0, 0))
    by_holder = [
        IN_SMEM,
        IN_SMEM,
        IN_SMEM,
        whole_query,
    ]
    by_holder += [
        pl.BlockSpec((1, 1, stored, HEAD_DIM), lambda k: (k, 0, 0, 0)) for _ in range(ABREAST)
    ]
    with jax.named_scope("peaks"):
        top = call(
            far_peak_kernel,
            jax.ShapeDtypeStruct((8, 2 * SEG_LEN), F32),
            by_holder,
            whole_top,
            grid=(count // ABREAST,),
            scratch_shapes=[pltpu.VMEM((8, 2 * SEG_LEN), F32)],
        )(side, logical, starts, query, *caches)
    with jax.named_scope("attend"):
        attended = call(
            functools.partial(whole_attend_kernel, rows),
            jax.ShapeDtypeStruct((count, half, TOKENS), BF16),
            by_holder
            + [
                pl.BlockSpec((1, 1, stored, HEAD_DIM), lambda k: (k, 1, 0, 0))
                for _ in range(ABREAST)
            ]
            + [
                pl.BlockSpec((count, 2, 4 * rows, HEAD_DIM), lambda k: (0, 0, 0, 0)),
                whole_top,
            ],
            pl.BlockSpec((count, half, TOKENS), lambda k: (0, 0, 0)),
            grid=(count // ABREAST,),
            scratch_shapes=[
                pltpu.VMEM((1, 2 * SEG_LEN), F32),
                pltpu.VMEM((8, 2 * SEG_LEN), F32),
                pltpu.VMEM((HEAD_DIM, 2 * SEG_LEN), F32),
                pltpu.VMEM((ABREAST * stored, 2 * SEG_LEN), BF16),
                pltpu.VMEM((count * 4 * rows, 2 * SEG_LEN), BF16),
            ],
        )(side, logical, starts, query, *caches, *caches, fresh, top)
        return exchange(attended, "kv")


def layer(
    which, x, mine, gain, query_proj, kv_proj, out_proj, keys, values, logical, starts, index, core,
    later=None,
):
    count = lax.axis_size("kv")
    peers = lax.axis_size("tp")
    rows = SEG_LEN // count
    half = HEAD_DIM // 2
    width = query_proj.shape[0]
    share = TOKENS // 2
    part = share // peers
    with jax.named_scope("project"):
        shape = jax.ShapeDtypeStruct((count, 7 * 8, TOKENS), jnp.int32)
        if which == 0:
            squares = call(
                functools.partial(squares_kernel, count),
                jax.ShapeDtypeStruct((count, 8, TOKENS), F32),
                [IN_VMEM] * 2,
                IN_VMEM,
            )(x, jnp.pad(logical.astype(F32), (0, TOKENS - logical.shape[0]))[None])
            squares = exchange(squares, "kv")
            all_logical = squares[:, 1, 0 : logical.shape[0]].astype(jnp.int32)
            sent = call(
                functools.partial(first_project_kernel, count), shape, [IN_VMEM] * 5, IN_VMEM
            )(x, squares, gain, query_proj, kv_proj)
        else:
            sent = call(
                functools.partial(project_kernel, count),
                shape,
                [IN_SMEM] + [IN_VMEM] * 5,
                IN_VMEM,
                scratch_shapes=[pltpu.VMEM((TOKENS, width + 128), BF16)],
            )(core, x[0], x[1], gain, query_proj, kv_proj)
        parts = exchange(sent, "kv")
    if which == 0:
        attended, later = split_attention(parts, keys, values, logical, starts, index, later)
        later = (later, gathered_blocks(all_logical, core[0], index[0]))
        kernel, scratch = output_kernel, []
    else:
        attended = whole_attention(parts, keys, logical, starts, index)
        kernel, scratch = folded_output_kernel, [pltpu.VMEM((GROUP * HEAD_DIM, TOKENS), BF16)]
    with jax.named_scope("output"):
        keep, send = call(
            kernel,
            (jax.ShapeDtypeStruct((share, width), F32),) * 2,
            [IN_SMEM] + [IN_VMEM] * 2,
            (IN_VMEM, IN_VMEM),
            scratch_shapes=[pltpu.VMEM((TOKENS, width), F32)] + scratch,
        )(core, attended, out_proj)
        half_sum = call(
            add_kernel,
            jax.ShapeDtypeStruct((share, width), F32),
            [IN_VMEM] * 2,
            IN_VMEM,
        )(keep, swap(send))
        parts = exchange(half_sum.reshape(peers, part, width), "tp")
    with jax.named_scope("residual"):
        if which == LAYERS - 1:
            produced = call(
                last_residual_kernel,
                jax.ShapeDtypeStruct((peers, part, width), BF16),
                [IN_VMEM] * 2,
                IN_VMEM,
            )(parts, mine)
            mine = None
        else:
            mine, squares = call(
                functools.partial(residual_kernel, count),
                (
                    jax.ShapeDtypeStruct((part, width), BF16),
                    jax.ShapeDtypeStruct((count, 8, 128), F32),
                ),
                [IN_VMEM] * 2,
                (IN_VMEM, IN_VMEM),
            )(parts, mine)
            produced = call(
                spread_kernel,
                jax.ShapeDtypeStruct((peers, part, width + 128), BF16),
                [IN_VMEM] * 2,
                IN_VMEM,
            )(exchange(squares, "kv"), mine)
        own = exchange(produced, "tp").reshape(share, -1)
        return (own, swap(own)), mine, later


def per_device(
    segments_in, gain, query_weight, kv_weight, out_weight, kv_cache, block_logical, segment_block
):
    width = segments_in.shape[2]
    core = lax.axis_index("section")
    core_at = core.astype(jnp.int32)[None]
    index = lax.axis_index("kv").astype(jnp.int32)[None]
    per_core = GROUP * HEAD_DIM
    share = TOKENS // 2

    def pick(which):
        at = which * per_core
        kv_at = which * HEAD_DIM
        return (
            lax.dynamic_slice_in_dim(query_weight[0], at, per_core, 1),
            lax.dynamic_slice_in_dim(kv_weight[0], kv_at, HEAD_DIM, 2).reshape(width, -1),
            lax.dynamic_slice_in_dim(kv_cache[0, :, 0], kv_at, HEAD_DIM, 1),
            lax.dynamic_slice_in_dim(kv_cache[0, :, 1], kv_at, HEAD_DIM, 1),
            lax.dynamic_slice_in_dim(out_weight[0], at, per_core, 0),
            gain,
        )

    kept = pick(core)
    received = tuple(swap(v) for v in pick(1 - core))
    x = segments_in.reshape(TOKENS, width)
    part = share // lax.axis_size("tp")
    mine = lax.dynamic_slice_in_dim(x, core * share + lax.axis_index("tp") * part, part, 0)
    params = [
        [jnp.where(core == which, here, other) for here, other in zip(kept, received)]
        for which in range(LAYERS)
    ]
    cache = call(
        cache_kernel,
        jax.ShapeDtypeStruct((2,) + params[1][2].shape, BF16),
        [IN_VMEM] * 2,
        IN_VMEM,
    )(params[1][2], params[1][3])
    query_proj, kv_proj, keys, values, out_proj, gain_row = params[0]
    first, mine, (caches, numbers) = layer(
        0, x, mine, gain_row, query_proj, kv_proj, out_proj, keys, values,
        block_logical, segment_block, index, core_at, cache,
    )
    query_proj, kv_proj, _, _, out_proj, gain_row = params[1]
    second, _, _ = layer(
        1, first, mine, gain_row, query_proj, kv_proj, out_proj, caches, None,
        numbers, segment_block, lax.rem(index, 2), core_at,
    )
    outputs = first + second
    result = call(
        choose_kernel,
        jax.ShapeDtypeStruct((TOKENS, width), BF16),
        [IN_SMEM] + [IN_VMEM] * 4,
        IN_VMEM,
    )(core_at, *outputs)
    return result.reshape(1, NSEG, SEG_LEN, width)


def solution(mesh):
    placed = (
        P(None, None, "kv"),
        P("section", "kv"),
        P("section", "kv", "tp"),
        P("section", "kv", None, "tp"),
        P("section", "tp", "kv"),
        P("section", "kv", None, "tp"),
        P("kv"),
        P(),
    )
    return jax.shard_map(
        per_device,
        mesh=mesh,
        in_specs=placed,
        out_specs=P("section", None, None, "kv"),
        check_vma=False,
    )
```

```python
import functools
import math

import jax
import jax.numpy as jnp
from jax import lax
from jax.experimental import pallas as pl
from jax.experimental.pallas import tpu as pltpu
from jax.sharding import PartitionSpec as P

D = 8192
HEAD_DIM = 128
BLOCK = 128
NSEG = 3
SEG_LEN = 128
TOKENS = NSEG * SEG_LEN
GROUP = 8
LAYERS = 2
EPSILON = 1e-05
CLOSED = -1e30
FRESH = 128
RANGE = 520000.0
MIDDLE = 524288
LEVELS = 2048
MASS_UNIT = 262144.0
NEAR_MASS_UNIT = 65536.0
HEADS_STEP = 2
SCALE = math.log2(math.e) / math.sqrt(HEAD_DIM)
F32 = jnp.float32
BF16 = jnp.bfloat16
VMEM_BYTES = 48 * 1024 * 1024


def call(kernel, out_shape, in_specs, out_specs, **rest):
    return pl.pallas_call(
        kernel,
        out_shape=out_shape,
        in_specs=in_specs,
        out_specs=out_specs,
        compiler_params=pltpu.CompilerParams(vmem_limit_bytes=VMEM_BYTES),
        **rest,
    )


IN_VMEM = pl.BlockSpec(memory_space=pltpu.VMEM)
IN_SMEM = pl.BlockSpec(memory_space=pltpu.SMEM)


RING = 4


def encode(block):
    top = jnp.maximum(jnp.max(jnp.abs(block), axis=0, keepdims=True), 1e-30)
    level = jnp.ceil(jnp.log2(top) * 16.0)
    value = jnp.round(block * (jnp.exp2(level * (-1.0 / 16.0)) * RANGE))
    return value.astype(jnp.int32) + MIDDLE, level.astype(jnp.int32)


def level_factor(level):
    return jnp.exp2(level.astype(F32) * (1.0 / 16.0)) * (1.0 / RANGE)


def pack(value):
    part = [value[8 * at : 8 * at + 8] for at in range(8)]
    lows = [
        part[5] & 0xFFF,
        (part[5] >> 12) | ((part[6] & 0xF) << 8),
        (part[6] >> 4) & 0xFFF,
        (part[6] >> 16) | ((part[7] & 0xFF) << 4),
        part[7] >> 8,
    ]
    return [(part[at] << 12) | lows[at] for at in range(5)]


def top_bits(word):
    return lax.shift_right_logical(word, jnp.int32(12))


def unpack(words):
    lows = [word & 0xFFF for word in words]
    part = [top_bits(word) for word in words]
    part.append(lows[0] | ((lows[1] & 0xFF) << 12))
    part.append((lows[1] >> 8) | (lows[2] << 4) | ((lows[3] & 0xF) << 16))
    part.append((lows[3] >> 4) | (lows[4] << 8))
    return (jnp.concatenate(part, axis=0) - MIDDLE).astype(F32)


def first_rows(rows, count=8):
    place = lax.broadcasted_iota(jnp.int32, (count, rows[0].shape[1]), 0)
    filled = jnp.zeros_like(place)
    for number, row in enumerate(rows):
        filled = jnp.where(place == number, row, filled)
    return filled


def square_rows(x):
    squares = jnp.sum(x * x, axis=1, keepdims=True)
    squares = jnp.broadcast_to(squares, (x.shape[0], 128))
    missing = -x.shape[0] % 128
    if missing:
        squares = jnp.concatenate([squares, jnp.zeros((missing, 128), F32)], axis=0)
    return squares.T[0:8]


def norm_columns(parts_ref):
    total = parts_ref[0]
    for peer in range(1, parts_ref.shape[0]):
        total = total + parts_ref[peer]
    factor = lax.rsqrt(total[0:1] / D + EPSILON)
    return jnp.broadcast_to(factor, (128, factor.shape[1])).T


def squares_kernel(count, x_ref, logical_ref, out_ref):
    rows = square_rows(x_ref[...].astype(F32))
    row = lax.broadcasted_iota(jnp.int32, rows.shape, 0)
    rows = jnp.where(row == 0, rows, logical_ref[...])
    for peer in range(count):
        out_ref[peer] = rows


def cache_kernel(keys_ref, values_ref, out_ref):
    out_ref[0] = keys_ref[...]
    for block in range(values_ref.shape[0] // BLOCK):
        at = slice(block * BLOCK, (block + 1) * BLOCK)
        out_ref[1, at, :] = values_ref[at, :].T


def first_project_kernel(count, x_ref, squares_ref, gain_ref, query_ref, kv_ref, out_ref):
    factor = norm_columns(squares_ref)[:, 0:1]
    normed = (x_ref[...].astype(F32) * factor * gain_ref[...]).astype(BF16)
    project(count, normed, query_ref, kv_ref, out_ref)


def project_kernel(count, core_ref, own_ref, other_ref, gain_ref, query_ref, kv_ref, out_ref, x_ref):
    share = TOKENS // 2
    width = gain_ref.shape[1]
    x_ref[pl.ds(core_ref[0] * share, share), :] = own_ref[...]
    x_ref[pl.ds((1 - core_ref[0]) * share, share), :] = other_ref[...]
    thirds = x_ref[:, width : width + 128].astype(F32)
    factor = thirds[:, 0:1] + thirds[:, 1:2] + thirds[:, 2:3]
    normed = (x_ref[:, 0:width].astype(F32) * factor * gain_ref[...]).astype(BF16)
    project(count, normed, query_ref, kv_ref, out_ref, True)


def project(count, scaled, query_ref, kv_ref, out_ref, crossed=False):
    half = HEAD_DIM // 2
    columns = query_ref.shape[1]
    rows = SEG_LEN // count
    fresh = jnp.dot(scaled, kv_ref[...], preferred_element_type=F32)
    for start in range(0, columns, 256):
        part = jnp.dot(scaled, query_ref[:, start : start + 256], preferred_element_type=F32)
        turned = part.T
        for piece in range(256 // half):
            at = start // half + piece
            peer = at % RING * RING + at // RING if crossed else at
            block = turned[piece * half : (piece + 1) * half]
            query, query_level = encode(block)
            words = pack(query)
            kinds = []
            for kind in range(2):
                lanes = slice(kind * HEAD_DIM, (kind + 1) * HEAD_DIM)
                block = jnp.concatenate(
                    [
                        fresh[seg * SEG_LEN + peer * rows : seg * SEG_LEN + (peer + 1) * rows, lanes]
                        for seg in range(NSEG)
                    ],
                    axis=1,
                )
                kinds.append(encode(block))
            levels = first_rows([query_level, kinds[0][1], kinds[1][1]]) + LEVELS
            words.append((kinds[0][0] << 12) | levels)
            words.append(kinds[1][0] << 12)
            for at, word in enumerate(words):
                out_ref[peer, 8 * at : 8 * at + 8, :] = word


def add_projection(count, parts_ref):
    half = HEAD_DIM // 2
    rows = SEG_LEN // count
    query = jnp.zeros((half, TOKENS), F32)
    fresh = [jnp.zeros((rows, TOKENS), F32) for _ in range(2)]
    for peer in range(count):
        words = [parts_ref[peer, 8 * at : 8 * at + 8, :] for at in range(7)]
        factors = level_factor((words[5] & 0xFFF) - LEVELS)
        query = query + unpack(words[0:5]) * factors[0:1]
        for kind in range(2):
            value = (top_bits(words[5 + kind]) - MIDDLE).astype(F32)
            fresh[kind] = fresh[kind] + value * factors[1 + kind : 2 + kind]
    return query, fresh


def finish_projection_kernel(count, parts_ref, query_out, fresh_out):
    rows = SEG_LEN // count
    query, fresh = add_projection(count, parts_ref)
    query = query.astype(BF16)
    for peer in range(count):
        query_out[peer] = query
    filler = jnp.zeros((FRESH - NSEG * rows, HEAD_DIM), F32)
    for kind in range(2):
        pieces = [
            fresh[kind][:, seg * SEG_LEN : (seg + 1) * SEG_LEN] for seg in range(NSEG)
        ]
        fresh_out[kind] = jnp.concatenate(pieces + [filler], axis=0).astype(BF16)


def finish_crossed_kernel(count, parts_ref, query_out, fresh_out):
    rows = SEG_LEN // count
    query, fresh = add_projection(count, parts_ref)
    query = query.astype(BF16)
    for peer in range(RING):
        query_out[peer] = query
    filler = jnp.zeros((rows, HEAD_DIM), F32)
    for kind in range(2):
        pieces = [
            fresh[kind][:, seg * SEG_LEN : (seg + 1) * SEG_LEN] for seg in range(NSEG)
        ]
        fresh_out[kind] = jnp.concatenate(pieces + [filler], axis=0).astype(BF16)


def near_mask(rows, slot_ref, seg):
    key_row = lax.broadcasted_iota(jnp.int32, (4 * rows, SEG_LEN), 0)
    token = lax.broadcasted_iota(jnp.int32, (4 * rows, SEG_LEN), 1)
    local = key_row - seg * rows
    inside = (local >= 0) & (local < rows)
    return jnp.concatenate(
        [
            jnp.where(inside & (local + slot_ref[slot] * rows <= token), 1.0, 0.0)
            for slot in range(RING)
        ],
        axis=0,
    ) > 0.5


def near_peak_kernel(rows, slot_ref, logical_ref, start_ref, query_ref, *refs):
    caches, fresh, out_ref = refs[0:RING], refs[RING : 2 * RING], refs[2 * RING]
    blocks = caches[0].shape[1] // BLOCK
    found = []
    for head in range(query_ref.shape[0]):
        query = query_ref[head]
        keys = jnp.concatenate([part[0] for part in fresh], axis=0)
        scores = jnp.dot(keys, query, preferred_element_type=F32)
        tops = []
        for seg in range(NSEG):
            lanes = slice(seg * SEG_LEN, (seg + 1) * SEG_LEN)
            masked = jnp.where(near_mask(rows, slot_ref, seg), scores[:, lanes], CLOSED)
            tops.append(jnp.max(masked.reshape(-1, 8, SEG_LEN), axis=0))
        for number in range(RING * blocks):
            block = number % blocks
            keys = caches[number // blocks][0, block * BLOCK : (block + 1) * BLOCK, :]
            scores = jnp.dot(keys, query, preferred_element_type=F32)
            top = jnp.max(scores.reshape(BLOCK // 8, 8, TOKENS), axis=0)
            for seg in range(NSEG):
                lanes = slice(seg * SEG_LEN, (seg + 1) * SEG_LEN)
                is_open = logical_ref[number] < start_ref[seg]
                tops[seg] = jnp.maximum(tops[seg], jnp.where(is_open, top[:, lanes], CLOSED))
        found.append(
            jnp.concatenate([jnp.max(top, axis=0, keepdims=True) for top in tops], axis=1)
        )
    found = jnp.concatenate(found * 4, axis=0)
    for peer in range(RING):
        out_ref[peer] = found


def near_attend_kernel(rows, slot_ref, logical_ref, start_ref, query_ref, *refs):
    caches, fresh = refs[0:RING], refs[RING : 2 * RING]
    peaks_ref, out_ref, weights = refs[2 * RING :]
    blocks = caches[0].shape[1] // BLOCK
    stored = RING * blocks * BLOCK
    half = HEAD_DIM // 2
    head = pl.program_id(0)
    query = query_ref[0]
    peak = peaks_ref[0]
    for peer in range(1, RING):
        peak = jnp.maximum(peak, peaks_ref[peer])
    peak = jnp.where(head == 0, peak[0:1], peak[1:2])
    keys = jnp.concatenate([part[0] for part in fresh], axis=0)
    scores = jnp.dot(keys, query, preferred_element_type=F32)
    masses = []
    for seg in range(NSEG):
        lanes = slice(seg * SEG_LEN, (seg + 1) * SEG_LEN)
        weight = jnp.exp2((scores[:, lanes] - peak[:, lanes]) * SCALE)
        weight = jnp.where(near_mask(rows, slot_ref, seg), weight, 0.0)
        weights[stored : stored + 4 * RING * rows, lanes] = weight.astype(BF16)
        masses.append(jnp.sum(weight.reshape(-1, 8, SEG_LEN), axis=0))
    for number in range(RING * blocks):
        block = number % blocks
        keys = caches[number // blocks][0, block * BLOCK : (block + 1) * BLOCK, :]
        scores = jnp.dot(keys, query, preferred_element_type=F32)
        for seg in range(NSEG):
            lanes = slice(seg * SEG_LEN, (seg + 1) * SEG_LEN)
            is_open = logical_ref[number] < start_ref[seg]
            offset = jnp.where(is_open, peak[:, lanes], -CLOSED)
            weight = jnp.exp2((scores[:, lanes] - offset) * SCALE)
            weights[number * BLOCK : (number + 1) * BLOCK, lanes] = weight.astype(BF16)
            masses[seg] = masses[seg] + jnp.sum(weight.reshape(BLOCK // 8, 8, SEG_LEN), axis=0)
    turned = [
        cache[1, block * BLOCK : (block + 1) * BLOCK, :] for cache in caches for block in range(blocks)
    ]
    turned.append(jnp.concatenate([part[1] for part in fresh], axis=0).T)
    sums = jnp.dot(jnp.concatenate(turned, axis=1), weights[...], preferred_element_type=F32)
    mass = jnp.concatenate([jnp.sum(part, axis=0, keepdims=True) for part in masses], axis=1)
    mass = jnp.round(mass * NEAR_MASS_UNIT).astype(jnp.int32)
    for piece in range(2):
        value, level = encode(sums[piece * half : (piece + 1) * half])
        for at, word in enumerate(pack(value) + [first_rows([level, mass])]):
            out_ref[piece, 8 * at : 8 * at + 8, :] = word


def fresh_mask(rows, index_ref, seg):
    key_row = lax.broadcasted_iota(jnp.int32, (FRESH, SEG_LEN), 0)
    token = lax.broadcasted_iota(jnp.int32, (FRESH, SEG_LEN), 1)
    local = key_row - seg * rows
    return (local >= 0) & (local < rows) & (local + index_ref[0] * rows <= token)


def peak_kernel(
    rows, index_ref, logical_ref, start_ref, query_ref, keys_ref, fresh_ref, out_ref, peaks
):
    blocks = keys_ref.shape[0] // BLOCK
    heads = query_ref.shape[0]
    step = pl.program_id(0)
    for head in range(heads):
        query = query_ref[head]
        scores = jnp.dot(fresh_ref[0], query, preferred_element_type=F32)
        tops = []
        for seg in range(NSEG):
            lanes = slice(seg * SEG_LEN, (seg + 1) * SEG_LEN)
            masked = jnp.where(fresh_mask(rows, index_ref, seg), scores[:, lanes], CLOSED)
            tops.append(jnp.max(masked.reshape(FRESH // 8, 8, SEG_LEN), axis=0))
        for block in range(blocks):
            at = slice(block * BLOCK, (block + 1) * BLOCK)
            scores = jnp.dot(keys_ref[at, :], query, preferred_element_type=F32)
            top = jnp.max(scores.reshape(BLOCK // 8, 8, TOKENS), axis=0)
            for seg in range(NSEG):
                lanes = slice(seg * SEG_LEN, (seg + 1) * SEG_LEN)
                is_open = logical_ref[block] < start_ref[seg]
                tops[seg] = jnp.maximum(tops[seg], jnp.where(is_open, top[:, lanes], CLOSED))
        peaks[step * heads + head] = jnp.concatenate(
            [jnp.max(top, axis=0, keepdims=True) for top in tops], axis=1
        )

    @pl.when(step == pl.num_programs(0) - 1)
    def _():
        found = jnp.concatenate([peaks[head] for head in range(GROUP)], axis=0)
        for peer in range(out_ref.shape[0]):
            out_ref[peer] = found


def attend_kernel(
    rows, index_ref, logical_ref, start_ref, query_ref, keys_ref, values_ref, fresh_ref, peaks_ref,
    out_ref, turned_values, peaks, weights,
):
    blocks = keys_ref.shape[0] // BLOCK
    stored = blocks * BLOCK
    half = HEAD_DIM // 2
    heads = query_ref.shape[0]
    step = pl.program_id(0)

    @pl.when(step == 0)
    def _():
        for block in range(blocks):
            at = slice(block * BLOCK, (block + 1) * BLOCK)
            turned_values[:, at] = values_ref[at, :].T
        turned_values[:, stored : stored + FRESH] = fresh_ref[1].T
        top = peaks_ref[0]
        for peer in range(1, peaks_ref.shape[0]):
            top = jnp.maximum(top, peaks_ref[peer])
        for head in range(GROUP):
            peaks[head] = top[head : head + 1]

    for head in range(heads):
        query = query_ref[head]
        peak = peaks[step * heads + head]
        scores = jnp.dot(fresh_ref[0], query, preferred_element_type=F32)
        masses = []
        for seg in range(NSEG):
            lanes = slice(seg * SEG_LEN, (seg + 1) * SEG_LEN)
            weight = jnp.exp2((scores[:, lanes] - peak[:, lanes]) * SCALE)
            weight = jnp.where(fresh_mask(rows, index_ref, seg), weight, 0.0)
            weights[head, stored : stored + FRESH, lanes] = weight.astype(BF16)
            masses.append(jnp.sum(weight.reshape(FRESH // 8, 8, SEG_LEN), axis=0))
        for block in range(blocks):
            at = slice(block * BLOCK, (block + 1) * BLOCK)
            scores = jnp.dot(keys_ref[at, :], query, preferred_element_type=F32)
            for seg in range(NSEG):
                lanes = slice(seg * SEG_LEN, (seg + 1) * SEG_LEN)
                is_open = logical_ref[block] < start_ref[seg]
                offset = jnp.where(is_open, peak[:, lanes], -CLOSED)
                weight = jnp.exp2((scores[:, lanes] - offset) * SCALE)
                weights[head, at, lanes] = weight.astype(BF16)
                masses[seg] = masses[seg] + jnp.sum(
                    weight.reshape(BLOCK // 8, 8, SEG_LEN), axis=0
                )
        sums = jnp.dot(turned_values[...], weights[head], preferred_element_type=F32)
        mass = jnp.concatenate(
            [jnp.sum(part, axis=0, keepdims=True) for part in masses], axis=1
        )
        mass = jnp.round(mass * MASS_UNIT).astype(jnp.int32)
        for piece in range(2):
            value, level = encode(sums[piece * half : (piece + 1) * half])
            for at, word in enumerate(pack(value) + [first_rows([level, mass])]):
                out_ref[2 * head + piece, 8 * at : 8 * at + 8, :] = word


def combine_kernel(count, unit, parts_ref, out_ref):
    half = HEAD_DIM // 2
    mass = jnp.zeros((1, TOKENS), F32)
    sums = jnp.zeros((half, TOKENS), F32)
    for peer in range(count):
        words = [parts_ref[peer, 8 * at : 8 * at + 8, :] for at in range(6)]
        mass = mass + words[5][1:2].astype(F32) * (1.0 / unit)
        sums = sums + unpack(words[0:5]) * level_factor(words[5][0:1])
    attended = (sums / mass).astype(BF16)
    for peer in range(out_ref.shape[0]):
        out_ref[peer] = attended


def output_kernel(core_ref, attended_ref, weight_ref, keep_ref, send_ref, scratch):
    project_output(core_ref, attended_ref, weight_ref, keep_ref, send_ref, scratch)


def project_output(core_ref, attended_ref, weight_ref, keep_ref, send_ref, scratch):
    share = TOKENS // 2
    scratch[...] = lax.dot_general(
        attended_ref[...], weight_ref[...], (((0,), (0,)), ((), ())), preferred_element_type=F32
    )
    keep_ref[...] = scratch[pl.ds(core_ref[0] * share, share), :]
    send_ref[...] = scratch[pl.ds((1 - core_ref[0]) * share, share), :]


def crossed_output_kernel(core_ref, parts_ref, weight_ref, keep_ref, send_ref, scratch, attended):
    half = HEAD_DIM // 2
    for at in range(parts_ref.shape[0]):
        attended[at * half : (at + 1) * half, :] = parts_ref[at % RING * RING + at // RING]
    project_output(core_ref, attended, weight_ref, keep_ref, send_ref, scratch)


def add_kernel(keep_ref, received_ref, out_ref):
    out_ref[...] = keep_ref[...] + received_ref[...]


def add_residual(parts_ref, x_ref):
    total = parts_ref[0]
    for peer in range(1, parts_ref.shape[0]):
        total = total + parts_ref[peer]
    return (x_ref[...].astype(F32) + total).astype(BF16)


def residual_kernel(count, parts_ref, x_ref, out_ref, squares_ref):
    produced = add_residual(parts_ref, x_ref)
    out_ref[...] = produced
    rows = square_rows(produced.astype(F32))
    for peer in range(count):
        squares_ref[peer] = rows


def last_residual_kernel(parts_ref, x_ref, out_ref):
    produced = add_residual(parts_ref, x_ref)
    for peer in range(out_ref.shape[0]):
        out_ref[peer] = produced


def spread_kernel(squares_ref, x_ref, out_ref):
    tokens, width = x_ref.shape
    factor = norm_columns(squares_ref)[0:tokens]
    first = factor.astype(BF16).astype(F32)
    second = (factor - first).astype(BF16).astype(F32)
    lane = lax.broadcasted_iota(jnp.int32, factor.shape, 1)
    thirds = jnp.where(lane == 0, first, jnp.where(lane == 1, second, factor - first - second))
    for peer in range(out_ref.shape[0]):
        out_ref[peer, :, 0:width] = x_ref[...]
        out_ref[peer, :, width : width + 128] = thirds.astype(BF16)


def choose_kernel(core_ref, own0_ref, other0_ref, own1_ref, other1_ref, out_ref):
    share = TOKENS // 2
    width = out_ref.shape[1]
    first = core_ref[0] == 0
    at = pl.ds(core_ref[0] * share, share)
    out_ref[at, :] = jnp.where(first, own0_ref[:, 0:width], own1_ref[...])
    at = pl.ds((1 - core_ref[0]) * share, share)
    out_ref[at, :] = jnp.where(first, other0_ref[:, 0:width], other1_ref[...])


def exchange(value, axes):
    return lax.all_to_all(value, axes, 0, 0, tiled=True)


def swap(value):
    return lax.ppermute(value, "section", [(0, 1), (1, 0)])


def around_y(value, step):
    pairs = []
    for kv in range(RING * RING):
        z, y = divmod(kv, RING)
        pairs.append((kv, z * RING + (y + step) % RING))
    return lax.ppermute(value, "kv", pairs)


def over_z(value):
    groups = [[z * RING + y for z in range(RING)] for y in range(RING)]
    return lax.all_to_all(value, "kv", 0, 0, tiled=True, axis_index_groups=groups)


def near_holders(index):
    offsets = jnp.array([0, -1, 1, 2], jnp.int32)
    return index // RING * RING + (index % RING + offsets) % RING


def split_attention(parts, keys, values, logical, starts, index, cache):
    parts, cache = lax.optimization_barrier((parts, cache))
    sides = (around_y(cache, 1), around_y(cache, -1))
    count = lax.axis_size("kv")
    rows = SEG_LEN // count
    half = HEAD_DIM // 2
    with jax.named_scope("queries"):
        query, fresh = call(
            functools.partial(finish_projection_kernel, count),
            (
                jax.ShapeDtypeStruct((count, half, TOKENS), BF16),
                jax.ShapeDtypeStruct((2, FRESH, HEAD_DIM), BF16),
            ),
            [IN_VMEM],
            (IN_VMEM, IN_VMEM),
        )(parts)
        query = exchange(query, "kv").reshape(GROUP, HEAD_DIM, TOKENS)
        query, sides = lax.optimization_barrier((query, sides))
        opposite = jnp.stack([around_y(sides[0][0], 1), around_y(sides[1][1], -1)])
    stored = keys.shape[0]
    by_head = [
        IN_SMEM,
        IN_SMEM,
        IN_SMEM,
        pl.BlockSpec((HEADS_STEP, HEAD_DIM, TOKENS), lambda h: (h, 0, 0)),
        pl.BlockSpec((stored, HEAD_DIM), lambda h: (0, 0)),
    ]
    whole_values = pl.BlockSpec((stored, HEAD_DIM), lambda h: (0, 0))
    whole_fresh = pl.BlockSpec((2, FRESH, HEAD_DIM), lambda h: (0, 0, 0))
    whole_peaks = pl.BlockSpec((count, GROUP, TOKENS), lambda h: (0, 0, 0))
    with jax.named_scope("peaks"):
        peaks = call(
            functools.partial(peak_kernel, rows),
            jax.ShapeDtypeStruct((count, GROUP, TOKENS), F32),
            by_head + [whole_fresh],
            whole_peaks,
            grid=(GROUP // HEADS_STEP,),
            scratch_shapes=[pltpu.VMEM((GROUP, 1, TOKENS), F32)],
        )(index, logical, starts, query, keys, fresh)
        peaks = exchange(peaks, "kv")
    with jax.named_scope("attend"):
        sent = call(
            functools.partial(attend_kernel, rows),
            jax.ShapeDtypeStruct((count, 6 * 8, TOKENS), jnp.int32),
            by_head + [whole_values, whole_fresh, whole_peaks],
            pl.BlockSpec((2 * HEADS_STEP, 6 * 8, TOKENS), lambda h: (h, 0, 0)),
            grid=(GROUP // HEADS_STEP,),
            scratch_shapes=[
                pltpu.VMEM((HEAD_DIM, stored + FRESH), BF16),
                pltpu.VMEM((GROUP, 1, TOKENS), F32),
                pltpu.VMEM((HEADS_STEP, stored + FRESH, TOKENS), BF16),
            ],
        )(index, logical, starts, query, keys, values, fresh, peaks)
        parts = exchange(sent, "kv")
    with jax.named_scope("combine"):
        attended = call(
            functools.partial(combine_kernel, count, MASS_UNIT),
            jax.ShapeDtypeStruct((count, half, TOKENS), BF16),
            [IN_VMEM],
            IN_VMEM,
        )(parts)
        attended = exchange(attended, "kv").reshape(GROUP * HEAD_DIM, TOKENS)
        return attended, (cache,) + sides + (opposite,)


def near_attention(parts, caches, logical, starts, holders):
    count = lax.axis_size("kv")
    rows = SEG_LEN // count
    half = HEAD_DIM // 2
    with jax.named_scope("queries"):
        query, fresh = call(
            functools.partial(finish_crossed_kernel, count),
            (
                jax.ShapeDtypeStruct((RING, half, TOKENS), BF16),
                jax.ShapeDtypeStruct((2, 4 * rows, HEAD_DIM), BF16),
            ),
            [IN_VMEM],
            (IN_VMEM, IN_VMEM),
        )(parts)
        fresh = (fresh,) + tuple(around_y(fresh, step) for step in (1, -1, 2))
        query = over_z(query).reshape(2, HEAD_DIM, TOKENS)
    with jax.named_scope("peaks"):
        peaks = call(
            functools.partial(near_peak_kernel, rows),
            jax.ShapeDtypeStruct((RING, 8, TOKENS), F32),
            [IN_SMEM] * 3 + [IN_VMEM] * (1 + 2 * RING),
            IN_VMEM,
        )(holders, logical, starts, query, *caches, *fresh)
        peaks = over_z(peaks)
    with jax.named_scope("attend"):
        stored = RING * caches[0].shape[1]
        sent = call(
            functools.partial(near_attend_kernel, rows),
            jax.ShapeDtypeStruct((RING, 6 * 8, TOKENS), jnp.int32),
            [IN_SMEM] * 3
            + [pl.BlockSpec((1, HEAD_DIM, TOKENS), lambda h: (h, 0, 0))]
            + [IN_VMEM] * (2 * RING + 1),
            pl.BlockSpec((2, 6 * 8, TOKENS), lambda h: (h, 0, 0)),
            grid=(2,),
            scratch_shapes=[pltpu.VMEM((stored + 4 * RING * rows, TOKENS), BF16)],
        )(holders, logical, starts, query, *caches, *fresh, peaks)
        parts = over_z(sent)
    with jax.named_scope("combine"):
        attended = call(
            functools.partial(combine_kernel, RING, NEAR_MASS_UNIT),
            jax.ShapeDtypeStruct((count, half, TOKENS), BF16),
            [IN_VMEM],
            IN_VMEM,
        )(parts)
        return exchange(attended, "kv")


def layer(
    which, x, mine, gain, query_proj, kv_proj, out_proj, keys, values, logical, starts, index, core,
    later=None,
):
    count = lax.axis_size("kv")
    peers = lax.axis_size("tp")
    rows = SEG_LEN // count
    half = HEAD_DIM // 2
    width = query_proj.shape[0]
    share = TOKENS // 2
    part = share // peers
    with jax.named_scope("project"):
        shape = jax.ShapeDtypeStruct((count, 7 * 8, TOKENS), jnp.int32)
        if which == 0:
            squares = call(
                functools.partial(squares_kernel, count),
                jax.ShapeDtypeStruct((count, 8, TOKENS), F32),
                [IN_VMEM] * 2,
                IN_VMEM,
            )(x, jnp.pad(logical.astype(F32), (0, TOKENS - logical.shape[0]))[None])
            squares = exchange(squares, "kv")
            all_logical = squares[:, 1, 0 : logical.shape[0]].astype(jnp.int32)
            sent = call(
                functools.partial(first_project_kernel, count), shape, [IN_VMEM] * 5, IN_VMEM
            )(x, squares, gain, query_proj, kv_proj)
        else:
            sent = call(
                functools.partial(project_kernel, count),
                shape,
                [IN_SMEM] + [IN_VMEM] * 5,
                IN_VMEM,
                scratch_shapes=[pltpu.VMEM((TOKENS, width + 128), BF16)],
            )(core, x[0], x[1], gain, query_proj, kv_proj)
        parts = exchange(sent, "kv")
    if which == 0:
        attended, later = split_attention(parts, keys, values, logical, starts, index, later)
        holders = near_holders(index[0])
        later = (later, all_logical[holders].reshape(-1), holders)
        kernel, scratch = output_kernel, []
    else:
        attended = near_attention(parts, keys, logical, starts, index)
        kernel, scratch = crossed_output_kernel, [pltpu.VMEM((GROUP * HEAD_DIM, TOKENS), BF16)]
    with jax.named_scope("output"):
        keep, send = call(
            kernel,
            (jax.ShapeDtypeStruct((share, width), F32),) * 2,
            [IN_SMEM] + [IN_VMEM] * 2,
            (IN_VMEM, IN_VMEM),
            scratch_shapes=[pltpu.VMEM((TOKENS, width), F32)] + scratch,
        )(core, attended, out_proj)
        half_sum = call(
            add_kernel,
            jax.ShapeDtypeStruct((share, width), F32),
            [IN_VMEM] * 2,
            IN_VMEM,
        )(keep, swap(send))
        parts = exchange(half_sum.reshape(peers, part, width), "tp")
    with jax.named_scope("residual"):
        if which == LAYERS - 1:
            produced = call(
                last_residual_kernel,
                jax.ShapeDtypeStruct((peers, part, width), BF16),
                [IN_VMEM] * 2,
                IN_VMEM,
            )(parts, mine)
            mine = None
        else:
            mine, squares = call(
                functools.partial(residual_kernel, count),
                (
                    jax.ShapeDtypeStruct((part, width), BF16),
                    jax.ShapeDtypeStruct((count, 8, 128), F32),
                ),
                [IN_VMEM] * 2,
                (IN_VMEM, IN_VMEM),
            )(parts, mine)
            produced = call(
                spread_kernel,
                jax.ShapeDtypeStruct((peers, part, width + 128), BF16),
                [IN_VMEM] * 2,
                IN_VMEM,
            )(exchange(squares, "kv"), mine)
        own = exchange(produced, "tp").reshape(share, -1)
        return (own, swap(own)), mine, later


def per_device(
    segments_in, gain, query_weight, kv_weight, out_weight, kv_cache, block_logical, segment_block
):
    width = segments_in.shape[2]
    core = lax.axis_index("section")
    core_at = core.astype(jnp.int32)[None]
    index = lax.axis_index("kv").astype(jnp.int32)[None]
    per_core = GROUP * HEAD_DIM
    share = TOKENS // 2

    def pick(which):
        at = which * per_core
        kv_at = which * HEAD_DIM
        return (
            lax.dynamic_slice_in_dim(query_weight[0], at, per_core, 1),
            lax.dynamic_slice_in_dim(kv_weight[0], kv_at, HEAD_DIM, 2).reshape(width, -1),
            lax.dynamic_slice_in_dim(kv_cache[0, :, 0], kv_at, HEAD_DIM, 1),
            lax.dynamic_slice_in_dim(kv_cache[0, :, 1], kv_at, HEAD_DIM, 1),
            lax.dynamic_slice_in_dim(out_weight[0], at, per_core, 0),
            gain,
        )

    kept = pick(core)
    received = tuple(swap(v) for v in pick(1 - core))
    x = segments_in.reshape(TOKENS, width)
    part = share // lax.axis_size("tp")
    mine = lax.dynamic_slice_in_dim(x, core * share + lax.axis_index("tp") * part, part, 0)
    params = [
        [jnp.where(core == which, here, other) for here, other in zip(kept, received)]
        for which in range(LAYERS)
    ]
    cache = call(
        cache_kernel,
        jax.ShapeDtypeStruct((2,) + params[1][2].shape, BF16),
        [IN_VMEM] * 2,
        IN_VMEM,
    )(params[1][2], params[1][3])
    query_proj, kv_proj, keys, values, out_proj, gain_row = params[0]
    first, mine, (caches, numbers, holders) = layer(
        0, x, mine, gain_row, query_proj, kv_proj, out_proj, keys, values,
        block_logical, segment_block, index, core_at, cache,
    )
    query_proj, kv_proj, _, _, out_proj, gain_row = params[1]
    second, _, _ = layer(
        1, first, mine, gain_row, query_proj, kv_proj, out_proj, caches, None,
        numbers, segment_block, holders, core_at,
    )
    outputs = first + second
    result = call(
        choose_kernel,
        jax.ShapeDtypeStruct((TOKENS, width), BF16),
        [IN_SMEM] + [IN_VMEM] * 4,
        IN_VMEM,
    )(core_at, *outputs)
    return result.reshape(1, NSEG, SEG_LEN, width)


def solution(mesh):
    placed = (
        P(None, None, "kv"),
        P("section", "kv"),
        P("section", "kv", "tp"),
        P("section", "kv", None, "tp"),
        P("section", "tp", "kv"),
        P("section", "kv", None, "tp"),
        P("kv"),
        P(),
    )
    return jax.shard_map(
        per_device,
        mesh=mesh,
        in_specs=placed,
        out_specs=P("section", None, None, "kv"),
        check_vma=False,
    )
```

```python
import functools
import math

import jax
import jax.numpy as jnp
from jax import lax
from jax.experimental import pallas as pl
from jax.experimental.pallas import tpu as pltpu
from jax.sharding import PartitionSpec as P

D = 8192
HEAD_DIM = 128
BLOCK = 128
NSEG = 3
SEG_LEN = 128
TOKENS = NSEG * SEG_LEN
GROUP = 8
LAYERS = 2
EPSILON = 1e-05
CLOSED = -1e30
FRESH = 128
RANGE = 520000.0
MIDDLE = 524288
LEVELS = 2048
MASS_UNIT = 262144.0
NEAR_MASS_UNIT = 65536.0
HEADS_STEP = 2
SCALE = math.log2(math.e) / math.sqrt(HEAD_DIM)
F32 = jnp.float32
BF16 = jnp.bfloat16
VMEM_BYTES = 48 * 1024 * 1024


def call(kernel, out_shape, in_specs, out_specs, **rest):
    return pl.pallas_call(
        kernel,
        out_shape=out_shape,
        in_specs=in_specs,
        out_specs=out_specs,
        compiler_params=pltpu.CompilerParams(vmem_limit_bytes=VMEM_BYTES),
        **rest,
    )


IN_VMEM = pl.BlockSpec(memory_space=pltpu.VMEM)
IN_SMEM = pl.BlockSpec(memory_space=pltpu.SMEM)


RING = 4


def encode(block):
    top = jnp.maximum(jnp.max(jnp.abs(block), axis=0, keepdims=True), 1e-30)
    level = jnp.ceil(jnp.log2(top) * 16.0)
    value = jnp.round(block * (jnp.exp2(level * (-1.0 / 16.0)) * RANGE))
    return value.astype(jnp.int32) + MIDDLE, level.astype(jnp.int32)


def level_factor(level):
    return jnp.exp2(level.astype(F32) * (1.0 / 16.0)) * (1.0 / RANGE)


def pack(value):
    part = [value[8 * at : 8 * at + 8] for at in range(8)]
    lows = [
        part[5] & 0xFFF,
        (part[5] >> 12) | ((part[6] & 0xF) << 8),
        (part[6] >> 4) & 0xFFF,
        (part[6] >> 16) | ((part[7] & 0xFF) << 4),
        part[7] >> 8,
    ]
    return [(part[at] << 12) | lows[at] for at in range(5)]


def top_bits(word):
    return lax.shift_right_logical(word, jnp.int32(12))


def unpack(words):
    lows = [word & 0xFFF for word in words]
    part = [top_bits(word) for word in words]
    part.append(lows[0] | ((lows[1] & 0xFF) << 12))
    part.append((lows[1] >> 8) | (lows[2] << 4) | ((lows[3] & 0xF) << 16))
    part.append((lows[3] >> 4) | (lows[4] << 8))
    return (jnp.concatenate(part, axis=0) - MIDDLE).astype(F32)


def first_rows(rows, count=8):
    place = lax.broadcasted_iota(jnp.int32, (count, rows[0].shape[1]), 0)
    filled = jnp.zeros_like(place)
    for number, row in enumerate(rows):
        filled = jnp.where(place == number, row, filled)
    return filled


def square_rows(x):
    squares = jnp.sum(x * x, axis=1, keepdims=True)
    squares = jnp.broadcast_to(squares, (x.shape[0], 128))
    missing = -x.shape[0] % 128
    if missing:
        squares = jnp.concatenate([squares, jnp.zeros((missing, 128), F32)], axis=0)
    return squares.T[0:8]


def norm_columns(parts_ref):
    total = parts_ref[0]
    for peer in range(1, parts_ref.shape[0]):
        total = total + parts_ref[peer]
    factor = lax.rsqrt(total[0:1] / D + EPSILON)
    return jnp.broadcast_to(factor, (128, factor.shape[1])).T


def squares_kernel(count, x_ref, logical_ref, out_ref):
    rows = square_rows(x_ref[...].astype(F32))
    row = lax.broadcasted_iota(jnp.int32, rows.shape, 0)
    rows = jnp.where(row == 0, rows, logical_ref[...])
    for peer in range(count):
        out_ref[peer] = rows


def cache_kernel(keys_ref, values_ref, out_ref):
    out_ref[0] = keys_ref[...]
    for block in range(values_ref.shape[0] // BLOCK):
        at = slice(block * BLOCK, (block + 1) * BLOCK)
        out_ref[1, at, :] = values_ref[at, :].T


def first_project_kernel(count, x_ref, squares_ref, gain_ref, query_ref, kv_ref, out_ref):
    factor = norm_columns(squares_ref)[:, 0:1]
    normed = (x_ref[...].astype(F32) * factor * gain_ref[...]).astype(BF16)
    project(count, normed, query_ref, kv_ref, out_ref)


def project_kernel(count, core_ref, own_ref, other_ref, gain_ref, query_ref, kv_ref, out_ref, x_ref):
    share = TOKENS // 2
    width = gain_ref.shape[1]
    x_ref[pl.ds(core_ref[0] * share, share), :] = own_ref[...]
    x_ref[pl.ds((1 - core_ref[0]) * share, share), :] = other_ref[...]
    thirds = x_ref[:, width : width + 128].astype(F32)
    factor = thirds[:, 0:1] + thirds[:, 1:2] + thirds[:, 2:3]
    normed = (x_ref[:, 0:width].astype(F32) * factor * gain_ref[...]).astype(BF16)
    project(count, normed, query_ref, kv_ref, out_ref, True)


def project(count, scaled, query_ref, kv_ref, out_ref, crossed=False):
    half = HEAD_DIM // 2
    columns = query_ref.shape[1]
    rows = SEG_LEN // count
    fresh = jnp.dot(scaled, kv_ref[...], preferred_element_type=F32)
    for start in range(0, columns, 256):
        part = jnp.dot(scaled, query_ref[:, start : start + 256], preferred_element_type=F32)
        turned = part.T
        for piece in range(256 // half):
            at = start // half + piece
            peer = at % RING * RING + at // RING if crossed else at
            block = turned[piece * half : (piece + 1) * half]
            query, query_level = encode(block)
            words = pack(query)
            kinds = []
            for kind in range(2):
                lanes = slice(kind * HEAD_DIM, (kind + 1) * HEAD_DIM)
                block = jnp.concatenate(
                    [
                        fresh[seg * SEG_LEN + peer * rows : seg * SEG_LEN + (peer + 1) * rows, lanes]
                        for seg in range(NSEG)
                    ],
                    axis=1,
                )
                kinds.append(encode(block))
            levels = first_rows([query_level, kinds[0][1], kinds[1][1]]) + LEVELS
            words.append((kinds[0][0] << 12) | levels)
            words.append(kinds[1][0] << 12)
            for at, word in enumerate(words):
                out_ref[peer, 8 * at : 8 * at + 8, :] = word


def add_projection(count, parts_ref):
    half = HEAD_DIM // 2
    rows = SEG_LEN // count
    query = jnp.zeros((half, TOKENS), F32)
    fresh = [jnp.zeros((rows, TOKENS), F32) for _ in range(2)]
    for peer in range(count):
        words = [parts_ref[peer, 8 * at : 8 * at + 8, :] for at in range(7)]
        factors = level_factor((words[5] & 0xFFF) - LEVELS)
        query = query + unpack(words[0:5]) * factors[0:1]
        for kind in range(2):
            value = (top_bits(words[5 + kind]) - MIDDLE).astype(F32)
            fresh[kind] = fresh[kind] + value * factors[1 + kind : 2 + kind]
    return query, fresh


def finish_projection_kernel(count, parts_ref, query_out, fresh_out):
    rows = SEG_LEN // count
    query, fresh = add_projection(count, parts_ref)
    query = query.astype(BF16)
    for peer in range(count):
        query_out[peer] = query
    filler = jnp.zeros((FRESH - NSEG * rows, HEAD_DIM), F32)
    for kind in range(2):
        pieces = [
            fresh[kind][:, seg * SEG_LEN : (seg + 1) * SEG_LEN] for seg in range(NSEG)
        ]
        fresh_out[kind] = jnp.concatenate(pieces + [filler], axis=0).astype(BF16)


def finish_crossed_kernel(count, parts_ref, query_out, fresh_out):
    rows = SEG_LEN // count
    query, fresh = add_projection(count, parts_ref)
    query = query.astype(BF16)
    for peer in range(RING):
        query_out[peer] = query
    filler = jnp.zeros((rows, HEAD_DIM), F32)
    for kind in range(2):
        pieces = [
            fresh[kind][:, seg * SEG_LEN : (seg + 1) * SEG_LEN] for seg in range(NSEG)
        ]
        fresh_out[kind] = jnp.concatenate(pieces + [filler], axis=0).astype(BF16)


def near_mask(rows, slot_ref, seg):
    key_row = lax.broadcasted_iota(jnp.int32, (4 * rows, SEG_LEN), 0)
    token = lax.broadcasted_iota(jnp.int32, (4 * rows, SEG_LEN), 1)
    local = key_row - seg * rows
    inside = (local >= 0) & (local < rows)
    return jnp.concatenate(
        [
            jnp.where(inside & (local + slot_ref[slot] * rows <= token), 1.0, 0.0)
            for slot in range(RING)
        ],
        axis=0,
    ) > 0.5


def near_peak_kernel(rows, slot_ref, logical_ref, start_ref, query_ref, *refs):
    caches, fresh, out_ref = refs[0:RING], refs[RING : 2 * RING], refs[2 * RING]
    blocks = caches[0].shape[1] // BLOCK
    found = []
    for head in range(query_ref.shape[0]):
        query = query_ref[head]
        keys = jnp.concatenate([part[0] for part in fresh], axis=0)
        scores = jnp.dot(keys, query, preferred_element_type=F32)
        tops = []
        for seg in range(NSEG):
            lanes = slice(seg * SEG_LEN, (seg + 1) * SEG_LEN)
            masked = jnp.where(near_mask(rows, slot_ref, seg), scores[:, lanes], CLOSED)
            tops.append(jnp.max(masked.reshape(-1, 8, SEG_LEN), axis=0))
        for number in range(RING * blocks):
            block = number % blocks
            keys = caches[number // blocks][0, block * BLOCK : (block + 1) * BLOCK, :]
            scores = jnp.dot(keys, query, preferred_element_type=F32)
            top = jnp.max(scores.reshape(BLOCK // 8, 8, TOKENS), axis=0)
            for seg in range(NSEG):
                lanes = slice(seg * SEG_LEN, (seg + 1) * SEG_LEN)
                is_open = logical_ref[number] < start_ref[seg]
                tops[seg] = jnp.maximum(tops[seg], jnp.where(is_open, top[:, lanes], CLOSED))
        found.append(
            jnp.concatenate([jnp.max(top, axis=0, keepdims=True) for top in tops], axis=1)
        )
    found = jnp.concatenate(found * 4, axis=0)
    for peer in range(RING):
        out_ref[peer] = found


def near_attend_kernel(rows, slot_ref, logical_ref, start_ref, query_ref, *refs):
    caches, fresh = refs[0:RING], refs[RING : 2 * RING]
    peaks_ref, out_ref, weights = refs[2 * RING :]
    blocks = caches[0].shape[1] // BLOCK
    stored = RING * blocks * BLOCK
    half = HEAD_DIM // 2
    head = pl.program_id(0)
    query = query_ref[0]
    peak = peaks_ref[0]
    for peer in range(1, RING):
        peak = jnp.maximum(peak, peaks_ref[peer])
    peak = jnp.where(head == 0, peak[0:1], peak[1:2])
    keys = jnp.concatenate([part[0] for part in fresh], axis=0)
    scores = jnp.dot(keys, query, preferred_element_type=F32)
    masses = []
    for seg in range(NSEG):
        lanes = slice(seg * SEG_LEN, (seg + 1) * SEG_LEN)
        weight = jnp.exp2((scores[:, lanes] - peak[:, lanes]) * SCALE)
        weight = jnp.where(near_mask(rows, slot_ref, seg), weight, 0.0)
        weights[stored : stored + 4 * RING * rows, lanes] = weight.astype(BF16)
        masses.append(jnp.sum(weight.reshape(-1, 8, SEG_LEN), axis=0))
    for number in range(RING * blocks):
        block = number % blocks
        keys = caches[number // blocks][0, block * BLOCK : (block + 1) * BLOCK, :]
        scores = jnp.dot(keys, query, preferred_element_type=F32)
        for seg in range(NSEG):
            lanes = slice(seg * SEG_LEN, (seg + 1) * SEG_LEN)
            is_open = logical_ref[number] < start_ref[seg]
            offset = jnp.where(is_open, peak[:, lanes], -CLOSED)
            weight = jnp.exp2((scores[:, lanes] - offset) * SCALE)
            weights[number * BLOCK : (number + 1) * BLOCK, lanes] = weight.astype(BF16)
            masses[seg] = masses[seg] + jnp.sum(weight.reshape(BLOCK // 8, 8, SEG_LEN), axis=0)
    turned = [
        cache[1, block * BLOCK : (block + 1) * BLOCK, :] for cache in caches for block in range(blocks)
    ]
    turned.append(jnp.concatenate([part[1] for part in fresh], axis=0).T)
    sums = jnp.dot(jnp.concatenate(turned, axis=1), weights[...], preferred_element_type=F32)
    mass = jnp.concatenate([jnp.sum(part, axis=0, keepdims=True) for part in masses], axis=1)
    mass = jnp.round(mass * NEAR_MASS_UNIT).astype(jnp.int32)
    for piece in range(2):
        value, level = encode(sums[piece * half : (piece + 1) * half])
        for at, word in enumerate(pack(value) + [first_rows([level, mass])]):
            out_ref[piece, 8 * at : 8 * at + 8, :] = word


def fresh_mask(rows, index_ref, seg):
    key_row = lax.broadcasted_iota(jnp.int32, (FRESH, SEG_LEN), 0)
    token = lax.broadcasted_iota(jnp.int32, (FRESH, SEG_LEN), 1)
    local = key_row - seg * rows
    return (local >= 0) & (local < rows) & (local + index_ref[0] * rows <= token)


def peak_kernel(
    rows, index_ref, logical_ref, start_ref, query_ref, keys_ref, fresh_ref, out_ref, peaks
):
    blocks = keys_ref.shape[0] // BLOCK
    heads = query_ref.shape[0]
    step = pl.program_id(0)
    for head in range(heads):
        query = query_ref[head]
        scores = jnp.dot(fresh_ref[0], query, preferred_element_type=F32)
        tops = []
        for seg in range(NSEG):
            lanes = slice(seg * SEG_LEN, (seg + 1) * SEG_LEN)
            masked = jnp.where(fresh_mask(rows, index_ref, seg), scores[:, lanes], CLOSED)
            tops.append(jnp.max(masked.reshape(FRESH // 8, 8, SEG_LEN), axis=0))
        for block in range(blocks):
            at = slice(block * BLOCK, (block + 1) * BLOCK)
            scores = jnp.dot(keys_ref[at, :], query, preferred_element_type=F32)
            top = jnp.max(scores.reshape(BLOCK // 8, 8, TOKENS), axis=0)
            for seg in range(NSEG):
                lanes = slice(seg * SEG_LEN, (seg + 1) * SEG_LEN)
                is_open = logical_ref[block] < start_ref[seg]
                tops[seg] = jnp.maximum(tops[seg], jnp.where(is_open, top[:, lanes], CLOSED))
        peaks[step * heads + head] = jnp.concatenate(
            [jnp.max(top, axis=0, keepdims=True) for top in tops], axis=1
        )

    @pl.when(step == pl.num_programs(0) - 1)
    def _():
        found = jnp.concatenate([peaks[head] for head in range(GROUP)], axis=0)
        for peer in range(out_ref.shape[0]):
            out_ref[peer] = found


def attend_kernel(
    rows, index_ref, logical_ref, start_ref, query_ref, keys_ref, values_ref, fresh_ref, peaks_ref,
    out_ref, turned_values, peaks, weights,
):
    blocks = keys_ref.shape[0] // BLOCK
    stored = blocks * BLOCK
    half = HEAD_DIM // 2
    heads = query_ref.shape[0]
    step = pl.program_id(0)

    @pl.when(step == 0)
    def _():
        for block in range(blocks):
            at = slice(block * BLOCK, (block + 1) * BLOCK)
            turned_values[:, at] = values_ref[at, :].T
        turned_values[:, stored : stored + FRESH] = fresh_ref[1].T
        top = peaks_ref[0]
        for peer in range(1, peaks_ref.shape[0]):
            top = jnp.maximum(top, peaks_ref[peer])
        for head in range(GROUP):
            peaks[head] = top[head : head + 1]

    for head in range(heads):
        query = query_ref[head]
        peak = peaks[step * heads + head]
        scores = jnp.dot(fresh_ref[0], query, preferred_element_type=F32)
        masses = []
        for seg in range(NSEG):
            lanes = slice(seg * SEG_LEN, (seg + 1) * SEG_LEN)
            weight = jnp.exp2((scores[:, lanes] - peak[:, lanes]) * SCALE)
            weight = jnp.where(fresh_mask(rows, index_ref, seg), weight, 0.0)
            weights[head, stored : stored + FRESH, lanes] = weight.astype(BF16)
            masses.append(jnp.sum(weight.reshape(FRESH // 8, 8, SEG_LEN), axis=0))
        for block in range(blocks):
            at = slice(block * BLOCK, (block + 1) * BLOCK)
            scores = jnp.dot(keys_ref[at, :], query, preferred_element_type=F32)
            for seg in range(NSEG):
                lanes = slice(seg * SEG_LEN, (seg + 1) * SEG_LEN)
                is_open = logical_ref[block] < start_ref[seg]
                offset = jnp.where(is_open, peak[:, lanes], -CLOSED)
                weight = jnp.exp2((scores[:, lanes] - offset) * SCALE)
                weights[head, at, lanes] = weight.astype(BF16)
                masses[seg] = masses[seg] + jnp.sum(
                    weight.reshape(BLOCK // 8, 8, SEG_LEN), axis=0
                )
        sums = jnp.dot(turned_values[...], weights[head], preferred_element_type=F32)
        mass = jnp.concatenate(
            [jnp.sum(part, axis=0, keepdims=True) for part in masses], axis=1
        )
        mass = jnp.round(mass * MASS_UNIT).astype(jnp.int32)
        for piece in range(2):
            value, level = encode(sums[piece * half : (piece + 1) * half])
            for at, word in enumerate(pack(value) + [first_rows([level, mass])]):
                out_ref[2 * head + piece, 8 * at : 8 * at + 8, :] = word


def combine_kernel(count, unit, parts_ref, out_ref):
    half = HEAD_DIM // 2
    mass = jnp.zeros((1, TOKENS), F32)
    sums = jnp.zeros((half, TOKENS), F32)
    for peer in range(count):
        words = [parts_ref[peer, 8 * at : 8 * at + 8, :] for at in range(6)]
        mass = mass + words[5][1:2].astype(F32) * (1.0 / unit)
        sums = sums + unpack(words[0:5]) * level_factor(words[5][0:1])
    attended = (sums / mass).astype(BF16)
    for peer in range(out_ref.shape[0]):
        out_ref[peer] = attended


def output_kernel(core_ref, attended_ref, weight_ref, keep_ref, send_ref, scratch):
    project_output(core_ref, attended_ref, weight_ref, keep_ref, send_ref, scratch)


def project_output(core_ref, attended_ref, weight_ref, keep_ref, send_ref, scratch):
    share = TOKENS // 2
    scratch[...] = lax.dot_general(
        attended_ref[...], weight_ref[...], (((0,), (0,)), ((), ())), preferred_element_type=F32
    )
    keep_ref[...] = scratch[pl.ds(core_ref[0] * share, share), :]
    send_ref[...] = scratch[pl.ds((1 - core_ref[0]) * share, share), :]


def crossed_output_kernel(core_ref, parts_ref, weight_ref, keep_ref, send_ref, scratch, attended):
    half = HEAD_DIM // 2
    for at in range(parts_ref.shape[0]):
        attended[at * half : (at + 1) * half, :] = parts_ref[at % RING * RING + at // RING]
    project_output(core_ref, attended, weight_ref, keep_ref, send_ref, scratch)


def add_kernel(keep_ref, received_ref, out_ref):
    out_ref[...] = keep_ref[...] + received_ref[...]


def add_residual(parts_ref, x_ref):
    total = parts_ref[0]
    for peer in range(1, parts_ref.shape[0]):
        total = total + parts_ref[peer]
    return (x_ref[...].astype(F32) + total).astype(BF16)


def residual_kernel(count, parts_ref, x_ref, out_ref, squares_ref):
    produced = add_residual(parts_ref, x_ref)
    out_ref[...] = produced
    rows = square_rows(produced.astype(F32))
    for peer in range(count):
        squares_ref[peer] = rows


def last_residual_kernel(parts_ref, x_ref, out_ref):
    produced = add_residual(parts_ref, x_ref)
    for peer in range(out_ref.shape[0]):
        out_ref[peer] = produced


def spread_kernel(squares_ref, x_ref, out_ref):
    tokens, width = x_ref.shape
    factor = norm_columns(squares_ref)[0:tokens]
    first = factor.astype(BF16).astype(F32)
    second = (factor - first).astype(BF16).astype(F32)
    lane = lax.broadcasted_iota(jnp.int32, factor.shape, 1)
    thirds = jnp.where(lane == 0, first, jnp.where(lane == 1, second, factor - first - second))
    for peer in range(out_ref.shape[0]):
        out_ref[peer, :, 0:width] = x_ref[...]
        out_ref[peer, :, width : width + 128] = thirds.astype(BF16)


def choose_kernel(core_ref, own0_ref, other0_ref, own1_ref, other1_ref, out_ref):
    share = TOKENS // 2
    width = out_ref.shape[1]
    first = core_ref[0] == 0
    at = pl.ds(core_ref[0] * share, share)
    out_ref[at, :] = jnp.where(first, own0_ref[:, 0:width], own1_ref[...])
    at = pl.ds((1 - core_ref[0]) * share, share)
    out_ref[at, :] = jnp.where(first, other0_ref[:, 0:width], other1_ref[...])


def exchange(value, axes):
    return lax.all_to_all(value, axes, 0, 0, tiled=True)


def swap(value):
    return lax.ppermute(value, "section", [(0, 1), (1, 0)])


def around_y(value, step):
    pairs = []
    for kv in range(RING * RING):
        z, y = divmod(kv, RING)
        pairs.append((kv, z * RING + (y + step) % RING))
    return lax.ppermute(value, "kv", pairs)


def over_z(value):
    groups = [[z * RING + y for z in range(RING)] for y in range(RING)]
    return lax.all_to_all(value, "kv", 0, 0, tiled=True, axis_index_groups=groups)


def near_holders(index):
    offsets = jnp.array([0, -1, 1, 2], jnp.int32)
    return index // RING * RING + (index % RING + offsets) % RING


def split_attention(parts, keys, values, logical, starts, index):
    count = lax.axis_size("kv")
    rows = SEG_LEN // count
    half = HEAD_DIM // 2
    with jax.named_scope("queries"):
        query, fresh = call(
            functools.partial(finish_projection_kernel, count),
            (
                jax.ShapeDtypeStruct((count, half, TOKENS), BF16),
                jax.ShapeDtypeStruct((2, FRESH, HEAD_DIM), BF16),
            ),
            [IN_VMEM],
            (IN_VMEM, IN_VMEM),
        )(parts)
        query = exchange(query, "kv").reshape(GROUP, HEAD_DIM, TOKENS)
    stored = keys.shape[0]
    by_head = [
        IN_SMEM,
        IN_SMEM,
        IN_SMEM,
        pl.BlockSpec((HEADS_STEP, HEAD_DIM, TOKENS), lambda h: (h, 0, 0)),
        pl.BlockSpec((stored, HEAD_DIM), lambda h: (0, 0)),
    ]
    whole_values = pl.BlockSpec((stored, HEAD_DIM), lambda h: (0, 0))
    whole_fresh = pl.BlockSpec((2, FRESH, HEAD_DIM), lambda h: (0, 0, 0))
    whole_peaks = pl.BlockSpec((count, GROUP, TOKENS), lambda h: (0, 0, 0))
    with jax.named_scope("peaks"):
        peaks = call(
            functools.partial(peak_kernel, rows),
            jax.ShapeDtypeStruct((count, GROUP, TOKENS), F32),
            by_head + [whole_fresh],
            whole_peaks,
            grid=(GROUP // HEADS_STEP,),
            scratch_shapes=[pltpu.VMEM((GROUP, 1, TOKENS), F32)],
        )(index, logical, starts, query, keys, fresh)
        peaks = exchange(peaks, "kv")
    with jax.named_scope("attend"):
        sent = call(
            functools.partial(attend_kernel, rows),
            jax.ShapeDtypeStruct((count, 6 * 8, TOKENS), jnp.int32),
            by_head + [whole_values, whole_fresh, whole_peaks],
            pl.BlockSpec((2 * HEADS_STEP, 6 * 8, TOKENS), lambda h: (h, 0, 0)),
            grid=(GROUP // HEADS_STEP,),
            scratch_shapes=[
                pltpu.VMEM((HEAD_DIM, stored + FRESH), BF16),
                pltpu.VMEM((GROUP, 1, TOKENS), F32),
                pltpu.VMEM((HEADS_STEP, stored + FRESH, TOKENS), BF16),
            ],
        )(index, logical, starts, query, keys, values, fresh, peaks)
        parts = exchange(sent, "kv")
    with jax.named_scope("combine"):
        attended = call(
            functools.partial(combine_kernel, count, MASS_UNIT),
            jax.ShapeDtypeStruct((count, half, TOKENS), BF16),
            [IN_VMEM],
            IN_VMEM,
        )(parts)
        return exchange(attended, "kv").reshape(GROUP * HEAD_DIM, TOKENS)


def near_attention(parts, caches, logical, starts, holders):
    count = lax.axis_size("kv")
    rows = SEG_LEN // count
    half = HEAD_DIM // 2
    with jax.named_scope("queries"):
        query, fresh = call(
            functools.partial(finish_crossed_kernel, count),
            (
                jax.ShapeDtypeStruct((RING, half, TOKENS), BF16),
                jax.ShapeDtypeStruct((2, 4 * rows, HEAD_DIM), BF16),
            ),
            [IN_VMEM],
            (IN_VMEM, IN_VMEM),
        )(parts)
        fresh = (fresh,) + tuple(around_y(fresh, step) for step in (1, -1, 2))
        query = over_z(query).reshape(2, HEAD_DIM, TOKENS)
    with jax.named_scope("peaks"):
        peaks = call(
            functools.partial(near_peak_kernel, rows),
            jax.ShapeDtypeStruct((RING, 8, TOKENS), F32),
            [IN_SMEM] * 3 + [IN_VMEM] * (1 + 2 * RING),
            IN_VMEM,
        )(holders, logical, starts, query, *caches, *fresh)
        peaks = over_z(peaks)
    with jax.named_scope("attend"):
        stored = RING * caches[0].shape[1]
        sent = call(
            functools.partial(near_attend_kernel, rows),
            jax.ShapeDtypeStruct((RING, 6 * 8, TOKENS), jnp.int32),
            [IN_SMEM] * 3
            + [pl.BlockSpec((1, HEAD_DIM, TOKENS), lambda h: (h, 0, 0))]
            + [IN_VMEM] * (2 * RING + 1),
            pl.BlockSpec((2, 6 * 8, TOKENS), lambda h: (h, 0, 0)),
            grid=(2,),
            scratch_shapes=[pltpu.VMEM((stored + 4 * RING * rows, TOKENS), BF16)],
        )(holders, logical, starts, query, *caches, *fresh, peaks)
        parts = over_z(sent)
    with jax.named_scope("combine"):
        attended = call(
            functools.partial(combine_kernel, RING, NEAR_MASS_UNIT),
            jax.ShapeDtypeStruct((count, half, TOKENS), BF16),
            [IN_VMEM],
            IN_VMEM,
        )(parts)
        return exchange(attended, "kv")


def layer(
    which, x, mine, gain, query_proj, kv_proj, out_proj, keys, values, logical, starts, index, core,
    squares=None,
):
    count = lax.axis_size("kv")
    peers = lax.axis_size("tp")
    rows = SEG_LEN // count
    half = HEAD_DIM // 2
    width = query_proj.shape[0]
    share = TOKENS // 2
    part = share // peers
    with jax.named_scope("project"):
        shape = jax.ShapeDtypeStruct((count, 7 * 8, TOKENS), jnp.int32)
        if which == 0:
            squares = exchange(squares, "kv")
            all_logical = squares[:, 1, 0 : logical.shape[0]].astype(jnp.int32)
            sent = call(
                functools.partial(first_project_kernel, count), shape, [IN_VMEM] * 5, IN_VMEM
            )(x, squares, gain, query_proj, kv_proj)
        else:
            sent = call(
                functools.partial(project_kernel, count),
                shape,
                [IN_SMEM] + [IN_VMEM] * 5,
                IN_VMEM,
                scratch_shapes=[pltpu.VMEM((TOKENS, width + 128), BF16)],
            )(core, x[0], x[1], gain, query_proj, kv_proj)
        if which == 0:
            sent, keys = lax.optimization_barrier((sent, keys))
        parts = exchange(sent, "kv")
    later = None
    if which == 0:
        keys, values, later = values(keys)
        attended = split_attention(parts, keys, values, logical, starts, index)
        attended, later = lax.optimization_barrier((attended, later))
        sides = (around_y(later, 1), around_y(later, -1))
        kernel, scratch = output_kernel, []
    else:
        attended = near_attention(parts, keys, logical, starts, index)
        kernel, scratch = crossed_output_kernel, [pltpu.VMEM((GROUP * HEAD_DIM, TOKENS), BF16)]
    with jax.named_scope("output"):
        keep, send = call(
            kernel,
            (jax.ShapeDtypeStruct((share, width), F32),) * 2,
            [IN_SMEM] + [IN_VMEM] * 2,
            (IN_VMEM, IN_VMEM),
            scratch_shapes=[pltpu.VMEM((TOKENS, width), F32)] + scratch,
        )(core, attended, out_proj)
        half_sum = call(
            add_kernel,
            jax.ShapeDtypeStruct((share, width), F32),
            [IN_VMEM] * 2,
            IN_VMEM,
        )(keep, swap(send))
        parts = exchange(half_sum.reshape(peers, part, width), "tp")
    with jax.named_scope("residual"):
        if which == LAYERS - 1:
            produced = call(
                last_residual_kernel,
                jax.ShapeDtypeStruct((peers, part, width), BF16),
                [IN_VMEM] * 2,
                IN_VMEM,
            )(parts, mine)
            mine = None
        else:
            mine, squares = call(
                functools.partial(residual_kernel, count),
                (
                    jax.ShapeDtypeStruct((part, width), BF16),
                    jax.ShapeDtypeStruct((count, 8, 128), F32),
                ),
                [IN_VMEM] * 2,
                (IN_VMEM, IN_VMEM),
            )(parts, mine)
            squares = exchange(squares, "kv")
            squares, sides = lax.optimization_barrier((squares, sides))
            opposite = jnp.stack([around_y(sides[0][0], 1), around_y(sides[1][1], -1)])
            holders = near_holders(index[0])
            later = ((later,) + sides + (opposite,), all_logical[holders].reshape(-1), holders)
            produced = call(
                spread_kernel,
                jax.ShapeDtypeStruct((peers, part, width + 128), BF16),
                [IN_VMEM] * 2,
                IN_VMEM,
            )(squares, mine)
        own = exchange(produced, "tp").reshape(share, -1)
        return (own, swap(own)), mine, later


def per_device(
    segments_in, gain, query_weight, kv_weight, out_weight, kv_cache, block_logical, segment_block
):
    width = segments_in.shape[2]
    core = lax.axis_index("section")
    core_at = core.astype(jnp.int32)[None]
    index = lax.axis_index("kv").astype(jnp.int32)[None]
    per_core = GROUP * HEAD_DIM
    share = TOKENS // 2

    x = segments_in.reshape(TOKENS, width)
    count = lax.axis_size("kv")
    blocks = block_logical.shape[0]
    squares = call(
        functools.partial(squares_kernel, count),
        jax.ShapeDtypeStruct((count, 8, TOKENS), F32),
        [IN_VMEM] * 2,
        IN_VMEM,
    )(x, jnp.pad(block_logical.astype(F32), (0, TOKENS - blocks))[None])
    squares, query_weight, kv_weight, out_weight = lax.optimization_barrier(
        (squares, query_weight, kv_weight, out_weight)
    )

    def pick(which):
        at = which * per_core
        kv_at = which * HEAD_DIM
        return (
            lax.dynamic_slice_in_dim(query_weight[0], at, per_core, 1),
            lax.dynamic_slice_in_dim(kv_weight[0], kv_at, HEAD_DIM, 2).reshape(width, -1),
            lax.dynamic_slice_in_dim(out_weight[0], at, per_core, 0),
            gain,
        )

    kept = pick(core)
    received = tuple(swap(v) for v in pick(1 - core))
    part = share // lax.axis_size("tp")
    mine = lax.dynamic_slice_in_dim(x, core * share + lax.axis_index("tp") * part, part, 0)
    params = [
        [jnp.where(core == which, here, other) for here, other in zip(kept, received)]
        for which in range(LAYERS)
    ]

    def cut_cache(cache):
        def cut(which):
            return tuple(
                lax.dynamic_slice_in_dim(cache[0, :, kind], which * HEAD_DIM, HEAD_DIM, 1)
                for kind in range(2)
            )

        pairs = [(here, swap(there)) for here, there in zip(cut(core), cut(1 - core))]
        keys, values = (jnp.where(core == 0, here, other) for here, other in pairs)
        later = call(
            cache_kernel,
            jax.ShapeDtypeStruct((2,) + keys.shape, BF16),
            [IN_VMEM] * 2,
            IN_VMEM,
        )(*(jnp.where(core == 1, here, other) for here, other in pairs))
        return keys, values, later

    query_proj, kv_proj, out_proj, gain_row = params[0]
    first, mine, (caches, numbers, holders) = layer(
        0, x, mine, gain_row, query_proj, kv_proj, out_proj, kv_cache, cut_cache,
        block_logical, segment_block, index, core_at, squares,
    )
    query_proj, kv_proj, out_proj, gain_row = params[1]
    second, _, _ = layer(
        1, first, mine, gain_row, query_proj, kv_proj, out_proj, caches, None,
        numbers, segment_block, holders, core_at,
    )
    outputs = first + second
    result = call(
        choose_kernel,
        jax.ShapeDtypeStruct((TOKENS, width), BF16),
        [IN_SMEM] + [IN_VMEM] * 4,
        IN_VMEM,
    )(core_at, *outputs)
    return result.reshape(1, NSEG, SEG_LEN, width)


def solution(mesh):
    placed = (
        P(None, None, "kv"),
        P("section", "kv"),
        P("section", "kv", "tp"),
        P("section", "kv", None, "tp"),
        P("section", "tp", "kv"),
        P("section", "kv", None, "tp"),
        P("kv"),
        P(),
    )
    return jax.shard_map(
        per_device,
        mesh=mesh,
        in_specs=placed,
        out_specs=P("section", None, None, "kv"),
        check_vma=False,
    )
```

```python
import functools
import math

import jax
import jax.numpy as jnp
from jax import lax
from jax.experimental import pallas as pl
from jax.experimental.pallas import tpu as pltpu
from jax.sharding import PartitionSpec as P

D = 8192
HEAD_DIM = 128
BLOCK = 128
NSEG = 3
SEG_LEN = 128
TOKENS = NSEG * SEG_LEN
GROUP = 8
LAYERS = 2
EPSILON = 1e-05
CLOSED = -1e30
FRESH = 128
RANGE = 520000.0
MIDDLE = 524288
LEVELS = 2048
MASS_UNIT = 262144.0
NEAR_MASS_UNIT = 65536.0
HEADS_STEP = 2
SCALE = math.log2(math.e) / math.sqrt(HEAD_DIM)
F32 = jnp.float32
BF16 = jnp.bfloat16
VMEM_BYTES = 48 * 1024 * 1024


def call(kernel, out_shape, in_specs, out_specs, **rest):
    return pl.pallas_call(
        kernel,
        out_shape=out_shape,
        in_specs=in_specs,
        out_specs=out_specs,
        compiler_params=pltpu.CompilerParams(vmem_limit_bytes=VMEM_BYTES),
        **rest,
    )


IN_VMEM = pl.BlockSpec(memory_space=pltpu.VMEM)
IN_SMEM = pl.BlockSpec(memory_space=pltpu.SMEM)


RING = 4


def encode(block):
    top = jnp.maximum(jnp.max(jnp.abs(block), axis=0, keepdims=True), 1e-30)
    level = jnp.ceil(jnp.log2(top) * 16.0)
    value = jnp.round(block * (jnp.exp2(level * (-1.0 / 16.0)) * RANGE))
    return value.astype(jnp.int32) + MIDDLE, level.astype(jnp.int32)


def level_factor(level):
    return jnp.exp2(level.astype(F32) * (1.0 / 16.0)) * (1.0 / RANGE)


def pack(value):
    part = [value[8 * at : 8 * at + 8] for at in range(8)]
    lows = [
        part[5] & 0xFFF,
        (part[5] >> 12) | ((part[6] & 0xF) << 8),
        (part[6] >> 4) & 0xFFF,
        (part[6] >> 16) | ((part[7] & 0xFF) << 4),
        part[7] >> 8,
    ]
    return [(part[at] << 12) | lows[at] for at in range(5)]


def top_bits(word):
    return lax.shift_right_logical(word, jnp.int32(12))


def unpack(words):
    lows = [word & 0xFFF for word in words]
    part = [top_bits(word) for word in words]
    part.append(lows[0] | ((lows[1] & 0xFF) << 12))
    part.append((lows[1] >> 8) | (lows[2] << 4) | ((lows[3] & 0xF) << 16))
    part.append((lows[3] >> 4) | (lows[4] << 8))
    return (jnp.concatenate(part, axis=0) - MIDDLE).astype(F32)


def first_rows(rows, count=8):
    place = lax.broadcasted_iota(jnp.int32, (count, rows[0].shape[1]), 0)
    filled = jnp.zeros_like(place)
    for number, row in enumerate(rows):
        filled = jnp.where(place == number, row, filled)
    return filled


def square_rows(x):
    squares = jnp.sum(x * x, axis=1, keepdims=True)
    squares = jnp.broadcast_to(squares, (x.shape[0], 128))
    missing = -x.shape[0] % 128
    if missing:
        squares = jnp.concatenate([squares, jnp.zeros((missing, 128), F32)], axis=0)
    return squares.T[0:8]


def norm_columns(parts_ref):
    total = parts_ref[0]
    for peer in range(1, parts_ref.shape[0]):
        total = total + parts_ref[peer]
    factor = lax.rsqrt(total[0:1] / D + EPSILON)
    return jnp.broadcast_to(factor, (128, factor.shape[1])).T


def squares_kernel(count, x_ref, logical_ref, out_ref):
    rows = square_rows(x_ref[...].astype(F32))
    row = lax.broadcasted_iota(jnp.int32, rows.shape, 0)
    rows = jnp.where(row == 0, rows, logical_ref[...])
    for peer in range(count):
        out_ref[peer] = rows


def cache_kernel(keys_ref, values_ref, out_ref):
    out_ref[0] = keys_ref[...]
    for block in range(values_ref.shape[0] // BLOCK):
        at = slice(block * BLOCK, (block + 1) * BLOCK)
        out_ref[1, at, :] = values_ref[at, :].T


def first_project_kernel(count, x_ref, squares_ref, gain_ref, query_ref, kv_ref, out_ref):
    factor = norm_columns(squares_ref)[:, 0:1]
    normed = (x_ref[...].astype(F32) * factor * gain_ref[...]).astype(BF16)
    project(count, normed, query_ref, kv_ref, out_ref)


def project_kernel(count, core_ref, own_ref, other_ref, gain_ref, query_ref, kv_ref, out_ref, x_ref):
    share = TOKENS // 2
    width = gain_ref.shape[1]
    x_ref[pl.ds(core_ref[0] * share, share), :] = own_ref[...]
    x_ref[pl.ds((1 - core_ref[0]) * share, share), :] = other_ref[...]
    thirds = x_ref[:, width : width + 128].astype(F32)
    factor = thirds[:, 0:1] + thirds[:, 1:2] + thirds[:, 2:3]
    normed = (x_ref[:, 0:width].astype(F32) * factor * gain_ref[...]).astype(BF16)
    project(count, normed, query_ref, kv_ref, out_ref, True)


def project(count, scaled, query_ref, kv_ref, out_ref, crossed=False):
    half = HEAD_DIM // 2
    columns = query_ref.shape[1]
    rows = SEG_LEN // count
    fresh = jnp.dot(scaled, kv_ref[...], preferred_element_type=F32)
    for start in range(0, columns, 256):
        part = jnp.dot(scaled, query_ref[:, start : start + 256], preferred_element_type=F32)
        turned = part.T
        for piece in range(256 // half):
            at = start // half + piece
            peer = at % RING * RING + at // RING if crossed else at
            block = turned[piece * half : (piece + 1) * half]
            query, query_level = encode(block)
            words = pack(query)
            kinds = []
            for kind in range(2):
                lanes = slice(kind * HEAD_DIM, (kind + 1) * HEAD_DIM)
                block = jnp.concatenate(
                    [
                        fresh[seg * SEG_LEN + peer * rows : seg * SEG_LEN + (peer + 1) * rows, lanes]
                        for seg in range(NSEG)
                    ],
                    axis=1,
                )
                kinds.append(encode(block))
            levels = first_rows([query_level, kinds[0][1], kinds[1][1]]) + LEVELS
            words.append((kinds[0][0] << 12) | levels)
            words.append(kinds[1][0] << 12)
            for at, word in enumerate(words):
                out_ref[peer, 8 * at : 8 * at + 8, :] = word


def add_projection(count, parts_ref):
    half = HEAD_DIM // 2
    rows = SEG_LEN // count
    query = jnp.zeros((half, TOKENS), F32)
    fresh = [jnp.zeros((rows, TOKENS), F32) for _ in range(2)]
    for peer in range(count):
        words = [parts_ref[peer, 8 * at : 8 * at + 8, :] for at in range(7)]
        factors = level_factor((words[5] & 0xFFF) - LEVELS)
        query = query + unpack(words[0:5]) * factors[0:1]
        for kind in range(2):
            value = (top_bits(words[5 + kind]) - MIDDLE).astype(F32)
            fresh[kind] = fresh[kind] + value * factors[1 + kind : 2 + kind]
    return query, fresh


def finish_projection_kernel(count, parts_ref, query_out, fresh_out):
    rows = SEG_LEN // count
    query, fresh = add_projection(count, parts_ref)
    query = query.astype(BF16)
    for peer in range(count):
        query_out[peer] = query
    filler = jnp.zeros((FRESH - NSEG * rows, HEAD_DIM), F32)
    for kind in range(2):
        pieces = [
            fresh[kind][:, seg * SEG_LEN : (seg + 1) * SEG_LEN] for seg in range(NSEG)
        ]
        fresh_out[kind] = jnp.concatenate(pieces + [filler], axis=0).astype(BF16)


def finish_crossed_kernel(count, parts_ref, query_out, fresh_out):
    rows = SEG_LEN // count
    query, fresh = add_projection(count, parts_ref)
    query = query.astype(BF16)
    for peer in range(RING):
        query_out[peer] = query
    filler = jnp.zeros((rows, HEAD_DIM), F32)
    for kind in range(2):
        pieces = [
            fresh[kind][:, seg * SEG_LEN : (seg + 1) * SEG_LEN] for seg in range(NSEG)
        ]
        fresh_out[kind] = jnp.concatenate(pieces + [filler], axis=0).astype(BF16)


def near_mask(rows, slot_ref, seg):
    key_row = lax.broadcasted_iota(jnp.int32, (4 * rows, SEG_LEN), 0)
    token = lax.broadcasted_iota(jnp.int32, (4 * rows, SEG_LEN), 1)
    local = key_row - seg * rows
    inside = (local >= 0) & (local < rows)
    return jnp.concatenate(
        [
            jnp.where(inside & (local + slot_ref[slot] * rows <= token), 1.0, 0.0)
            for slot in range(RING)
        ],
        axis=0,
    ) > 0.5


def near_peak_kernel(rows, slot_ref, logical_ref, start_ref, query_ref, *refs):
    caches, fresh, out_ref = refs[0:RING], refs[RING : 2 * RING], refs[2 * RING]
    blocks = caches[0].shape[1] // BLOCK
    found = []
    for head in range(query_ref.shape[0]):
        query = query_ref[head]
        keys = jnp.concatenate([part[0] for part in fresh], axis=0)
        scores = jnp.dot(keys, query, preferred_element_type=F32)
        tops = []
        for seg in range(NSEG):
            lanes = slice(seg * SEG_LEN, (seg + 1) * SEG_LEN)
            masked = jnp.where(near_mask(rows, slot_ref, seg), scores[:, lanes], CLOSED)
            tops.append(jnp.max(masked.reshape(-1, 8, SEG_LEN), axis=0))
        for number in range(RING * blocks):
            block = number % blocks
            keys = caches[number // blocks][0, block * BLOCK : (block + 1) * BLOCK, :]
            scores = jnp.dot(keys, query, preferred_element_type=F32)
            top = jnp.max(scores.reshape(BLOCK // 8, 8, TOKENS), axis=0)
            for seg in range(NSEG):
                lanes = slice(seg * SEG_LEN, (seg + 1) * SEG_LEN)
                is_open = logical_ref[number] < start_ref[seg]
                tops[seg] = jnp.maximum(tops[seg], jnp.where(is_open, top[:, lanes], CLOSED))
        found.append(
            jnp.concatenate([jnp.max(top, axis=0, keepdims=True) for top in tops], axis=1)
        )
    found = jnp.concatenate(found * 4, axis=0)
    for peer in range(RING):
        out_ref[peer] = found


def near_attend_kernel(rows, slot_ref, logical_ref, start_ref, query_ref, *refs):
    caches, fresh = refs[0:RING], refs[RING : 2 * RING]
    peaks_ref, out_ref, weights = refs[2 * RING :]
    blocks = caches[0].shape[1] // BLOCK
    stored = RING * blocks * BLOCK
    half = HEAD_DIM // 2
    head = pl.program_id(0)
    query = query_ref[0]
    peak = peaks_ref[0]
    for peer in range(1, RING):
        peak = jnp.maximum(peak, peaks_ref[peer])
    peak = jnp.where(head == 0, peak[0:1], peak[1:2])
    keys = jnp.concatenate([part[0] for part in fresh], axis=0)
    scores = jnp.dot(keys, query, preferred_element_type=F32)
    masses = []
    for seg in range(NSEG):
        lanes = slice(seg * SEG_LEN, (seg + 1) * SEG_LEN)
        weight = jnp.exp2((scores[:, lanes] - peak[:, lanes]) * SCALE)
        weight = jnp.where(near_mask(rows, slot_ref, seg), weight, 0.0)
        weights[stored : stored + 4 * RING * rows, lanes] = weight.astype(BF16)
        masses.append(jnp.sum(weight.reshape(-1, 8, SEG_LEN), axis=0))
    for number in range(RING * blocks):
        block = number % blocks
        keys = caches[number // blocks][0, block * BLOCK : (block + 1) * BLOCK, :]
        scores = jnp.dot(keys, query, preferred_element_type=F32)
        for seg in range(NSEG):
            lanes = slice(seg * SEG_LEN, (seg + 1) * SEG_LEN)
            is_open = logical_ref[number] < start_ref[seg]
            offset = jnp.where(is_open, peak[:, lanes], -CLOSED)
            weight = jnp.exp2((scores[:, lanes] - offset) * SCALE)
            weights[number * BLOCK : (number + 1) * BLOCK, lanes] = weight.astype(BF16)
            masses[seg] = masses[seg] + jnp.sum(weight.reshape(BLOCK // 8, 8, SEG_LEN), axis=0)
    turned = [
        cache[1, block * BLOCK : (block + 1) * BLOCK, :] for cache in caches for block in range(blocks)
    ]
    turned.append(jnp.concatenate([part[1] for part in fresh], axis=0).T)
    sums = jnp.dot(jnp.concatenate(turned, axis=1), weights[...], preferred_element_type=F32)
    mass = jnp.concatenate([jnp.sum(part, axis=0, keepdims=True) for part in masses], axis=1)
    mass = jnp.round(mass * NEAR_MASS_UNIT).astype(jnp.int32)
    for piece in range(2):
        value, level = encode(sums[piece * half : (piece + 1) * half])
        for at, word in enumerate(pack(value) + [first_rows([level, mass])]):
            out_ref[piece, 8 * at : 8 * at + 8, :] = word


def fresh_mask(rows, index_ref, seg):
    key_row = lax.broadcasted_iota(jnp.int32, (FRESH, SEG_LEN), 0)
    token = lax.broadcasted_iota(jnp.int32, (FRESH, SEG_LEN), 1)
    local = key_row - seg * rows
    return (local >= 0) & (local < rows) & (local + index_ref[0] * rows <= token)


def peak_kernel(
    rows, index_ref, logical_ref, start_ref, query_ref, keys_ref, fresh_ref, out_ref, peaks
):
    blocks = keys_ref.shape[0] // BLOCK
    heads = query_ref.shape[0]
    step = pl.program_id(0)
    for head in range(heads):
        query = query_ref[head]
        scores = jnp.dot(fresh_ref[0], query, preferred_element_type=F32)
        tops = []
        for seg in range(NSEG):
            lanes = slice(seg * SEG_LEN, (seg + 1) * SEG_LEN)
            masked = jnp.where(fresh_mask(rows, index_ref, seg), scores[:, lanes], CLOSED)
            tops.append(jnp.max(masked.reshape(FRESH // 8, 8, SEG_LEN), axis=0))
        for block in range(blocks):
            at = slice(block * BLOCK, (block + 1) * BLOCK)
            scores = jnp.dot(keys_ref[at, :], query, preferred_element_type=F32)
            top = jnp.max(scores.reshape(BLOCK // 8, 8, TOKENS), axis=0)
            for seg in range(NSEG):
                lanes = slice(seg * SEG_LEN, (seg + 1) * SEG_LEN)
                is_open = logical_ref[block] < start_ref[seg]
                tops[seg] = jnp.maximum(tops[seg], jnp.where(is_open, top[:, lanes], CLOSED))
        peaks[step * heads + head] = jnp.concatenate(
            [jnp.max(top, axis=0, keepdims=True) for top in tops], axis=1
        )

    @pl.when(step == pl.num_programs(0) - 1)
    def _():
        found = jnp.concatenate([peaks[head] for head in range(GROUP)], axis=0)
        for peer in range(out_ref.shape[0]):
            out_ref[peer] = found


def attend_kernel(
    rows, index_ref, logical_ref, start_ref, query_ref, keys_ref, values_ref, fresh_ref, peaks_ref,
    out_ref, turned_values, peaks, weights,
):
    blocks = keys_ref.shape[0] // BLOCK
    stored = blocks * BLOCK
    half = HEAD_DIM // 2
    heads = query_ref.shape[0]
    step = pl.program_id(0)

    @pl.when(step == 0)
    def _():
        for block in range(blocks):
            at = slice(block * BLOCK, (block + 1) * BLOCK)
            turned_values[:, at] = values_ref[at, :].T
        turned_values[:, stored : stored + FRESH] = fresh_ref[1].T
        top = peaks_ref[0]
        for peer in range(1, peaks_ref.shape[0]):
            top = jnp.maximum(top, peaks_ref[peer])
        for head in range(GROUP):
            peaks[head] = top[head : head + 1]

    for head in range(heads):
        query = query_ref[head]
        peak = peaks[step * heads + head]
        scores = jnp.dot(fresh_ref[0], query, preferred_element_type=F32)
        masses = []
        for seg in range(NSEG):
            lanes = slice(seg * SEG_LEN, (seg + 1) * SEG_LEN)
            weight = jnp.exp2((scores[:, lanes] - peak[:, lanes]) * SCALE)
            weight = jnp.where(fresh_mask(rows, index_ref, seg), weight, 0.0)
            weights[head, stored : stored + FRESH, lanes] = weight.astype(BF16)
            masses.append(jnp.sum(weight.reshape(FRESH // 8, 8, SEG_LEN), axis=0))
        for block in range(blocks):
            at = slice(block * BLOCK, (block + 1) * BLOCK)
            scores = jnp.dot(keys_ref[at, :], query, preferred_element_type=F32)
            for seg in range(NSEG):
                lanes = slice(seg * SEG_LEN, (seg + 1) * SEG_LEN)
                is_open = logical_ref[block] < start_ref[seg]
                offset = jnp.where(is_open, peak[:, lanes], -CLOSED)
                weight = jnp.exp2((scores[:, lanes] - offset) * SCALE)
                weights[head, at, lanes] = weight.astype(BF16)
                masses[seg] = masses[seg] + jnp.sum(
                    weight.reshape(BLOCK // 8, 8, SEG_LEN), axis=0
                )
        sums = jnp.dot(turned_values[...], weights[head], preferred_element_type=F32)
        mass = jnp.concatenate(
            [jnp.sum(part, axis=0, keepdims=True) for part in masses], axis=1
        )
        mass = jnp.round(mass * MASS_UNIT).astype(jnp.int32)
        for piece in range(2):
            value, level = encode(sums[piece * half : (piece + 1) * half])
            for at, word in enumerate(pack(value) + [first_rows([level, mass])]):
                out_ref[2 * head + piece, 8 * at : 8 * at + 8, :] = word


def combine_kernel(count, unit, parts_ref, out_ref):
    half = HEAD_DIM // 2
    mass = jnp.zeros((1, TOKENS), F32)
    sums = jnp.zeros((half, TOKENS), F32)
    for peer in range(count):
        words = [parts_ref[peer, 8 * at : 8 * at + 8, :] for at in range(6)]
        mass = mass + words[5][1:2].astype(F32) * (1.0 / unit)
        sums = sums + unpack(words[0:5]) * level_factor(words[5][0:1])
    attended = (sums / mass).astype(BF16)
    for peer in range(out_ref.shape[0]):
        out_ref[peer] = attended


def output_kernel(core_ref, attended_ref, weight_ref, keep_ref, send_ref, scratch):
    project_output(core_ref, attended_ref, weight_ref, keep_ref, send_ref, scratch)


def project_output(core_ref, attended_ref, weight_ref, keep_ref, send_ref, scratch):
    share = TOKENS // 2
    scratch[...] = lax.dot_general(
        attended_ref[...], weight_ref[...], (((0,), (0,)), ((), ())), preferred_element_type=F32
    )
    keep_ref[...] = scratch[pl.ds(core_ref[0] * share, share), :]
    send_ref[...] = scratch[pl.ds((1 - core_ref[0]) * share, share), :]


def crossed_output_kernel(core_ref, parts_ref, weight_ref, keep_ref, send_ref, scratch, attended):
    half = HEAD_DIM // 2
    for at in range(parts_ref.shape[0]):
        attended[at * half : (at + 1) * half, :] = parts_ref[at % RING * RING + at // RING]
    project_output(core_ref, attended, weight_ref, keep_ref, send_ref, scratch)


def add_kernel(keep_ref, received_ref, out_ref):
    out_ref[...] = keep_ref[...] + received_ref[...]


def add_residual(parts_ref, x_ref):
    total = parts_ref[0]
    for peer in range(1, parts_ref.shape[0]):
        total = total + parts_ref[peer]
    return (x_ref[...].astype(F32) + total).astype(BF16)


def residual_kernel(count, parts_ref, x_ref, out_ref, squares_ref):
    produced = add_residual(parts_ref, x_ref)
    out_ref[...] = produced
    rows = square_rows(produced.astype(F32))
    for peer in range(count):
        squares_ref[peer] = rows


def last_residual_kernel(parts_ref, x_ref, out_ref):
    produced = add_residual(parts_ref, x_ref)
    for peer in range(out_ref.shape[0]):
        out_ref[peer] = produced


def spread_kernel(squares_ref, x_ref, out_ref):
    tokens, width = x_ref.shape
    factor = norm_columns(squares_ref)[0:tokens]
    first = factor.astype(BF16).astype(F32)
    second = (factor - first).astype(BF16).astype(F32)
    lane = lax.broadcasted_iota(jnp.int32, factor.shape, 1)
    thirds = jnp.where(lane == 0, first, jnp.where(lane == 1, second, factor - first - second))
    for peer in range(out_ref.shape[0]):
        out_ref[peer, :, 0:width] = x_ref[...]
        out_ref[peer, :, width : width + 128] = thirds.astype(BF16)


def choose_kernel(core_ref, own0_ref, other0_ref, own1_ref, other1_ref, out_ref):
    share = TOKENS // 2
    width = out_ref.shape[1]
    first = core_ref[0] == 0
    at = pl.ds(core_ref[0] * share, share)
    out_ref[at, :] = jnp.where(first, own0_ref[:, 0:width], own1_ref[...])
    at = pl.ds((1 - core_ref[0]) * share, share)
    out_ref[at, :] = jnp.where(first, other0_ref[:, 0:width], other1_ref[...])


def exchange(value, axes):
    return lax.all_to_all(value, axes, 0, 0, tiled=True)


def swap(value):
    return lax.ppermute(value, "section", [(0, 1), (1, 0)])


def around_y(value, step):
    pairs = []
    for kv in range(RING * RING):
        z, y = divmod(kv, RING)
        pairs.append((kv, z * RING + (y + step) % RING))
    return lax.ppermute(value, "kv", pairs)


def over_z(value):
    groups = [[z * RING + y for z in range(RING)] for y in range(RING)]
    return lax.all_to_all(value, "kv", 0, 0, tiled=True, axis_index_groups=groups)


def near_holders(index):
    offsets = jnp.array([0, -1, 1, 2], jnp.int32)
    return index // RING * RING + (index % RING + offsets) % RING


def split_attention(parts, keys, values, logical, starts, index, out_proj):
    count = lax.axis_size("kv")
    rows = SEG_LEN // count
    half = HEAD_DIM // 2
    with jax.named_scope("queries"):
        query, fresh = call(
            functools.partial(finish_projection_kernel, count),
            (
                jax.ShapeDtypeStruct((count, half, TOKENS), BF16),
                jax.ShapeDtypeStruct((2, FRESH, HEAD_DIM), BF16),
            ),
            [IN_VMEM],
            (IN_VMEM, IN_VMEM),
        )(parts)
        query = exchange(query, "kv").reshape(GROUP, HEAD_DIM, TOKENS)
    stored = keys.shape[0]
    by_head = [
        IN_SMEM,
        IN_SMEM,
        IN_SMEM,
        pl.BlockSpec((HEADS_STEP, HEAD_DIM, TOKENS), lambda h: (h, 0, 0)),
        pl.BlockSpec((stored, HEAD_DIM), lambda h: (0, 0)),
    ]
    whole_values = pl.BlockSpec((stored, HEAD_DIM), lambda h: (0, 0))
    whole_fresh = pl.BlockSpec((2, FRESH, HEAD_DIM), lambda h: (0, 0, 0))
    whole_peaks = pl.BlockSpec((count, GROUP, TOKENS), lambda h: (0, 0, 0))
    with jax.named_scope("peaks"):
        peaks = call(
            functools.partial(peak_kernel, rows),
            jax.ShapeDtypeStruct((count, GROUP, TOKENS), F32),
            by_head + [whole_fresh],
            whole_peaks,
            grid=(GROUP // HEADS_STEP,),
            scratch_shapes=[pltpu.VMEM((GROUP, 1, TOKENS), F32)],
        )(index, logical, starts, query, keys, fresh)
        peaks = exchange(peaks, "kv")
    with jax.named_scope("attend"):
        sent = call(
            functools.partial(attend_kernel, rows),
            jax.ShapeDtypeStruct((count, 6 * 8, TOKENS), jnp.int32),
            by_head + [whole_values, whole_fresh, whole_peaks],
            pl.BlockSpec((2 * HEADS_STEP, 6 * 8, TOKENS), lambda h: (h, 0, 0)),
            grid=(GROUP // HEADS_STEP,),
            scratch_shapes=[
                pltpu.VMEM((HEAD_DIM, stored + FRESH), BF16),
                pltpu.VMEM((GROUP, 1, TOKENS), F32),
                pltpu.VMEM((HEADS_STEP, stored + FRESH, TOKENS), BF16),
            ],
        )(index, logical, starts, query, keys, values, fresh, peaks)
        parts = exchange(sent, "kv")
        parts, out_proj = lax.optimization_barrier((parts, out_proj))
    with jax.named_scope("combine"):
        attended = call(
            functools.partial(combine_kernel, count, MASS_UNIT),
            jax.ShapeDtypeStruct((count, half, TOKENS), BF16),
            [IN_VMEM],
            IN_VMEM,
        )(parts)
        return exchange(attended, "kv").reshape(GROUP * HEAD_DIM, TOKENS), out_proj


def near_attention(parts, caches, logical, starts, holders):
    count = lax.axis_size("kv")
    rows = SEG_LEN // count
    half = HEAD_DIM // 2
    with jax.named_scope("queries"):
        query, fresh = call(
            functools.partial(finish_crossed_kernel, count),
            (
                jax.ShapeDtypeStruct((RING, half, TOKENS), BF16),
                jax.ShapeDtypeStruct((2, 4 * rows, HEAD_DIM), BF16),
            ),
            [IN_VMEM],
            (IN_VMEM, IN_VMEM),
        )(parts)
        fresh = (fresh,) + tuple(around_y(fresh, step) for step in (1, -1, 2))
        query = over_z(query).reshape(2, HEAD_DIM, TOKENS)
    with jax.named_scope("peaks"):
        peaks = call(
            functools.partial(near_peak_kernel, rows),
            jax.ShapeDtypeStruct((RING, 8, TOKENS), F32),
            [IN_SMEM] * 3 + [IN_VMEM] * (1 + 2 * RING),
            IN_VMEM,
        )(holders, logical, starts, query, *caches, *fresh)
        peaks = over_z(peaks)
    with jax.named_scope("attend"):
        stored = RING * caches[0].shape[1]
        sent = call(
            functools.partial(near_attend_kernel, rows),
            jax.ShapeDtypeStruct((RING, 6 * 8, TOKENS), jnp.int32),
            [IN_SMEM] * 3
            + [pl.BlockSpec((1, HEAD_DIM, TOKENS), lambda h: (h, 0, 0))]
            + [IN_VMEM] * (2 * RING + 1),
            pl.BlockSpec((2, 6 * 8, TOKENS), lambda h: (h, 0, 0)),
            grid=(2,),
            scratch_shapes=[pltpu.VMEM((stored + 4 * RING * rows, TOKENS), BF16)],
        )(holders, logical, starts, query, *caches, *fresh, peaks)
        parts = over_z(sent)
    with jax.named_scope("combine"):
        attended = call(
            functools.partial(combine_kernel, RING, NEAR_MASS_UNIT),
            jax.ShapeDtypeStruct((count, half, TOKENS), BF16),
            [IN_VMEM],
            IN_VMEM,
        )(parts)
        return exchange(attended, "kv")


def layer(
    which, x, mine, gain, query_proj, kv_proj, out_proj, keys, values, logical, starts, index, core,
    squares=None,
):
    count = lax.axis_size("kv")
    peers = lax.axis_size("tp")
    rows = SEG_LEN // count
    half = HEAD_DIM // 2
    width = query_proj.shape[0]
    share = TOKENS // 2
    part = share // peers
    with jax.named_scope("project"):
        shape = jax.ShapeDtypeStruct((count, 7 * 8, TOKENS), jnp.int32)
        if which == 0:
            squares = exchange(squares, "kv")
            all_logical = squares[:, 1, 0 : logical.shape[0]].astype(jnp.int32)
            sent = call(
                functools.partial(first_project_kernel, count), shape, [IN_VMEM] * 5, IN_VMEM
            )(x, squares, gain, query_proj, kv_proj)
        else:
            sent = call(
                functools.partial(project_kernel, count),
                shape,
                [IN_SMEM] + [IN_VMEM] * 5,
                IN_VMEM,
                scratch_shapes=[pltpu.VMEM((TOKENS, width + 128), BF16)],
            )(core, x[0], x[1], gain, query_proj, kv_proj)
        if which == 0:
            sent, keys = lax.optimization_barrier((sent, keys))
        parts = exchange(sent, "kv")
    later = None
    if which == 0:
        keys, values, later = values(keys)
        attended, out_proj = split_attention(parts, keys, values, logical, starts, index, out_proj)
        kernel, scratch = output_kernel, []
    else:
        attended = near_attention(parts, keys, logical, starts, index)
        kernel, scratch = crossed_output_kernel, [pltpu.VMEM((GROUP * HEAD_DIM, TOKENS), BF16)]
    with jax.named_scope("output"):
        keep, send = call(
            kernel,
            (jax.ShapeDtypeStruct((share, width), F32),) * 2,
            [IN_SMEM] + [IN_VMEM] * 2,
            (IN_VMEM, IN_VMEM),
            scratch_shapes=[pltpu.VMEM((TOKENS, width), F32)] + scratch,
        )(core, attended, out_proj)
        half_sum = call(
            add_kernel,
            jax.ShapeDtypeStruct((share, width), F32),
            [IN_VMEM] * 2,
            IN_VMEM,
        )(keep, swap(send))
        if which == 0:
            half_sum, later = lax.optimization_barrier((half_sum, later))
            sides = (around_y(later, 1), around_y(later, -1))
        parts = exchange(half_sum.reshape(peers, part, width), "tp")
    with jax.named_scope("residual"):
        if which == LAYERS - 1:
            produced = call(
                last_residual_kernel,
                jax.ShapeDtypeStruct((peers, part, width), BF16),
                [IN_VMEM] * 2,
                IN_VMEM,
            )(parts, mine)
            mine = None
        else:
            mine, squares = call(
                functools.partial(residual_kernel, count),
                (
                    jax.ShapeDtypeStruct((part, width), BF16),
                    jax.ShapeDtypeStruct((count, 8, 128), F32),
                ),
                [IN_VMEM] * 2,
                (IN_VMEM, IN_VMEM),
            )(parts, mine)
            squares = exchange(squares, "kv")
            squares, before, after = lax.optimization_barrier((squares, sides[0][0], sides[1][1]))
            opposite = jnp.stack([around_y(before, 1), around_y(after, -1)])
            holders = near_holders(index[0])
            later = ((later,) + sides + (opposite,), all_logical[holders].reshape(-1), holders)
            produced = call(
                spread_kernel,
                jax.ShapeDtypeStruct((peers, part, width + 128), BF16),
                [IN_VMEM] * 2,
                IN_VMEM,
            )(squares, mine)
        own = exchange(produced, "tp").reshape(share, -1)
        return (own, swap(own)), mine, later


def per_device(
    segments_in, gain, query_weight, kv_weight, out_weight, kv_cache, block_logical, segment_block
):
    width = segments_in.shape[2]
    core = lax.axis_index("section")
    core_at = core.astype(jnp.int32)[None]
    index = lax.axis_index("kv").astype(jnp.int32)[None]
    per_core = GROUP * HEAD_DIM
    share = TOKENS // 2

    x = segments_in.reshape(TOKENS, width)
    count = lax.axis_size("kv")
    blocks = block_logical.shape[0]
    squares = call(
        functools.partial(squares_kernel, count),
        jax.ShapeDtypeStruct((count, 8, TOKENS), F32),
        [IN_VMEM] * 2,
        IN_VMEM,
    )(x, jnp.pad(block_logical.astype(F32), (0, TOKENS - blocks))[None])
    squares, query_weight, kv_weight, out_weight = lax.optimization_barrier(
        (squares, query_weight, kv_weight, out_weight)
    )

    def pick(which):
        at = which * per_core
        kv_at = which * HEAD_DIM
        return (
            lax.dynamic_slice_in_dim(query_weight[0], at, per_core, 1),
            lax.dynamic_slice_in_dim(kv_weight[0], kv_at, HEAD_DIM, 2).reshape(width, -1),
            lax.dynamic_slice_in_dim(out_weight[0], at, per_core, 0),
            gain,
        )

    kept = pick(core)
    received = tuple(swap(v) for v in pick(1 - core))
    part = share // lax.axis_size("tp")
    mine = lax.dynamic_slice_in_dim(x, core * share + lax.axis_index("tp") * part, part, 0)
    params = [
        [jnp.where(core == which, here, other) for here, other in zip(kept, received)]
        for which in range(LAYERS)
    ]

    def cut_cache(cache):
        def cut(which):
            return tuple(
                lax.dynamic_slice_in_dim(cache[0, :, kind], which * HEAD_DIM, HEAD_DIM, 1)
                for kind in range(2)
            )

        pairs = [(here, swap(there)) for here, there in zip(cut(core), cut(1 - core))]
        keys, values = (jnp.where(core == 0, here, other) for here, other in pairs)
        later = call(
            cache_kernel,
            jax.ShapeDtypeStruct((2,) + keys.shape, BF16),
            [IN_VMEM] * 2,
            IN_VMEM,
        )(*(jnp.where(core == 1, here, other) for here, other in pairs))
        return keys, values, later

    query_proj, kv_proj, out_proj, gain_row = params[0]
    first, mine, (caches, numbers, holders) = layer(
        0, x, mine, gain_row, query_proj, kv_proj, out_proj, kv_cache, cut_cache,
        block_logical, segment_block, index, core_at, squares,
    )
    query_proj, kv_proj, out_proj, gain_row = params[1]
    second, _, _ = layer(
        1, first, mine, gain_row, query_proj, kv_proj, out_proj, caches, None,
        numbers, segment_block, holders, core_at,
    )
    outputs = first + second
    result = call(
        choose_kernel,
        jax.ShapeDtypeStruct((TOKENS, width), BF16),
        [IN_SMEM] + [IN_VMEM] * 4,
        IN_VMEM,
    )(core_at, *outputs)
    return result.reshape(1, NSEG, SEG_LEN, width)


def solution(mesh):
    placed = (
        P(None, None, "kv"),
        P("section", "kv"),
        P("section", "kv", "tp"),
        P("section", "kv", None, "tp"),
        P("section", "tp", "kv"),
        P("section", "kv", None, "tp"),
        P("kv"),
        P(),
    )
    return jax.shard_map(
        per_device,
        mesh=mesh,
        in_specs=placed,
        out_specs=P("section", None, None, "kv"),
        check_vma=False,
    )
```

```python
import functools
import math

import jax
import jax.numpy as jnp
from jax import lax
from jax.experimental import pallas as pl
from jax.experimental.pallas import tpu as pltpu
from jax.sharding import PartitionSpec as P

D = 8192
HEAD_DIM = 128
BLOCK = 128
NSEG = 3
SEG_LEN = 128
TOKENS = NSEG * SEG_LEN
GROUP = 8
LAYERS = 2
EPSILON = 1e-05
CLOSED = -1e30
FRESH = 128
RANGE = 520000.0
MIDDLE = 524288
LEVELS = 2048
MASS_UNIT = 262144.0
NEAR_MASS_UNIT = 65536.0
HEADS_STEP = 4
SCALE = math.log2(math.e) / math.sqrt(HEAD_DIM)
F32 = jnp.float32
BF16 = jnp.bfloat16
VMEM_BYTES = 48 * 1024 * 1024


def call(kernel, out_shape, in_specs, out_specs, **rest):
    return pl.pallas_call(
        kernel,
        out_shape=out_shape,
        in_specs=in_specs,
        out_specs=out_specs,
        compiler_params=pltpu.CompilerParams(vmem_limit_bytes=VMEM_BYTES),
        **rest,
    )


IN_VMEM = pl.BlockSpec(memory_space=pltpu.VMEM)
IN_SMEM = pl.BlockSpec(memory_space=pltpu.SMEM)


RING = 4


def encode(block):
    top = jnp.maximum(jnp.max(jnp.abs(block), axis=0, keepdims=True), 1e-30)
    level = jnp.ceil(jnp.log2(top) * 16.0)
    value = jnp.round(block * (jnp.exp2(level * (-1.0 / 16.0)) * RANGE))
    return value.astype(jnp.int32) + MIDDLE, level.astype(jnp.int32)


def level_factor(level):
    return jnp.exp2(level.astype(F32) * (1.0 / 16.0)) * (1.0 / RANGE)


def pack(value):
    part = [value[8 * at : 8 * at + 8] for at in range(8)]
    lows = [
        part[5] & 0xFFF,
        (part[5] >> 12) | ((part[6] & 0xF) << 8),
        (part[6] >> 4) & 0xFFF,
        (part[6] >> 16) | ((part[7] & 0xFF) << 4),
        part[7] >> 8,
    ]
    return [(part[at] << 12) | lows[at] for at in range(5)]


def top_bits(word):
    return lax.shift_right_logical(word, jnp.int32(12))


def unpack(words):
    lows = [word & 0xFFF for word in words]
    part = [top_bits(word) for word in words]
    part.append(lows[0] | ((lows[1] & 0xFF) << 12))
    part.append((lows[1] >> 8) | (lows[2] << 4) | ((lows[3] & 0xF) << 16))
    part.append((lows[3] >> 4) | (lows[4] << 8))
    return (jnp.concatenate(part, axis=0) - MIDDLE).astype(F32)


def first_rows(rows, count=8):
    place = lax.broadcasted_iota(jnp.int32, (count, rows[0].shape[1]), 0)
    filled = jnp.zeros_like(place)
    for number, row in enumerate(rows):
        filled = jnp.where(place == number, row, filled)
    return filled


def square_rows(x):
    squares = jnp.sum(x * x, axis=1, keepdims=True)
    squares = jnp.broadcast_to(squares, (x.shape[0], 128))
    missing = -x.shape[0] % 128
    if missing:
        squares = jnp.concatenate([squares, jnp.zeros((missing, 128), F32)], axis=0)
    return squares.T[0:8]


def norm_columns(parts_ref):
    total = parts_ref[0]
    for peer in range(1, parts_ref.shape[0]):
        total = total + parts_ref[peer]
    factor = lax.rsqrt(total[0:1] / D + EPSILON)
    return jnp.broadcast_to(factor, (128, factor.shape[1])).T


def squares_kernel(count, x_ref, logical_ref, out_ref):
    rows = square_rows(x_ref[...].astype(F32))
    row = lax.broadcasted_iota(jnp.int32, rows.shape, 0)
    rows = jnp.where(row == 0, rows, logical_ref[...])
    for peer in range(count):
        out_ref[peer] = rows


def cache_kernel(keys_ref, values_ref, out_ref):
    out_ref[0] = keys_ref[...]
    for block in range(values_ref.shape[0] // BLOCK):
        at = slice(block * BLOCK, (block + 1) * BLOCK)
        out_ref[1, at, :] = values_ref[at, :].T


def first_project_kernel(count, x_ref, squares_ref, gain_ref, query_ref, kv_ref, out_ref):
    factor = norm_columns(squares_ref)[:, 0:1]
    normed = (x_ref[...].astype(F32) * factor * gain_ref[...]).astype(BF16)
    project(count, normed, query_ref, kv_ref, out_ref)


def project_kernel(count, core_ref, own_ref, other_ref, gain_ref, query_ref, kv_ref, out_ref, x_ref):
    share = TOKENS // 2
    width = gain_ref.shape[1]
    x_ref[pl.ds(core_ref[0] * share, share), :] = own_ref[...]
    x_ref[pl.ds((1 - core_ref[0]) * share, share), :] = other_ref[...]
    thirds = x_ref[:, width : width + 128].astype(F32)
    factor = thirds[:, 0:1] + thirds[:, 1:2] + thirds[:, 2:3]
    normed = (x_ref[:, 0:width].astype(F32) * factor * gain_ref[...]).astype(BF16)
    project(count, normed, query_ref, kv_ref, out_ref, True)


def project(count, scaled, query_ref, kv_ref, out_ref, crossed=False):
    half = HEAD_DIM // 2
    columns = query_ref.shape[1]
    rows = SEG_LEN // count
    fresh = jnp.dot(scaled, kv_ref[...], preferred_element_type=F32)
    for start in range(0, columns, 256):
        part = jnp.dot(scaled, query_ref[:, start : start + 256], preferred_element_type=F32)
        turned = part.T
        for piece in range(256 // half):
            at = start // half + piece
            peer = at % RING * RING + at // RING if crossed else at
            block = turned[piece * half : (piece + 1) * half]
            query, query_level = encode(block)
            words = pack(query)
            kinds = []
            for kind in range(2):
                lanes = slice(kind * HEAD_DIM, (kind + 1) * HEAD_DIM)
                block = jnp.concatenate(
                    [
                        fresh[seg * SEG_LEN + peer * rows : seg * SEG_LEN + (peer + 1) * rows, lanes]
                        for seg in range(NSEG)
                    ],
                    axis=1,
                )
                kinds.append(encode(block))
            levels = first_rows([query_level, kinds[0][1], kinds[1][1]]) + LEVELS
            words.append((kinds[0][0] << 12) | levels)
            words.append(kinds[1][0] << 12)
            for at, word in enumerate(words):
                out_ref[peer, 8 * at : 8 * at + 8, :] = word


def add_projection(count, parts_ref):
    half = HEAD_DIM // 2
    rows = SEG_LEN // count
    query = jnp.zeros((half, TOKENS), F32)
    fresh = [jnp.zeros((rows, TOKENS), F32) for _ in range(2)]
    for peer in range(count):
        words = [parts_ref[peer, 8 * at : 8 * at + 8, :] for at in range(7)]
        factors = level_factor((words[5] & 0xFFF) - LEVELS)
        query = query + unpack(words[0:5]) * factors[0:1]
        for kind in range(2):
            value = (top_bits(words[5 + kind]) - MIDDLE).astype(F32)
            fresh[kind] = fresh[kind] + value * factors[1 + kind : 2 + kind]
    return query, fresh


def finish_projection_kernel(count, parts_ref, query_out, fresh_out):
    rows = SEG_LEN // count
    query, fresh = add_projection(count, parts_ref)
    query = query.astype(BF16)
    for peer in range(count):
        query_out[peer] = query
    filler = jnp.zeros((FRESH - NSEG * rows, HEAD_DIM), F32)
    for kind in range(2):
        pieces = [
            fresh[kind][:, seg * SEG_LEN : (seg + 1) * SEG_LEN] for seg in range(NSEG)
        ]
        fresh_out[kind] = jnp.concatenate(pieces + [filler], axis=0).astype(BF16)


def finish_crossed_kernel(count, parts_ref, query_out, fresh_out):
    rows = SEG_LEN // count
    query, fresh = add_projection(count, parts_ref)
    query = query.astype(BF16)
    for peer in range(RING):
        query_out[peer] = query
    filler = jnp.zeros((rows, HEAD_DIM), F32)
    for kind in range(2):
        pieces = [
            fresh[kind][:, seg * SEG_LEN : (seg + 1) * SEG_LEN] for seg in range(NSEG)
        ]
        fresh_out[kind] = jnp.concatenate(pieces + [filler], axis=0).astype(BF16)


def near_mask(rows, slot_ref, seg):
    key_row = lax.broadcasted_iota(jnp.int32, (4 * rows, SEG_LEN), 0)
    token = lax.broadcasted_iota(jnp.int32, (4 * rows, SEG_LEN), 1)
    local = key_row - seg * rows
    inside = (local >= 0) & (local < rows)
    return jnp.concatenate(
        [
            jnp.where(inside & (local + slot_ref[slot] * rows <= token), 1.0, 0.0)
            for slot in range(RING)
        ],
        axis=0,
    ) > 0.5


def near_peak_kernel(rows, slot_ref, logical_ref, start_ref, query_ref, *refs):
    caches, fresh, out_ref = refs[0:RING], refs[RING : 2 * RING], refs[2 * RING]
    blocks = caches[0].shape[1] // BLOCK
    found = []
    for head in range(query_ref.shape[0]):
        query = query_ref[head]
        keys = jnp.concatenate([part[0] for part in fresh], axis=0)
        scores = jnp.dot(keys, query, preferred_element_type=F32)
        tops = []
        for seg in range(NSEG):
            lanes = slice(seg * SEG_LEN, (seg + 1) * SEG_LEN)
            masked = jnp.where(near_mask(rows, slot_ref, seg), scores[:, lanes], CLOSED)
            tops.append(jnp.max(masked.reshape(-1, 8, SEG_LEN), axis=0))
        for number in range(RING * blocks):
            block = number % blocks
            keys = caches[number // blocks][0, block * BLOCK : (block + 1) * BLOCK, :]
            scores = jnp.dot(keys, query, preferred_element_type=F32)
            top = jnp.max(scores.reshape(BLOCK // 8, 8, TOKENS), axis=0)
            for seg in range(NSEG):
                lanes = slice(seg * SEG_LEN, (seg + 1) * SEG_LEN)
                is_open = logical_ref[number] < start_ref[seg]
                tops[seg] = jnp.maximum(tops[seg], jnp.where(is_open, top[:, lanes], CLOSED))
        found.append(
            jnp.concatenate([jnp.max(top, axis=0, keepdims=True) for top in tops], axis=1)
        )
    found = jnp.concatenate(found * 4, axis=0)
    for peer in range(RING):
        out_ref[peer] = found


def near_attend_kernel(rows, slot_ref, logical_ref, start_ref, query_ref, *refs):
    caches, fresh = refs[0:RING], refs[RING : 2 * RING]
    peaks_ref, out_ref, weights = refs[2 * RING :]
    blocks = caches[0].shape[1] // BLOCK
    stored = RING * blocks * BLOCK
    half = HEAD_DIM // 2
    head = pl.program_id(0)
    query = query_ref[0]
    peak = peaks_ref[0]
    for peer in range(1, RING):
        peak = jnp.maximum(peak, peaks_ref[peer])
    peak = jnp.where(head == 0, peak[0:1], peak[1:2])
    keys = jnp.concatenate([part[0] for part in fresh], axis=0)
    scores = jnp.dot(keys, query, preferred_element_type=F32)
    masses = []
    for seg in range(NSEG):
        lanes = slice(seg * SEG_LEN, (seg + 1) * SEG_LEN)
        weight = jnp.exp2((scores[:, lanes] - peak[:, lanes]) * SCALE)
        weight = jnp.where(near_mask(rows, slot_ref, seg), weight, 0.0)
        weights[stored : stored + 4 * RING * rows, lanes] = weight.astype(BF16)
        masses.append(jnp.sum(weight.reshape(-1, 8, SEG_LEN), axis=0))
    for number in range(RING * blocks):
        block = number % blocks
        keys = caches[number // blocks][0, block * BLOCK : (block + 1) * BLOCK, :]
        scores = jnp.dot(keys, query, preferred_element_type=F32)
        for seg in range(NSEG):
            lanes = slice(seg * SEG_LEN, (seg + 1) * SEG_LEN)
            is_open = logical_ref[number] < start_ref[seg]
            offset = jnp.where(is_open, peak[:, lanes], -CLOSED)
            weight = jnp.exp2((scores[:, lanes] - offset) * SCALE)
            weights[number * BLOCK : (number + 1) * BLOCK, lanes] = weight.astype(BF16)
            masses[seg] = masses[seg] + jnp.sum(weight.reshape(BLOCK // 8, 8, SEG_LEN), axis=0)
    turned = [
        cache[1, block * BLOCK : (block + 1) * BLOCK, :] for cache in caches for block in range(blocks)
    ]
    turned.append(jnp.concatenate([part[1] for part in fresh], axis=0).T)
    sums = jnp.dot(jnp.concatenate(turned, axis=1), weights[...], preferred_element_type=F32)
    mass = jnp.concatenate([jnp.sum(part, axis=0, keepdims=True) for part in masses], axis=1)
    mass = jnp.round(mass * NEAR_MASS_UNIT).astype(jnp.int32)
    for piece in range(2):
        value, level = encode(sums[piece * half : (piece + 1) * half])
        for at, word in enumerate(pack(value) + [first_rows([level, mass])]):
            out_ref[piece, 8 * at : 8 * at + 8, :] = word


def fresh_mask(rows, index_ref, seg):
    key_row = lax.broadcasted_iota(jnp.int32, (FRESH, SEG_LEN), 0)
    token = lax.broadcasted_iota(jnp.int32, (FRESH, SEG_LEN), 1)
    local = key_row - seg * rows
    return (local >= 0) & (local < rows) & (local + index_ref[0] * rows <= token)


def peak_kernel(
    rows, index_ref, logical_ref, start_ref, query_ref, cache_ref, fresh_ref, out_ref, peaks
):
    blocks = cache_ref.shape[1] // BLOCK
    heads = query_ref.shape[0]
    step = pl.program_id(0)
    for head in range(heads):
        query = query_ref[head]
        scores = jnp.dot(fresh_ref[0], query, preferred_element_type=F32)
        tops = []
        for seg in range(NSEG):
            lanes = slice(seg * SEG_LEN, (seg + 1) * SEG_LEN)
            masked = jnp.where(fresh_mask(rows, index_ref, seg), scores[:, lanes], CLOSED)
            tops.append(jnp.max(masked.reshape(FRESH // 8, 8, SEG_LEN), axis=0))
        for block in range(blocks):
            at = slice(block * BLOCK, (block + 1) * BLOCK)
            scores = jnp.dot(cache_ref[0, at, :], query, preferred_element_type=F32)
            top = jnp.max(scores.reshape(BLOCK // 8, 8, TOKENS), axis=0)
            for seg in range(NSEG):
                lanes = slice(seg * SEG_LEN, (seg + 1) * SEG_LEN)
                is_open = logical_ref[block] < start_ref[seg]
                tops[seg] = jnp.maximum(tops[seg], jnp.where(is_open, top[:, lanes], CLOSED))
        peaks[step * heads + head] = jnp.concatenate(
            [jnp.max(top, axis=0, keepdims=True) for top in tops], axis=1
        )

    @pl.when(step == pl.num_programs(0) - 1)
    def _():
        found = jnp.concatenate([peaks[head] for head in range(GROUP)], axis=0)
        for peer in range(out_ref.shape[0]):
            out_ref[peer] = found


def attend_kernel(
    rows, index_ref, logical_ref, start_ref, query_ref, cache_ref, fresh_ref, peaks_ref,
    out_ref, peaks, weights,
):
    blocks = cache_ref.shape[1] // BLOCK
    stored = blocks * BLOCK
    half = HEAD_DIM // 2
    heads = query_ref.shape[0]
    step = pl.program_id(0)

    @pl.when(step == 0)
    def _():
        top = peaks_ref[0]
        for peer in range(1, peaks_ref.shape[0]):
            top = jnp.maximum(top, peaks_ref[peer])
        for head in range(GROUP):
            peaks[head] = top[head : head + 1]

    turned = [cache_ref[1, block * BLOCK : (block + 1) * BLOCK, :] for block in range(blocks)]
    turned = jnp.concatenate(turned + [fresh_ref[1].T], axis=1)
    for head in range(heads):
        query = query_ref[head]
        peak = peaks[step * heads + head]
        scores = jnp.dot(fresh_ref[0], query, preferred_element_type=F32)
        masses = []
        for seg in range(NSEG):
            lanes = slice(seg * SEG_LEN, (seg + 1) * SEG_LEN)
            weight = jnp.exp2((scores[:, lanes] - peak[:, lanes]) * SCALE)
            weight = jnp.where(fresh_mask(rows, index_ref, seg), weight, 0.0)
            weights[head, stored : stored + FRESH, lanes] = weight.astype(BF16)
            masses.append(jnp.sum(weight.reshape(FRESH // 8, 8, SEG_LEN), axis=0))
        for block in range(blocks):
            at = slice(block * BLOCK, (block + 1) * BLOCK)
            scores = jnp.dot(cache_ref[0, at, :], query, preferred_element_type=F32)
            for seg in range(NSEG):
                lanes = slice(seg * SEG_LEN, (seg + 1) * SEG_LEN)
                is_open = logical_ref[block] < start_ref[seg]
                offset = jnp.where(is_open, peak[:, lanes], -CLOSED)
                weight = jnp.exp2((scores[:, lanes] - offset) * SCALE)
                weights[head, at, lanes] = weight.astype(BF16)
                masses[seg] = masses[seg] + jnp.sum(
                    weight.reshape(BLOCK // 8, 8, SEG_LEN), axis=0
                )
        sums = jnp.dot(turned, weights[head], preferred_element_type=F32)
        mass = jnp.concatenate(
            [jnp.sum(part, axis=0, keepdims=True) for part in masses], axis=1
        )
        mass = jnp.round(mass * MASS_UNIT).astype(jnp.int32)
        for piece in range(2):
            value, level = encode(sums[piece * half : (piece + 1) * half])
            for at, word in enumerate(pack(value) + [first_rows([level, mass])]):
                out_ref[2 * head + piece, 8 * at : 8 * at + 8, :] = word


def combine_kernel(count, unit, parts_ref, out_ref):
    half = HEAD_DIM // 2
    mass = jnp.zeros((1, TOKENS), F32)
    sums = jnp.zeros((half, TOKENS), F32)
    for peer in range(count):
        words = [parts_ref[peer, 8 * at : 8 * at + 8, :] for at in range(6)]
        mass = mass + words[5][1:2].astype(F32) * (1.0 / unit)
        sums = sums + unpack(words[0:5]) * level_factor(words[5][0:1])
    attended = (sums / mass).astype(BF16)
    for peer in range(out_ref.shape[0]):
        out_ref[peer] = attended


def output_kernel(core_ref, attended_ref, weight_ref, keep_ref, send_ref, scratch):
    project_output(core_ref, attended_ref, weight_ref, keep_ref, send_ref, scratch)


def project_output(core_ref, attended_ref, weight_ref, keep_ref, send_ref, scratch):
    share = TOKENS // 2
    scratch[...] = lax.dot_general(
        attended_ref[...], weight_ref[...], (((0,), (0,)), ((), ())), preferred_element_type=F32
    )
    keep_ref[...] = scratch[pl.ds(core_ref[0] * share, share), :]
    send_ref[...] = scratch[pl.ds((1 - core_ref[0]) * share, share), :]


def crossed_output_kernel(core_ref, parts_ref, weight_ref, keep_ref, send_ref, scratch, attended):
    half = HEAD_DIM // 2
    for at in range(parts_ref.shape[0]):
        attended[at * half : (at + 1) * half, :] = parts_ref[at % RING * RING + at // RING]
    project_output(core_ref, attended, weight_ref, keep_ref, send_ref, scratch)


def add_kernel(keep_ref, received_ref, out_ref):
    out_ref[...] = keep_ref[...] + received_ref[...]


def add_residual(parts_ref, x_ref):
    total = parts_ref[0]
    for peer in range(1, parts_ref.shape[0]):
        total = total + parts_ref[peer]
    return (x_ref[...].astype(F32) + total).astype(BF16)


def residual_kernel(count, parts_ref, x_ref, out_ref, squares_ref):
    produced = add_residual(parts_ref, x_ref)
    out_ref[...] = produced
    rows = square_rows(produced.astype(F32))
    for peer in range(count):
        squares_ref[peer] = rows


def last_residual_kernel(parts_ref, x_ref, out_ref):
    produced = add_residual(parts_ref, x_ref)
    for peer in range(out_ref.shape[0]):
        out_ref[peer] = produced


def spread_kernel(squares_ref, x_ref, out_ref):
    tokens, width = x_ref.shape
    factor = norm_columns(squares_ref)[0:tokens]
    first = factor.astype(BF16).astype(F32)
    second = (factor - first).astype(BF16).astype(F32)
    lane = lax.broadcasted_iota(jnp.int32, factor.shape, 1)
    thirds = jnp.where(lane == 0, first, jnp.where(lane == 1, second, factor - first - second))
    for peer in range(out_ref.shape[0]):
        out_ref[peer, :, 0:width] = x_ref[...]
        out_ref[peer, :, width : width + 128] = thirds.astype(BF16)


def choose_kernel(core_ref, own0_ref, other0_ref, own1_ref, other1_ref, out_ref):
    share = TOKENS // 2
    width = out_ref.shape[1]
    first = core_ref[0] == 0
    at = pl.ds(core_ref[0] * share, share)
    out_ref[at, :] = jnp.where(first, own0_ref[:, 0:width], own1_ref[...])
    at = pl.ds((1 - core_ref[0]) * share, share)
    out_ref[at, :] = jnp.where(first, other0_ref[:, 0:width], other1_ref[...])


def exchange(value, axes):
    return lax.all_to_all(value, axes, 0, 0, tiled=True)


def swap(value):
    return lax.ppermute(value, "section", [(0, 1), (1, 0)])


def around_y(value, step):
    pairs = []
    for kv in range(RING * RING):
        z, y = divmod(kv, RING)
        pairs.append((kv, z * RING + (y + step) % RING))
    return lax.ppermute(value, "kv", pairs)


def over_z(value):
    groups = [[z * RING + y for z in range(RING)] for y in range(RING)]
    return lax.all_to_all(value, "kv", 0, 0, tiled=True, axis_index_groups=groups)


def near_holders(index):
    offsets = jnp.array([0, -1, 1, 2], jnp.int32)
    return index // RING * RING + (index % RING + offsets) % RING


def split_attention(parts, cache, logical, starts, index, out_proj):
    count = lax.axis_size("kv")
    rows = SEG_LEN // count
    half = HEAD_DIM // 2
    with jax.named_scope("queries"):
        query, fresh = call(
            functools.partial(finish_projection_kernel, count),
            (
                jax.ShapeDtypeStruct((count, half, TOKENS), BF16),
                jax.ShapeDtypeStruct((2, FRESH, HEAD_DIM), BF16),
            ),
            [IN_VMEM],
            (IN_VMEM, IN_VMEM),
        )(parts)
        query = exchange(query, "kv").reshape(GROUP, HEAD_DIM, TOKENS)
    stored = cache.shape[1]
    by_head = [
        IN_SMEM,
        IN_SMEM,
        IN_SMEM,
        pl.BlockSpec((HEADS_STEP, HEAD_DIM, TOKENS), lambda h: (h, 0, 0)),
        pl.BlockSpec((2, stored, HEAD_DIM), lambda h: (0, 0, 0)),
    ]
    whole_fresh = pl.BlockSpec((2, FRESH, HEAD_DIM), lambda h: (0, 0, 0))
    whole_peaks = pl.BlockSpec((count, GROUP, TOKENS), lambda h: (0, 0, 0))
    with jax.named_scope("peaks"):
        peaks = call(
            functools.partial(peak_kernel, rows),
            jax.ShapeDtypeStruct((count, GROUP, TOKENS), F32),
            by_head + [whole_fresh],
            whole_peaks,
            grid=(GROUP // HEADS_STEP,),
            scratch_shapes=[pltpu.VMEM((GROUP, 1, TOKENS), F32)],
        )(index, logical, starts, query, cache, fresh)
        peaks = exchange(peaks, "kv")
    with jax.named_scope("attend"):
        sent = call(
            functools.partial(attend_kernel, rows),
            jax.ShapeDtypeStruct((count, 6 * 8, TOKENS), jnp.int32),
            by_head + [whole_fresh, whole_peaks],
            pl.BlockSpec((2 * HEADS_STEP, 6 * 8, TOKENS), lambda h: (h, 0, 0)),
            grid=(GROUP // HEADS_STEP,),
            scratch_shapes=[
                pltpu.VMEM((GROUP, 1, TOKENS), F32),
                pltpu.VMEM((HEADS_STEP, stored + FRESH, TOKENS), BF16),
            ],
        )(index, logical, starts, query, cache, fresh, peaks)
        parts = exchange(sent, "kv")
        parts, out_proj = lax.optimization_barrier((parts, out_proj))
    with jax.named_scope("combine"):
        attended = call(
            functools.partial(combine_kernel, count, MASS_UNIT),
            jax.ShapeDtypeStruct((count, half, TOKENS), BF16),
            [IN_VMEM],
            IN_VMEM,
        )(parts)
        return exchange(attended, "kv").reshape(GROUP * HEAD_DIM, TOKENS), out_proj


def near_attention(parts, caches, logical, starts, holders):
    count = lax.axis_size("kv")
    rows = SEG_LEN // count
    half = HEAD_DIM // 2
    with jax.named_scope("queries"):
        query, fresh = call(
            functools.partial(finish_crossed_kernel, count),
            (
                jax.ShapeDtypeStruct((RING, half, TOKENS), BF16),
                jax.ShapeDtypeStruct((2, 4 * rows, HEAD_DIM), BF16),
            ),
            [IN_VMEM],
            (IN_VMEM, IN_VMEM),
        )(parts)
        fresh = (fresh,) + tuple(around_y(fresh, step) for step in (1, -1, 2))
        query = over_z(query).reshape(2, HEAD_DIM, TOKENS)
    with jax.named_scope("peaks"):
        peaks = call(
            functools.partial(near_peak_kernel, rows),
            jax.ShapeDtypeStruct((RING, 8, TOKENS), F32),
            [IN_SMEM] * 3 + [IN_VMEM] * (1 + 2 * RING),
            IN_VMEM,
        )(holders, logical, starts, query, *caches, *fresh)
        peaks = over_z(peaks)
    with jax.named_scope("attend"):
        stored = RING * caches[0].shape[1]
        sent = call(
            functools.partial(near_attend_kernel, rows),
            jax.ShapeDtypeStruct((RING, 6 * 8, TOKENS), jnp.int32),
            [IN_SMEM] * 3
            + [pl.BlockSpec((1, HEAD_DIM, TOKENS), lambda h: (h, 0, 0))]
            + [IN_VMEM] * (2 * RING + 1),
            pl.BlockSpec((2, 6 * 8, TOKENS), lambda h: (h, 0, 0)),
            grid=(2,),
            scratch_shapes=[pltpu.VMEM((stored + 4 * RING * rows, TOKENS), BF16)],
        )(holders, logical, starts, query, *caches, *fresh, peaks)
        parts = over_z(sent)
    with jax.named_scope("combine"):
        attended = call(
            functools.partial(combine_kernel, RING, NEAR_MASS_UNIT),
            jax.ShapeDtypeStruct((count, half, TOKENS), BF16),
            [IN_VMEM],
            IN_VMEM,
        )(parts)
        return exchange(attended, "kv")


def layer(
    which, x, mine, gain, query_proj, kv_proj, out_proj, keys, values, logical, starts, index, core,
    squares=None,
):
    count = lax.axis_size("kv")
    peers = lax.axis_size("tp")
    rows = SEG_LEN // count
    half = HEAD_DIM // 2
    width = query_proj.shape[0]
    share = TOKENS // 2
    part = share // peers
    with jax.named_scope("project"):
        shape = jax.ShapeDtypeStruct((count, 7 * 8, TOKENS), jnp.int32)
        if which == 0:
            squares = exchange(squares, "kv")
            all_logical = squares[:, 1, 0 : logical.shape[0]].astype(jnp.int32)
            sent = call(
                functools.partial(first_project_kernel, count), shape, [IN_VMEM] * 5, IN_VMEM
            )(x, squares, gain, query_proj, kv_proj)
        else:
            sent = call(
                functools.partial(project_kernel, count),
                shape,
                [IN_SMEM] + [IN_VMEM] * 5,
                IN_VMEM,
                scratch_shapes=[pltpu.VMEM((TOKENS, width + 128), BF16)],
            )(core, x[0], x[1], gain, query_proj, kv_proj)
        if which == 0:
            sent, keys = lax.optimization_barrier((sent, keys))
        parts = exchange(sent, "kv")
    later = None
    if which == 0:
        now, later = values(keys)
        attended, out_proj = split_attention(parts, now, logical, starts, index, out_proj)
        kernel, scratch = output_kernel, []
    else:
        attended = near_attention(parts, keys, logical, starts, index)
        kernel, scratch = crossed_output_kernel, [pltpu.VMEM((GROUP * HEAD_DIM, TOKENS), BF16)]
    with jax.named_scope("output"):
        keep, send = call(
            kernel,
            (jax.ShapeDtypeStruct((share, width), F32),) * 2,
            [IN_SMEM] + [IN_VMEM] * 2,
            (IN_VMEM, IN_VMEM),
            scratch_shapes=[pltpu.VMEM((TOKENS, width), F32)] + scratch,
        )(core, attended, out_proj)
        half_sum = call(
            add_kernel,
            jax.ShapeDtypeStruct((share, width), F32),
            [IN_VMEM] * 2,
            IN_VMEM,
        )(keep, swap(send))
        if which == 0:
            half_sum, later = lax.optimization_barrier((half_sum, later))
            sides = (around_y(later, 1), around_y(later, -1))
        parts = exchange(half_sum.reshape(peers, part, width), "tp")
    with jax.named_scope("residual"):
        if which == LAYERS - 1:
            produced = call(
                last_residual_kernel,
                jax.ShapeDtypeStruct((peers, part, width), BF16),
                [IN_VMEM] * 2,
                IN_VMEM,
            )(parts, mine)
            mine = None
        else:
            mine, squares = call(
                functools.partial(residual_kernel, count),
                (
                    jax.ShapeDtypeStruct((part, width), BF16),
                    jax.ShapeDtypeStruct((count, 8, 128), F32),
                ),
                [IN_VMEM] * 2,
                (IN_VMEM, IN_VMEM),
            )(parts, mine)
            squares = exchange(squares, "kv")
            squares, before, after = lax.optimization_barrier((squares, sides[0][0], sides[1][1]))
            opposite = jnp.stack([around_y(before, 1), around_y(after, -1)])
            holders = near_holders(index[0])
            produced = call(
                spread_kernel,
                jax.ShapeDtypeStruct((peers, part, width + 128), BF16),
                [IN_VMEM] * 2,
                IN_VMEM,
            )(squares, mine)
        own = exchange(produced, "tp").reshape(share, -1)
        if which == 0:
            own, opposite = lax.optimization_barrier((own, opposite))
            later = ((later,) + sides + (opposite,), all_logical[holders].reshape(-1), holders)
        return (own, swap(own)), mine, later


def per_device(
    segments_in, gain, query_weight, kv_weight, out_weight, kv_cache, block_logical, segment_block
):
    width = segments_in.shape[2]
    core = lax.axis_index("section")
    core_at = core.astype(jnp.int32)[None]
    index = lax.axis_index("kv").astype(jnp.int32)[None]
    per_core = GROUP * HEAD_DIM
    share = TOKENS // 2

    x = segments_in.reshape(TOKENS, width)
    count = lax.axis_size("kv")
    blocks = block_logical.shape[0]
    squares = call(
        functools.partial(squares_kernel, count),
        jax.ShapeDtypeStruct((count, 8, TOKENS), F32),
        [IN_VMEM] * 2,
        IN_VMEM,
    )(x, jnp.pad(block_logical.astype(F32), (0, TOKENS - blocks))[None])
    squares, query_weight, kv_weight, out_weight = lax.optimization_barrier(
        (squares, query_weight, kv_weight, out_weight)
    )

    def pick(which):
        at = which * per_core
        kv_at = which * HEAD_DIM
        return (
            lax.dynamic_slice_in_dim(query_weight[0], at, per_core, 1),
            lax.dynamic_slice_in_dim(kv_weight[0], kv_at, HEAD_DIM, 2).reshape(width, -1),
            lax.dynamic_slice_in_dim(out_weight[0], at, per_core, 0),
            gain,
        )

    kept = pick(core)
    received = tuple(swap(v) for v in pick(1 - core))
    part = share // lax.axis_size("tp")
    mine = lax.dynamic_slice_in_dim(x, core * share + lax.axis_index("tp") * part, part, 0)
    params = [
        [jnp.where(core == which, here, other) for here, other in zip(kept, received)]
        for which in range(LAYERS)
    ]

    def cut_cache(cache):
        def cut(which):
            return tuple(
                lax.dynamic_slice_in_dim(cache[0, :, kind], which * HEAD_DIM, HEAD_DIM, 1)
                for kind in range(2)
            )

        pairs = [(here, swap(there)) for here, there in zip(cut(core), cut(1 - core))]
        return tuple(
            call(
                cache_kernel,
                jax.ShapeDtypeStruct((2,) + pairs[0][0].shape, BF16),
                [IN_VMEM] * 2,
                IN_VMEM,
            )(*(jnp.where(core == which, here, other) for here, other in pairs))
            for which in range(LAYERS)
        )

    query_proj, kv_proj, out_proj, gain_row = params[0]
    first, mine, (caches, numbers, holders) = layer(
        0, x, mine, gain_row, query_proj, kv_proj, out_proj, kv_cache, cut_cache,
        block_logical, segment_block, index, core_at, squares,
    )
    query_proj, kv_proj, out_proj, gain_row = params[1]
    second, _, _ = layer(
        1, first, mine, gain_row, query_proj, kv_proj, out_proj, caches, None,
        numbers, segment_block, holders, core_at,
    )
    outputs = first + second
    result = call(
        choose_kernel,
        jax.ShapeDtypeStruct((TOKENS, width), BF16),
        [IN_SMEM] + [IN_VMEM] * 4,
        IN_VMEM,
    )(core_at, *outputs)
    return result.reshape(1, NSEG, SEG_LEN, width)


def solution(mesh):
    placed = (
        P(None, None, "kv"),
        P("section", "kv"),
        P("section", "kv", "tp"),
        P("section", "kv", None, "tp"),
        P("section", "tp", "kv"),
        P("section", "kv", None, "tp"),
        P("kv"),
        P(),
    )
    return jax.shard_map(
        per_device,
        mesh=mesh,
        in_specs=placed,
        out_specs=P("section", None, None, "kv"),
        check_vma=False,
    )
```

```python
import functools
import math

import jax
import jax.numpy as jnp
from jax import lax
from jax.experimental import pallas as pl
from jax.experimental.pallas import tpu as pltpu
from jax.sharding import PartitionSpec as P

D = 8192
HEAD_DIM = 128
BLOCK = 128
NSEG = 3
SEG_LEN = 128
TOKENS = NSEG * SEG_LEN
GROUP = 8
LAYERS = 2
EPSILON = 1e-05
CLOSED = -1e30
FRESH = 128
RANGE = 520000.0
MIDDLE = 524288
LEVELS = 2048
MASS_UNIT = 262144.0
NEAR_MASS_UNIT = 65536.0
HEADS_STEP = 4
SCALE = math.log2(math.e) / math.sqrt(HEAD_DIM)
F32 = jnp.float32
BF16 = jnp.bfloat16
VMEM_BYTES = 48 * 1024 * 1024


def call(kernel, out_shape, in_specs, out_specs, **rest):
    return pl.pallas_call(
        kernel,
        out_shape=out_shape,
        in_specs=in_specs,
        out_specs=out_specs,
        compiler_params=pltpu.CompilerParams(vmem_limit_bytes=VMEM_BYTES),
        **rest,
    )


IN_VMEM = pl.BlockSpec(memory_space=pltpu.VMEM)
IN_SMEM = pl.BlockSpec(memory_space=pltpu.SMEM)


RING = 4


def encode(block):
    top = jnp.maximum(jnp.max(jnp.abs(block), axis=0, keepdims=True), 1e-30)
    level = jnp.ceil(jnp.log2(top) * 16.0)
    value = jnp.round(block * (jnp.exp2(level * (-1.0 / 16.0)) * RANGE))
    return value.astype(jnp.int32) + MIDDLE, level.astype(jnp.int32)


def level_factor(level):
    return jnp.exp2(level.astype(F32) * (1.0 / 16.0)) * (1.0 / RANGE)


def pack(value):
    part = [value[8 * at : 8 * at + 8] for at in range(8)]
    lows = [
        part[5] & 0xFFF,
        (part[5] >> 12) | ((part[6] & 0xF) << 8),
        (part[6] >> 4) & 0xFFF,
        (part[6] >> 16) | ((part[7] & 0xFF) << 4),
        part[7] >> 8,
    ]
    return [(part[at] << 12) | lows[at] for at in range(5)]


def top_bits(word):
    return lax.shift_right_logical(word, jnp.int32(12))


def unpack(words):
    lows = [word & 0xFFF for word in words]
    part = [top_bits(word) for word in words]
    part.append(lows[0] | ((lows[1] & 0xFF) << 12))
    part.append((lows[1] >> 8) | (lows[2] << 4) | ((lows[3] & 0xF) << 16))
    part.append((lows[3] >> 4) | (lows[4] << 8))
    return (jnp.concatenate(part, axis=0) - MIDDLE).astype(F32)


def first_rows(rows, count=8):
    place = lax.broadcasted_iota(jnp.int32, (count, rows[0].shape[1]), 0)
    filled = jnp.zeros_like(place)
    for number, row in enumerate(rows):
        filled = jnp.where(place == number, row, filled)
    return filled


def square_rows(x):
    squares = jnp.sum(x * x, axis=1, keepdims=True)
    squares = jnp.broadcast_to(squares, (x.shape[0], 128))
    missing = -x.shape[0] % 128
    if missing:
        squares = jnp.concatenate([squares, jnp.zeros((missing, 128), F32)], axis=0)
    return squares.T[0:8]


def norm_columns(parts_ref):
    total = parts_ref[0]
    for peer in range(1, parts_ref.shape[0]):
        total = total + parts_ref[peer]
    factor = lax.rsqrt(total[0:1] / D + EPSILON)
    return jnp.broadcast_to(factor, (128, factor.shape[1])).T


def squares_kernel(count, x_ref, logical_ref, out_ref):
    rows = square_rows(x_ref[...].astype(F32))
    row = lax.broadcasted_iota(jnp.int32, rows.shape, 0)
    rows = jnp.where(row == 0, rows, logical_ref[...])
    for peer in range(count):
        out_ref[peer] = rows


def cache_kernel(keys_ref, values_ref, out_ref):
    out_ref[0] = keys_ref[...]
    for block in range(values_ref.shape[0] // BLOCK):
        at = slice(block * BLOCK, (block + 1) * BLOCK)
        out_ref[1, at, :] = values_ref[at, :].T


def first_project_kernel(count, x_ref, squares_ref, gain_ref, query_ref, kv_ref, out_ref):
    factor = norm_columns(squares_ref)[:, 0:1]
    normed = (x_ref[...].astype(F32) * factor * gain_ref[...]).astype(BF16)
    project(count, normed, query_ref, kv_ref, out_ref)


def project_kernel(count, core_ref, own_ref, other_ref, gain_ref, query_ref, kv_ref, out_ref, x_ref):
    share = TOKENS // 2
    width = gain_ref.shape[1]
    x_ref[pl.ds(core_ref[0] * share, share), :] = own_ref[...]
    x_ref[pl.ds((1 - core_ref[0]) * share, share), :] = other_ref[...]
    thirds = x_ref[:, width : width + 128].astype(F32)
    factor = thirds[:, 0:1] + thirds[:, 1:2] + thirds[:, 2:3]
    normed = (x_ref[:, 0:width].astype(F32) * factor * gain_ref[...]).astype(BF16)
    project(count, normed, query_ref, kv_ref, out_ref, True)


def project(count, scaled, query_ref, kv_ref, out_ref, crossed=False):
    half = HEAD_DIM // 2
    columns = query_ref.shape[1]
    rows = SEG_LEN // count
    fresh = jnp.dot(scaled, kv_ref[...], preferred_element_type=F32)
    for start in range(0, columns, 256):
        part = jnp.dot(scaled, query_ref[:, start : start + 256], preferred_element_type=F32)
        turned = part.T
        for piece in range(256 // half):
            at = start // half + piece
            peer = at % RING * RING + at // RING if crossed else at
            block = turned[piece * half : (piece + 1) * half]
            query, query_level = encode(block)
            words = pack(query)
            kinds = []
            for kind in range(2):
                lanes = slice(kind * HEAD_DIM, (kind + 1) * HEAD_DIM)
                block = jnp.concatenate(
                    [
                        fresh[seg * SEG_LEN + peer * rows : seg * SEG_LEN + (peer + 1) * rows, lanes]
                        for seg in range(NSEG)
                    ],
                    axis=1,
                )
                kinds.append(encode(block))
            levels = first_rows([query_level, kinds[0][1], kinds[1][1]]) + LEVELS
            words.append((kinds[0][0] << 12) | levels)
            words.append(kinds[1][0] << 12)
            for at, word in enumerate(words):
                out_ref[peer, 8 * at : 8 * at + 8, :] = word


def add_projection(count, parts_ref):
    half = HEAD_DIM // 2
    rows = SEG_LEN // count
    query = jnp.zeros((half, TOKENS), F32)
    fresh = [jnp.zeros((rows, TOKENS), F32) for _ in range(2)]
    for peer in range(count):
        words = [parts_ref[peer, 8 * at : 8 * at + 8, :] for at in range(7)]
        factors = level_factor((words[5] & 0xFFF) - LEVELS)
        query = query + unpack(words[0:5]) * factors[0:1]
        for kind in range(2):
            value = (top_bits(words[5 + kind]) - MIDDLE).astype(F32)
            fresh[kind] = fresh[kind] + value * factors[1 + kind : 2 + kind]
    return query, fresh


def finish_projection_kernel(count, parts_ref, query_out, fresh_out):
    rows = SEG_LEN // count
    query, fresh = add_projection(count, parts_ref)
    query = query.astype(BF16)
    for peer in range(count):
        query_out[peer] = query
    filler = jnp.zeros((FRESH - NSEG * rows, HEAD_DIM), F32)
    for kind in range(2):
        pieces = [
            fresh[kind][:, seg * SEG_LEN : (seg + 1) * SEG_LEN] for seg in range(NSEG)
        ]
        fresh_out[kind] = jnp.concatenate(pieces + [filler], axis=0).astype(BF16)


def finish_crossed_kernel(count, parts_ref, query_out, fresh_out):
    rows = SEG_LEN // count
    query, fresh = add_projection(count, parts_ref)
    query = query.astype(BF16)
    for peer in range(RING):
        query_out[peer] = query
    filler = jnp.zeros((rows, HEAD_DIM), F32)
    for kind in range(2):
        pieces = [
            fresh[kind][:, seg * SEG_LEN : (seg + 1) * SEG_LEN] for seg in range(NSEG)
        ]
        fresh_out[kind] = jnp.concatenate(pieces + [filler], axis=0).astype(BF16)


def near_mask(rows, slot_ref, seg):
    key_row = lax.broadcasted_iota(jnp.int32, (4 * rows, SEG_LEN), 0)
    token = lax.broadcasted_iota(jnp.int32, (4 * rows, SEG_LEN), 1)
    local = key_row - seg * rows
    inside = (local >= 0) & (local < rows)
    return jnp.concatenate(
        [
            jnp.where(inside & (local + slot_ref[slot] * rows <= token), 1.0, 0.0)
            for slot in range(RING)
        ],
        axis=0,
    ) > 0.5


def near_peak_kernel(rows, slot_ref, logical_ref, start_ref, query_ref, *refs):
    caches, fresh, out_ref = refs[0:RING], refs[RING : 2 * RING], refs[2 * RING]
    blocks = caches[0].shape[1] // BLOCK
    found = []
    for head in range(query_ref.shape[0]):
        query = query_ref[head]
        keys = jnp.concatenate([part[0] for part in fresh], axis=0)
        scores = jnp.dot(keys, query, preferred_element_type=F32)
        tops = []
        for seg in range(NSEG):
            lanes = slice(seg * SEG_LEN, (seg + 1) * SEG_LEN)
            masked = jnp.where(near_mask(rows, slot_ref, seg), scores[:, lanes], CLOSED)
            tops.append(jnp.max(masked.reshape(-1, 8, SEG_LEN), axis=0))
        for number in range(RING * blocks):
            block = number % blocks
            keys = caches[number // blocks][0, block * BLOCK : (block + 1) * BLOCK, :]
            scores = jnp.dot(keys, query, preferred_element_type=F32)
            top = jnp.max(scores.reshape(BLOCK // 8, 8, TOKENS), axis=0)
            for seg in range(NSEG):
                lanes = slice(seg * SEG_LEN, (seg + 1) * SEG_LEN)
                is_open = logical_ref[number] < start_ref[seg]
                tops[seg] = jnp.maximum(tops[seg], jnp.where(is_open, top[:, lanes], CLOSED))
        found.append(
            jnp.concatenate([jnp.max(top, axis=0, keepdims=True) for top in tops], axis=1)
        )
    found = jnp.concatenate(found * 4, axis=0)
    for peer in range(RING):
        out_ref[peer] = found


def near_attend_kernel(rows, slot_ref, logical_ref, start_ref, query_ref, *refs):
    caches, fresh = refs[0:RING], refs[RING : 2 * RING]
    peaks_ref, out_ref, weights = refs[2 * RING :]
    blocks = caches[0].shape[1] // BLOCK
    stored = RING * blocks * BLOCK
    half = HEAD_DIM // 2
    head = pl.program_id(0)
    query = query_ref[0]
    peak = peaks_ref[0]
    for peer in range(1, RING):
        peak = jnp.maximum(peak, peaks_ref[peer])
    peak = jnp.where(head == 0, peak[0:1], peak[1:2])
    keys = jnp.concatenate([part[0] for part in fresh], axis=0)
    scores = jnp.dot(keys, query, preferred_element_type=F32)
    masses = []
    for seg in range(NSEG):
        lanes = slice(seg * SEG_LEN, (seg + 1) * SEG_LEN)
        weight = jnp.exp2((scores[:, lanes] - peak[:, lanes]) * SCALE)
        weight = jnp.where(near_mask(rows, slot_ref, seg), weight, 0.0)
        weights[stored : stored + 4 * RING * rows, lanes] = weight.astype(BF16)
        masses.append(jnp.sum(weight.reshape(-1, 8, SEG_LEN), axis=0))
    for number in range(RING * blocks):
        block = number % blocks
        keys = caches[number // blocks][0, block * BLOCK : (block + 1) * BLOCK, :]
        scores = jnp.dot(keys, query, preferred_element_type=F32)
        for seg in range(NSEG):
            lanes = slice(seg * SEG_LEN, (seg + 1) * SEG_LEN)
            is_open = logical_ref[number] < start_ref[seg]
            offset = jnp.where(is_open, peak[:, lanes], -CLOSED)
            weight = jnp.exp2((scores[:, lanes] - offset) * SCALE)
            weights[number * BLOCK : (number + 1) * BLOCK, lanes] = weight.astype(BF16)
            masses[seg] = masses[seg] + jnp.sum(weight.reshape(BLOCK // 8, 8, SEG_LEN), axis=0)
    turned = [
        cache[1, block * BLOCK : (block + 1) * BLOCK, :] for cache in caches for block in range(blocks)
    ]
    turned.append(jnp.concatenate([part[1] for part in fresh], axis=0).T)
    sums = jnp.dot(jnp.concatenate(turned, axis=1), weights[...], preferred_element_type=F32)
    mass = jnp.concatenate([jnp.sum(part, axis=0, keepdims=True) for part in masses], axis=1)
    mass = jnp.round(mass * NEAR_MASS_UNIT).astype(jnp.int32)
    for piece in range(2):
        value, level = encode(sums[piece * half : (piece + 1) * half])
        for at, word in enumerate(pack(value) + [first_rows([level, mass])]):
            out_ref[piece, 8 * at : 8 * at + 8, :] = word


def fresh_mask(rows, index_ref, seg):
    key_row = lax.broadcasted_iota(jnp.int32, (FRESH, SEG_LEN), 0)
    token = lax.broadcasted_iota(jnp.int32, (FRESH, SEG_LEN), 1)
    local = key_row - seg * rows
    return (local >= 0) & (local < rows) & (local + index_ref[0] * rows <= token)


def peak_kernel(
    rows, index_ref, logical_ref, start_ref, query_ref, cache_ref, fresh_ref, out_ref, peaks
):
    blocks = cache_ref.shape[1] // BLOCK
    heads = query_ref.shape[0]
    step = pl.program_id(0)
    for head in range(heads):
        query = query_ref[head]
        scores = jnp.dot(fresh_ref[0], query, preferred_element_type=F32)
        tops = []
        for seg in range(NSEG):
            lanes = slice(seg * SEG_LEN, (seg + 1) * SEG_LEN)
            masked = jnp.where(fresh_mask(rows, index_ref, seg), scores[:, lanes], CLOSED)
            tops.append(jnp.max(masked.reshape(FRESH // 8, 8, SEG_LEN), axis=0))
        for block in range(blocks):
            at = slice(block * BLOCK, (block + 1) * BLOCK)
            scores = jnp.dot(cache_ref[0, at, :], query, preferred_element_type=F32)
            top = jnp.max(scores.reshape(BLOCK // 8, 8, TOKENS), axis=0)
            for seg in range(NSEG):
                lanes = slice(seg * SEG_LEN, (seg + 1) * SEG_LEN)
                is_open = logical_ref[block] < start_ref[seg]
                tops[seg] = jnp.maximum(tops[seg], jnp.where(is_open, top[:, lanes], CLOSED))
        peaks[step * heads + head] = jnp.concatenate(
            [jnp.max(top, axis=0, keepdims=True) for top in tops], axis=1
        )

    @pl.when(step == pl.num_programs(0) - 1)
    def _():
        found = jnp.concatenate([peaks[head] for head in range(GROUP)], axis=0)
        for peer in range(out_ref.shape[0]):
            out_ref[peer] = found


def attend_kernel(
    rows, index_ref, logical_ref, start_ref, query_ref, cache_ref, fresh_ref, peaks_ref,
    out_ref, peaks, weights,
):
    blocks = cache_ref.shape[1] // BLOCK
    stored = blocks * BLOCK
    half = HEAD_DIM // 2
    heads = query_ref.shape[0]
    step = pl.program_id(0)

    @pl.when(step == 0)
    def _():
        top = peaks_ref[0]
        for peer in range(1, peaks_ref.shape[0]):
            top = jnp.maximum(top, peaks_ref[peer])
        for head in range(GROUP):
            peaks[head] = top[head : head + 1]

    turned = [cache_ref[1, block * BLOCK : (block + 1) * BLOCK, :] for block in range(blocks)]
    turned = jnp.concatenate(turned + [fresh_ref[1].T], axis=1)
    for head in range(heads):
        query = query_ref[head]
        peak = peaks[step * heads + head]
        scores = jnp.dot(fresh_ref[0], query, preferred_element_type=F32)
        masses = []
        for seg in range(NSEG):
            lanes = slice(seg * SEG_LEN, (seg + 1) * SEG_LEN)
            weight = jnp.exp2((scores[:, lanes] - peak[:, lanes]) * SCALE)
            weight = jnp.where(fresh_mask(rows, index_ref, seg), weight, 0.0)
            weights[head, stored : stored + FRESH, lanes] = weight.astype(BF16)
            masses.append(jnp.sum(weight.reshape(FRESH // 8, 8, SEG_LEN), axis=0))
        for block in range(blocks):
            at = slice(block * BLOCK, (block + 1) * BLOCK)
            scores = jnp.dot(cache_ref[0, at, :], query, preferred_element_type=F32)
            for seg in range(NSEG):
                lanes = slice(seg * SEG_LEN, (seg + 1) * SEG_LEN)
                is_open = logical_ref[block] < start_ref[seg]
                offset = jnp.where(is_open, peak[:, lanes], -CLOSED)
                weight = jnp.exp2((scores[:, lanes] - offset) * SCALE)
                weights[head, at, lanes] = weight.astype(BF16)
                masses[seg] = masses[seg] + jnp.sum(
                    weight.reshape(BLOCK // 8, 8, SEG_LEN), axis=0
                )
        sums = jnp.dot(turned, weights[head], preferred_element_type=F32)
        mass = jnp.concatenate(
            [jnp.sum(part, axis=0, keepdims=True) for part in masses], axis=1
        )
        mass = jnp.round(mass * MASS_UNIT).astype(jnp.int32)
        for piece in range(2):
            value, level = encode(sums[piece * half : (piece + 1) * half])
            for at, word in enumerate(pack(value) + [first_rows([level, mass])]):
                out_ref[2 * head + piece, 8 * at : 8 * at + 8, :] = word


def combine_kernel(count, unit, parts_ref, out_ref):
    half = HEAD_DIM // 2
    mass = jnp.zeros((1, TOKENS), F32)
    sums = jnp.zeros((half, TOKENS), F32)
    for peer in range(count):
        words = [parts_ref[peer, 8 * at : 8 * at + 8, :] for at in range(6)]
        mass = mass + words[5][1:2].astype(F32) * (1.0 / unit)
        sums = sums + unpack(words[0:5]) * level_factor(words[5][0:1])
    attended = (sums / mass).astype(BF16)
    for peer in range(out_ref.shape[0]):
        out_ref[peer] = attended


def output_kernel(core_ref, attended_ref, weight_ref, keep_ref, send_ref, scratch):
    project_output(core_ref, attended_ref, weight_ref, keep_ref, send_ref, scratch)


def project_output(core_ref, attended_ref, weight_ref, keep_ref, send_ref, scratch):
    share = TOKENS // 2
    scratch[...] = lax.dot_general(
        attended_ref[...], weight_ref[...], (((0,), (0,)), ((), ())), preferred_element_type=F32
    )
    keep_ref[...] = scratch[pl.ds(core_ref[0] * share, share), :]
    send_ref[...] = scratch[pl.ds((1 - core_ref[0]) * share, share), :]


def crossed_output_kernel(core_ref, parts_ref, weight_ref, keep_ref, send_ref, scratch, attended):
    half = HEAD_DIM // 2
    for at in range(parts_ref.shape[0]):
        attended[at * half : (at + 1) * half, :] = parts_ref[at % RING * RING + at // RING]
    project_output(core_ref, attended, weight_ref, keep_ref, send_ref, scratch)


def add_kernel(keep_ref, received_ref, out_ref):
    out_ref[...] = keep_ref[...] + received_ref[...]


def add_residual(parts_ref, x_ref):
    total = parts_ref[0]
    for peer in range(1, parts_ref.shape[0]):
        total = total + parts_ref[peer]
    return (x_ref[...].astype(F32) + total).astype(BF16)


def residual_kernel(count, parts_ref, x_ref, out_ref, squares_ref):
    produced = add_residual(parts_ref, x_ref)
    out_ref[...] = produced
    rows = square_rows(produced.astype(F32))
    for peer in range(count):
        squares_ref[peer] = rows


def last_residual_kernel(parts_ref, x_ref, out_ref):
    produced = add_residual(parts_ref, x_ref)
    for peer in range(out_ref.shape[0]):
        out_ref[peer] = produced


def spread_kernel(squares_ref, x_ref, out_ref):
    tokens, width = x_ref.shape
    factor = norm_columns(squares_ref)[0:tokens]
    first = factor.astype(BF16).astype(F32)
    second = (factor - first).astype(BF16).astype(F32)
    lane = lax.broadcasted_iota(jnp.int32, factor.shape, 1)
    thirds = jnp.where(lane == 0, first, jnp.where(lane == 1, second, factor - first - second))
    for peer in range(out_ref.shape[0]):
        out_ref[peer, :, 0:width] = x_ref[...]
        out_ref[peer, :, width : width + 128] = thirds.astype(BF16)


def choose_kernel(core_ref, own0_ref, other0_ref, own1_ref, other1_ref, out_ref):
    share = TOKENS // 2
    width = out_ref.shape[1]
    first = core_ref[0] == 0
    at = pl.ds(core_ref[0] * share, share)
    out_ref[at, :] = jnp.where(first, own0_ref[:, 0:width], own1_ref[...])
    at = pl.ds((1 - core_ref[0]) * share, share)
    out_ref[at, :] = jnp.where(first, other0_ref[:, 0:width], other1_ref[...])


def exchange(value, axes):
    return lax.all_to_all(value, axes, 0, 0, tiled=True)


def swap(value):
    return lax.ppermute(value, "section", [(0, 1), (1, 0)])


def around_y(value, step):
    pairs = []
    for kv in range(RING * RING):
        z, y = divmod(kv, RING)
        pairs.append((kv, z * RING + (y + step) % RING))
    return lax.ppermute(value, "kv", pairs)


def over_z(value):
    groups = [[z * RING + y for z in range(RING)] for y in range(RING)]
    return lax.all_to_all(value, "kv", 0, 0, tiled=True, axis_index_groups=groups)


def near_holders(index):
    offsets = jnp.array([0, -1, 1, 2], jnp.int32)
    return index // RING * RING + (index % RING + offsets) % RING


def split_attention(parts, cache, logical, starts, index, out_proj):
    count = lax.axis_size("kv")
    rows = SEG_LEN // count
    half = HEAD_DIM // 2
    with jax.named_scope("queries"):
        query, fresh = call(
            functools.partial(finish_projection_kernel, count),
            (
                jax.ShapeDtypeStruct((count, half, TOKENS), BF16),
                jax.ShapeDtypeStruct((2, FRESH, HEAD_DIM), BF16),
            ),
            [IN_VMEM],
            (IN_VMEM, IN_VMEM),
        )(parts)
        query = exchange(query, "kv").reshape(GROUP, HEAD_DIM, TOKENS)
    stored = cache.shape[1]
    by_head = [
        IN_SMEM,
        IN_SMEM,
        IN_SMEM,
        pl.BlockSpec((HEADS_STEP, HEAD_DIM, TOKENS), lambda h: (h, 0, 0)),
        pl.BlockSpec((2, stored, HEAD_DIM), lambda h: (0, 0, 0)),
    ]
    whole_fresh = pl.BlockSpec((2, FRESH, HEAD_DIM), lambda h: (0, 0, 0))
    whole_peaks = pl.BlockSpec((count, GROUP, TOKENS), lambda h: (0, 0, 0))
    with jax.named_scope("peaks"):
        peaks = call(
            functools.partial(peak_kernel, rows),
            jax.ShapeDtypeStruct((count, GROUP, TOKENS), F32),
            by_head + [whole_fresh],
            whole_peaks,
            grid=(GROUP // HEADS_STEP,),
            scratch_shapes=[pltpu.VMEM((GROUP, 1, TOKENS), F32)],
        )(index, logical, starts, query, cache, fresh)
        peaks = exchange(peaks, "kv")
    with jax.named_scope("attend"):
        sent = call(
            functools.partial(attend_kernel, rows),
            jax.ShapeDtypeStruct((count, 6 * 8, TOKENS), jnp.int32),
            by_head + [whole_fresh, whole_peaks],
            pl.BlockSpec((2 * HEADS_STEP, 6 * 8, TOKENS), lambda h: (h, 0, 0)),
            grid=(GROUP // HEADS_STEP,),
            scratch_shapes=[
                pltpu.VMEM((GROUP, 1, TOKENS), F32),
                pltpu.VMEM((HEADS_STEP, stored + FRESH, TOKENS), BF16),
            ],
        )(index, logical, starts, query, cache, fresh, peaks)
        parts = exchange(sent, "kv")
        parts, out_proj = lax.optimization_barrier((parts, out_proj))
    with jax.named_scope("combine"):
        attended = call(
            functools.partial(combine_kernel, count, MASS_UNIT),
            jax.ShapeDtypeStruct((count, half, TOKENS), BF16),
            [IN_VMEM],
            IN_VMEM,
        )(parts)
        return exchange(attended, "kv").reshape(GROUP * HEAD_DIM, TOKENS), out_proj


def near_attention(parts, caches, logical, starts, holders):
    count = lax.axis_size("kv")
    rows = SEG_LEN // count
    half = HEAD_DIM // 2
    with jax.named_scope("queries"):
        query, fresh = call(
            functools.partial(finish_crossed_kernel, count),
            (
                jax.ShapeDtypeStruct((RING, half, TOKENS), BF16),
                jax.ShapeDtypeStruct((2, 4 * rows, HEAD_DIM), BF16),
            ),
            [IN_VMEM],
            (IN_VMEM, IN_VMEM),
        )(parts)
        fresh = (fresh,) + tuple(around_y(fresh, step) for step in (1, -1, 2))
        query = over_z(query).reshape(2, HEAD_DIM, TOKENS)
    with jax.named_scope("peaks"):
        peaks = call(
            functools.partial(near_peak_kernel, rows),
            jax.ShapeDtypeStruct((RING, 8, TOKENS), F32),
            [IN_SMEM] * 3 + [IN_VMEM] * (1 + 2 * RING),
            IN_VMEM,
        )(holders, logical, starts, query, *caches, *fresh)
        peaks = over_z(peaks)
    with jax.named_scope("attend"):
        stored = RING * caches[0].shape[1]
        sent = call(
            functools.partial(near_attend_kernel, rows),
            jax.ShapeDtypeStruct((RING, 6 * 8, TOKENS), jnp.int32),
            [IN_SMEM] * 3
            + [pl.BlockSpec((1, HEAD_DIM, TOKENS), lambda h: (h, 0, 0))]
            + [IN_VMEM] * (2 * RING + 1),
            pl.BlockSpec((2, 6 * 8, TOKENS), lambda h: (h, 0, 0)),
            grid=(2,),
            scratch_shapes=[pltpu.VMEM((stored + 4 * RING * rows, TOKENS), BF16)],
        )(holders, logical, starts, query, *caches, *fresh, peaks)
        parts = over_z(sent)
    with jax.named_scope("combine"):
        attended = call(
            functools.partial(combine_kernel, RING, NEAR_MASS_UNIT),
            jax.ShapeDtypeStruct((count, half, TOKENS), BF16),
            [IN_VMEM],
            IN_VMEM,
        )(parts)
        return exchange(attended, "kv")


def layer(
    which, x, mine, gain, query_proj, kv_proj, out_proj, keys, values, logical, starts, index, core,
    squares=None,
):
    count = lax.axis_size("kv")
    peers = lax.axis_size("tp")
    rows = SEG_LEN // count
    half = HEAD_DIM // 2
    width = query_proj.shape[0]
    share = TOKENS // 2
    part = share // peers
    with jax.named_scope("project"):
        shape = jax.ShapeDtypeStruct((count, 7 * 8, TOKENS), jnp.int32)
        if which == 0:
            squares = exchange(squares, "kv")
            all_logical = squares[:, 1, 0 : logical.shape[0]].astype(jnp.int32)
            sent = call(
                functools.partial(first_project_kernel, count), shape, [IN_VMEM] * 5, IN_VMEM
            )(x, squares, gain, query_proj, kv_proj)
        else:
            sent = call(
                functools.partial(project_kernel, count),
                shape,
                [IN_SMEM] + [IN_VMEM] * 5,
                IN_VMEM,
                scratch_shapes=[pltpu.VMEM((TOKENS, width + 128), BF16)],
            )(core, x[0], x[1], gain, query_proj, kv_proj)
        if which == 0:
            sent, keys = lax.optimization_barrier((sent, keys))
        parts = exchange(sent, "kv")
    later = None
    if which == 0:
        now, later = values(keys)
        attended, out_proj = split_attention(parts, now, logical, starts, index, out_proj)
        kernel, scratch = output_kernel, []
    else:
        attended = near_attention(parts, keys, logical, starts, index)
        kernel, scratch = crossed_output_kernel, [pltpu.VMEM((GROUP * HEAD_DIM, TOKENS), BF16)]
    with jax.named_scope("output"):
        keep, send = call(
            kernel,
            (jax.ShapeDtypeStruct((share, width), F32),) * 2,
            [IN_SMEM] + [IN_VMEM] * 2,
            (IN_VMEM, IN_VMEM),
            scratch_shapes=[pltpu.VMEM((TOKENS, width), F32)] + scratch,
        )(core, attended, out_proj)
        half_sum = call(
            add_kernel,
            jax.ShapeDtypeStruct((share, width), F32),
            [IN_VMEM] * 2,
            IN_VMEM,
        )(keep, swap(send))
        if which == 0:
            half_sum, later = lax.optimization_barrier((half_sum, later))
            sides = (around_y(later, 1), around_y(later, -1))
        parts = exchange(half_sum.reshape(peers, part, width), "tp")
    with jax.named_scope("residual"):
        if which == LAYERS - 1:
            produced = call(
                last_residual_kernel,
                jax.ShapeDtypeStruct((peers, part, width), BF16),
                [IN_VMEM] * 2,
                IN_VMEM,
            )(parts, mine)
            mine = None
        else:
            mine, squares = call(
                functools.partial(residual_kernel, count),
                (
                    jax.ShapeDtypeStruct((part, width), BF16),
                    jax.ShapeDtypeStruct((count, 8, 128), F32),
                ),
                [IN_VMEM] * 2,
                (IN_VMEM, IN_VMEM),
            )(parts, mine)
            squares = exchange(squares, "kv")
            squares, before, after = lax.optimization_barrier((squares, sides[0][0], sides[1][1]))
            opposite = jnp.stack([around_y(before, 1), around_y(after, -1)])
            holders = near_holders(index[0])
            produced = call(
                spread_kernel,
                jax.ShapeDtypeStruct((peers, part, width + 128), BF16),
                [IN_VMEM] * 2,
                IN_VMEM,
            )(squares, mine)
        own = exchange(produced, "tp").reshape(share, -1)
        if which == 0:
            later = ((later,) + sides + (opposite,), all_logical[holders].reshape(-1), holders)
        return (own, swap(own)), mine, later


def per_device(
    segments_in, gain, query_weight, kv_weight, out_weight, kv_cache, block_logical, segment_block
):
    width = segments_in.shape[2]
    core = lax.axis_index("section")
    core_at = core.astype(jnp.int32)[None]
    index = lax.axis_index("kv").astype(jnp.int32)[None]
    per_core = GROUP * HEAD_DIM
    share = TOKENS // 2

    x = segments_in.reshape(TOKENS, width)
    count = lax.axis_size("kv")
    blocks = block_logical.shape[0]
    squares = call(
        functools.partial(squares_kernel, count),
        jax.ShapeDtypeStruct((count, 8, TOKENS), F32),
        [IN_VMEM] * 2,
        IN_VMEM,
    )(x, jnp.pad(block_logical.astype(F32), (0, TOKENS - blocks))[None])
    squares, query_weight, kv_weight, out_weight = lax.optimization_barrier(
        (squares, query_weight, kv_weight, out_weight)
    )

    def pick(which):
        at = which * per_core
        kv_at = which * HEAD_DIM
        return (
            lax.dynamic_slice_in_dim(query_weight[0], at, per_core, 1),
            lax.dynamic_slice_in_dim(kv_weight[0], kv_at, HEAD_DIM, 2).reshape(width, -1),
            lax.dynamic_slice_in_dim(out_weight[0], at, per_core, 0),
            gain,
        )

    kept = pick(core)
    received = tuple(swap(v) for v in pick(1 - core))
    part = share // lax.axis_size("tp")
    mine = lax.dynamic_slice_in_dim(x, core * share + lax.axis_index("tp") * part, part, 0)
    params = [
        [jnp.where(core == which, here, other) for here, other in zip(kept, received)]
        for which in range(LAYERS)
    ]

    def cut_cache(cache):
        def cut(which):
            return tuple(
                lax.dynamic_slice_in_dim(cache[0, :, kind], which * HEAD_DIM, HEAD_DIM, 1)
                for kind in range(2)
            )

        pairs = [(here, swap(there)) for here, there in zip(cut(core), cut(1 - core))]
        return tuple(
            call(
                cache_kernel,
                jax.ShapeDtypeStruct((2,) + pairs[0][0].shape, BF16),
                [IN_VMEM] * 2,
                IN_VMEM,
            )(*(jnp.where(core == which, here, other) for here, other in pairs))
            for which in range(LAYERS)
        )

    query_proj, kv_proj, out_proj, gain_row = params[0]
    first, mine, (caches, numbers, holders) = layer(
        0, x, mine, gain_row, query_proj, kv_proj, out_proj, kv_cache, cut_cache,
        block_logical, segment_block, index, core_at, squares,
    )
    query_proj, kv_proj, out_proj, gain_row = params[1]
    second, _, _ = layer(
        1, first, mine, gain_row, query_proj, kv_proj, out_proj, caches, None,
        numbers, segment_block, holders, core_at,
    )
    outputs = first + second
    result = call(
        choose_kernel,
        jax.ShapeDtypeStruct((TOKENS, width), BF16),
        [IN_SMEM] + [IN_VMEM] * 4,
        IN_VMEM,
    )(core_at, *outputs)
    return result.reshape(1, NSEG, SEG_LEN, width)


def solution(mesh):
    placed = (
        P(None, None, "kv"),
        P("section", "kv"),
        P("section", "kv", "tp"),
        P("section", "kv", None, "tp"),
        P("section", "tp", "kv"),
        P("section", "kv", None, "tp"),
        P("kv"),
        P(),
    )
    return jax.shard_map(
        per_device,
        mesh=mesh,
        in_specs=placed,
        out_specs=P("section", None, None, "kv"),
        check_vma=False,
    )
```

```python
import functools
import math

import jax
import jax.numpy as jnp
from jax import lax
from jax.experimental import pallas as pl
from jax.experimental.pallas import tpu as pltpu
from jax.sharding import PartitionSpec as P

D = 8192
HEAD_DIM = 128
BLOCK = 128
NSEG = 3
SEG_LEN = 128
TOKENS = NSEG * SEG_LEN
GROUP = 8
LAYERS = 2
EPSILON = 1e-05
CLOSED = -1e30
FRESH = 128
RANGE = 520000.0
MIDDLE = 524288
LEVELS = 2048
MASS_UNIT = 262144.0
NEAR_MASS_UNIT = 65536.0
HEADS_STEP = 4
SCALE = math.log2(math.e) / math.sqrt(HEAD_DIM)
F32 = jnp.float32
BF16 = jnp.bfloat16
VMEM_BYTES = 48 * 1024 * 1024


def call(kernel, out_shape, in_specs, out_specs, **rest):
    return pl.pallas_call(
        kernel,
        out_shape=out_shape,
        in_specs=in_specs,
        out_specs=out_specs,
        compiler_params=pltpu.CompilerParams(vmem_limit_bytes=VMEM_BYTES),
        **rest,
    )


IN_VMEM = pl.BlockSpec(memory_space=pltpu.VMEM)
IN_SMEM = pl.BlockSpec(memory_space=pltpu.SMEM)


RING = 4


def encode(block):
    top = jnp.maximum(jnp.max(jnp.abs(block), axis=0, keepdims=True), 1e-30)
    level = jnp.ceil(jnp.log2(top) * 16.0)
    value = jnp.round(block * (jnp.exp2(level * (-1.0 / 16.0)) * RANGE))
    return value.astype(jnp.int32) + MIDDLE, level.astype(jnp.int32)


def level_factor(level):
    return jnp.exp2(level.astype(F32) * (1.0 / 16.0)) * (1.0 / RANGE)


def pack(value):
    part = [value[8 * at : 8 * at + 8] for at in range(8)]
    lows = [
        part[5] & 0xFFF,
        (part[5] >> 12) | ((part[6] & 0xF) << 8),
        (part[6] >> 4) & 0xFFF,
        (part[6] >> 16) | ((part[7] & 0xFF) << 4),
        part[7] >> 8,
    ]
    return [(part[at] << 12) | lows[at] for at in range(5)]


def top_bits(word):
    return lax.shift_right_logical(word, jnp.int32(12))


def unpack(words):
    lows = [word & 0xFFF for word in words]
    part = [top_bits(word) for word in words]
    part.append(lows[0] | ((lows[1] & 0xFF) << 12))
    part.append((lows[1] >> 8) | (lows[2] << 4) | ((lows[3] & 0xF) << 16))
    part.append((lows[3] >> 4) | (lows[4] << 8))
    return (jnp.concatenate(part, axis=0) - MIDDLE).astype(F32)


def first_rows(rows, count=8):
    place = lax.broadcasted_iota(jnp.int32, (count, rows[0].shape[1]), 0)
    filled = jnp.zeros_like(place)
    for number, row in enumerate(rows):
        filled = jnp.where(place == number, row, filled)
    return filled


def square_rows(x):
    squares = jnp.sum(x * x, axis=1, keepdims=True)
    squares = jnp.broadcast_to(squares, (x.shape[0], 128))
    missing = -x.shape[0] % 128
    if missing:
        squares = jnp.concatenate([squares, jnp.zeros((missing, 128), F32)], axis=0)
    return squares.T[0:8]


def norm_columns(parts_ref):
    total = parts_ref[0]
    for peer in range(1, parts_ref.shape[0]):
        total = total + parts_ref[peer]
    factor = lax.rsqrt(total[0:1] / D + EPSILON)
    return jnp.broadcast_to(factor, (128, factor.shape[1])).T


def squares_kernel(count, x_ref, logical_ref, out_ref):
    rows = square_rows(x_ref[...].astype(F32))
    row = lax.broadcasted_iota(jnp.int32, rows.shape, 0)
    rows = jnp.where(row == 0, rows, logical_ref[...])
    for peer in range(count):
        out_ref[peer] = rows


def cache_kernel(keys_ref, values_ref, out_ref):
    out_ref[0] = keys_ref[...]
    for block in range(values_ref.shape[0] // BLOCK):
        at = slice(block * BLOCK, (block + 1) * BLOCK)
        out_ref[1, at, :] = values_ref[at, :].T


def first_project_kernel(count, x_ref, squares_ref, gain_ref, query_ref, kv_ref, out_ref):
    factor = norm_columns(squares_ref)[:, 0:1]
    normed = (x_ref[...].astype(F32) * factor * gain_ref[...]).astype(BF16)
    project(count, normed, query_ref, kv_ref, out_ref)


def project_kernel(count, core_ref, own_ref, other_ref, gain_ref, query_ref, kv_ref, out_ref, x_ref):
    share = TOKENS // 2
    width = gain_ref.shape[1]
    x_ref[pl.ds(core_ref[0] * share, share), :] = own_ref[...]
    x_ref[pl.ds((1 - core_ref[0]) * share, share), :] = other_ref[...]
    thirds = x_ref[:, width : width + 128].astype(F32)
    factor = thirds[:, 0:1] + thirds[:, 1:2] + thirds[:, 2:3]
    normed = (x_ref[:, 0:width].astype(F32) * factor * gain_ref[...]).astype(BF16)
    project(count, normed, query_ref, kv_ref, out_ref, True)


def project(count, scaled, query_ref, kv_ref, out_ref, crossed=False):
    half = HEAD_DIM // 2
    columns = query_ref.shape[1]
    rows = SEG_LEN // count
    fresh = jnp.dot(scaled, kv_ref[...], preferred_element_type=F32)
    for start in range(0, columns, 256):
        part = jnp.dot(scaled, query_ref[:, start : start + 256], preferred_element_type=F32)
        turned = part.T
        for piece in range(256 // half):
            at = start // half + piece
            peer = at % RING * RING + at // RING if crossed else at
            block = turned[piece * half : (piece + 1) * half]
            query, query_level = encode(block)
            words = pack(query)
            kinds = []
            for kind in range(2):
                lanes = slice(kind * HEAD_DIM, (kind + 1) * HEAD_DIM)
                block = jnp.concatenate(
                    [
                        fresh[seg * SEG_LEN + peer * rows : seg * SEG_LEN + (peer + 1) * rows, lanes]
                        for seg in range(NSEG)
                    ],
                    axis=1,
                )
                kinds.append(encode(block))
            levels = first_rows([query_level, kinds[0][1], kinds[1][1]]) + LEVELS
            words.append((kinds[0][0] << 12) | levels)
            words.append(kinds[1][0] << 12)
            for at, word in enumerate(words):
                out_ref[peer, 8 * at : 8 * at + 8, :] = word


def add_projection(count, parts_ref):
    half = HEAD_DIM // 2
    rows = SEG_LEN // count
    query = jnp.zeros((half, TOKENS), F32)
    fresh = [jnp.zeros((rows, TOKENS), F32) for _ in range(2)]
    for peer in range(count):
        words = [parts_ref[peer, 8 * at : 8 * at + 8, :] for at in range(7)]
        factors = level_factor((words[5] & 0xFFF) - LEVELS)
        query = query + unpack(words[0:5]) * factors[0:1]
        for kind in range(2):
            value = (top_bits(words[5 + kind]) - MIDDLE).astype(F32)
            fresh[kind] = fresh[kind] + value * factors[1 + kind : 2 + kind]
    return query, fresh


def finish_projection_kernel(count, parts_ref, query_out, fresh_out):
    rows = SEG_LEN // count
    query, fresh = add_projection(count, parts_ref)
    query = query.astype(BF16)
    for peer in range(count):
        query_out[peer] = query
    filler = jnp.zeros((FRESH - NSEG * rows, HEAD_DIM), F32)
    for kind in range(2):
        pieces = [
            fresh[kind][:, seg * SEG_LEN : (seg + 1) * SEG_LEN] for seg in range(NSEG)
        ]
        fresh_out[kind] = jnp.concatenate(pieces + [filler], axis=0).astype(BF16)


def finish_crossed_kernel(count, parts_ref, query_out, fresh_out):
    rows = SEG_LEN // count
    query, fresh = add_projection(count, parts_ref)
    query = query.astype(BF16)
    for peer in range(RING):
        query_out[peer] = query
    filler = jnp.zeros((rows, HEAD_DIM), F32)
    for kind in range(2):
        pieces = [
            fresh[kind][:, seg * SEG_LEN : (seg + 1) * SEG_LEN] for seg in range(NSEG)
        ]
        fresh_out[kind] = jnp.concatenate(pieces + [filler], axis=0).astype(BF16)


def near_mask(rows, slot_ref, seg):
    key_row = lax.broadcasted_iota(jnp.int32, (4 * rows, SEG_LEN), 0)
    token = lax.broadcasted_iota(jnp.int32, (4 * rows, SEG_LEN), 1)
    local = key_row - seg * rows
    inside = (local >= 0) & (local < rows)
    return jnp.concatenate(
        [
            jnp.where(inside & (local + slot_ref[slot] * rows <= token), 1.0, 0.0)
            for slot in range(RING)
        ],
        axis=0,
    ) > 0.5


def near_peak_kernel(rows, slot_ref, logical_ref, start_ref, query_ref, *refs):
    caches, fresh, out_ref = refs[0:RING], refs[RING : 2 * RING], refs[2 * RING]
    blocks = caches[0].shape[1] // BLOCK
    found = []
    for head in range(query_ref.shape[0]):
        query = query_ref[head]
        keys = jnp.concatenate([part[0] for part in fresh], axis=0)
        scores = jnp.dot(keys, query, preferred_element_type=F32)
        tops = []
        for seg in range(NSEG):
            lanes = slice(seg * SEG_LEN, (seg + 1) * SEG_LEN)
            masked = jnp.where(near_mask(rows, slot_ref, seg), scores[:, lanes], CLOSED)
            tops.append(jnp.max(masked.reshape(-1, 8, SEG_LEN), axis=0))
        for number in range(RING * blocks):
            block = number % blocks
            keys = caches[number // blocks][0, block * BLOCK : (block + 1) * BLOCK, :]
            scores = jnp.dot(keys, query, preferred_element_type=F32)
            top = jnp.max(scores.reshape(BLOCK // 8, 8, TOKENS), axis=0)
            for seg in range(NSEG):
                lanes = slice(seg * SEG_LEN, (seg + 1) * SEG_LEN)
                is_open = logical_ref[number] < start_ref[seg]
                tops[seg] = jnp.maximum(tops[seg], jnp.where(is_open, top[:, lanes], CLOSED))
        found.append(
            jnp.concatenate([jnp.max(top, axis=0, keepdims=True) for top in tops], axis=1)
        )
    found = jnp.concatenate(found * 4, axis=0)
    for peer in range(RING):
        out_ref[peer] = found


def near_attend_kernel(rows, slot_ref, logical_ref, start_ref, query_ref, *refs):
    caches, fresh = refs[0:RING], refs[RING : 2 * RING]
    peaks_ref, out_ref, weights = refs[2 * RING :]
    blocks = caches[0].shape[1] // BLOCK
    stored = RING * blocks * BLOCK
    half = HEAD_DIM // 2
    head = pl.program_id(0)
    query = query_ref[0]
    peak = peaks_ref[0]
    for peer in range(1, RING):
        peak = jnp.maximum(peak, peaks_ref[peer])
    peak = jnp.where(head == 0, peak[0:1], peak[1:2])
    keys = jnp.concatenate([part[0] for part in fresh], axis=0)
    scores = jnp.dot(keys, query, preferred_element_type=F32)
    masses = []
    for seg in range(NSEG):
        lanes = slice(seg * SEG_LEN, (seg + 1) * SEG_LEN)
        weight = jnp.exp2((scores[:, lanes] - peak[:, lanes]) * SCALE)
        weight = jnp.where(near_mask(rows, slot_ref, seg), weight, 0.0)
        weights[stored : stored + 4 * RING * rows, lanes] = weight.astype(BF16)
        masses.append(jnp.sum(weight.reshape(-1, 8, SEG_LEN), axis=0))
    for number in range(RING * blocks):
        block = number % blocks
        keys = caches[number // blocks][0, block * BLOCK : (block + 1) * BLOCK, :]
        scores = jnp.dot(keys, query, preferred_element_type=F32)
        for seg in range(NSEG):
            lanes = slice(seg * SEG_LEN, (seg + 1) * SEG_LEN)
            is_open = logical_ref[number] < start_ref[seg]
            offset = jnp.where(is_open, peak[:, lanes], -CLOSED)
            weight = jnp.exp2((scores[:, lanes] - offset) * SCALE)
            weights[number * BLOCK : (number + 1) * BLOCK, lanes] = weight.astype(BF16)
            masses[seg] = masses[seg] + jnp.sum(weight.reshape(BLOCK // 8, 8, SEG_LEN), axis=0)
    turned = [
        cache[1, block * BLOCK : (block + 1) * BLOCK, :] for cache in caches for block in range(blocks)
    ]
    turned.append(jnp.concatenate([part[1] for part in fresh], axis=0).T)
    sums = jnp.dot(jnp.concatenate(turned, axis=1), weights[...], preferred_element_type=F32)
    mass = jnp.concatenate([jnp.sum(part, axis=0, keepdims=True) for part in masses], axis=1)
    mass = jnp.round(mass * NEAR_MASS_UNIT).astype(jnp.int32)
    for piece in range(2):
        value, level = encode(sums[piece * half : (piece + 1) * half])
        for at, word in enumerate(pack(value) + [first_rows([level, mass])]):
            out_ref[piece, 8 * at : 8 * at + 8, :] = word


def fresh_mask(rows, index_ref, seg):
    key_row = lax.broadcasted_iota(jnp.int32, (FRESH, SEG_LEN), 0)
    token = lax.broadcasted_iota(jnp.int32, (FRESH, SEG_LEN), 1)
    local = key_row - seg * rows
    return (local >= 0) & (local < rows) & (local + index_ref[0] * rows <= token)


def peak_kernel(
    rows, index_ref, logical_ref, start_ref, query_ref, cache_ref, fresh_ref, out_ref, peaks
):
    blocks = cache_ref.shape[1] // BLOCK
    heads = query_ref.shape[0]
    step = pl.program_id(0)
    for head in range(heads):
        query = query_ref[head]
        scores = jnp.dot(fresh_ref[0], query, preferred_element_type=F32)
        tops = []
        for seg in range(NSEG):
            lanes = slice(seg * SEG_LEN, (seg + 1) * SEG_LEN)
            masked = jnp.where(fresh_mask(rows, index_ref, seg), scores[:, lanes], CLOSED)
            tops.append(jnp.max(masked.reshape(FRESH // 8, 8, SEG_LEN), axis=0))
        for block in range(blocks):
            at = slice(block * BLOCK, (block + 1) * BLOCK)
            scores = jnp.dot(cache_ref[0, at, :], query, preferred_element_type=F32)
            top = jnp.max(scores.reshape(BLOCK // 8, 8, TOKENS), axis=0)
            for seg in range(NSEG):
                lanes = slice(seg * SEG_LEN, (seg + 1) * SEG_LEN)
                is_open = logical_ref[block] < start_ref[seg]
                tops[seg] = jnp.maximum(tops[seg], jnp.where(is_open, top[:, lanes], CLOSED))
        peaks[step * heads + head] = jnp.concatenate(
            [jnp.max(top, axis=0, keepdims=True) for top in tops], axis=1
        )

    @pl.when(step == pl.num_programs(0) - 1)
    def _():
        found = jnp.concatenate([peaks[head] for head in range(GROUP)], axis=0)
        for peer in range(out_ref.shape[0]):
            out_ref[peer] = found


def attend_kernel(
    rows, index_ref, logical_ref, start_ref, query_ref, cache_ref, fresh_ref, peaks_ref,
    out_ref, peaks, weights,
):
    blocks = cache_ref.shape[1] // BLOCK
    stored = blocks * BLOCK
    half = HEAD_DIM // 2
    heads = query_ref.shape[0]
    step = pl.program_id(0)

    @pl.when(step == 0)
    def _():
        top = peaks_ref[0]
        for peer in range(1, peaks_ref.shape[0]):
            top = jnp.maximum(top, peaks_ref[peer])
        for head in range(GROUP):
            peaks[head] = top[head : head + 1]

    turned = [cache_ref[1, block * BLOCK : (block + 1) * BLOCK, :] for block in range(blocks)]
    turned = jnp.concatenate(turned + [fresh_ref[1].T], axis=1)
    for head in range(heads):
        query = query_ref[head]
        peak = peaks[step * heads + head]
        scores = jnp.dot(fresh_ref[0], query, preferred_element_type=F32)
        masses = []
        for seg in range(NSEG):
            lanes = slice(seg * SEG_LEN, (seg + 1) * SEG_LEN)
            weight = jnp.exp2((scores[:, lanes] - peak[:, lanes]) * SCALE)
            weight = jnp.where(fresh_mask(rows, index_ref, seg), weight, 0.0)
            weights[head, stored : stored + FRESH, lanes] = weight.astype(BF16)
            masses.append(jnp.sum(weight.reshape(FRESH // 8, 8, SEG_LEN), axis=0))
        for block in range(blocks):
            at = slice(block * BLOCK, (block + 1) * BLOCK)
            scores = jnp.dot(cache_ref[0, at, :], query, preferred_element_type=F32)
            for seg in range(NSEG):
                lanes = slice(seg * SEG_LEN, (seg + 1) * SEG_LEN)
                is_open = logical_ref[block] < start_ref[seg]
                offset = jnp.where(is_open, peak[:, lanes], -CLOSED)
                weight = jnp.exp2((scores[:, lanes] - offset) * SCALE)
                weights[head, at, lanes] = weight.astype(BF16)
                masses[seg] = masses[seg] + jnp.sum(
                    weight.reshape(BLOCK // 8, 8, SEG_LEN), axis=0
                )
        sums = jnp.dot(turned, weights[head], preferred_element_type=F32)
        mass = jnp.concatenate(
            [jnp.sum(part, axis=0, keepdims=True) for part in masses], axis=1
        )
        mass = jnp.round(mass * MASS_UNIT).astype(jnp.int32)
        for piece in range(2):
            value, level = encode(sums[piece * half : (piece + 1) * half])
            for at, word in enumerate(pack(value) + [first_rows([level, mass])]):
                out_ref[2 * head + piece, 8 * at : 8 * at + 8, :] = word


def combine_kernel(count, unit, parts_ref, out_ref):
    half = HEAD_DIM // 2
    mass = jnp.zeros((1, TOKENS), F32)
    sums = jnp.zeros((half, TOKENS), F32)
    for peer in range(count):
        words = [parts_ref[peer, 8 * at : 8 * at + 8, :] for at in range(6)]
        mass = mass + words[5][1:2].astype(F32) * (1.0 / unit)
        sums = sums + unpack(words[0:5]) * level_factor(words[5][0:1])
    attended = (sums / mass).astype(BF16)
    for peer in range(out_ref.shape[0]):
        out_ref[peer] = attended


def output_kernel(core_ref, attended_ref, weight_ref, keep_ref, send_ref, scratch):
    project_output(core_ref, attended_ref, weight_ref, keep_ref, send_ref, scratch)


def project_output(core_ref, attended_ref, weight_ref, keep_ref, send_ref, scratch):
    share = TOKENS // 2
    scratch[...] = lax.dot_general(
        attended_ref[...], weight_ref[...], (((0,), (0,)), ((), ())), preferred_element_type=F32
    )
    keep_ref[...] = scratch[pl.ds(core_ref[0] * share, share), :]
    send_ref[...] = scratch[pl.ds((1 - core_ref[0]) * share, share), :]


def crossed_output_kernel(core_ref, parts_ref, weight_ref, keep_ref, send_ref, scratch, attended):
    half = HEAD_DIM // 2
    for at in range(parts_ref.shape[0]):
        attended[at * half : (at + 1) * half, :] = parts_ref[at % RING * RING + at // RING]
    project_output(core_ref, attended, weight_ref, keep_ref, send_ref, scratch)


def add_kernel(keep_ref, received_ref, out_ref):
    out_ref[...] = keep_ref[...] + received_ref[...]


def add_residual(parts_ref, x_ref):
    total = parts_ref[0]
    for peer in range(1, parts_ref.shape[0]):
        total = total + parts_ref[peer]
    return (x_ref[...].astype(F32) + total).astype(BF16)


def residual_kernel(count, parts_ref, x_ref, out_ref, squares_ref):
    produced = add_residual(parts_ref, x_ref)
    out_ref[...] = produced
    rows = square_rows(produced.astype(F32))
    for peer in range(count):
        squares_ref[peer] = rows


def last_residual_kernel(parts_ref, x_ref, out_ref):
    produced = add_residual(parts_ref, x_ref)
    for peer in range(out_ref.shape[0]):
        out_ref[peer] = produced


def spread_kernel(squares_ref, x_ref, out_ref):
    tokens, width = x_ref.shape
    factor = norm_columns(squares_ref)[0:tokens]
    first = factor.astype(BF16).astype(F32)
    second = (factor - first).astype(BF16).astype(F32)
    lane = lax.broadcasted_iota(jnp.int32, factor.shape, 1)
    thirds = jnp.where(lane == 0, first, jnp.where(lane == 1, second, factor - first - second))
    for peer in range(out_ref.shape[0]):
        out_ref[peer, :, 0:width] = x_ref[...]
        out_ref[peer, :, width : width + 128] = thirds.astype(BF16)


def choose_kernel(core_ref, own0_ref, other0_ref, own1_ref, other1_ref, out_ref):
    share = TOKENS // 2
    width = out_ref.shape[1]
    first = core_ref[0] == 0
    at = pl.ds(core_ref[0] * share, share)
    out_ref[at, :] = jnp.where(first, own0_ref[:, 0:width], own1_ref[...])
    at = pl.ds((1 - core_ref[0]) * share, share)
    out_ref[at, :] = jnp.where(first, other0_ref[:, 0:width], other1_ref[...])


def exchange(value, axes):
    return lax.all_to_all(value, axes, 0, 0, tiled=True)


def swap(value):
    return lax.ppermute(value, "section", [(0, 1), (1, 0)])


def around_y(value, step):
    pairs = []
    for kv in range(RING * RING):
        z, y = divmod(kv, RING)
        pairs.append((kv, z * RING + (y + step) % RING))
    return lax.ppermute(value, "kv", pairs)


def over_z(value):
    groups = [[z * RING + y for z in range(RING)] for y in range(RING)]
    return lax.all_to_all(value, "kv", 0, 0, tiled=True, axis_index_groups=groups)


def near_holders(index):
    offsets = jnp.array([0, -1, 1, 2], jnp.int32)
    return index // RING * RING + (index % RING + offsets) % RING


def split_attention(parts, cache, logical, starts, index, out_proj):
    count = lax.axis_size("kv")
    rows = SEG_LEN // count
    half = HEAD_DIM // 2
    with jax.named_scope("queries"):
        query, fresh = call(
            functools.partial(finish_projection_kernel, count),
            (
                jax.ShapeDtypeStruct((count, half, TOKENS), BF16),
                jax.ShapeDtypeStruct((2, FRESH, HEAD_DIM), BF16),
            ),
            [IN_VMEM],
            (IN_VMEM, IN_VMEM),
        )(parts)
        query = exchange(query, "kv").reshape(GROUP, HEAD_DIM, TOKENS)
    stored = cache.shape[1]
    by_head = [
        IN_SMEM,
        IN_SMEM,
        IN_SMEM,
        pl.BlockSpec((HEADS_STEP, HEAD_DIM, TOKENS), lambda h: (h, 0, 0)),
        pl.BlockSpec((2, stored, HEAD_DIM), lambda h: (0, 0, 0)),
    ]
    whole_fresh = pl.BlockSpec((2, FRESH, HEAD_DIM), lambda h: (0, 0, 0))
    whole_peaks = pl.BlockSpec((count, GROUP, TOKENS), lambda h: (0, 0, 0))
    with jax.named_scope("peaks"):
        peaks = call(
            functools.partial(peak_kernel, rows),
            jax.ShapeDtypeStruct((count, GROUP, TOKENS), F32),
            by_head + [whole_fresh],
            whole_peaks,
            grid=(GROUP // HEADS_STEP,),
            scratch_shapes=[pltpu.VMEM((GROUP, 1, TOKENS), F32)],
        )(index, logical, starts, query, cache, fresh)
        peaks = exchange(peaks, "kv")
    with jax.named_scope("attend"):
        sent = call(
            functools.partial(attend_kernel, rows),
            jax.ShapeDtypeStruct((count, 6 * 8, TOKENS), jnp.int32),
            by_head + [whole_fresh, whole_peaks],
            pl.BlockSpec((2 * HEADS_STEP, 6 * 8, TOKENS), lambda h: (h, 0, 0)),
            grid=(GROUP // HEADS_STEP,),
            scratch_shapes=[
                pltpu.VMEM((GROUP, 1, TOKENS), F32),
                pltpu.VMEM((HEADS_STEP, stored + FRESH, TOKENS), BF16),
            ],
        )(index, logical, starts, query, cache, fresh, peaks)
        parts = exchange(sent, "kv")
        parts, out_proj = lax.optimization_barrier((parts, out_proj))
    with jax.named_scope("combine"):
        attended = call(
            functools.partial(combine_kernel, count, MASS_UNIT),
            jax.ShapeDtypeStruct((count, half, TOKENS), BF16),
            [IN_VMEM],
            IN_VMEM,
        )(parts)
        return exchange(attended, "kv").reshape(GROUP * HEAD_DIM, TOKENS), out_proj


def near_attention(parts, caches, logical, starts, holders):
    count = lax.axis_size("kv")
    rows = SEG_LEN // count
    half = HEAD_DIM // 2
    with jax.named_scope("queries"):
        query, fresh = call(
            functools.partial(finish_crossed_kernel, count),
            (
                jax.ShapeDtypeStruct((RING, half, TOKENS), BF16),
                jax.ShapeDtypeStruct((2, 4 * rows, HEAD_DIM), BF16),
            ),
            [IN_VMEM],
            (IN_VMEM, IN_VMEM),
        )(parts)
        fresh = (fresh,) + tuple(around_y(fresh, step) for step in (1, -1, 2))
        query = over_z(query).reshape(2, HEAD_DIM, TOKENS)
    with jax.named_scope("peaks"):
        peaks = call(
            functools.partial(near_peak_kernel, rows),
            jax.ShapeDtypeStruct((RING, 8, TOKENS), F32),
            [IN_SMEM] * 3 + [IN_VMEM] * (1 + 2 * RING),
            IN_VMEM,
        )(holders, logical, starts, query, *caches, *fresh)
        peaks = over_z(peaks)
    with jax.named_scope("attend"):
        stored = RING * caches[0].shape[1]
        sent = call(
            functools.partial(near_attend_kernel, rows),
            jax.ShapeDtypeStruct((RING, 6 * 8, TOKENS), jnp.int32),
            [IN_SMEM] * 3
            + [pl.BlockSpec((1, HEAD_DIM, TOKENS), lambda h: (h, 0, 0))]
            + [IN_VMEM] * (2 * RING + 1),
            pl.BlockSpec((2, 6 * 8, TOKENS), lambda h: (h, 0, 0)),
            grid=(2,),
            scratch_shapes=[pltpu.VMEM((stored + 4 * RING * rows, TOKENS), BF16)],
        )(holders, logical, starts, query, *caches, *fresh, peaks)
        parts = over_z(sent)
    with jax.named_scope("combine"):
        attended = call(
            functools.partial(combine_kernel, RING, NEAR_MASS_UNIT),
            jax.ShapeDtypeStruct((count, half, TOKENS), BF16),
            [IN_VMEM],
            IN_VMEM,
        )(parts)
        return exchange(attended, "kv")


def layer(
    which, x, mine, gain, query_proj, kv_proj, out_proj, keys, values, logical, starts, index, core,
    squares=None,
):
    count = lax.axis_size("kv")
    peers = lax.axis_size("tp")
    rows = SEG_LEN // count
    half = HEAD_DIM // 2
    width = query_proj.shape[0]
    share = TOKENS // 2
    part = share // peers
    with jax.named_scope("project"):
        shape = jax.ShapeDtypeStruct((count, 7 * 8, TOKENS), jnp.int32)
        if which == 0:
            squares = exchange(squares, "kv")
            all_logical = squares[:, 1, 0 : logical.shape[0]].astype(jnp.int32)
            sent = call(
                functools.partial(first_project_kernel, count), shape, [IN_VMEM] * 5, IN_VMEM
            )(x, squares, gain, query_proj, kv_proj)
        else:
            sent = call(
                functools.partial(project_kernel, count),
                shape,
                [IN_SMEM] + [IN_VMEM] * 5,
                IN_VMEM,
                scratch_shapes=[pltpu.VMEM((TOKENS, width + 128), BF16)],
            )(core, x[0], x[1], gain, query_proj, kv_proj)
        if which == 0:
            sent, keys = lax.optimization_barrier((sent, keys))
        parts = exchange(sent, "kv")
    later = None
    if which == 0:
        now, later = values(keys)
        attended, out_proj = split_attention(parts, now, logical, starts, index, out_proj)
        kernel, scratch = output_kernel, []
    else:
        attended = near_attention(parts, keys, logical, starts, index)
        kernel, scratch = crossed_output_kernel, [pltpu.VMEM((GROUP * HEAD_DIM, TOKENS), BF16)]
    with jax.named_scope("output"):
        keep, send = call(
            kernel,
            (jax.ShapeDtypeStruct((share, width), F32),) * 2,
            [IN_SMEM] + [IN_VMEM] * 2,
            (IN_VMEM, IN_VMEM),
            scratch_shapes=[pltpu.VMEM((TOKENS, width), F32)] + scratch,
        )(core, attended, out_proj)
        half_sum = call(
            add_kernel,
            jax.ShapeDtypeStruct((share, width), F32),
            [IN_VMEM] * 2,
            IN_VMEM,
        )(keep, swap(send))
        if which == 0:
            half_sum, later = lax.optimization_barrier((half_sum, later))
            sides = tuple(around_y(later, step) for step in (1, -1, 2))
        parts = exchange(half_sum.reshape(peers, part, width), "tp")
    with jax.named_scope("residual"):
        if which == LAYERS - 1:
            produced = call(
                last_residual_kernel,
                jax.ShapeDtypeStruct((peers, part, width), BF16),
                [IN_VMEM] * 2,
                IN_VMEM,
            )(parts, mine)
            mine = None
        else:
            mine, squares = call(
                functools.partial(residual_kernel, count),
                (
                    jax.ShapeDtypeStruct((part, width), BF16),
                    jax.ShapeDtypeStruct((count, 8, 128), F32),
                ),
                [IN_VMEM] * 2,
                (IN_VMEM, IN_VMEM),
            )(parts, mine)
            squares = exchange(squares, "kv")
            holders = near_holders(index[0])
            produced = call(
                spread_kernel,
                jax.ShapeDtypeStruct((peers, part, width + 128), BF16),
                [IN_VMEM] * 2,
                IN_VMEM,
            )(squares, mine)
        own = exchange(produced, "tp").reshape(share, -1)
        if which == 0:
            later = ((later,) + sides, all_logical[holders].reshape(-1), holders)
        return (own, swap(own)), mine, later


def per_device(
    segments_in, gain, query_weight, kv_weight, out_weight, kv_cache, block_logical, segment_block
):
    width = segments_in.shape[2]
    core = lax.axis_index("section")
    core_at = core.astype(jnp.int32)[None]
    index = lax.axis_index("kv").astype(jnp.int32)[None]
    per_core = GROUP * HEAD_DIM
    share = TOKENS // 2

    x = segments_in.reshape(TOKENS, width)
    count = lax.axis_size("kv")
    blocks = block_logical.shape[0]
    squares = call(
        functools.partial(squares_kernel, count),
        jax.ShapeDtypeStruct((count, 8, TOKENS), F32),
        [IN_VMEM] * 2,
        IN_VMEM,
    )(x, jnp.pad(block_logical.astype(F32), (0, TOKENS - blocks))[None])
    squares, query_weight, kv_weight, out_weight = lax.optimization_barrier(
        (squares, query_weight, kv_weight, out_weight)
    )

    def pick(which):
        at = which * per_core
        kv_at = which * HEAD_DIM
        return (
            lax.dynamic_slice_in_dim(query_weight[0], at, per_core, 1),
            lax.dynamic_slice_in_dim(kv_weight[0], kv_at, HEAD_DIM, 2).reshape(width, -1),
            lax.dynamic_slice_in_dim(out_weight[0], at, per_core, 0),
            gain,
        )

    kept = pick(core)
    received = tuple(swap(v) for v in pick(1 - core))
    part = share // lax.axis_size("tp")
    mine = lax.dynamic_slice_in_dim(x, core * share + lax.axis_index("tp") * part, part, 0)
    params = [
        [jnp.where(core == which, here, other) for here, other in zip(kept, received)]
        for which in range(LAYERS)
    ]

    def cut_cache(cache):
        def cut(which):
            return tuple(
                lax.dynamic_slice_in_dim(cache[0, :, kind], which * HEAD_DIM, HEAD_DIM, 1)
                for kind in range(2)
            )

        pairs = [(here, swap(there)) for here, there in zip(cut(core), cut(1 - core))]
        return tuple(
            call(
                cache_kernel,
                jax.ShapeDtypeStruct((2,) + pairs[0][0].shape, BF16),
                [IN_VMEM] * 2,
                IN_VMEM,
            )(*(jnp.where(core == which, here, other) for here, other in pairs))
            for which in range(LAYERS)
        )

    query_proj, kv_proj, out_proj, gain_row = params[0]
    first, mine, (caches, numbers, holders) = layer(
        0, x, mine, gain_row, query_proj, kv_proj, out_proj, kv_cache, cut_cache,
        block_logical, segment_block, index, core_at, squares,
    )
    query_proj, kv_proj, out_proj, gain_row = params[1]
    second, _, _ = layer(
        1, first, mine, gain_row, query_proj, kv_proj, out_proj, caches, None,
        numbers, segment_block, holders, core_at,
    )
    outputs = first + second
    result = call(
        choose_kernel,
        jax.ShapeDtypeStruct((TOKENS, width), BF16),
        [IN_SMEM] + [IN_VMEM] * 4,
        IN_VMEM,
    )(core_at, *outputs)
    return result.reshape(1, NSEG, SEG_LEN, width)


def solution(mesh):
    placed = (
        P(None, None, "kv"),
        P("section", "kv"),
        P("section", "kv", "tp"),
        P("section", "kv", None, "tp"),
        P("section", "tp", "kv"),
        P("section", "kv", None, "tp"),
        P("kv"),
        P(),
    )
    return jax.shard_map(
        per_device,
        mesh=mesh,
        in_specs=placed,
        out_specs=P("section", None, None, "kv"),
        check_vma=False,
    )
```

```python
import functools
import math

import jax
import jax.numpy as jnp
from jax import lax
from jax.experimental import pallas as pl
from jax.experimental.pallas import tpu as pltpu
from jax.sharding import PartitionSpec as P

D = 8192
HEAD_DIM = 128
BLOCK = 128
NSEG = 3
SEG_LEN = 128
TOKENS = NSEG * SEG_LEN
GROUP = 8
LAYERS = 2
EPSILON = 1e-05
CLOSED = -1e30
FRESH = 128
RANGE = 520000.0
MIDDLE = 524288
LEVELS = 2048
MASS_UNIT = 262144.0
NEAR_MASS_UNIT = 65536.0
HEADS_STEP = 4
SCALE = math.log2(math.e) / math.sqrt(HEAD_DIM)
F32 = jnp.float32
BF16 = jnp.bfloat16
VMEM_BYTES = 48 * 1024 * 1024


def call(kernel, out_shape, in_specs, out_specs, **rest):
    return pl.pallas_call(
        kernel,
        out_shape=out_shape,
        in_specs=in_specs,
        out_specs=out_specs,
        compiler_params=pltpu.CompilerParams(vmem_limit_bytes=VMEM_BYTES),
        **rest,
    )


IN_VMEM = pl.BlockSpec(memory_space=pltpu.VMEM)
IN_SMEM = pl.BlockSpec(memory_space=pltpu.SMEM)


RING = 4


def encode(block):
    top = jnp.maximum(jnp.max(jnp.abs(block), axis=0, keepdims=True), 1e-30)
    level = jnp.ceil(jnp.log2(top) * 16.0)
    value = jnp.round(block * (jnp.exp2(level * (-1.0 / 16.0)) * RANGE))
    return value.astype(jnp.int32) + MIDDLE, level.astype(jnp.int32)


def level_factor(level):
    return jnp.exp2(level.astype(F32) * (1.0 / 16.0)) * (1.0 / RANGE)


def pack(value):
    part = [value[8 * at : 8 * at + 8] for at in range(8)]
    lows = [
        part[5] & 0xFFF,
        (part[5] >> 12) | ((part[6] & 0xF) << 8),
        (part[6] >> 4) & 0xFFF,
        (part[6] >> 16) | ((part[7] & 0xFF) << 4),
        part[7] >> 8,
    ]
    return [(part[at] << 12) | lows[at] for at in range(5)]


def top_bits(word):
    return lax.shift_right_logical(word, jnp.int32(12))


def unpack(words):
    lows = [word & 0xFFF for word in words]
    part = [top_bits(word) for word in words]
    part.append(lows[0] | ((lows[1] & 0xFF) << 12))
    part.append((lows[1] >> 8) | (lows[2] << 4) | ((lows[3] & 0xF) << 16))
    part.append((lows[3] >> 4) | (lows[4] << 8))
    return (jnp.concatenate(part, axis=0) - MIDDLE).astype(F32)


def first_rows(rows, count=8):
    place = lax.broadcasted_iota(jnp.int32, (count, rows[0].shape[1]), 0)
    filled = jnp.zeros_like(place)
    for number, row in enumerate(rows):
        filled = jnp.where(place == number, row, filled)
    return filled


def square_rows(x):
    squares = jnp.sum(x * x, axis=1, keepdims=True)
    squares = jnp.broadcast_to(squares, (x.shape[0], 128))
    missing = -x.shape[0] % 128
    if missing:
        squares = jnp.concatenate([squares, jnp.zeros((missing, 128), F32)], axis=0)
    return squares.T[0:8]


def norm_columns(parts_ref):
    total = parts_ref[0]
    for peer in range(1, parts_ref.shape[0]):
        total = total + parts_ref[peer]
    factor = lax.rsqrt(total[0:1] / D + EPSILON)
    return jnp.broadcast_to(factor, (128, factor.shape[1])).T


def squares_kernel(count, x_ref, logical_ref, out_ref):
    rows = square_rows(x_ref[...].astype(F32))
    row = lax.broadcasted_iota(jnp.int32, rows.shape, 0)
    rows = jnp.where(row == 0, rows, logical_ref[...])
    for peer in range(count):
        out_ref[peer] = rows


def cache_kernel(keys_ref, values_ref, out_ref):
    out_ref[0] = keys_ref[...]
    for block in range(values_ref.shape[0] // BLOCK):
        at = slice(block * BLOCK, (block + 1) * BLOCK)
        out_ref[1, at, :] = values_ref[at, :].T


def first_project_kernel(count, x_ref, squares_ref, gain_ref, query_ref, kv_ref, out_ref):
    factor = norm_columns(squares_ref)[:, 0:1]
    normed = (x_ref[...].astype(F32) * factor * gain_ref[...]).astype(BF16)
    project(count, normed, query_ref, kv_ref, out_ref, True)


def project_kernel(count, core_ref, own_ref, other_ref, gain_ref, query_ref, kv_ref, out_ref, x_ref):
    share = TOKENS // 2
    width = gain_ref.shape[1]
    x_ref[pl.ds(core_ref[0] * share, share), :] = own_ref[...]
    x_ref[pl.ds((1 - core_ref[0]) * share, share), :] = other_ref[...]
    thirds = x_ref[:, width : width + 128].astype(F32)
    factor = thirds[:, 0:1] + thirds[:, 1:2] + thirds[:, 2:3]
    normed = (x_ref[:, 0:width].astype(F32) * factor * gain_ref[...]).astype(BF16)
    project(count, normed, query_ref, kv_ref, out_ref, True)


def project(count, scaled, query_ref, kv_ref, out_ref, crossed=False):
    half = HEAD_DIM // 2
    columns = query_ref.shape[1]
    rows = SEG_LEN // count
    fresh = jnp.dot(scaled, kv_ref[...], preferred_element_type=F32)
    for start in range(0, columns, 256):
        part = jnp.dot(scaled, query_ref[:, start : start + 256], preferred_element_type=F32)
        turned = part.T
        for piece in range(256 // half):
            at = start // half + piece
            peer = at % RING * RING + at // RING if crossed else at
            block = turned[piece * half : (piece + 1) * half]
            query, query_level = encode(block)
            words = pack(query)
            kinds = []
            for kind in range(2):
                lanes = slice(kind * HEAD_DIM, (kind + 1) * HEAD_DIM)
                block = jnp.concatenate(
                    [
                        fresh[seg * SEG_LEN + peer * rows : seg * SEG_LEN + (peer + 1) * rows, lanes]
                        for seg in range(NSEG)
                    ],
                    axis=1,
                )
                kinds.append(encode(block))
            levels = first_rows([query_level, kinds[0][1], kinds[1][1]]) + LEVELS
            words.append((kinds[0][0] << 12) | levels)
            words.append(kinds[1][0] << 12)
            for at, word in enumerate(words):
                out_ref[peer, 8 * at : 8 * at + 8, :] = word


def add_projection(count, parts_ref):
    half = HEAD_DIM // 2
    rows = SEG_LEN // count
    query = jnp.zeros((half, TOKENS), F32)
    fresh = [jnp.zeros((rows, TOKENS), F32) for _ in range(2)]
    for peer in range(count):
        words = [parts_ref[peer, 8 * at : 8 * at + 8, :] for at in range(7)]
        factors = level_factor((words[5] & 0xFFF) - LEVELS)
        query = query + unpack(words[0:5]) * factors[0:1]
        for kind in range(2):
            value = (top_bits(words[5 + kind]) - MIDDLE).astype(F32)
            fresh[kind] = fresh[kind] + value * factors[1 + kind : 2 + kind]
    return query, fresh


def finish_projection_kernel(count, parts_ref, query_out, fresh_out):
    rows = SEG_LEN // count
    query, fresh = add_projection(count, parts_ref)
    query = query.astype(BF16)
    for peer in range(count):
        query_out[peer] = query
    filler = jnp.zeros((FRESH - NSEG * rows, HEAD_DIM), F32)
    for kind in range(2):
        pieces = [
            fresh[kind][:, seg * SEG_LEN : (seg + 1) * SEG_LEN] for seg in range(NSEG)
        ]
        fresh_out[kind] = jnp.concatenate(pieces + [filler], axis=0).astype(BF16)


def finish_crossed_kernel(count, parts_ref, query_out, fresh_out):
    rows = SEG_LEN // count
    query, fresh = add_projection(count, parts_ref)
    query = query.astype(BF16)
    for peer in range(RING):
        query_out[peer] = query
    filler = jnp.zeros((rows, HEAD_DIM), F32)
    for kind in range(2):
        pieces = [
            fresh[kind][:, seg * SEG_LEN : (seg + 1) * SEG_LEN] for seg in range(NSEG)
        ]
        fresh_out[kind] = jnp.concatenate(pieces + [filler], axis=0).astype(BF16)


def near_mask(rows, slot_ref, seg):
    key_row = lax.broadcasted_iota(jnp.int32, (4 * rows, SEG_LEN), 0)
    token = lax.broadcasted_iota(jnp.int32, (4 * rows, SEG_LEN), 1)
    local = key_row - seg * rows
    inside = (local >= 0) & (local < rows)
    return jnp.concatenate(
        [
            jnp.where(inside & (local + slot_ref[slot] * rows <= token), 1.0, 0.0)
            for slot in range(RING)
        ],
        axis=0,
    ) > 0.5


def near_peak_kernel(rows, slot_ref, logical_ref, start_ref, query_ref, *refs):
    caches, fresh, out_ref = refs[0:RING], refs[RING : 2 * RING], refs[2 * RING]
    blocks = caches[0].shape[1] // BLOCK
    found = []
    for head in range(query_ref.shape[0]):
        query = query_ref[head]
        keys = jnp.concatenate([part[0] for part in fresh], axis=0)
        scores = jnp.dot(keys, query, preferred_element_type=F32)
        tops = []
        for seg in range(NSEG):
            lanes = slice(seg * SEG_LEN, (seg + 1) * SEG_LEN)
            masked = jnp.where(near_mask(rows, slot_ref, seg), scores[:, lanes], CLOSED)
            tops.append(jnp.max(masked.reshape(-1, 8, SEG_LEN), axis=0))
        for number in range(RING * blocks):
            block = number % blocks
            keys = caches[number // blocks][0, block * BLOCK : (block + 1) * BLOCK, :]
            scores = jnp.dot(keys, query, preferred_element_type=F32)
            top = jnp.max(scores.reshape(BLOCK // 8, 8, TOKENS), axis=0)
            for seg in range(NSEG):
                lanes = slice(seg * SEG_LEN, (seg + 1) * SEG_LEN)
                is_open = logical_ref[number] < start_ref[seg]
                tops[seg] = jnp.maximum(tops[seg], jnp.where(is_open, top[:, lanes], CLOSED))
        found.append(
            jnp.concatenate([jnp.max(top, axis=0, keepdims=True) for top in tops], axis=1)
        )
    found = jnp.concatenate(found * 4, axis=0)
    for peer in range(RING):
        out_ref[peer] = found


def near_attend_kernel(rows, slot_ref, logical_ref, start_ref, query_ref, *refs):
    caches, fresh = refs[0:RING], refs[RING : 2 * RING]
    peaks_ref, out_ref, weights = refs[2 * RING :]
    blocks = caches[0].shape[1] // BLOCK
    stored = RING * blocks * BLOCK
    half = HEAD_DIM // 2
    head = pl.program_id(0)
    query = query_ref[0]
    peak = peaks_ref[0]
    for peer in range(1, RING):
        peak = jnp.maximum(peak, peaks_ref[peer])
    peak = jnp.where(head == 0, peak[0:1], peak[1:2])
    keys = jnp.concatenate([part[0] for part in fresh], axis=0)
    scores = jnp.dot(keys, query, preferred_element_type=F32)
    masses = []
    for seg in range(NSEG):
        lanes = slice(seg * SEG_LEN, (seg + 1) * SEG_LEN)
        weight = jnp.exp2((scores[:, lanes] - peak[:, lanes]) * SCALE)
        weight = jnp.where(near_mask(rows, slot_ref, seg), weight, 0.0)
        weights[stored : stored + 4 * RING * rows, lanes] = weight.astype(BF16)
        masses.append(jnp.sum(weight.reshape(-1, 8, SEG_LEN), axis=0))
    for number in range(RING * blocks):
        block = number % blocks
        keys = caches[number // blocks][0, block * BLOCK : (block + 1) * BLOCK, :]
        scores = jnp.dot(keys, query, preferred_element_type=F32)
        for seg in range(NSEG):
            lanes = slice(seg * SEG_LEN, (seg + 1) * SEG_LEN)
            is_open = logical_ref[number] < start_ref[seg]
            offset = jnp.where(is_open, peak[:, lanes], -CLOSED)
            weight = jnp.exp2((scores[:, lanes] - offset) * SCALE)
            weights[number * BLOCK : (number + 1) * BLOCK, lanes] = weight.astype(BF16)
            masses[seg] = masses[seg] + jnp.sum(weight.reshape(BLOCK // 8, 8, SEG_LEN), axis=0)
    turned = [
        cache[1, block * BLOCK : (block + 1) * BLOCK, :] for cache in caches for block in range(blocks)
    ]
    turned.append(jnp.concatenate([part[1] for part in fresh], axis=0).T)
    sums = jnp.dot(jnp.concatenate(turned, axis=1), weights[...], preferred_element_type=F32)
    mass = jnp.concatenate([jnp.sum(part, axis=0, keepdims=True) for part in masses], axis=1)
    mass = jnp.round(mass * NEAR_MASS_UNIT).astype(jnp.int32)
    for piece in range(2):
        value, level = encode(sums[piece * half : (piece + 1) * half])
        for at, word in enumerate(pack(value) + [first_rows([level, mass])]):
            out_ref[piece, 8 * at : 8 * at + 8, :] = word


def fresh_mask(rows, index_ref, seg):
    key_row = lax.broadcasted_iota(jnp.int32, (FRESH, SEG_LEN), 0)
    token = lax.broadcasted_iota(jnp.int32, (FRESH, SEG_LEN), 1)
    local = key_row - seg * rows
    return (local >= 0) & (local < rows) & (local + index_ref[0] * rows <= token)


def peak_kernel(
    rows, index_ref, logical_ref, start_ref, query_ref, cache_ref, fresh_ref, out_ref, peaks
):
    blocks = cache_ref.shape[1] // BLOCK
    heads = query_ref.shape[0]
    step = pl.program_id(0)
    for head in range(heads):
        query = query_ref[head]
        scores = jnp.dot(fresh_ref[0], query, preferred_element_type=F32)
        tops = []
        for seg in range(NSEG):
            lanes = slice(seg * SEG_LEN, (seg + 1) * SEG_LEN)
            masked = jnp.where(fresh_mask(rows, index_ref, seg), scores[:, lanes], CLOSED)
            tops.append(jnp.max(masked.reshape(FRESH // 8, 8, SEG_LEN), axis=0))
        for block in range(blocks):
            at = slice(block * BLOCK, (block + 1) * BLOCK)
            scores = jnp.dot(cache_ref[0, at, :], query, preferred_element_type=F32)
            top = jnp.max(scores.reshape(BLOCK // 8, 8, TOKENS), axis=0)
            for seg in range(NSEG):
                lanes = slice(seg * SEG_LEN, (seg + 1) * SEG_LEN)
                is_open = logical_ref[block] < start_ref[seg]
                tops[seg] = jnp.maximum(tops[seg], jnp.where(is_open, top[:, lanes], CLOSED))
        peaks[step * heads + head] = jnp.concatenate(
            [jnp.max(top, axis=0, keepdims=True) for top in tops], axis=1
        )

    @pl.when(step == pl.num_programs(0) - 1)
    def _():
        found = jnp.concatenate([peaks[head] for head in range(GROUP)], axis=0)
        for peer in range(out_ref.shape[0]):
            out_ref[peer] = found


def attend_kernel(
    rows, index_ref, logical_ref, start_ref, query_ref, cache_ref, fresh_ref, peaks_ref,
    out_ref, peaks, weights,
):
    blocks = cache_ref.shape[1] // BLOCK
    stored = blocks * BLOCK
    half = HEAD_DIM // 2
    heads = query_ref.shape[0]
    step = pl.program_id(0)

    @pl.when(step == 0)
    def _():
        top = peaks_ref[0]
        for peer in range(1, peaks_ref.shape[0]):
            top = jnp.maximum(top, peaks_ref[peer])
        for head in range(GROUP):
            peaks[head] = top[head : head + 1]

    turned = [cache_ref[1, block * BLOCK : (block + 1) * BLOCK, :] for block in range(blocks)]
    turned = jnp.concatenate(turned + [fresh_ref[1].T], axis=1)
    for head in range(heads):
        query = query_ref[head]
        peak = peaks[step * heads + head]
        scores = jnp.dot(fresh_ref[0], query, preferred_element_type=F32)
        masses = []
        for seg in range(NSEG):
            lanes = slice(seg * SEG_LEN, (seg + 1) * SEG_LEN)
            weight = jnp.exp2((scores[:, lanes] - peak[:, lanes]) * SCALE)
            weight = jnp.where(fresh_mask(rows, index_ref, seg), weight, 0.0)
            weights[head, stored : stored + FRESH, lanes] = weight.astype(BF16)
            masses.append(jnp.sum(weight.reshape(FRESH // 8, 8, SEG_LEN), axis=0))
        for block in range(blocks):
            at = slice(block * BLOCK, (block + 1) * BLOCK)
            scores = jnp.dot(cache_ref[0, at, :], query, preferred_element_type=F32)
            for seg in range(NSEG):
                lanes = slice(seg * SEG_LEN, (seg + 1) * SEG_LEN)
                is_open = logical_ref[block] < start_ref[seg]
                offset = jnp.where(is_open, peak[:, lanes], -CLOSED)
                weight = jnp.exp2((scores[:, lanes] - offset) * SCALE)
                weights[head, at, lanes] = weight.astype(BF16)
                masses[seg] = masses[seg] + jnp.sum(
                    weight.reshape(BLOCK // 8, 8, SEG_LEN), axis=0
                )
        sums = jnp.dot(turned, weights[head], preferred_element_type=F32)
        mass = jnp.concatenate(
            [jnp.sum(part, axis=0, keepdims=True) for part in masses], axis=1
        )
        mass = jnp.round(mass * MASS_UNIT).astype(jnp.int32)
        for piece in range(2):
            value, level = encode(sums[piece * half : (piece + 1) * half])
            for at, word in enumerate(pack(value) + [first_rows([level, mass])]):
                out_ref[2 * head + piece, 8 * at : 8 * at + 8, :] = word


def combine_kernel(count, unit, parts_ref, out_ref):
    half = HEAD_DIM // 2
    mass = jnp.zeros((1, TOKENS), F32)
    sums = jnp.zeros((half, TOKENS), F32)
    for peer in range(count):
        words = [parts_ref[peer, 8 * at : 8 * at + 8, :] for at in range(6)]
        mass = mass + words[5][1:2].astype(F32) * (1.0 / unit)
        sums = sums + unpack(words[0:5]) * level_factor(words[5][0:1])
    attended = (sums / mass).astype(BF16)
    for peer in range(out_ref.shape[0]):
        out_ref[peer] = attended


def output_kernel(core_ref, attended_ref, weight_ref, keep_ref, send_ref, scratch):
    project_output(core_ref, attended_ref, weight_ref, keep_ref, send_ref, scratch)


def project_output(core_ref, attended_ref, weight_ref, keep_ref, send_ref, scratch):
    share = TOKENS // 2
    scratch[...] = lax.dot_general(
        attended_ref[...], weight_ref[...], (((0,), (0,)), ((), ())), preferred_element_type=F32
    )
    keep_ref[...] = scratch[pl.ds(core_ref[0] * share, share), :]
    send_ref[...] = scratch[pl.ds((1 - core_ref[0]) * share, share), :]


def crossed_output_kernel(core_ref, parts_ref, weight_ref, keep_ref, send_ref, scratch, attended):
    half = HEAD_DIM // 2
    for at in range(parts_ref.shape[0]):
        attended[at * half : (at + 1) * half, :] = parts_ref[at % RING * RING + at // RING]
    project_output(core_ref, attended, weight_ref, keep_ref, send_ref, scratch)


def add_kernel(keep_ref, received_ref, out_ref):
    out_ref[...] = keep_ref[...] + received_ref[...]


def add_residual(parts_ref, x_ref):
    total = parts_ref[0]
    for peer in range(1, parts_ref.shape[0]):
        total = total + parts_ref[peer]
    return (x_ref[...].astype(F32) + total).astype(BF16)


def residual_kernel(count, parts_ref, x_ref, out_ref, squares_ref):
    produced = add_residual(parts_ref, x_ref)
    out_ref[...] = produced
    rows = square_rows(produced.astype(F32))
    for peer in range(count):
        squares_ref[peer] = rows


def last_residual_kernel(parts_ref, x_ref, out_ref):
    produced = add_residual(parts_ref, x_ref)
    for peer in range(out_ref.shape[0]):
        out_ref[peer] = produced


def spread_kernel(squares_ref, x_ref, out_ref):
    tokens, width = x_ref.shape
    factor = norm_columns(squares_ref)[0:tokens]
    first = factor.astype(BF16).astype(F32)
    second = (factor - first).astype(BF16).astype(F32)
    lane = lax.broadcasted_iota(jnp.int32, factor.shape, 1)
    thirds = jnp.where(lane == 0, first, jnp.where(lane == 1, second, factor - first - second))
    for peer in range(out_ref.shape[0]):
        out_ref[peer, :, 0:width] = x_ref[...]
        out_ref[peer, :, width : width + 128] = thirds.astype(BF16)


def choose_kernel(core_ref, own0_ref, other0_ref, own1_ref, other1_ref, out_ref):
    share = TOKENS // 2
    width = out_ref.shape[1]
    first = core_ref[0] == 0
    at = pl.ds(core_ref[0] * share, share)
    out_ref[at, :] = jnp.where(first, own0_ref[:, 0:width], own1_ref[...])
    at = pl.ds((1 - core_ref[0]) * share, share)
    out_ref[at, :] = jnp.where(first, other0_ref[:, 0:width], other1_ref[...])


def exchange(value, axes):
    return lax.all_to_all(value, axes, 0, 0, tiled=True)


def swap(value):
    return lax.ppermute(value, "section", [(0, 1), (1, 0)])


def around_y(value, step):
    pairs = []
    for kv in range(RING * RING):
        z, y = divmod(kv, RING)
        pairs.append((kv, z * RING + (y + step) % RING))
    return lax.ppermute(value, "kv", pairs)


def over_z(value):
    groups = [[z * RING + y for z in range(RING)] for y in range(RING)]
    return lax.all_to_all(value, "kv", 0, 0, tiled=True, axis_index_groups=groups)


def near_holders(index):
    offsets = jnp.array([0, -1, 1, 2], jnp.int32)
    return index // RING * RING + (index % RING + offsets) % RING


def split_attention(parts, cache, logical, starts, index, out_proj):
    count = lax.axis_size("kv")
    rows = SEG_LEN // count
    half = HEAD_DIM // 2
    with jax.named_scope("queries"):
        query, fresh = call(
            functools.partial(finish_projection_kernel, count),
            (
                jax.ShapeDtypeStruct((count, half, TOKENS), BF16),
                jax.ShapeDtypeStruct((2, FRESH, HEAD_DIM), BF16),
            ),
            [IN_VMEM],
            (IN_VMEM, IN_VMEM),
        )(parts)
        query = exchange(query, "kv").reshape(GROUP, HEAD_DIM, TOKENS)
    stored = cache.shape[1]
    by_head = [
        IN_SMEM,
        IN_SMEM,
        IN_SMEM,
        pl.BlockSpec((HEADS_STEP, HEAD_DIM, TOKENS), lambda h: (h, 0, 0)),
        pl.BlockSpec((2, stored, HEAD_DIM), lambda h: (0, 0, 0)),
    ]
    whole_fresh = pl.BlockSpec((2, FRESH, HEAD_DIM), lambda h: (0, 0, 0))
    whole_peaks = pl.BlockSpec((count, GROUP, TOKENS), lambda h: (0, 0, 0))
    with jax.named_scope("peaks"):
        peaks = call(
            functools.partial(peak_kernel, rows),
            jax.ShapeDtypeStruct((count, GROUP, TOKENS), F32),
            by_head + [whole_fresh],
            whole_peaks,
            grid=(GROUP // HEADS_STEP,),
            scratch_shapes=[pltpu.VMEM((GROUP, 1, TOKENS), F32)],
        )(index, logical, starts, query, cache, fresh)
        peaks = exchange(peaks, "kv")
    with jax.named_scope("attend"):
        sent = call(
            functools.partial(attend_kernel, rows),
            jax.ShapeDtypeStruct((count, 6 * 8, TOKENS), jnp.int32),
            by_head + [whole_fresh, whole_peaks],
            pl.BlockSpec((2 * HEADS_STEP, 6 * 8, TOKENS), lambda h: (h, 0, 0)),
            grid=(GROUP // HEADS_STEP,),
            scratch_shapes=[
                pltpu.VMEM((GROUP, 1, TOKENS), F32),
                pltpu.VMEM((HEADS_STEP, stored + FRESH, TOKENS), BF16),
            ],
        )(index, logical, starts, query, cache, fresh, peaks)
        parts = exchange(sent, "kv")
        parts, out_proj = lax.optimization_barrier((parts, out_proj))
    with jax.named_scope("combine"):
        attended = call(
            functools.partial(combine_kernel, count, MASS_UNIT),
            jax.ShapeDtypeStruct((count, half, TOKENS), BF16),
            [IN_VMEM],
            IN_VMEM,
        )(parts)
        return exchange(attended, "kv").reshape(GROUP * HEAD_DIM, TOKENS), out_proj


def near_attention(parts, caches, logical, starts, holders):
    count = lax.axis_size("kv")
    rows = SEG_LEN // count
    half = HEAD_DIM // 2
    with jax.named_scope("queries"):
        query, fresh = call(
            functools.partial(finish_crossed_kernel, count),
            (
                jax.ShapeDtypeStruct((RING, half, TOKENS), BF16),
                jax.ShapeDtypeStruct((2, 4 * rows, HEAD_DIM), BF16),
            ),
            [IN_VMEM],
            (IN_VMEM, IN_VMEM),
        )(parts)
        fresh = (fresh,) + tuple(around_y(fresh, step) for step in (1, -1, 2))
        query = over_z(query).reshape(2, HEAD_DIM, TOKENS)
    with jax.named_scope("peaks"):
        peaks = call(
            functools.partial(near_peak_kernel, rows),
            jax.ShapeDtypeStruct((RING, 8, TOKENS), F32),
            [IN_SMEM] * 3 + [IN_VMEM] * (1 + 2 * RING),
            IN_VMEM,
        )(holders, logical, starts, query, *caches, *fresh)
        peaks = over_z(peaks)
    with jax.named_scope("attend"):
        stored = RING * caches[0].shape[1]
        sent = call(
            functools.partial(near_attend_kernel, rows),
            jax.ShapeDtypeStruct((RING, 6 * 8, TOKENS), jnp.int32),
            [IN_SMEM] * 3
            + [pl.BlockSpec((1, HEAD_DIM, TOKENS), lambda h: (h, 0, 0))]
            + [IN_VMEM] * (2 * RING + 1),
            pl.BlockSpec((2, 6 * 8, TOKENS), lambda h: (h, 0, 0)),
            grid=(2,),
            scratch_shapes=[pltpu.VMEM((stored + 4 * RING * rows, TOKENS), BF16)],
        )(holders, logical, starts, query, *caches, *fresh, peaks)
        parts = over_z(sent)
    with jax.named_scope("combine"):
        attended = call(
            functools.partial(combine_kernel, RING, NEAR_MASS_UNIT),
            jax.ShapeDtypeStruct((count, half, TOKENS), BF16),
            [IN_VMEM],
            IN_VMEM,
        )(parts)
        return exchange(attended, "kv")


def layer(
    which, x, mine, gain, query_proj, kv_proj, out_proj, keys, values, logical, starts, index, core,
    squares=None,
):
    count = lax.axis_size("kv")
    peers = lax.axis_size("tp")
    rows = SEG_LEN // count
    half = HEAD_DIM // 2
    width = query_proj.shape[0]
    share = TOKENS // 2
    part = share // peers
    with jax.named_scope("project"):
        shape = jax.ShapeDtypeStruct((count, 7 * 8, TOKENS), jnp.int32)
        if which == 0:
            squares, keys = lax.optimization_barrier((squares, keys))
            now, later = values(keys)
            ahead = (around_y(now, 1), around_y(now, -1))
            squares = exchange(squares, "kv")
            all_logical = squares[:, 1, 0 : logical.shape[0]].astype(jnp.int32)
            sent = call(
                functools.partial(first_project_kernel, count), shape, [IN_VMEM] * 5, IN_VMEM
            )(x, squares, gain, query_proj, kv_proj)
        else:
            sent = call(
                functools.partial(project_kernel, count),
                shape,
                [IN_SMEM] + [IN_VMEM] * 5,
                IN_VMEM,
                scratch_shapes=[pltpu.VMEM((TOKENS, width + 128), BF16)],
            )(core, x[0], x[1], gain, query_proj, kv_proj)
        parts = exchange(sent, "kv")
    if which == 0:
        holders = near_holders(index[0])
        numbers = all_logical[holders].reshape(-1)
        parts, before, after = lax.optimization_barrier((parts, ahead[0][0], ahead[1][1]))
        across = jnp.stack([around_y(before, 1), around_y(after, -1)])
        attended = near_attention(parts, (now,) + ahead + (across,), numbers, starts, holders)
    else:
        later = None
        attended = near_attention(parts, keys, logical, starts, index)
    kernel, scratch = crossed_output_kernel, [pltpu.VMEM((GROUP * HEAD_DIM, TOKENS), BF16)]
    with jax.named_scope("output"):
        keep, send = call(
            kernel,
            (jax.ShapeDtypeStruct((share, width), F32),) * 2,
            [IN_SMEM] + [IN_VMEM] * 2,
            (IN_VMEM, IN_VMEM),
            scratch_shapes=[pltpu.VMEM((TOKENS, width), F32)] + scratch,
        )(core, attended, out_proj)
        half_sum = call(
            add_kernel,
            jax.ShapeDtypeStruct((share, width), F32),
            [IN_VMEM] * 2,
            IN_VMEM,
        )(keep, swap(send))
        if which == 0:
            half_sum, later = lax.optimization_barrier((half_sum, later))
            sides = (around_y(later, 1), around_y(later, -1))
        parts = exchange(half_sum.reshape(peers, part, width), "tp")
    with jax.named_scope("residual"):
        if which == LAYERS - 1:
            produced = call(
                last_residual_kernel,
                jax.ShapeDtypeStruct((peers, part, width), BF16),
                [IN_VMEM] * 2,
                IN_VMEM,
            )(parts, mine)
            mine = None
        else:
            mine, squares = call(
                functools.partial(residual_kernel, count),
                (
                    jax.ShapeDtypeStruct((part, width), BF16),
                    jax.ShapeDtypeStruct((count, 8, 128), F32),
                ),
                [IN_VMEM] * 2,
                (IN_VMEM, IN_VMEM),
            )(parts, mine)
            squares = exchange(squares, "kv")
            squares, before, after = lax.optimization_barrier((squares, sides[0][0], sides[1][1]))
            opposite = jnp.stack([around_y(before, 1), around_y(after, -1)])
            holders = near_holders(index[0])
            produced = call(
                spread_kernel,
                jax.ShapeDtypeStruct((peers, part, width + 128), BF16),
                [IN_VMEM] * 2,
                IN_VMEM,
            )(squares, mine)
        own = exchange(produced, "tp").reshape(share, -1)
        if which == 0:
            later = ((later,) + sides + (opposite,), all_logical[holders].reshape(-1), holders)
        return (own, swap(own)), mine, later


def per_device(
    segments_in, gain, query_weight, kv_weight, out_weight, kv_cache, block_logical, segment_block
):
    width = segments_in.shape[2]
    core = lax.axis_index("section")
    core_at = core.astype(jnp.int32)[None]
    index = lax.axis_index("kv").astype(jnp.int32)[None]
    per_core = GROUP * HEAD_DIM
    share = TOKENS // 2

    x = segments_in.reshape(TOKENS, width)
    count = lax.axis_size("kv")
    blocks = block_logical.shape[0]
    squares = call(
        functools.partial(squares_kernel, count),
        jax.ShapeDtypeStruct((count, 8, TOKENS), F32),
        [IN_VMEM] * 2,
        IN_VMEM,
    )(x, jnp.pad(block_logical.astype(F32), (0, TOKENS - blocks))[None])
    squares, query_weight, kv_weight, out_weight = lax.optimization_barrier(
        (squares, query_weight, kv_weight, out_weight)
    )

    def pick(which):
        at = which * per_core
        kv_at = which * HEAD_DIM
        return (
            lax.dynamic_slice_in_dim(query_weight[0], at, per_core, 1),
            lax.dynamic_slice_in_dim(kv_weight[0], kv_at, HEAD_DIM, 2).reshape(width, -1),
            lax.dynamic_slice_in_dim(out_weight[0], at, per_core, 0),
            gain,
        )

    kept = pick(core)
    received = tuple(swap(v) for v in pick(1 - core))
    part = share // lax.axis_size("tp")
    mine = lax.dynamic_slice_in_dim(x, core * share + lax.axis_index("tp") * part, part, 0)
    params = [
        [jnp.where(core == which, here, other) for here, other in zip(kept, received)]
        for which in range(LAYERS)
    ]

    def cut_cache(cache):
        def cut(which):
            return tuple(
                lax.dynamic_slice_in_dim(cache[0, :, kind], which * HEAD_DIM, HEAD_DIM, 1)
                for kind in range(2)
            )

        pairs = [(here, swap(there)) for here, there in zip(cut(core), cut(1 - core))]
        return tuple(
            call(
                cache_kernel,
                jax.ShapeDtypeStruct((2,) + pairs[0][0].shape, BF16),
                [IN_VMEM] * 2,
                IN_VMEM,
            )(*(jnp.where(core == which, here, other) for here, other in pairs))
            for which in range(LAYERS)
        )

    query_proj, kv_proj, out_proj, gain_row = params[0]
    first, mine, (caches, numbers, holders) = layer(
        0, x, mine, gain_row, query_proj, kv_proj, out_proj, kv_cache, cut_cache,
        block_logical, segment_block, index, core_at, squares,
    )
    query_proj, kv_proj, out_proj, gain_row = params[1]
    second, _, _ = layer(
        1, first, mine, gain_row, query_proj, kv_proj, out_proj, caches, None,
        numbers, segment_block, holders, core_at,
    )
    outputs = first + second
    result = call(
        choose_kernel,
        jax.ShapeDtypeStruct((TOKENS, width), BF16),
        [IN_SMEM] + [IN_VMEM] * 4,
        IN_VMEM,
    )(core_at, *outputs)
    return result.reshape(1, NSEG, SEG_LEN, width)


def solution(mesh):
    placed = (
        P(None, None, "kv"),
        P("section", "kv"),
        P("section", "kv", "tp"),
        P("section", "kv", None, "tp"),
        P("section", "tp", "kv"),
        P("section", "kv", None, "tp"),
        P("kv"),
        P(),
    )
    return jax.shard_map(
        per_device,
        mesh=mesh,
        in_specs=placed,
        out_specs=P("section", None, None, "kv"),
        check_vma=False,
    )
```
